32 devices in a mesh: gx: 8 (over z, y), gy: 4 (over x, core).
Axes of the slice: x: 2, y: 2, z: 4, core: 2. Of those that a mesh axis runs over, the one named last changes fastest.
Arguments:
- template: bfloat16 [256, 128, 256], P('gx', 'gy'), may hold values from -6 to 6
- target_image: bfloat16 [256, 128, 256], P('gx', 'gy'), may hold values from -6 to 6
- velocity: float32 [3, 256, 128, 256], P(None, 'gx', 'gy'), may hold values from -6 to 6
- operators: bfloat16 [64, 3, 32, 32], replicated, may hold values from -1 to 1
- route: int32 [2, 8, 4, 8, 1], P(None, 'gx', 'gy'), may hold values from 0 to 7; in each aligned block of 8 rows (0 to 7, 8 to 15, ..., all dimensions but the last counted through in order) at most 2 rows name the same one
- target_brick: int32 [2, 8, 4, 8], P(None, 'gx', 'gy'), may hold values from 0 to 7
- operator_index: int32 [2, 8, 4, 8], P(None, 'gx', 'gy'), may hold values from 0 to 63
Outputs:
- velocity_grad: float32 [3, 256, 128, 256], P(None, 'gx', 'gy')
- template_grad: bfloat16 [256, 128, 256], P('gx', 'gy')
The draws below stay inside these ranges and needn't reach their ends.
Inputs may be any that keep to these rules, and one draw needn't show every extreme that they name: `route`: in every step, no device sends more than 2 of its bricks to one destination device, and some device sends exactly 2 to one; the destination keeps the second index.
All inputs are finite; a program needn't handle non-finite values.
Results may differ from the reference program's by a relative error of at most 0.0085.
Values may be sent and summed in bfloat16 or wider, within the bound.
No kernel may reach another device: no remote copies, remote signals or barrier semaphores. Data moves between devices by JAX's collectives and lax.ppermute only.
A program may use at most 128 MiB of HBM per device.

```python
import math
import jax
import jax.numpy as jnp
import numpy as np
from jax import lax

BE = 32
ZB = 8
STEPS = 2
NW = 64
CAP = 2
ROWS_X = 8
ROWS_Y = 4
NX = 256
NY = 128
NZ = 256


def touch_ends(result, own_key, smallest, high):
    place = [jax.random.randint(jax.random.fold_in(own_key, axis), (), 0, length) for axis, length in enumerate(result.shape)]
    widest = result.shape.index(max(result.shape))
    neighbour = place[:widest] + [(place[widest] + 1) % result.shape[widest]] + place[widest + 1:]
    return result.at[tuple(place)].set(smallest).at[tuple(neighbour)].set(high)


def level_of(own_key, extent, cuts, smallest, top_value):
    gain = 1.0
    for position, blocks in cuts:
        draws = jax.random.uniform(jax.random.fold_in(jax.random.fold_in(own_key, 6), position), (blocks,), jnp.float32, smallest / len(cuts), top_value / len(cuts))
        gain = gain * jnp.repeat(jnp.exp(draws), extent[position] // blocks).reshape((-1,) + (1,) * (len(extent) - 1 - position))
    return gain


def deal_out(key, own, number, rows, amount, top, limit, lean):
    order = jax.random.permutation(key, amount)
    packed, usual = load_shares(amount, rows * top, limit, lean, True), load_shares(amount, rows * top, limit, lean, False)
    places = jnp.arange(amount)

    def named(lengths, turn):
        used = int((lengths > 0).sum())
        fixed = max(1, used // 4)
        moved = fixed + (places - fixed + turn * (used - fixed)) % max(1, amount - fixed)
        return jnp.zeros((amount,), jnp.int32).at[order[jnp.where(places < fixed, places, moved)]].set(jnp.asarray(lengths, jnp.int32))

    lengths = jnp.where(number % 4 == 0, named(packed, number // 4), named(usual, number - number // 4 - 1))
    mixed = jax.random.permutation(jax.random.fold_in(own, 3), amount)
    giver, sink = mixed[0:amount // 2 * 2:2], mixed[1:amount // 2 * 2:2]
    slack = jnp.minimum(lengths[giver] - 1, limit - lengths[sink]) // 2
    slack = jnp.where((giver == order[0]) | (sink == order[0]) | (lengths[sink] == 0), 0, jnp.maximum(slack, 0))
    moved = jax.random.randint(jax.random.fold_in(own, 4), (amount // 2,), 0, 1 << 20) % (slack + 1)
    lengths = lengths.at[giver].add(-moved).at[sink].add(moved)
    members = jnp.searchsorted(jnp.cumsum(lengths), jnp.arange(rows * top), side="right").astype(jnp.int32)
    listing = members.reshape(top, rows).T
    listing = listing[jax.random.permutation(jax.random.fold_in(own, 1), rows)]
    turn = jax.random.randint(jax.random.fold_in(own, 2), (rows, 1), 0, top)
    return jnp.take_along_axis(listing, (jnp.arange(top)[None, :] + turn) % top, axis=1)


def load_shares(number_of, total, limit, skew, full):
    loads = [(1 << 20) // math.isqrt(standing ** skew) + 1 for standing in range(1, number_of + 1)]
    largest = limit if full else min(limit, max(-(-total // number_of), total * loads[0] // sum(loads)))
    least = 1 if total - largest >= number_of - 1 else 0
    given, rest = [largest] + [least] * (number_of - 1), total - largest - least * (number_of - 1)
    while rest > 0:
        movable = [i for i in range(1, number_of) if given[i] < largest] or [i for i in range(1, number_of) if given[i] < limit]
        mass, budget = sum([loads[i] for i in movable]), rest
        for i in movable:
            more = min(limit - given[i], max(1, budget * loads[i] // mass), rest)
            given[i] = given[i] + more
            rest = rest - more
    return np.array(given)


def normal_values(stream_key, extent, spread, most, cuts=(), held_as=jnp.bfloat16):
    level = level_of(stream_key, extent, cuts, -0.22, 0.18) if cuts else 1.0
    result = jax.random.normal(stream_key, extent, jnp.float32) * spread * level
    return jnp.minimum(jnp.maximum(result, -most), most).astype(held_as)


def setup_inputs(seed: int = 0) -> dict:
    splits = jax.random.split(jax.random.key(seed), 8)
    template = normal_values(splits[0], (NX, NY, NZ), 1.0, 6.0, ((0, 8), (1, 4)))
    target_image = normal_values(splits[1], (NX, NY, NZ), 1.0, 6.0, ((0, 8), (1, 4)))
    velocity = normal_values(splits[2], (3, NX, NY, NZ), 1.0, 6.0, ((1, 8), (2, 4)), jnp.float32)
    operators = normal_values(splits[3], (NW, 3, BE, BE), BE ** -0.5, 1.0)
    route_keys = jax.random.split(jax.random.fold_in(splits[4], 1), STEPS * ROWS_X * ROWS_Y * ZB // ZB)
    route_turns = jax.random.permutation(jax.random.fold_in(splits[4], 3), STEPS * ROWS_X * ROWS_Y * ZB // ZB)
    route = jax.vmap(lambda own, number: deal_out(jax.random.fold_in(splits[4], 2), own, number, ZB, ROWS_X, 1, CAP, 2))(route_keys, route_turns).reshape((STEPS, ROWS_X, ROWS_Y, ZB, 1))
    target_brick = touch_ends(jax.random.randint(splits[5], (STEPS, ROWS_X, ROWS_Y, ZB), 0, ZB), jax.random.fold_in(splits[5], 1), 0, ZB - 1).astype(jnp.int32)
    operator_index = touch_ends(jax.random.randint(splits[6], (STEPS, ROWS_X, ROWS_Y, ZB), 0, NW), jax.random.fold_in(splits[6], 1), 0, NW - 1).astype(jnp.int32)
    return {"template": template, "target_image": target_image, "velocity": velocity, "operators": operators, "route": route, "target_brick": target_brick, "operator_index": operator_index}


HIGHEST_PRECISION = lax.Precision.HIGHEST


def to_bricks(field_in):
    shaped = field_in.reshape(ROWS_X, BE, ROWS_Y, BE, ZB, BE)
    return shaped.transpose(0, 2, 4, 1, 3, 5)


def from_bricks(bricks):
    return bricks.transpose(0, 3, 1, 4, 2, 5).reshape(ROWS_X * BE, ROWS_Y * BE, ZB * BE)


def apply_operator(matrices, bricks, flipped):
    matrices = matrices.astype(jnp.float32)
    values_f = bricks.astype(jnp.float32)
    if flipped:
        forms_list = ["...ax,...abc->...xbc", "...by,...xbc->...xyc", "...cz,...xyc->...xyz"]
    else:
        forms_list = ["...xa,...abc->...xbc", "...yb,...xbc->...xyc", "...zc,...xyc->...xyz"]
    for axis_id in range(3):
        values_f = jnp.einsum(forms_list[axis_id], matrices[..., axis_id, :, :], values_f, precision=HIGHEST_PRECISION)
    return values_f


def sixth_order(padded, axis_id):
    array_rank = padded.ndim

    def shifted(offset):
        slicer = []
        for dimension in range(array_rank):
            if dimension < array_rank - 3:
                slicer.append(slice(None))
            elif dimension == array_rank - 3 + axis_id:
                slicer.append(slice(3 + offset, padded.shape[dimension] - 3 + offset))
            else:
                slicer.append(slice(3, padded.shape[dimension] - 3))
        return padded[tuple(slicer)]

    return 0.75 * (shifted(1) - shifted(-1)) - 0.15 * (shifted(2) - shifted(-2)) + (shifted(3) - shifted(-3)) / 60.0


def pad_grid(field_in):
    widths = [(0, 0)] * (field_in.ndim - 3) + [(3, 3)] * 3
    return jnp.pad(field_in, widths)


def reference(template, target_image, velocity, operators, route, target_brick, operator_index):
    column = jnp.arange(ROWS_Y, dtype=jnp.int32)[None, :, None]
    states = [template]
    for section_id in range(STEPS):
        bricks = to_bricks(states[-1])
        matrices = operators[operator_index[section_id]]
        moved_bricks = apply_operator(matrices, bricks, False).astype(jnp.bfloat16)
        totals = jnp.zeros(bricks.shape, jnp.float32)
        totals = totals.at[route[section_id, :, :, :, 0], column, target_brick[section_id]].add(moved_bricks.astype(jnp.float32))
        states.append(from_bricks(totals.astype(jnp.bfloat16)))
    adjoint = (states[-1].astype(jnp.float32) - target_image.astype(jnp.float32)).astype(jnp.bfloat16)
    accumulated = jnp.zeros((3,) + template.shape, jnp.float32)
    for section_id in reversed(range(STEPS)):
        padded = pad_grid(states[section_id].astype(jnp.float32))
        weight = adjoint.astype(jnp.float32)
        accumulated = accumulated + jnp.stack([weight * sixth_order(padded, axis_id) for axis_id in range(3)])
        pulled = to_bricks(adjoint)[route[section_id, :, :, :, 0], column, target_brick[section_id]]
        matrices = operators[operator_index[section_id]]
        adjoint = from_bricks(apply_operator(matrices, pulled, True).astype(jnp.bfloat16))
    velocity_pad = pad_grid(velocity)
    divergence = sixth_order(velocity_pad[0], 0) + sixth_order(velocity_pad[1], 1) + sixth_order(velocity_pad[2], 2)
    divergence_pad = pad_grid(divergence)
    regular = jnp.stack([sixth_order(divergence_pad, axis_id) for axis_id in range(3)])
    velocity_grad = accumulated / STEPS - 0.25 * regular
    return velocity_grad, adjoint
```

```python
import functools

import jax
import jax.numpy as jnp
from jax import lax
from jax.experimental import pallas as pl
from jax.experimental.pallas import tpu as pltpu
from jax.sharding import PartitionSpec as P

STEPS = 2
CAP = 2
RIM = 3
F32 = jnp.float32
BF16 = jnp.bfloat16
NT = (((1,), (1,)), ((), ()))
NN = (((1,), (0,)), ((), ()))
TAPS = ((1, 0.75), (2, -0.15), (3, 1.0 / 60.0))


def iota(shape, dim):
    return lax.broadcasted_iota(jnp.int32, shape, dim)


def mm(left, right, dims=NN):
    return lax.dot_general(left, right, dims, preferred_element_type=F32)


def halves(value):
    high = value.astype(BF16)
    return high, (value - high.astype(F32)).astype(BF16)


def spread_rows(operators, picks, axis):
    rows = jnp.concatenate([operators[pick, axis] for pick in picks], axis=0)
    edge = rows.shape[1]
    lanes = edge * len(picks)
    copies = (iota((edge, lanes), 1) % edge == iota((edge, lanes), 0)).astype(F32).astype(BF16)
    return mm(rows, copies)


def same_block(size, edge):
    return iota((size, size), 0) // edge == iota((size, size), 1) // edge


def block_diagonal(spread, edge, flipped):
    size = spread.shape[0]
    matrix = jnp.where(same_block(size, edge), spread, 0.0).astype(BF16)
    if flipped:
        one = (iota((size, size), 0) == iota((size, size), 1)).astype(F32).astype(BF16)
        matrix = mm(one, matrix, NT).astype(BF16)
    return matrix


def swap_chunks(parts):
    lane = iota(parts[0].shape, 1)
    for bit, shift in ((1, 32), (2, 64)):
        keep = (lane & shift) == 0
        fresh = list(parts)
        for index in range(4):
            if index & bit:
                continue
            one, two = parts[index], parts[index | bit]
            fresh[index] = jnp.where(keep, one, pltpu.roll(two, shift, 1))
            fresh[index | bit] = jnp.where(keep, pltpu.roll(one, 128 - shift, 1), two)
        parts = fresh
    return parts


def swap_brick(block, folded, turned, brick):
    slabs = []
    for ph in range(4):
        slabs.append(
            jnp.concatenate(
                [
                    block[(qs // 2) * 32 + ph * 8 : (qs // 2) * 32 + ph * 8 + 8, (qs % 2) * 128 : (qs % 2) * 128 + 128]
                    for qs in range(8)
                ],
                axis=0,
            )
        )
    slabs = swap_chunks(slabs)
    for qh in range(4):
        folded[brick * 4 + qh] = slabs[qh]
    for ps in range(8):
        value = jnp.concatenate(
            [folded[brick * 4 + qh, pl.ds(ps, 8, stride=8), :] for qh in range(4)], axis=0
        )
        turned[brick * 32 : brick * 32 + 32, ps * 128 : ps * 128 + 128] = value


def middle_and_last(start, spread_mid, last, folded, turned, flipped):
    size = spread_mid.shape[0]
    bricks = size // 32
    mask = same_block(size, 32)
    for brick in range(bricks):
        rows = spread_mid[brick * 32 : brick * 32 + 32]
        line = jnp.where(mask, jnp.concatenate([rows] * 8, axis=0), 0.0).astype(BF16)
        block = start[brick * 32 : brick * 32 + 32, :]
        block = jnp.concatenate([block[:, g * 256 : g * 256 + 256] for g in range(4)], axis=0)
        high, low = halves(block)
        both = mm(jnp.concatenate([high, low], axis=0), line, NN if flipped else NT)
        swap_brick(both[:128] + both[128:], folded, turned, brick)
    out = []
    for g in range(4):
        high, low = halves(turned[:, g * 256 : g * 256 + 256])
        out.append(mm(last, high) + mm(last, low))
    return out


def slot_numbers(route, step, bricks):
    own = [route[step, 0, 0, b, 0] for b in range(bricks)]
    slots = []
    for b in range(bricks):
        rank = jnp.int32(0)
        for other in range(b):
            rank = rank + (own[other] == own[b]).astype(jnp.int32)
        slots.append(own[b] * CAP + rank)
    return slots


def forward_kernel(step, first, last, from_native, *refs):
    if from_native:
        picks, route, operators, field, send, start, folded, turned = refs
    else:
        picks, route, landing, operators, arrived, send, field, start, folded, turned, total = refs
    bricks = 8
    chosen = [picks[step, 0, 0, b] for b in range(bricks)]
    slots = slot_numbers(route, step, bricks)
    begin = block_diagonal(spread_rows(operators, chosen, first), 32, False)
    if from_native:
        for g in range(4):
            block = jnp.concatenate(
                [field[qh * 8 + qs] for qs in (2 * g, 2 * g + 1) for qh in range(4)], axis=0
            )
            start[:, g * 256 : g * 256 + 256] = mm(begin, block, NT)
    else:
        gather_sum(step - 1, landing, arrived, total)
        field[...] = total[...].astype(BF16)
        stored = field[...].reshape(256, 1024)
        for g in range(4):
            start[:, g * 256 : g * 256 + 256] = mm(begin, stored[:, g * 256 : g * 256 + 256])
    spread_mid = spread_rows(operators, chosen, 1)
    end = block_diagonal(spread_rows(operators, chosen, last), 32, False)
    out = middle_and_last(start, spread_mid, end, folded, turned, False)
    for g in range(4):
        moved = out[g].astype(BF16)
        for b in range(bricks):
            send[slots[b], :, g * 256 : g * 256 + 256] = moved[b * 32 : b * 32 + 32]


def gather_sum(step, landing, arrived, total):
    total[...] = jnp.zeros(total.shape, F32)

    def add(slot, carry):
        brick = landing[step, slot]

        @pl.when(brick >= 0)
        def _():
            total[brick] = total[brick] + arrived[slot].astype(F32)

        return carry

    lax.fori_loop(0, arrived.shape[0], add, 0)


def hand_out(step, landing, field, send):
    def put(slot, carry):
        brick = landing[step, slot]

        @pl.when(brick >= 0)
        def _():
            send[slot] = field[brick]

        return carry

    lax.fori_loop(0, send.shape[0], put, 0)


def residual_kernel(landing, arrived, target, send, adjoint, total):
    gather_sum(1, landing, arrived, total)
    for b in range(8):
        final = total[b].astype(BF16).astype(F32)
        adjoint[b] = (final - target[b].astype(F32)).astype(BF16)
    hand_out(1, landing, adjoint, send)


def backward_kernel(step, first, last, *refs):
    if step:
        picks, route, landing, operators, arrived, send, adjoint, start, folded, turned = refs
    else:
        picks, route, operators, arrived, adjoint, start, folded, turned = refs
    bricks = 8
    chosen = [picks[step, 0, 0, b] for b in range(bricks)]
    slots = slot_numbers(route, step, bricks)
    begin = block_diagonal(spread_rows(operators, chosen, first), 32, True)
    stored = jnp.concatenate([arrived[slots[b]] for b in range(bricks)], axis=0)
    for g in range(4):
        start[:, g * 256 : g * 256 + 256] = mm(begin, stored[:, g * 256 : g * 256 + 256])
    spread_mid = spread_rows(operators, chosen, 1)
    end = block_diagonal(spread_rows(operators, chosen, last), 32, True)
    out = middle_and_last(start, spread_mid, end, folded, turned, True)
    if step:
        for g in range(4):
            moved = out[g].astype(BF16)
            for b in range(bricks):
                adjoint[b, :, g * 256 : g * 256 + 256] = moved[b * 32 : b * 32 + 32]
        hand_out(0, landing, adjoint, send)
    else:
        for g in range(4):
            to_native(out[g].astype(BF16), g, adjoint)


def to_native(block, g, field):
    size = block.shape[0]
    one = (iota((size, size), 0) == iota((size, size), 1)).astype(F32).astype(BF16)
    flat = mm(one, block, NT).astype(field.dtype)
    for index in range(8):
        x = (index % 4) * 8 + 2 * g + index // 4
        field[x] = flat[index * 32 : index * 32 + 32]


def x_form_to_native(source, folded, turned, field):
    for b in range(8):
        block = source[b].astype(F32)
        block = jnp.concatenate([block[:, g * 256 : g * 256 + 256] for g in range(4)], axis=0)
        swap_brick(block, folded, turned, b)
    for g in range(4):
        to_native(turned[:, g * 256 : g * 256 + 256].astype(BF16), g, field)


def tap(offset):
    value = jnp.zeros(offset.shape, F32)
    for step, weight in TAPS:
        value = jnp.where(offset == step, weight, value)
        value = jnp.where(offset == -step, -weight, value)
    return value


def stencils():
    size = 256
    row, col = iota((size, size), 0), iota((size, size), 1)
    along_y = halves(jnp.where(row // 32 == col // 32, tap(col - row), 0.0))
    along_z = halves(tap(row - col))
    row, col = iota((size, 48), 0), iota((size, 48), 1)
    layer = col // 8
    place = jnp.where(layer < RIM, layer - RIM, layer - RIM + 32)
    rim_y = halves(jnp.where(row // 32 == col % 8, tap(place - row % 32), 0.0))
    return along_y, rim_y, along_z


def rim_picker():
    row, col = iota((48, 256), 0), iota((48, 256), 1)
    layer = row // 8
    place = jnp.where(layer < RIM, layer, layer - RIM + 29)
    return ((row % 8 == col // 32) & (place == col % 32)).astype(F32).astype(BF16)


def difference_x(padded, g):
    total = None
    for step, weight in TAPS:
        ahead = padded[pl.ds(8 * g + RIM + step, 8)]
        behind = padded[pl.ds(8 * g + RIM - step, 8)]
        term = weight * (ahead - behind)
        total = term if total is None else total + term
    return total.reshape(256, 256)


def difference_y(parts, rims, along_y, rim_y):
    total = mm(along_y[0], parts[0]) + mm(along_y[1], parts[0])
    if len(parts) > 1:
        total = total + mm(along_y[0], parts[1])
    return total + mm(rim_y[0], rims) + mm(rim_y[1], rims)


def difference_z(parts, along_z):
    total = mm(parts[0], along_z[0]) + mm(parts[0], along_z[1])
    if len(parts) > 1:
        total = total + mm(parts[1], along_z[0])
    return total


def rim_rows(before, after, base, g):
    rows = [before[base + h, (g // 2) * 16 : (g // 2) * 16 + 16, :].astype(F32) for h in range(RIM)]
    rows += [after[base + h, (g // 2) * 16 : (g // 2) * 16 + 16, :].astype(F32) for h in range(RIM)]
    half = (g % 2) * 8
    return jnp.concatenate([value[half : half + 8] for value in rows], axis=0).astype(BF16)


def put_rims(blocks, base, low_y, high_y):
    picker = rim_picker()
    for pair in range(2):
        left, right = mm(picker, blocks[2 * pair]), mm(picker, blocks[2 * pair + 1])
        for layer in range(2 * RIM):
            value = jnp.concatenate(
                [left[layer * 8 : layer * 8 + 8], right[layer * 8 : layer * 8 + 8]], axis=0
            ).astype(BF16)
            target = low_y if layer < RIM else high_y
            target[base + layer % RIM, pair * 16 : pair * 16 + 16, :] = value


def opening_kernel(template, target, first_x, last_x, mid_v, low_x, high_x, low_y, high_y, target_z):
    low_x[0:RIM] = template[0:RIM]
    high_x[0:RIM] = template[29:32]
    low_x[RIM : 2 * RIM] = first_x[0, 0:RIM].astype(BF16)
    high_x[RIM : 2 * RIM] = last_x[0, 1:4].astype(BF16)
    put_rims([template[8 * g : 8 * g + 8].reshape(256, 256) for g in range(4)], 0, low_y, high_y)
    put_rims([mid_v[0, 8 * g : 8 * g + 8].astype(BF16).reshape(256, 256) for g in range(4)], RIM, low_y, high_y)
    one = (iota((256, 256), 0) == iota((256, 256), 1)).astype(F32).astype(BF16)
    for g in range(4):
        block = jnp.concatenate(
            [target[qh * 8 + qs] for qs in (2 * g, 2 * g + 1) for qh in range(4)], axis=0
        )
        flat = mm(one, block, NT).astype(BF16)
        for b in range(8):
            target_z[b, :, g * 256 : g * 256 + 256] = flat[b * 32 : b * 32 + 32]


def divergence_kernel(velocity, before_x, after_x, before_y, after_y, divergence, padded):
    along_y, rim_y, along_z = stencils()
    padded[0:RIM] = before_x[RIM : 2 * RIM].astype(F32)
    padded[RIM : RIM + 32] = velocity[0]
    padded[RIM + 32 : 2 * RIM + 32] = after_x[RIM : 2 * RIM].astype(F32)
    for g in range(4):
        along_one = halves(velocity[1, 8 * g : 8 * g + 8].reshape(256, 256))
        along_two = halves(velocity[2, 8 * g : 8 * g + 8].reshape(256, 256))
        total = (
            difference_x(padded, g)
            + difference_y(along_one, rim_rows(before_y, after_y, RIM, g), along_y, rim_y)
            + difference_z(along_two, along_z)
        )
        divergence[8 * g : 8 * g + 8] = total.reshape(8, 32, 256)


def rims_kernel(state, divergence, native, low_x, high_x, low_y, high_y, folded, turned):
    x_form_to_native(state, folded, turned, native)
    low_x[0:RIM] = native[0:RIM]
    high_x[0:RIM] = native[29:32]
    low_x[RIM : 2 * RIM] = divergence[0:RIM].astype(BF16)
    high_x[RIM : 2 * RIM] = divergence[29:32].astype(BF16)
    put_rims([native[8 * g : 8 * g + 8].reshape(256, 256) for g in range(4)], 0, low_y, high_y)
    put_rims(
        [divergence[8 * g : 8 * g + 8].astype(BF16).reshape(256, 256) for g in range(4)], RIM, low_y, high_y
    )


def gradient_kernel(
    template,
    state,
    divergence,
    adjoint_two,
    adjoint_one,
    b0x,
    a0x,
    b0y,
    a0y,
    b1x,
    a1x,
    b1y,
    a1y,
    gradient,
    folded,
    turned,
    weight_two,
    weight_one,
    pad_zero,
    pad_one,
    pad_div,
):
    x_form_to_native(adjoint_one, folded, turned, weight_one)
    stored = adjoint_two[...].reshape(256, 1024)
    for g in range(4):
        to_native(stored[:, g * 256 : g * 256 + 256], g, weight_two)
    along_y, rim_y, along_z = stencils()
    for padded, before, middle, after, base in (
        (pad_zero, b0x, template, a0x, 0),
        (pad_one, b1x, state, a1x, 0),
        (pad_div, b1x, divergence, a1x, RIM),
    ):
        padded[0:RIM] = before[base : base + RIM].astype(F32)
        padded[RIM : RIM + 32] = middle[...].astype(F32)
        padded[RIM + 32 : 2 * RIM + 32] = after[base : base + RIM].astype(F32)
    for g in range(4):
        zero = (template[8 * g : 8 * g + 8].reshape(256, 256),)
        one = (state[8 * g : 8 * g + 8].reshape(256, 256),)
        div = halves(divergence[8 * g : 8 * g + 8].reshape(256, 256))
        weigh_one = 0.5 * weight_one[8 * g : 8 * g + 8].reshape(256, 256)
        weigh_two = 0.5 * weight_two[8 * g : 8 * g + 8].reshape(256, 256)
        for axis in range(3):
            if axis == 0:
                parts = [difference_x(padded, g) for padded in (pad_zero, pad_one, pad_div)]
            elif axis == 1:
                parts = [
                    difference_y(zero, rim_rows(b0y, a0y, 0, g), along_y, rim_y),
                    difference_y(one, rim_rows(b1y, a1y, 0, g), along_y, rim_y),
                    difference_y(div, rim_rows(b1y, a1y, RIM, g), along_y, rim_y),
                ]
            else:
                parts = [difference_z(value, along_z) for value in (zero, one, div)]
            value = weigh_one * parts[0] + weigh_two * parts[1] - 0.25 * parts[2]
            gradient[axis, 8 * g : 8 * g + 8] = value.reshape(8, 32, 256)


def plan_kernel(codes, landing):
    me = lax.axis_index("gx")
    for step in range(STEPS):

        def row(source, carry):
            for slot in range(CAP):
                landing[step, source * CAP + slot] = jnp.int32(-1)
            rank = jnp.int32(0)
            for b in range(8):
                code = codes[source, step * 8 + b]
                hit = (code >> 3) == me

                @pl.when(hit)
                def _():
                    landing[step, source * CAP + rank] = code & 7

                rank = rank + hit.astype(jnp.int32)
            return carry

        lax.fori_loop(0, codes.shape[0], row, 0)


SCALAR = pl.BlockSpec(memory_space=pltpu.SMEM)
WHOLE = pl.BlockSpec(memory_space=pltpu.VMEM)
FOLDED = (32, 64, 128)
FLAT = (256, 1024)
NATIVE = (32, 32, 256)
FORM = (8, 32, 1024)


def call(kernel, out, specs, scratch, cost):
    many = isinstance(out, (list, tuple))
    return pl.pallas_call(
        kernel,
        out_shape=out,
        in_specs=specs,
        out_specs=[WHOLE] * len(out) if many else WHOLE,
        scratch_shapes=scratch,
        compiler_params=pltpu.CompilerParams(vmem_limit_bytes=48 * 1024 * 1024),
        cost_estimate=pl.CostEstimate(flops=cost, bytes_accessed=8 * 1024 * 1024, transcendentals=0),
    )


def like(shape, dtype):
    return jax.ShapeDtypeStruct(shape, dtype)


def neighbours(low_x, high_x, low_y, high_y):
    moved = []
    for low, high, axis in ((low_x, high_x, "gx"), (low_y, high_y, "gy")):
        size = lax.axis_size(axis)
        up = [(i, i + 1) for i in range(size - 1)]
        down = [(i + 1, i) for i in range(size - 1)]
        moved += [lax.ppermute(high, axis, up), lax.ppermute(low, axis, down)]
    return moved


def swap_slots(send):
    return lax.all_to_all(send, "gx", split_axis=0, concat_axis=0, tiled=True)


def shards(template, target_image, velocity, operators, route, target_brick, operator_index):
    peers = lax.axis_size("gx")
    slots = like((peers * CAP, 32, 1024), BF16)
    turning = [pltpu.VMEM(FLAT, F32), pltpu.VMEM(FOLDED, F32), pltpu.VMEM(FLAT, F32)]
    total = [pltpu.VMEM(FORM, F32)]
    work = 1 << 31

    codes = (route[:, 0, 0, :, 0] * 8 + target_brick[:, 0, 0]).reshape(STEPS * 8)
    codes = lax.all_gather(codes, "gx")
    landing = pl.pallas_call(
        plan_kernel,
        out_shape=like((STEPS, peers * CAP), jnp.int32),
        in_specs=[SCALAR],
        out_specs=SCALAR,
    )(codes)

    send = call(
        functools.partial(forward_kernel, 0, 2, 0, True), slots, [SCALAR, SCALAR, WHOLE, WHOLE], turning, work
    )(operator_index, route, operators, template)
    arrived = swap_slots(send)

    rim = like((2 * RIM, 32, 256), BF16)
    low_x, high_x, low_y, high_y, target_z = pl.pallas_call(
        opening_kernel,
        out_shape=[rim] * 4 + [like(FORM, BF16)],
        grid=(1,),
        in_specs=[
            pl.BlockSpec(NATIVE, lambda i: (0, 0, 0)),
            pl.BlockSpec(NATIVE, lambda i: (0, 0, 0)),
            pl.BlockSpec((1, 4, 32, 256), lambda i: (0, 0, 0, 0)),
            pl.BlockSpec((1, 4, 32, 256), lambda i: (0, 7, 0, 0)),
            pl.BlockSpec((1, 32, 32, 256), lambda i: (1, 0, 0, 0)),
        ],
        out_specs=[pl.BlockSpec((2 * RIM, 32, 256), lambda i: (0, 0, 0))] * 4
        + [pl.BlockSpec(FORM, lambda i: (0, 0, 0))],
        compiler_params=pltpu.CompilerParams(vmem_limit_bytes=48 * 1024 * 1024),
        cost_estimate=pl.CostEstimate(flops=work, bytes_accessed=8 * 1024 * 1024, transcendentals=0),
    )(template, target_image, velocity, velocity, velocity)
    b0x, a0x, b0y, a0y = neighbours(low_x, high_x, low_y, high_y)
    divergence = call(
        divergence_kernel, like(NATIVE, F32), [WHOLE] * 5, [pltpu.VMEM((38, 32, 256), F32)], work
    )(velocity, b0x, a0x, b0y, a0y)

    send, state_x = call(
        functools.partial(forward_kernel, 1, 0, 2, False),
        [slots, like(FORM, BF16)],
        [SCALAR, SCALAR, SCALAR, WHOLE, WHOLE],
        turning + total,
        work,
    )(operator_index, route, landing, operators, arrived)
    arrived = swap_slots(send)

    state, low_x, high_x, low_y, high_y = call(
        rims_kernel,
        [like(NATIVE, BF16)] + [rim] * 4,
        [WHOLE] * 2,
        turning[1:],
        work,
    )(state_x, divergence)
    b1x, a1x, b1y, a1y = neighbours(low_x, high_x, low_y, high_y)

    send, adjoint_two = call(
        residual_kernel, [slots, like(FORM, BF16)], [SCALAR, WHOLE, WHOLE], total, work
    )(landing, arrived, target_z)
    arrived = swap_slots(send)

    send, adjoint_one = call(
        functools.partial(backward_kernel, 1, 2, 0),
        [slots, like(FORM, BF16)],
        [SCALAR, SCALAR, SCALAR, WHOLE, WHOLE],
        turning,
        work,
    )(operator_index, route, landing, operators, arrived)
    arrived = swap_slots(send)

    gradient = call(
        gradient_kernel,
        like((3,) + NATIVE, F32),
        [WHOLE] * 13,
        turning[1:] + [pltpu.VMEM(NATIVE, F32)] * 2 + [pltpu.VMEM((38, 32, 256), F32)] * 3,
        work,
    )(template, state, divergence, adjoint_two, adjoint_one, b0x, a0x, b0y, a0y, b1x, a1x, b1y, a1y)

    adjoint = call(
        functools.partial(backward_kernel, 0, 0, 2),
        like(NATIVE, BF16),
        [SCALAR, SCALAR, WHOLE, WHOLE],
        turning,
        work,
    )(operator_index, route, operators, arrived)
    return gradient, adjoint


def solution(mesh):
    placed = (
        P("gx", "gy", None),
        P("gx", "gy", None),
        P(None, "gx", "gy", None),
        P(),
        P(None, "gx", "gy", None, None),
        P(None, "gx", "gy", None),
        P(None, "gx", "gy", None),
    )
    return jax.shard_map(
        shards,
        mesh=mesh,
        in_specs=placed,
        out_specs=(P(None, "gx", "gy", None), P("gx", "gy", None)),
        check_vma=False,
    )
```

```python
import functools

import jax
import jax.numpy as jnp
from jax import lax
from jax.experimental import pallas as pl
from jax.experimental.pallas import tpu as pltpu
from jax.sharding import PartitionSpec as P

STEPS = 2
CAP = 2
RIM = 3
F32 = jnp.float32
BF16 = jnp.bfloat16
NT = (((1,), (1,)), ((), ()))
NN = (((1,), (0,)), ((), ()))
TAPS = ((1, 0.75), (2, -0.15), (3, 1.0 / 60.0))


def iota(shape, dim):
    return lax.broadcasted_iota(jnp.int32, shape, dim)


def mm(left, right, dims=NN):
    return lax.dot_general(left, right, dims, preferred_element_type=F32)


def halves(value):
    high = value.astype(BF16)
    return high, (value - high.astype(F32)).astype(BF16)


def table_rows(operators, picks, axis):
    lane = iota((operators.shape[1], 256), 1)
    chosen = jnp.zeros(lane.shape, jnp.int32)
    for b, pick in enumerate(picks):
        chosen = jnp.where(lane // 32 == b, pick, chosen)
    one_hot = (iota(lane.shape, 0) == chosen).astype(F32).astype(BF16)
    found = mm(operators[axis * 1024 : axis * 1024 + 1024, :], one_hot)
    within = iota((32, 256), 1) % 32
    total = jnp.zeros((32, 256), F32)
    for x in range(32):
        total = jnp.where(within == x, found[x * 32 : x * 32 + 32], total)
    return total


def same_block(size, edge):
    return iota((size, size), 0) // edge == iota((size, size), 1) // edge


def identity():
    return (iota((256, 256), 0) == iota((256, 256), 1)).astype(F32).astype(BF16)


def flipped_diagonal(table):
    return jnp.where(same_block(256, 32), jnp.concatenate([table] * 8, axis=0), 0.0).astype(BF16)


def diagonal(table):
    return mm(identity(), flipped_diagonal(table), NT).astype(BF16)


def spread(table):
    copies = (iota((256, 256), 0) % 32 == iota((256, 256), 1) % 32).astype(F32).astype(BF16)
    return mm(flipped_diagonal(table), copies)


def swap_chunks(parts):
    lane = iota(parts[0].shape, 1)
    for bit, shift in ((1, 32), (2, 64)):
        keep = (lane & shift) == 0
        fresh = list(parts)
        for index in range(4):
            if index & bit:
                continue
            one, two = parts[index], parts[index | bit]
            fresh[index] = jnp.where(keep, one, pltpu.roll(two, shift, 1))
            fresh[index | bit] = jnp.where(keep, pltpu.roll(one, 128 - shift, 1), two)
        parts = fresh
    return parts


def swap_brick(block, folded, turned, brick):
    slabs = []
    for ph in range(4):
        slabs.append(
            jnp.concatenate(
                [
                    block[(qs // 2) * 32 + ph * 8 : (qs // 2) * 32 + ph * 8 + 8, (qs % 2) * 128 : (qs % 2) * 128 + 128]
                    for qs in range(8)
                ],
                axis=0,
            )
        )
    slabs = swap_chunks(slabs)
    for qh in range(4):
        folded[brick * 4 + qh] = slabs[qh]
    for ps in range(8):
        value = jnp.concatenate(
            [folded[brick * 4 + qh, pl.ds(ps, 8, stride=8), :] for qh in range(4)], axis=0
        )
        turned[brick * 32 : brick * 32 + 32, ps * 128 : ps * 128 + 128] = value


def lane_pair(field, g):
    return jnp.concatenate(
        [
            jnp.concatenate([field[b, qs * 32 : qs * 32 + 32, :] for b in range(8)], axis=0)
            for qs in (2 * g, 2 * g + 1)
        ],
        axis=1,
    )


def put_pair(field, g, value):
    for b in range(8):
        for half in range(2):
            rows = slice((2 * g + half) * 32, (2 * g + half) * 32 + 32)
            field[b, rows, :] = value[b * 32 : b * 32 + 32, half * 128 : half * 128 + 128]


def middle_and_last(start, spread_mid, last, folded, turned, flipped):
    mask = same_block(256, 32)
    for brick in range(8):
        rows = spread_mid[brick * 32 : brick * 32 + 32]
        line = jnp.where(mask, jnp.concatenate([rows] * 8, axis=0), 0.0).astype(BF16)
        block = start[brick * 32 : brick * 32 + 32, :]
        block = jnp.concatenate([block[:, g * 256 : g * 256 + 256] for g in range(4)], axis=0)
        high, low = halves(block)
        both = mm(jnp.concatenate([high, low], axis=0), line, NT if flipped else NN)
        swap_brick(both[:128] + both[128:], folded, turned, brick)
    for g in range(4):
        high, low = halves(turned[:, g * 256 : g * 256 + 256])
        yield g, (mm(last, high) + mm(last, low)).astype(BF16)


def slot_numbers(route, step):
    own = [route[step, 0, 0, b] for b in range(8)]
    slots = []
    for b in range(8):
        rank = jnp.int32(0)
        for other in range(b):
            rank = rank + (own[other] == own[b]).astype(jnp.int32)
        slots.append((own[b], rank))
    return slots


def fetch(source, target, sem):
    copy = pltpu.make_async_copy(source, target, sem)
    copy.start()
    return copy


def chunk(send, place):
    return send.at[place[0], pl.ds(pl.multiple_of(place[1] * 256, 256), 256), :]


def send_bricks(bricks, send, slots, sems):
    for copy in [fetch(bricks.at[b], chunk(send, slots[b]), sems.at[b]) for b in range(8)]:
        copy.wait()


def first_kernel(picks, route, landing, operators, field, send, tables, table_mem, field_mem, start, folded, turned, out, meta, meta_half, sems):
    loads = [fetch(operators, table_mem, sems.at[8]), fetch(field, field_mem, sems.at[9])]
    meta[...] = jnp.zeros(meta.shape, F32)
    for step in range(STEPS):
        for b, (place, rank) in enumerate(slot_numbers(route, step)):
            value = jnp.full((1, 128), landing[step, 0, 0, b] + 1, jnp.int32).astype(F32)
            meta[place, pl.ds(step * CAP + rank, 1), :] = value
    meta_half[...] = meta[...].astype(BF16)
    told = fetch(meta_half, send.at[:, 512:528, :], sems.at[10])
    chosen = [picks[0, 0, 0, b] for b in range(8)]
    loads[0].wait()
    found = [table_rows(table_mem, chosen, axis) for axis in range(3)]
    for axis in range(3):
        tables[axis] = found[axis].astype(BF16)
    begin = diagonal(found[2])
    loads[1].wait()
    for g in range(4):
        block = jnp.concatenate(
            [field_mem[qh * 8 + qs] for qs in (2 * g, 2 * g + 1) for qh in range(4)], axis=0
        )
        start[:, g * 256 : g * 256 + 256] = mm(begin, block, NT)
    for g, moved in middle_and_last(start, spread(found[1]), diagonal(found[0]), folded, turned, False):
        put_pair(out, g, moved)
    send_bricks(out, send, slot_numbers(route, 0), sems)
    told.wait()


def second_kernel(route, tables, arrived, *refs):
    send, state, landing_out, arrived_mem, meta_half, meta, landing, state_mem, total, start, folded, turned, out, sems = refs[-14:]
    loads = [
        fetch(arrived.at[:, 512:528, :], meta_half, sems.at[9]),
        fetch(arrived.at[:, 0:512, :], arrived_mem, sems.at[8]),
    ]
    begin = diagonal(tables[0].astype(F32))
    mid = spread(tables[1].astype(F32))
    end = diagonal(tables[2].astype(F32))
    loads[0].wait()
    meta[...] = meta_half[...].astype(F32).astype(jnp.int32)[:, 0:8, :]
    told = [fetch(meta, landing, sems.at[9]), fetch(meta, landing_out, sems.at[10])]
    total[...] = jnp.zeros(total.shape, F32)
    loads[1].wait()
    told[0].wait()
    gather_sum(0, landing, arrived_mem, total)
    for b in range(8):
        state_mem[b] = total[b].astype(BF16)
    kept = fetch(state_mem, state, sems.at[9])
    for g in range(4):
        start[:, g * 256 : g * 256 + 256] = mm(begin, lane_pair(state_mem, g))
    for g, moved in middle_and_last(start, mid, end, folded, turned, False):
        put_pair(out, g, moved)
    send_bricks(out, send, slot_numbers(route, 1), sems)
    kept.wait()
    told[1].wait()


def gather_sum(step, landing, arrived, total):
    def add(source, carry):
        for rank in range(CAP):
            brick = landing[source, step * CAP + rank, 0]

            @pl.when(brick > 0)
            def _():
                total[brick - 1] += arrived[source, rank * 256 : rank * 256 + 256, :].astype(F32)

        return carry

    lax.fori_loop(0, arrived.shape[0], add, 0)


def hand_out(step, landing, field, send, sems):
    def each(act):
        def body(source, carry):
            for rank in range(CAP):
                brick = landing[source, step * CAP + rank, 0]

                @pl.when(brick > 0)
                def _():
                    act(
                        pltpu.make_async_copy(
                            field.at[brick - 1],
                            send.at[source, rank * 256 : rank * 256 + 256, :],
                            sems.at[source * CAP + rank],
                        )
                    )

            return carry

        lax.fori_loop(0, send.shape[0], body, 0)

    each(lambda copy: copy.start())
    each(lambda copy: copy.wait())


def third_kernel(landing_in, arrived, target, *refs):
    send, adjoint, arrived_mem, landing, total, adjoint_mem, target_mem, sems, slot_sems = refs[-9:]
    loads = [
        fetch(landing_in, landing, sems.at[0]),
        fetch(arrived, arrived_mem, sems.at[1]),
        fetch(target, target_mem, sems.at[2]),
    ]
    total[...] = jnp.zeros(total.shape, F32)
    for load in loads:
        load.wait()
    gather_sum(1, landing, arrived_mem, total)
    for b in range(8):
        final = total[b].astype(BF16).astype(F32)
        adjoint_mem[b] = (final - target_mem[b].astype(F32)).astype(BF16)
    kept = fetch(adjoint_mem, adjoint, sems.at[0])
    hand_out(1, landing, adjoint_mem, send, slot_sems)
    kept.wait()


def pull_bricks(arrived, bricks, slots, sems):
    return [fetch(chunk(arrived, slots[b]), bricks.at[b], sems.at[b]) for b in range(8)]


def fourth_kernel(route, tables, landing_in, arrived, *refs):
    send, adjoint, bricks, landing, start, folded, turned, out, sems, slot_sems = refs[-10:]
    loads = pull_bricks(arrived, bricks, slot_numbers(route, 1), sems)
    told = fetch(landing_in, landing, sems.at[8])
    begin = flipped_diagonal(tables[2].astype(F32))
    mid = spread(tables[1].astype(F32))
    end = flipped_diagonal(tables[0].astype(F32))
    for load in loads:
        load.wait()
    for g in range(4):
        start[:, g * 256 : g * 256 + 256] = mm(begin, lane_pair(bricks, g))
    for g, moved in middle_and_last(start, mid, end, folded, turned, True):
        put_pair(out, g, moved)
    kept = fetch(out, adjoint, sems.at[0])
    told.wait()
    hand_out(0, landing, out, send, slot_sems)
    kept.wait()


def fifth_kernel(route, tables, arrived, *refs):
    adjoint, bricks, start, folded, turned, sems = refs[-6:]
    loads = pull_bricks(arrived, bricks, slot_numbers(route, 0), sems)
    begin = flipped_diagonal(tables[0].astype(F32))
    mid = spread(tables[1].astype(F32))
    end = flipped_diagonal(tables[2].astype(F32))
    for load in loads:
        load.wait()
    for g in range(4):
        start[:, g * 256 : g * 256 + 256] = mm(begin, lane_pair(bricks, g))
    for g, moved in middle_and_last(start, mid, end, folded, turned, True):
        to_native(moved, g, adjoint)


def to_native(block, g, field):
    flat = mm(identity(), block, NT).astype(field.dtype)
    for index in range(8):
        x = (index % 4) * 8 + 2 * g + index // 4
        field[x] = flat[index * 32 : index * 32 + 32]


def x_form_to_native(source, folded, turned, field):
    for b in range(8):
        block = source[b].astype(F32)
        block = jnp.concatenate(
            [
                jnp.concatenate([block[g * 64 : g * 64 + 32], block[g * 64 + 32 : g * 64 + 64]], axis=1)
                for g in range(4)
            ],
            axis=0,
        )
        swap_brick(block, folded, turned, b)
    for g in range(4):
        to_native(turned[:, g * 256 : g * 256 + 256].astype(BF16), g, field)


def tap(offset):
    value = jnp.zeros(offset.shape, F32)
    for step, weight in TAPS:
        value = jnp.where(offset == step, weight, value)
        value = jnp.where(offset == -step, -weight, value)
    return value


def stencils():
    size = 256
    row, col = iota((size, size), 0), iota((size, size), 1)
    along_y = halves(jnp.where(row // 32 == col // 32, tap(col - row), 0.0))
    along_z = halves(tap(row - col))
    row, col = iota((size, 48), 0), iota((size, 48), 1)
    layer = col // 8
    place = jnp.where(layer < RIM, layer - RIM, layer - RIM + 32)
    rim_y = halves(jnp.where(row // 32 == col % 8, tap(place - row % 32), 0.0))
    return along_y, rim_y, along_z


def rim_picker():
    row, col = iota((48, 256), 0), iota((48, 256), 1)
    layer = row // 8
    place = jnp.where(layer < RIM, layer, layer - RIM + 29)
    return ((row % 8 == col // 32) & (place == col % 32)).astype(F32).astype(BF16)


def difference_x(padded, g):
    total = None
    for step, weight in TAPS:
        ahead = padded[pl.ds(8 * g + RIM + step, 8)]
        behind = padded[pl.ds(8 * g + RIM - step, 8)]
        term = weight * (ahead - behind)
        total = term if total is None else total + term
    return total.reshape(256, 256)


def difference_y(parts, rims, along_y, rim_y):
    total = mm(along_y[0], parts[0]) + mm(along_y[1], parts[0])
    if len(parts) > 1:
        total = total + mm(along_y[0], parts[1])
    return total + mm(rim_y[0], rims) + mm(rim_y[1], rims)


def difference_z(parts, along_z):
    total = mm(parts[0], along_z[0]) + mm(parts[0], along_z[1])
    if len(parts) > 1:
        total = total + mm(parts[1], along_z[0])
    return total


def rim_rows(before, after, base, g):
    rows = [before[base + h, (g // 2) * 16 : (g // 2) * 16 + 16, :].astype(F32) for h in range(RIM)]
    rows += [after[base + h, (g // 2) * 16 : (g // 2) * 16 + 16, :].astype(F32) for h in range(RIM)]
    half = (g % 2) * 8
    return jnp.concatenate([value[half : half + 8] for value in rows], axis=0).astype(BF16)


def put_rims(blocks, base, low_y, high_y):
    picker = rim_picker()
    for pair in range(2):
        left, right = mm(picker, blocks[2 * pair]), mm(picker, blocks[2 * pair + 1])
        for layer in range(2 * RIM):
            value = jnp.concatenate(
                [left[layer * 8 : layer * 8 + 8], right[layer * 8 : layer * 8 + 8]], axis=0
            ).astype(BF16)
            target = low_y if layer < RIM else high_y
            target[base + layer % RIM, pair * 16 : pair * 16 + 16, :] = value


def opening_kernel(picks, operators, template, target, first_x, last_x, mid_v, sent, low_x, high_x, low_y, high_y, target_z, tables):
    chosen = [picks[1, 0, 0, b] for b in range(8)]
    for axis in range(3):
        tables[axis] = table_rows(operators, chosen, axis).astype(BF16)
    low_x[0:RIM] = template[0:RIM]
    high_x[0:RIM] = template[29:32]
    low_x[RIM : 2 * RIM] = first_x[0, 0:RIM].astype(BF16)
    high_x[RIM : 2 * RIM] = last_x[0, 1:4].astype(BF16)
    put_rims([template[8 * g : 8 * g + 8].reshape(256, 256) for g in range(4)], 0, low_y, high_y)
    put_rims([mid_v[0, 8 * g : 8 * g + 8].astype(BF16).reshape(256, 256) for g in range(4)], RIM, low_y, high_y)
    for g in range(4):
        block = jnp.concatenate(
            [target[qh * 8 + qs] for qs in (2 * g, 2 * g + 1) for qh in range(4)], axis=0
        )
        put_pair(target_z, g, mm(identity(), block, NT).astype(BF16))


def divergence_kernel(velocity, before_x, after_x, before_y, after_y, divergence, padded):
    along_y, rim_y, along_z = stencils()
    padded[0:RIM] = before_x[RIM : 2 * RIM].astype(F32)
    padded[RIM : RIM + 32] = velocity[0]
    padded[RIM + 32 : 2 * RIM + 32] = after_x[RIM : 2 * RIM].astype(F32)
    for g in range(4):
        along_one = halves(velocity[1, 8 * g : 8 * g + 8].reshape(256, 256))
        along_two = halves(velocity[2, 8 * g : 8 * g + 8].reshape(256, 256))
        total = (
            difference_x(padded, g)
            + difference_y(along_one, rim_rows(before_y, after_y, RIM, g), along_y, rim_y)
            + difference_z(along_two, along_z)
        )
        divergence[8 * g : 8 * g + 8] = total.reshape(8, 32, 256)


def rims_kernel(state, divergence, sent, native, low_x, high_x, low_y, high_y, folded, turned):
    x_form_to_native(state, folded, turned, native)
    low_x[0:RIM] = native[0:RIM]
    high_x[0:RIM] = native[29:32]
    low_x[RIM : 2 * RIM] = divergence[0:RIM].astype(BF16)
    high_x[RIM : 2 * RIM] = divergence[29:32].astype(BF16)
    put_rims([native[8 * g : 8 * g + 8].reshape(256, 256) for g in range(4)], 0, low_y, high_y)
    put_rims(
        [divergence[8 * g : 8 * g + 8].astype(BF16).reshape(256, 256) for g in range(4)], RIM, low_y, high_y
    )


def gradient_kernel(
    template,
    state,
    divergence,
    adjoint_two,
    adjoint_one,
    b0x,
    a0x,
    b0y,
    a0y,
    b1x,
    a1x,
    b1y,
    a1y,
    sent,
    gradient,
    folded,
    turned,
    weight_two,
    weight_one,
    pad_zero,
    pad_one,
    pad_div,
):
    x_form_to_native(adjoint_one, folded, turned, weight_one)
    for g in range(4):
        to_native(lane_pair(adjoint_two, g), g, weight_two)
    along_y, rim_y, along_z = stencils()
    for padded, before, middle, after, base in (
        (pad_zero, b0x, template, a0x, 0),
        (pad_one, b1x, state, a1x, 0),
        (pad_div, b1x, divergence, a1x, RIM),
    ):
        padded[0:RIM] = before[base : base + RIM].astype(F32)
        padded[RIM : RIM + 32] = middle[...].astype(F32)
        padded[RIM + 32 : 2 * RIM + 32] = after[base : base + RIM].astype(F32)
    for g in range(4):
        zero = (template[8 * g : 8 * g + 8].reshape(256, 256),)
        one = (state[8 * g : 8 * g + 8].reshape(256, 256),)
        div = halves(divergence[8 * g : 8 * g + 8].reshape(256, 256))
        weigh_one = 0.5 * weight_one[8 * g : 8 * g + 8].reshape(256, 256)
        weigh_two = 0.5 * weight_two[8 * g : 8 * g + 8].reshape(256, 256)
        for axis in range(3):
            if axis == 0:
                parts = [difference_x(padded, g) for padded in (pad_zero, pad_one, pad_div)]
            elif axis == 1:
                parts = [
                    difference_y(zero, rim_rows(b0y, a0y, 0, g), along_y, rim_y),
                    difference_y(one, rim_rows(b1y, a1y, 0, g), along_y, rim_y),
                    difference_y(div, rim_rows(b1y, a1y, RIM, g), along_y, rim_y),
                ]
            else:
                parts = [difference_z(value, along_z) for value in (zero, one, div)]
            value = weigh_one * parts[0] + weigh_two * parts[1] - 0.25 * parts[2]
            gradient[axis, 8 * g : 8 * g + 8] = value.reshape(8, 32, 256)


SCALAR = pl.BlockSpec(memory_space=pltpu.SMEM)
WHOLE = pl.BlockSpec(memory_space=pltpu.VMEM)
FAR = pl.BlockSpec(memory_space=pltpu.HBM)
FOLDED = (32, 64, 128)
FLAT = (256, 1024)
NATIVE = (32, 32, 256)
FORM = (8, 256, 128)
TABLES = (3, 32, 256)


def call(kernel, out, in_specs, out_specs, scratch, work=1 << 31):
    return pl.pallas_call(
        kernel,
        out_shape=out,
        in_specs=in_specs,
        out_specs=out_specs,
        scratch_shapes=scratch,
        compiler_params=pltpu.CompilerParams(vmem_limit_bytes=48 * 1024 * 1024),
        cost_estimate=pl.CostEstimate(flops=work, bytes_accessed=8 * 1024 * 1024, transcendentals=0),
    )


def like(shape, dtype):
    return jax.ShapeDtypeStruct(shape, dtype)


def neighbours(low_x, high_x, low_y, high_y):
    moved = []
    for low, high, axis in ((low_x, high_x, "gx"), (low_y, high_y, "gy")):
        size = lax.axis_size(axis)
        up = [(i, i + 1) for i in range(size - 1)]
        down = [(i + 1, i) for i in range(size - 1)]
        moved += [lax.ppermute(high, axis, up), lax.ppermute(low, axis, down)]
    return moved


def swap_slots(send):
    return lax.all_to_all(send, "gx", split_axis=0, concat_axis=0, tiled=True)


def shards(template, target_image, velocity, operators, route, target_brick, operator_index):
    peers = lax.axis_size("gx")
    sems = pltpu.SemaphoreType.DMA((16,))
    slot_sems = pltpu.SemaphoreType.DMA((peers * CAP,))
    turning = [pltpu.VMEM(FLAT, F32), pltpu.VMEM(FOLDED, F32), pltpu.VMEM(FLAT, F32)]
    form = pltpu.VMEM(FORM, BF16)
    total = pltpu.VMEM(FORM, F32)
    landed = pltpu.SMEM((peers, 8, 128), jnp.int32)
    slots = like((peers, 512, 128), BF16)
    table_rows_count = operators.shape[1] * operators.shape[2] * operators.shape[3]
    listed = operators.transpose(1, 2, 3, 0).reshape(table_rows_count, operators.shape[0])
    route = route.reshape(route.shape[:4])

    send, tables_zero = call(
        first_kernel,
        [like((peers, 528, 128), BF16), like(TABLES, BF16)],
        [SCALAR, SCALAR, SCALAR, FAR, FAR],
        [FAR, WHOLE],
        [pltpu.VMEM(listed.shape, BF16), pltpu.VMEM(NATIVE, BF16)]
        + turning
        + [form, pltpu.VMEM((peers, 16, 128), F32), pltpu.VMEM((peers, 16, 128), BF16), sems],
    )(operator_index, route, target_brick, listed, template)
    arrived = swap_slots(send)

    rim = like((2 * RIM, 32, 256), BF16)
    rim_spec = pl.BlockSpec((2 * RIM, 32, 256), lambda i: (0, 0, 0))
    low_x, high_x, low_y, high_y, target_z, tables_one = pl.pallas_call(
        opening_kernel,
        out_shape=[rim] * 4 + [like(FORM, BF16), like(TABLES, BF16)],
        grid=(1,),
        in_specs=[
            SCALAR,
            pl.BlockSpec(listed.shape, lambda i: (0, 0)),
            pl.BlockSpec(NATIVE, lambda i: (0, 0, 0)),
            pl.BlockSpec(NATIVE, lambda i: (0, 0, 0)),
            pl.BlockSpec((1, 4, 32, 256), lambda i: (0, 0, 0, 0)),
            pl.BlockSpec((1, 4, 32, 256), lambda i: (0, 7, 0, 0)),
            pl.BlockSpec((1, 32, 32, 256), lambda i: (1, 0, 0, 0)),
            FAR,
        ],
        out_specs=[rim_spec] * 4
        + [pl.BlockSpec(FORM, lambda i: (0, 0, 0)), pl.BlockSpec(TABLES, lambda i: (0, 0, 0))],
        compiler_params=pltpu.CompilerParams(vmem_limit_bytes=48 * 1024 * 1024),
        cost_estimate=pl.CostEstimate(flops=1 << 31, bytes_accessed=8 * 1024 * 1024, transcendentals=0),
    )(operator_index, listed, template, target_image, velocity, velocity, velocity, send)
    b0x, a0x, b0y, a0y = neighbours(low_x, high_x, low_y, high_y)
    divergence = call(
        divergence_kernel, like(NATIVE, F32), [WHOLE] * 5, WHOLE, [pltpu.VMEM((38, 32, 256), F32)]
    )(velocity, b0x, a0x, b0y, a0y)

    send, state_x, landing = call(
        second_kernel,
        [slots, like(FORM, BF16), like((peers, 8, 128), jnp.int32)],
        [SCALAR, WHOLE, FAR, FAR],
        [FAR] * 3,
        [
            pltpu.VMEM((peers, 512, 128), BF16),
            pltpu.VMEM((peers, 16, 128), BF16),
            pltpu.VMEM((peers, 8, 128), jnp.int32),
            landed,
            form,
            total,
        ]
        + turning
        + [form, sems],
    )(route, tables_one, arrived, divergence)
    arrived = swap_slots(send)

    state, low_x, high_x, low_y, high_y = call(
        rims_kernel, [like(NATIVE, BF16)] + [rim] * 4, [WHOLE] * 2 + [FAR], [WHOLE] * 5, turning[1:]
    )(state_x, divergence, send)
    b1x, a1x, b1y, a1y = neighbours(low_x, high_x, low_y, high_y)

    send, adjoint_two = call(
        third_kernel,
        [slots, like(FORM, BF16)],
        [FAR] * 7,
        [FAR] * 2,
        [pltpu.VMEM((peers, 512, 128), BF16), landed, total, form, form, sems, slot_sems],
    )(landing, arrived, target_z, b1x, a1x, b1y, a1y)
    arrived = swap_slots(send)

    send, adjoint_one = call(
        fourth_kernel,
        [slots, like(FORM, BF16)],
        [SCALAR, WHOLE, FAR, FAR],
        [FAR] * 2,
        [form, landed] + turning + [form, sems, slot_sems],
    )(route, tables_one, landing, arrived)
    arrived = swap_slots(send)

    gradient = call(
        gradient_kernel,
        like((3,) + NATIVE, F32),
        [WHOLE] * 13 + [FAR],
        WHOLE,
        turning[1:] + [pltpu.VMEM(NATIVE, F32)] * 2 + [pltpu.VMEM((38, 32, 256), F32)] * 3,
    )(template, state, divergence, adjoint_two, adjoint_one, b0x, a0x, b0y, a0y, b1x, a1x, b1y, a1y, send)

    adjoint = call(
        fifth_kernel, like(NATIVE, BF16), [SCALAR, WHOLE, FAR, FAR], WHOLE, [form] + turning + [sems]
    )(route, tables_zero, arrived, gradient)
    return gradient, adjoint


def solution(mesh):
    placed = (
        P("gx", "gy", None),
        P("gx", "gy", None),
        P(None, "gx", "gy", None),
        P(),
        P(None, "gx", "gy", None, None),
        P(None, "gx", "gy", None),
        P(None, "gx", "gy", None),
    )
    return jax.shard_map(
        shards,
        mesh=mesh,
        in_specs=placed,
        out_specs=(P(None, "gx", "gy", None), P("gx", "gy", None)),
        check_vma=False,
    )
```

```python
import functools

import jax
import jax.numpy as jnp
from jax import lax
from jax.experimental import pallas as pl
from jax.experimental.pallas import tpu as pltpu
from jax.sharding import PartitionSpec as P

STEPS = 2
CAP = 2
RIM = 3
F32 = jnp.float32
BF16 = jnp.bfloat16
NT = (((1,), (1,)), ((), ()))
NN = (((1,), (0,)), ((), ()))
TAPS = ((1, 0.75), (2, -0.15), (3, 1.0 / 60.0))


def iota(shape, dim):
    return lax.broadcasted_iota(jnp.int32, shape, dim)


def mm(left, right, dims=NN):
    return lax.dot_general(left, right, dims, preferred_element_type=F32)


def halves(value):
    high = value.astype(BF16)
    return high, (value - high.astype(F32)).astype(BF16)


def table_rows(operators, picks, axis):
    lane = iota((operators.shape[1], 256), 1)
    chosen = jnp.zeros(lane.shape, jnp.int32)
    for b, pick in enumerate(picks):
        chosen = jnp.where(lane // 32 == b, pick, chosen)
    one_hot = (iota(lane.shape, 0) == chosen).astype(F32).astype(BF16)
    found = mm(operators[axis * 1024 : axis * 1024 + 1024, :], one_hot)
    within = iota((32, 256), 1) % 32
    total = jnp.zeros((32, 256), F32)
    for x in range(32):
        total = jnp.where(within == x, found[x * 32 : x * 32 + 32], total)
    return total


def same_block(size, edge):
    return iota((size, size), 0) // edge == iota((size, size), 1) // edge


def identity():
    return (iota((256, 256), 0) == iota((256, 256), 1)).astype(F32).astype(BF16)


def flipped_diagonal(table):
    return jnp.where(same_block(256, 32), jnp.concatenate([table] * 8, axis=0), 0.0).astype(BF16)


def diagonal(table):
    return mm(identity(), flipped_diagonal(table), NT).astype(BF16)


def spread(table):
    copies = (iota((256, 256), 0) % 32 == iota((256, 256), 1) % 32).astype(F32).astype(BF16)
    return mm(flipped_diagonal(table), copies)


def swap_chunks(parts):
    lane = iota(parts[0].shape, 1)
    for bit, shift in ((1, 32), (2, 64)):
        keep = (lane & shift) == 0
        fresh = list(parts)
        for index in range(4):
            if index & bit:
                continue
            one, two = parts[index], parts[index | bit]
            fresh[index] = jnp.where(keep, one, pltpu.roll(two, shift, 1))
            fresh[index | bit] = jnp.where(keep, pltpu.roll(one, 128 - shift, 1), two)
        parts = fresh
    return parts


def swap_brick(block, folded, turned, brick):
    slabs = []
    for ph in range(4):
        slabs.append(
            jnp.concatenate(
                [
                    block[(qs // 2) * 32 + ph * 8 : (qs // 2) * 32 + ph * 8 + 8, (qs % 2) * 128 : (qs % 2) * 128 + 128]
                    for qs in range(8)
                ],
                axis=0,
            )
        )
    slabs = swap_chunks(slabs)
    for qh in range(4):
        folded[brick * 4 + qh] = slabs[qh]
    for ps in range(8):
        value = jnp.concatenate(
            [folded[brick * 4 + qh, pl.ds(ps, 8, stride=8), :] for qh in range(4)], axis=0
        )
        turned[brick * 32 : brick * 32 + 32, ps * 128 : ps * 128 + 128] = value


def lane_pair(field, g):
    return jnp.concatenate(
        [
            jnp.concatenate([field[b, qs * 32 : qs * 32 + 32, :] for b in range(8)], axis=0)
            for qs in (2 * g, 2 * g + 1)
        ],
        axis=1,
    )


def put_pair(field, g, value):
    for b in range(8):
        for half in range(2):
            rows = slice((2 * g + half) * 32, (2 * g + half) * 32 + 32)
            field[b, rows, :] = value[b * 32 : b * 32 + 32, half * 128 : half * 128 + 128]


def middle_and_last(start, spread_mid, last, folded, turned, flipped):
    mask = same_block(256, 32)
    for brick in range(8):
        rows = spread_mid[brick * 32 : brick * 32 + 32]
        line = jnp.where(mask, jnp.concatenate([rows] * 8, axis=0), 0.0).astype(BF16)
        block = start[brick * 32 : brick * 32 + 32, :]
        block = jnp.concatenate([block[:, g * 256 : g * 256 + 256] for g in range(4)], axis=0)
        high, low = halves(block)
        both = mm(jnp.concatenate([high, low], axis=0), line, NT if flipped else NN)
        swap_brick(both[:128] + both[128:], folded, turned, brick)
    for g in range(4):
        high, low = halves(turned[:, g * 256 : g * 256 + 256])
        yield g, (mm(last, high) + mm(last, low)).astype(BF16)


def slot_numbers(route, step):
    own = [route[step, 0, 0, b] for b in range(8)]
    slots = []
    for b in range(8):
        rank = jnp.int32(0)
        for other in range(b):
            rank = rank + (own[other] == own[b]).astype(jnp.int32)
        slots.append((own[b], rank))
    return slots


def fetch(source, target, sem):
    copy = pltpu.make_async_copy(source, target, sem)
    copy.start()
    return copy


def chunk(send, place):
    return send.at[place[0], pl.ds(pl.multiple_of(place[1] * 256, 256), 256), :]


def send_bricks(bricks, send, slots, sems):
    for copy in [fetch(bricks.at[b], chunk(send, slots[b]), sems.at[b]) for b in range(8)]:
        copy.wait()


def first_kernel(*refs):
    picks_in, route_in, landing_in, operators, field, send, tables = refs[:7]
    picks, route, landing, table_mem, field_mem, start, folded, turned, out, meta, meta_half, sems = refs[7:]
    told = [fetch(a, b, sems.at[11 + i]) for i, (a, b) in enumerate(((picks_in, picks), (route_in, route), (landing_in, landing)))]
    loads = [fetch(operators, table_mem, sems.at[8]), fetch(field, field_mem, sems.at[9])]
    for copy in told:
        copy.wait()
    meta[...] = jnp.zeros(meta.shape, F32)
    for step in range(STEPS):
        for b, (place, rank) in enumerate(slot_numbers(route, step)):
            value = jnp.full((1, 128), landing[step, 0, 0, b] + 1, jnp.int32).astype(F32)
            meta[place, pl.ds(step * CAP + rank, 1), :] = value
    meta_half[...] = meta[...].astype(BF16)
    told = fetch(meta_half, send.at[:, 512:528, :], sems.at[10])
    chosen = [picks[0, 0, 0, b] for b in range(8)]
    loads[0].wait()
    found = [table_rows(table_mem, chosen, axis) for axis in range(3)]
    for axis in range(3):
        tables[axis] = found[axis].astype(BF16)
    begin = diagonal(found[2])
    loads[1].wait()
    for g in range(4):
        block = jnp.concatenate(
            [field_mem[qh * 8 + qs] for qs in (2 * g, 2 * g + 1) for qh in range(4)], axis=0
        )
        start[:, g * 256 : g * 256 + 256] = mm(begin, block, NT)
    for g, moved in middle_and_last(start, spread(found[1]), diagonal(found[0]), folded, turned, False):
        put_pair(out, g, moved)
    send_bricks(out, send, slot_numbers(route, 0), sems)
    told.wait()


def second_kernel(route, tables, arrived, *refs):
    send, state, landing_out, arrived_mem, meta_half, meta, landing, state_mem, total, start, folded, turned, out, sems = refs[-14:]
    loads = [
        fetch(arrived.at[:, 512:528, :], meta_half, sems.at[9]),
        fetch(arrived.at[:, 0:512, :], arrived_mem, sems.at[8]),
    ]
    begin = diagonal(tables[0].astype(F32))
    mid = spread(tables[1].astype(F32))
    end = diagonal(tables[2].astype(F32))
    loads[0].wait()
    meta[...] = meta_half[...].astype(F32).astype(jnp.int32)[:, 0:8, :]
    told = [fetch(meta, landing, sems.at[9]), fetch(meta, landing_out, sems.at[10])]
    total[...] = jnp.zeros(total.shape, F32)
    loads[1].wait()
    told[0].wait()
    gather_sum(0, landing, arrived_mem, total)
    for b in range(8):
        state_mem[b] = total[b].astype(BF16)
    kept = fetch(state_mem, state, sems.at[9])
    for g in range(4):
        start[:, g * 256 : g * 256 + 256] = mm(begin, lane_pair(state_mem, g))
    for g, moved in middle_and_last(start, mid, end, folded, turned, False):
        put_pair(out, g, moved)
    send_bricks(out, send, slot_numbers(route, 1), sems)
    kept.wait()
    told[1].wait()


def gather_sum(step, landing, arrived, total):
    def add(source, carry):
        for rank in range(CAP):
            brick = landing[source, step * CAP + rank, 0]

            @pl.when(brick > 0)
            def _():
                total[brick - 1] += arrived[source, rank * 256 : rank * 256 + 256, :].astype(F32)

        return carry

    lax.fori_loop(0, arrived.shape[0], add, 0)


def hand_out(step, landing, field, send, sems):
    def each(act):
        def body(source, carry):
            for rank in range(CAP):
                brick = landing[source, step * CAP + rank, 0]

                @pl.when(brick > 0)
                def _():
                    act(
                        pltpu.make_async_copy(
                            field.at[brick - 1],
                            send.at[source, rank * 256 : rank * 256 + 256, :],
                            sems.at[source * CAP + rank],
                        )
                    )

            return carry

        lax.fori_loop(0, send.shape[0], body, 0)

    each(lambda copy: copy.start())
    each(lambda copy: copy.wait())


def third_kernel(landing_in, arrived, target, *refs):
    send, adjoint, arrived_mem, landing, total, adjoint_mem, target_mem, sems, slot_sems = refs[-9:]
    loads = [
        fetch(landing_in, landing, sems.at[0]),
        fetch(arrived, arrived_mem, sems.at[1]),
        fetch(target, target_mem, sems.at[2]),
    ]
    total[...] = jnp.zeros(total.shape, F32)
    for load in loads:
        load.wait()
    gather_sum(1, landing, arrived_mem, total)
    for b in range(8):
        final = total[b].astype(BF16).astype(F32)
        adjoint_mem[b] = (final - target_mem[b].astype(F32)).astype(BF16)
    kept = fetch(adjoint_mem, adjoint, sems.at[0])
    hand_out(1, landing, adjoint_mem, send, slot_sems)
    kept.wait()


def pull_bricks(arrived, bricks, slots, sems):
    return [fetch(chunk(arrived, slots[b]), bricks.at[b], sems.at[b]) for b in range(8)]


def fourth_kernel(route, tables, landing_in, arrived, *refs):
    send, adjoint, bricks, landing, start, folded, turned, out, sems, slot_sems = refs[-10:]
    loads = pull_bricks(arrived, bricks, slot_numbers(route, 1), sems)
    told = fetch(landing_in, landing, sems.at[8])
    begin = flipped_diagonal(tables[2].astype(F32))
    mid = spread(tables[1].astype(F32))
    end = flipped_diagonal(tables[0].astype(F32))
    for load in loads:
        load.wait()
    for g in range(4):
        start[:, g * 256 : g * 256 + 256] = mm(begin, lane_pair(bricks, g))
    for g, moved in middle_and_last(start, mid, end, folded, turned, True):
        put_pair(out, g, moved)
    kept = fetch(out, adjoint, sems.at[0])
    told.wait()
    hand_out(0, landing, out, send, slot_sems)
    kept.wait()


def fifth_kernel(route, tables, arrived, *refs):
    adjoint, bricks, start, folded, turned, sems = refs[-6:]
    loads = pull_bricks(arrived, bricks, slot_numbers(route, 0), sems)
    begin = flipped_diagonal(tables[0].astype(F32))
    mid = spread(tables[1].astype(F32))
    end = flipped_diagonal(tables[2].astype(F32))
    for load in loads:
        load.wait()
    for g in range(4):
        start[:, g * 256 : g * 256 + 256] = mm(begin, lane_pair(bricks, g))
    for g, moved in middle_and_last(start, mid, end, folded, turned, True):
        to_native(moved, g, adjoint)


def to_native(block, g, field):
    flat = mm(identity(), block, NT).astype(field.dtype)
    for index in range(8):
        x = (index % 4) * 8 + 2 * g + index // 4
        field[x] = flat[index * 32 : index * 32 + 32]


def x_form_to_native(source, folded, turned, field):
    for b in range(8):
        block = source[b].astype(F32)
        block = jnp.concatenate(
            [
                jnp.concatenate([block[g * 64 : g * 64 + 32], block[g * 64 + 32 : g * 64 + 64]], axis=1)
                for g in range(4)
            ],
            axis=0,
        )
        swap_brick(block, folded, turned, b)
    for g in range(4):
        to_native(turned[:, g * 256 : g * 256 + 256].astype(BF16), g, field)


def tap(offset):
    value = jnp.zeros(offset.shape, F32)
    for step, weight in TAPS:
        value = jnp.where(offset == step, weight, value)
        value = jnp.where(offset == -step, -weight, value)
    return value


def stencils():
    size = 256
    row, col = iota((size, size), 0), iota((size, size), 1)
    along_y = halves(jnp.where(row // 32 == col // 32, tap(col - row), 0.0))
    along_z = halves(tap(row - col))
    row, col = iota((size, 48), 0), iota((size, 48), 1)
    layer = col // 8
    place = jnp.where(layer < RIM, layer - RIM, layer - RIM + 32)
    rim_y = halves(jnp.where(row // 32 == col % 8, tap(place - row % 32), 0.0))
    return along_y, rim_y, along_z


def rim_picker():
    row, col = iota((48, 256), 0), iota((48, 256), 1)
    layer = row // 8
    place = jnp.where(layer < RIM, layer, layer - RIM + 29)
    return ((row % 8 == col // 32) & (place == col % 32)).astype(F32).astype(BF16)


def difference_x(padded, g):
    total = None
    for step, weight in TAPS:
        ahead = padded[pl.ds(8 * g + RIM + step, 8)]
        behind = padded[pl.ds(8 * g + RIM - step, 8)]
        term = weight * (ahead - behind)
        total = term if total is None else total + term
    return total.reshape(256, 256)


def difference_y(parts, rims, along_y, rim_y):
    total = mm(along_y[0], parts[0]) + mm(along_y[1], parts[0])
    if len(parts) > 1:
        total = total + mm(along_y[0], parts[1])
    return total + mm(rim_y[0], rims) + mm(rim_y[1], rims)


def difference_z(parts, along_z):
    total = mm(parts[0], along_z[0]) + mm(parts[0], along_z[1])
    if len(parts) > 1:
        total = total + mm(parts[1], along_z[0])
    return total


def rim_rows(before, after, base, g):
    rows = [before[base + h, (g // 2) * 16 : (g // 2) * 16 + 16, :].astype(F32) for h in range(RIM)]
    rows += [after[base + h, (g // 2) * 16 : (g // 2) * 16 + 16, :].astype(F32) for h in range(RIM)]
    half = (g % 2) * 8
    return jnp.concatenate([value[half : half + 8] for value in rows], axis=0).astype(BF16)


def put_rims(blocks, base, low_y, high_y):
    picker = rim_picker()
    for pair in range(2):
        left, right = mm(picker, blocks[2 * pair]), mm(picker, blocks[2 * pair + 1])
        for layer in range(2 * RIM):
            value = jnp.concatenate(
                [left[layer * 8 : layer * 8 + 8], right[layer * 8 : layer * 8 + 8]], axis=0
            ).astype(BF16)
            target = low_y if layer < RIM else high_y
            target[base + layer % RIM, pair * 16 : pair * 16 + 16, :] = value


def opening_kernel(picks, operators, template, target, first_x, last_x, mid_v, sent, low_x, high_x, low_y, high_y, target_z, tables):
    chosen = [picks[1, 0, 0, b] for b in range(8)]
    for axis in range(3):
        tables[axis] = table_rows(operators, chosen, axis).astype(BF16)
    low_x[0:RIM] = template[0:RIM]
    high_x[0:RIM] = template[29:32]
    low_x[RIM : 2 * RIM] = first_x[0, 0:RIM].astype(BF16)
    high_x[RIM : 2 * RIM] = last_x[0, 1:4].astype(BF16)
    put_rims([template[8 * g : 8 * g + 8].reshape(256, 256) for g in range(4)], 0, low_y, high_y)
    put_rims([mid_v[0, 8 * g : 8 * g + 8].astype(BF16).reshape(256, 256) for g in range(4)], RIM, low_y, high_y)
    for g in range(4):
        block = jnp.concatenate(
            [target[qh * 8 + qs] for qs in (2 * g, 2 * g + 1) for qh in range(4)], axis=0
        )
        put_pair(target_z, g, mm(identity(), block, NT).astype(BF16))


def divergence_kernel(velocity, before_x, after_x, before_y, after_y, sent, divergence, padded):
    along_y, rim_y, along_z = stencils()
    padded[0:RIM] = before_x[RIM : 2 * RIM].astype(F32)
    padded[RIM : RIM + 32] = velocity[0]
    padded[RIM + 32 : 2 * RIM + 32] = after_x[RIM : 2 * RIM].astype(F32)
    for g in range(4):
        along_one = halves(velocity[1, 8 * g : 8 * g + 8].reshape(256, 256))
        along_two = halves(velocity[2, 8 * g : 8 * g + 8].reshape(256, 256))
        total = (
            difference_x(padded, g)
            + difference_y(along_one, rim_rows(before_y, after_y, RIM, g), along_y, rim_y)
            + difference_z(along_two, along_z)
        )
        divergence[8 * g : 8 * g + 8] = total.reshape(8, 32, 256)


def rims_kernel(state, divergence, sent, native, low_x, high_x, low_y, high_y, folded, turned):
    x_form_to_native(state, folded, turned, native)
    low_x[0:RIM] = native[0:RIM]
    high_x[0:RIM] = native[29:32]
    low_x[RIM : 2 * RIM] = divergence[0:RIM].astype(BF16)
    high_x[RIM : 2 * RIM] = divergence[29:32].astype(BF16)
    put_rims([native[8 * g : 8 * g + 8].reshape(256, 256) for g in range(4)], 0, low_y, high_y)
    put_rims(
        [divergence[8 * g : 8 * g + 8].astype(BF16).reshape(256, 256) for g in range(4)], RIM, low_y, high_y
    )


def gradient_kernel(
    template,
    state,
    divergence,
    adjoint_two,
    adjoint_one,
    b0x,
    a0x,
    b0y,
    a0y,
    b1x,
    a1x,
    b1y,
    a1y,
    sent,
    gradient,
    folded,
    turned,
    weight_two,
    weight_one,
    pad_zero,
    pad_one,
    pad_div,
):
    x_form_to_native(adjoint_one, folded, turned, weight_one)
    for g in range(4):
        to_native(lane_pair(adjoint_two, g), g, weight_two)
    along_y, rim_y, along_z = stencils()
    for padded, before, middle, after, base in (
        (pad_zero, b0x, template, a0x, 0),
        (pad_one, b1x, state, a1x, 0),
        (pad_div, b1x, divergence, a1x, RIM),
    ):
        padded[0:RIM] = before[base : base + RIM].astype(F32)
        padded[RIM : RIM + 32] = middle[...].astype(F32)
        padded[RIM + 32 : 2 * RIM + 32] = after[base : base + RIM].astype(F32)
    for g in range(4):
        zero = (template[8 * g : 8 * g + 8].reshape(256, 256),)
        one = (state[8 * g : 8 * g + 8].reshape(256, 256),)
        div = halves(divergence[8 * g : 8 * g + 8].reshape(256, 256))
        weigh_one = 0.5 * weight_one[8 * g : 8 * g + 8].reshape(256, 256)
        weigh_two = 0.5 * weight_two[8 * g : 8 * g + 8].reshape(256, 256)
        for axis in range(3):
            if axis == 0:
                parts = [difference_x(padded, g) for padded in (pad_zero, pad_one, pad_div)]
            elif axis == 1:
                parts = [
                    difference_y(zero, rim_rows(b0y, a0y, 0, g), along_y, rim_y),
                    difference_y(one, rim_rows(b1y, a1y, 0, g), along_y, rim_y),
                    difference_y(div, rim_rows(b1y, a1y, RIM, g), along_y, rim_y),
                ]
            else:
                parts = [difference_z(value, along_z) for value in (zero, one, div)]
            value = weigh_one * parts[0] + weigh_two * parts[1] - 0.25 * parts[2]
            gradient[axis, 8 * g : 8 * g + 8] = value.reshape(8, 32, 256)


SCALAR = pl.BlockSpec(memory_space=pltpu.SMEM)
WHOLE = pl.BlockSpec(memory_space=pltpu.VMEM)
FAR = pl.BlockSpec(memory_space=pltpu.HBM)
FOLDED = (32, 64, 128)
FLAT = (256, 1024)
NATIVE = (32, 32, 256)
FORM = (8, 256, 128)
TABLES = (3, 32, 256)


def pinned(values):
    return [pltpu.with_memory_space_constraint(value, pltpu.HBM) for value in values]


def call(kernel, out, in_specs, out_specs, scratch, work=1 << 31):
    made = pl.pallas_call(
        kernel,
        out_shape=out,
        in_specs=in_specs,
        out_specs=out_specs,
        scratch_shapes=scratch,
        compiler_params=pltpu.CompilerParams(vmem_limit_bytes=48 * 1024 * 1024),
        cost_estimate=pl.CostEstimate(flops=work, bytes_accessed=8 * 1024 * 1024, transcendentals=0),
    )

    def apply(*values):
        specs = in_specs
        return made(*[pinned([v])[0] if spec is FAR else v for v, spec in zip(values, specs, strict=True)])

    return apply


def like(shape, dtype):
    return jax.ShapeDtypeStruct(shape, dtype)


def far(shape, dtype):
    return pltpu.HBM(shape, dtype)


def neighbours(low_x, high_x, low_y, high_y):
    moved = []
    for low, high, axis in ((low_x, high_x, "gx"), (low_y, high_y, "gy")):
        size = lax.axis_size(axis)
        up = [(i, i + 1) for i in range(size - 1)]
        down = [(i + 1, i) for i in range(size - 1)]
        moved += [lax.ppermute(high, axis, up), lax.ppermute(low, axis, down)]
    return moved


def swap_slots(send):
    return lax.all_to_all(send, "gx", split_axis=0, concat_axis=0, tiled=True)


def shards(template, target_image, velocity, operators, route, target_brick, operator_index):
    peers = lax.axis_size("gx")
    sems = pltpu.SemaphoreType.DMA((16,))
    slot_sems = pltpu.SemaphoreType.DMA((peers * CAP,))
    turning = [pltpu.VMEM(FLAT, F32), pltpu.VMEM(FOLDED, F32), pltpu.VMEM(FLAT, F32)]
    form = pltpu.VMEM(FORM, BF16)
    total = pltpu.VMEM(FORM, F32)
    landed = pltpu.SMEM((peers, 8, 128), jnp.int32)
    slots = far((peers, 512, 128), BF16)
    table_rows_count = operators.shape[1] * operators.shape[2] * operators.shape[3]
    listed = operators.transpose(1, 2, 3, 0).reshape(table_rows_count, operators.shape[0])
    route = route.reshape(route.shape[:4])

    send, tables_zero = call(
        first_kernel,
        [far((peers, 528, 128), BF16), like(TABLES, BF16)],
        [FAR] * 5,
        [FAR, WHOLE],
        [pltpu.SMEM(route.shape, jnp.int32)] * 3
        + [pltpu.VMEM(listed.shape, BF16), pltpu.VMEM(NATIVE, BF16)]
        + turning
        + [form, pltpu.VMEM((peers, 16, 128), F32), pltpu.VMEM((peers, 16, 128), BF16), sems],
    )(operator_index, route, target_brick, listed, template)
    arrived = swap_slots(send)

    rim = like((2 * RIM, 32, 256), BF16)
    rim_spec = pl.BlockSpec((2 * RIM, 32, 256), lambda i: (0, 0, 0))
    low_x, high_x, low_y, high_y, target_z, tables_one = pl.pallas_call(
        opening_kernel,
        out_shape=[rim] * 4 + [far(FORM, BF16), like(TABLES, BF16)],
        grid=(1,),
        in_specs=[
            SCALAR,
            pl.BlockSpec(listed.shape, lambda i: (0, 0)),
            pl.BlockSpec(NATIVE, lambda i: (0, 0, 0)),
            pl.BlockSpec(NATIVE, lambda i: (0, 0, 0)),
            pl.BlockSpec((1, 4, 32, 256), lambda i: (0, 0, 0, 0)),
            pl.BlockSpec((1, 4, 32, 256), lambda i: (0, 7, 0, 0)),
            pl.BlockSpec((1, 32, 32, 256), lambda i: (1, 0, 0, 0)),
            FAR,
        ],
        out_specs=[rim_spec] * 4
        + [pl.BlockSpec(FORM, lambda i: (0, 0, 0)), pl.BlockSpec(TABLES, lambda i: (0, 0, 0))],
        compiler_params=pltpu.CompilerParams(vmem_limit_bytes=48 * 1024 * 1024),
        cost_estimate=pl.CostEstimate(flops=1 << 31, bytes_accessed=8 * 1024 * 1024, transcendentals=0),
    )(operator_index, listed, template, target_image, velocity, velocity, velocity, *pinned([send]))
    b0x, a0x, b0y, a0y = neighbours(low_x, high_x, low_y, high_y)
    send, state_x, landing = call(
        second_kernel,
        [slots, far(FORM, BF16), far((peers, 8, 128), jnp.int32)],
        [SCALAR, WHOLE, FAR],
        [FAR] * 3,
        [
            pltpu.VMEM((peers, 512, 128), BF16),
            pltpu.VMEM((peers, 16, 128), BF16),
            pltpu.VMEM((peers, 8, 128), jnp.int32),
            landed,
            form,
            total,
        ]
        + turning
        + [form, sems],
    )(route, tables_one, arrived)
    arrived = swap_slots(send)

    divergence = call(
        divergence_kernel, like(NATIVE, F32), [WHOLE] * 5 + [FAR], WHOLE, [pltpu.VMEM((38, 32, 256), F32)]
    )(velocity, b0x, a0x, b0y, a0y, send)

    state, low_x, high_x, low_y, high_y = call(
        rims_kernel, [far(NATIVE, BF16)] + [rim] * 4, [WHOLE] * 2 + [FAR], [WHOLE] * 5, turning[1:]
    )(state_x, divergence, send)
    b1x, a1x, b1y, a1y = neighbours(low_x, high_x, low_y, high_y)

    send, adjoint_two = call(
        third_kernel,
        [slots, far(FORM, BF16)],
        [FAR] * 4,
        [FAR] * 2,
        [pltpu.VMEM((peers, 512, 128), BF16), landed, total, form, form, sems, slot_sems],
    )(landing, arrived, target_z, state)
    arrived = swap_slots(send)

    send, adjoint_one = call(
        fourth_kernel,
        [slots, far(FORM, BF16)],
        [SCALAR, WHOLE, FAR, FAR],
        [FAR] * 2,
        [form, landed] + turning + [form, sems, slot_sems],
    )(route, tables_one, landing, arrived)
    arrived = swap_slots(send)

    gradient = call(
        gradient_kernel,
        far((3,) + NATIVE, F32),
        [WHOLE] * 13 + [FAR],
        WHOLE,
        turning[1:] + [pltpu.VMEM(NATIVE, F32)] * 2 + [pltpu.VMEM((38, 32, 256), F32)] * 3,
    )(template, state, divergence, adjoint_two, adjoint_one, b0x, a0x, b0y, a0y, b1x, a1x, b1y, a1y, send)

    adjoint = call(
        fifth_kernel, like(NATIVE, BF16), [SCALAR, WHOLE, FAR, FAR], WHOLE, [form] + turning + [sems]
    )(route, tables_zero, arrived, gradient)
    return gradient, adjoint


def solution(mesh):
    placed = (
        P("gx", "gy", None),
        P("gx", "gy", None),
        P(None, "gx", "gy", None),
        P(),
        P(None, "gx", "gy", None, None),
        P(None, "gx", "gy", None),
        P(None, "gx", "gy", None),
    )
    return jax.shard_map(
        shards,
        mesh=mesh,
        in_specs=placed,
        out_specs=(P(None, "gx", "gy", None), P("gx", "gy", None)),
        check_vma=False,
    )
```

```python
import functools

import jax
import jax.numpy as jnp
from jax import lax
from jax.experimental import pallas as pl
from jax.experimental.pallas import tpu as pltpu
from jax.sharding import PartitionSpec as P

STEPS = 2
CAP = 2
RIM = 3
F32 = jnp.float32
BF16 = jnp.bfloat16
NT = (((1,), (1,)), ((), ()))
NN = (((1,), (0,)), ((), ()))
TAPS = ((1, 0.75), (2, -0.15), (3, 1.0 / 60.0))


def iota(shape, dim):
    return lax.broadcasted_iota(jnp.int32, shape, dim)


def mm(left, right, dims=NN):
    return lax.dot_general(left, right, dims, preferred_element_type=F32)


def halves(value):
    high = value.astype(BF16)
    return high, (value - high.astype(F32)).astype(BF16)


def table_rows(operators, picks, axis):
    lane = iota((operators.shape[1], 256), 1)
    chosen = jnp.zeros(lane.shape, jnp.int32)
    for b, pick in enumerate(picks):
        chosen = jnp.where(lane // 32 == b, pick, chosen)
    one_hot = (iota(lane.shape, 0) == chosen).astype(F32).astype(BF16)
    found = mm(operators[axis * 1024 : axis * 1024 + 1024, :], one_hot)
    within = iota((32, 256), 1) % 32
    total = jnp.zeros((32, 256), F32)
    for x in range(32):
        total = jnp.where(within == x, found[x * 32 : x * 32 + 32], total)
    return total


def same_block(size, edge):
    return iota((size, size), 0) // edge == iota((size, size), 1) // edge


def identity():
    return (iota((256, 256), 0) == iota((256, 256), 1)).astype(F32).astype(BF16)


def flipped_diagonal(table):
    return jnp.where(same_block(256, 32), jnp.concatenate([table] * 8, axis=0), 0.0).astype(BF16)


def diagonal(table):
    return mm(identity(), flipped_diagonal(table), NT).astype(BF16)


def spread(table):
    copies = (iota((256, 256), 0) % 32 == iota((256, 256), 1) % 32).astype(F32).astype(BF16)
    return mm(flipped_diagonal(table), copies)


def swap_chunks(parts):
    lane = iota(parts[0].shape, 1)
    for bit, shift in ((1, 32), (2, 64)):
        keep = (lane & shift) == 0
        fresh = list(parts)
        for index in range(4):
            if index & bit:
                continue
            one, two = parts[index], parts[index | bit]
            fresh[index] = jnp.where(keep, one, pltpu.roll(two, shift, 1))
            fresh[index | bit] = jnp.where(keep, pltpu.roll(one, 128 - shift, 1), two)
        parts = fresh
    return parts


def swap_brick(block, folded, turned, brick):
    slabs = []
    for ph in range(4):
        slabs.append(
            jnp.concatenate(
                [
                    block[(qs // 2) * 32 + ph * 8 : (qs // 2) * 32 + ph * 8 + 8, (qs % 2) * 128 : (qs % 2) * 128 + 128]
                    for qs in range(8)
                ],
                axis=0,
            )
        )
    slabs = swap_chunks(slabs)
    for qh in range(4):
        folded[brick * 4 + qh] = slabs[qh]
    for ps in range(8):
        value = jnp.concatenate(
            [folded[brick * 4 + qh, pl.ds(ps, 8, stride=8), :] for qh in range(4)], axis=0
        )
        turned[brick * 32 : brick * 32 + 32, ps * 128 : ps * 128 + 128] = value


def lane_pair(field, g):
    return jnp.concatenate(
        [
            jnp.concatenate([field[b, qs * 32 : qs * 32 + 32, :] for b in range(8)], axis=0)
            for qs in (2 * g, 2 * g + 1)
        ],
        axis=1,
    )


def put_pair(field, g, value):
    for b in range(8):
        for half in range(2):
            rows = slice((2 * g + half) * 32, (2 * g + half) * 32 + 32)
            field[b, rows, :] = value[b * 32 : b * 32 + 32, half * 128 : half * 128 + 128]


def middle_and_last(start, spread_mid, last, folded, turned, flipped):
    mask = same_block(256, 32)
    for brick in range(8):
        rows = spread_mid[brick * 32 : brick * 32 + 32]
        line = jnp.where(mask, jnp.concatenate([rows] * 8, axis=0), 0.0).astype(BF16)
        block = start[brick * 32 : brick * 32 + 32, :]
        block = jnp.concatenate([block[:, g * 256 : g * 256 + 256] for g in range(4)], axis=0)
        high, low = halves(block)
        both = mm(jnp.concatenate([high, low], axis=0), line, NT if flipped else NN)
        swap_brick(both[:128] + both[128:], folded, turned, brick)
    for g in range(4):
        high, low = halves(turned[:, g * 256 : g * 256 + 256])
        yield g, (mm(last, high) + mm(last, low)).astype(BF16)


def slot_numbers(route, step):
    own = [route[step, 0, 0, b] for b in range(8)]
    slots = []
    for b in range(8):
        rank = jnp.int32(0)
        for other in range(b):
            rank = rank + (own[other] == own[b]).astype(jnp.int32)
        slots.append((own[b], rank))
    return slots


def fetch(source, target, sem):
    copy = pltpu.make_async_copy(source, target, sem)
    copy.start()
    return copy


def chunk(send, place):
    return send.at[place[0], pl.ds(pl.multiple_of(place[1] * 256, 256), 256), :]


def send_bricks(bricks, send, slots, sems):
    for copy in [fetch(bricks.at[b], chunk(send, slots[b]), sems.at[b]) for b in range(8)]:
        copy.wait()


def first_kernel(*refs):
    picks_in, route_in, landing_in, operators, field, send, tables = refs[:7]
    picks, route, landing, table_mem, field_mem, start, folded, turned, out, meta, meta_half, sems = refs[7:]
    told = [fetch(a, b, sems.at[11 + i]) for i, (a, b) in enumerate(((picks_in, picks), (route_in, route), (landing_in, landing)))]
    loads = [fetch(operators, table_mem, sems.at[8]), fetch(field, field_mem, sems.at[9])]
    for copy in told:
        copy.wait()
    meta[...] = jnp.zeros(meta.shape, F32)
    for step in range(STEPS):
        for b, (place, rank) in enumerate(slot_numbers(route, step)):
            value = jnp.full((1, 128), landing[step, 0, 0, b] + 1, jnp.int32).astype(F32)
            meta[place, pl.ds(step * CAP + rank, 1), :] = value
    meta_half[...] = meta[...].astype(BF16)
    told = fetch(meta_half, send.at[:, 512:528, :], sems.at[10])
    chosen = [picks[0, 0, 0, b] for b in range(8)]
    loads[0].wait()
    found = [table_rows(table_mem, chosen, axis) for axis in range(3)]
    for axis in range(3):
        tables[axis] = found[axis].astype(BF16)
    begin = diagonal(found[2])
    loads[1].wait()
    for g in range(4):
        block = jnp.concatenate(
            [field_mem[qh * 8 + qs] for qs in (2 * g, 2 * g + 1) for qh in range(4)], axis=0
        )
        start[:, g * 256 : g * 256 + 256] = mm(begin, block, NT)
    for g, moved in middle_and_last(start, spread(found[1]), diagonal(found[0]), folded, turned, False):
        put_pair(out, g, moved)
    send_bricks(out, send, slot_numbers(route, 0), sems)
    told.wait()


def second_kernel(route, tables, arrived, *refs):
    send, state, landing_out, arrived_mem, meta_half, meta, landing, state_mem, total, start, folded, turned, out, sems = refs[-14:]
    loads = [
        fetch(arrived.at[:, 512:528, :], meta_half, sems.at[9]),
        fetch(arrived.at[:, 0:512, :], arrived_mem, sems.at[8]),
    ]
    begin = diagonal(tables[0].astype(F32))
    mid = spread(tables[1].astype(F32))
    end = diagonal(tables[2].astype(F32))
    loads[0].wait()
    meta[...] = meta_half[...].astype(F32).astype(jnp.int32)[:, 0:8, :]
    told = [fetch(meta, landing, sems.at[9]), fetch(meta, landing_out, sems.at[10])]
    total[...] = jnp.zeros(total.shape, F32)
    loads[1].wait()
    told[0].wait()
    gather_sum(0, landing, arrived_mem, total)
    for b in range(8):
        state_mem[b] = total[b].astype(BF16)
    kept = fetch(state_mem, state, sems.at[9])
    for g in range(4):
        start[:, g * 256 : g * 256 + 256] = mm(begin, lane_pair(state_mem, g))
    for g, moved in middle_and_last(start, mid, end, folded, turned, False):
        put_pair(out, g, moved)
    send_bricks(out, send, slot_numbers(route, 1), sems)
    kept.wait()
    told[1].wait()


def gather_sum(step, landing, arrived, total):
    def add(source, carry):
        for rank in range(CAP):
            brick = landing[source, step * CAP + rank, 0]

            @pl.when(brick > 0)
            def _():
                total[brick - 1] += arrived[source, rank * 256 : rank * 256 + 256, :].astype(F32)

        return carry

    lax.fori_loop(0, arrived.shape[0], add, 0)


def hand_out(step, landing, field, send, sems):
    def each(act):
        def body(source, carry):
            for rank in range(CAP):
                brick = landing[source, step * CAP + rank, 0]

                @pl.when(brick > 0)
                def _():
                    act(
                        pltpu.make_async_copy(
                            field.at[brick - 1],
                            send.at[source, rank * 256 : rank * 256 + 256, :],
                            sems.at[source * CAP + rank],
                        )
                    )

            return carry

        lax.fori_loop(0, send.shape[0], body, 0)

    each(lambda copy: copy.start())
    each(lambda copy: copy.wait())


def third_kernel(landing_in, arrived, target, *refs):
    send, adjoint, arrived_mem, landing, total, adjoint_mem, target_mem, sems, slot_sems = refs[-9:]
    loads = [
        fetch(landing_in, landing, sems.at[0]),
        fetch(arrived, arrived_mem, sems.at[1]),
        fetch(target, target_mem, sems.at[2]),
    ]
    total[...] = jnp.zeros(total.shape, F32)
    for load in loads:
        load.wait()
    gather_sum(1, landing, arrived_mem, total)
    for b in range(8):
        final = total[b].astype(BF16).astype(F32)
        adjoint_mem[b] = (final - target_mem[b].astype(F32)).astype(BF16)
    kept = fetch(adjoint_mem, adjoint, sems.at[0])
    hand_out(1, landing, adjoint_mem, send, slot_sems)
    kept.wait()


def pull_bricks(arrived, bricks, slots, sems):
    return [fetch(chunk(arrived, slots[b]), bricks.at[b], sems.at[b]) for b in range(8)]


def fourth_kernel(route, tables, landing_in, arrived, *refs):
    send, adjoint, bricks, landing, start, folded, turned, out, sems, slot_sems = refs[-10:]
    loads = pull_bricks(arrived, bricks, slot_numbers(route, 1), sems)
    told = fetch(landing_in, landing, sems.at[8])
    begin = flipped_diagonal(tables[2].astype(F32))
    mid = spread(tables[1].astype(F32))
    end = flipped_diagonal(tables[0].astype(F32))
    for load in loads:
        load.wait()
    for g in range(4):
        start[:, g * 256 : g * 256 + 256] = mm(begin, lane_pair(bricks, g))
    for g, moved in middle_and_last(start, mid, end, folded, turned, True):
        put_pair(out, g, moved)
    kept = fetch(out, adjoint, sems.at[0])
    told.wait()
    hand_out(0, landing, out, send, slot_sems)
    kept.wait()


def fifth_kernel(route, tables, arrived, *refs):
    adjoint, bricks, start, folded, turned, sems = refs[-6:]
    loads = pull_bricks(arrived, bricks, slot_numbers(route, 0), sems)
    begin = flipped_diagonal(tables[0].astype(F32))
    mid = spread(tables[1].astype(F32))
    end = flipped_diagonal(tables[2].astype(F32))
    for load in loads:
        load.wait()
    for g in range(4):
        start[:, g * 256 : g * 256 + 256] = mm(begin, lane_pair(bricks, g))
    for g, moved in middle_and_last(start, mid, end, folded, turned, True):
        to_native(moved, g, adjoint)


def to_native(block, g, field):
    flat = mm(identity(), block, NT).astype(field.dtype)
    for index in range(8):
        x = (index % 4) * 8 + 2 * g + index // 4
        field[x] = flat[index * 32 : index * 32 + 32]


def x_form_to_native(source, folded, turned, field):
    for b in range(8):
        block = source[b].astype(F32)
        block = jnp.concatenate(
            [
                jnp.concatenate([block[g * 64 : g * 64 + 32], block[g * 64 + 32 : g * 64 + 64]], axis=1)
                for g in range(4)
            ],
            axis=0,
        )
        swap_brick(block, folded, turned, b)
    for g in range(4):
        to_native(turned[:, g * 256 : g * 256 + 256].astype(BF16), g, field)


def tap(offset):
    value = jnp.zeros(offset.shape, F32)
    for step, weight in TAPS:
        value = jnp.where(offset == step, weight, value)
        value = jnp.where(offset == -step, -weight, value)
    return value


def stencils():
    size = 256
    row, col = iota((size, size), 0), iota((size, size), 1)
    along_y = halves(jnp.where(row // 32 == col // 32, tap(col - row), 0.0))
    along_z = halves(tap(row - col))
    row, col = iota((size, 48), 0), iota((size, 48), 1)
    layer = col // 8
    place = jnp.where(layer < RIM, layer - RIM, layer - RIM + 32)
    rim_y = halves(jnp.where(row // 32 == col % 8, tap(place - row % 32), 0.0))
    return along_y, rim_y, along_z


def rim_picker():
    row, col = iota((48, 256), 0), iota((48, 256), 1)
    layer = row // 8
    place = jnp.where(layer < RIM, layer, layer - RIM + 29)
    return ((row % 8 == col // 32) & (place == col % 32)).astype(F32).astype(BF16)


def difference_x(padded, g):
    total = None
    for step, weight in TAPS:
        ahead = padded[pl.ds(8 * g + RIM + step, 8)]
        behind = padded[pl.ds(8 * g + RIM - step, 8)]
        term = weight * (ahead - behind)
        total = term if total is None else total + term
    return total.reshape(256, 256)


def difference_y(parts, rims, along_y, rim_y):
    total = mm(along_y[0], parts[0]) + mm(along_y[1], parts[0])
    if len(parts) > 1:
        total = total + mm(along_y[0], parts[1])
    return total + mm(rim_y[0], rims) + mm(rim_y[1], rims)


def difference_z(parts, along_z):
    total = mm(parts[0], along_z[0]) + mm(parts[0], along_z[1])
    if len(parts) > 1:
        total = total + mm(parts[1], along_z[0])
    return total


def rim_rows(before, after, base, g):
    rows = [before[base + h, (g // 2) * 16 : (g // 2) * 16 + 16, :].astype(F32) for h in range(RIM)]
    rows += [after[base + h, (g // 2) * 16 : (g // 2) * 16 + 16, :].astype(F32) for h in range(RIM)]
    half = (g % 2) * 8
    return jnp.concatenate([value[half : half + 8] for value in rows], axis=0).astype(BF16)


def put_rims(blocks, base, low_y, high_y):
    picker = rim_picker()
    for pair in range(2):
        left, right = mm(picker, blocks[2 * pair]), mm(picker, blocks[2 * pair + 1])
        for layer in range(2 * RIM):
            value = jnp.concatenate(
                [left[layer * 8 : layer * 8 + 8], right[layer * 8 : layer * 8 + 8]], axis=0
            ).astype(BF16)
            target = low_y if layer < RIM else high_y
            target[base + layer % RIM, pair * 16 : pair * 16 + 16, :] = value


def opening_kernel(picks, operators, template, target, first_x, last_x, mid_v, sent, low_x, high_x, low_y, high_y, target_z, tables):
    chosen = [picks[1, 0, 0, b] for b in range(8)]
    for axis in range(3):
        tables[axis] = table_rows(operators, chosen, axis).astype(BF16)
    low_x[0:RIM] = template[0:RIM]
    high_x[0:RIM] = template[29:32]
    low_x[RIM : 2 * RIM] = first_x[0, 0:RIM].astype(BF16)
    high_x[RIM : 2 * RIM] = last_x[0, 1:4].astype(BF16)
    put_rims([template[8 * g : 8 * g + 8].reshape(256, 256) for g in range(4)], 0, low_y, high_y)
    put_rims([mid_v[0, 8 * g : 8 * g + 8].astype(BF16).reshape(256, 256) for g in range(4)], RIM, low_y, high_y)
    for g in range(4):
        block = jnp.concatenate(
            [target[qh * 8 + qs] for qs in (2 * g, 2 * g + 1) for qh in range(4)], axis=0
        )
        put_pair(target_z, g, mm(identity(), block, NT).astype(BF16))


def divergence_kernel(velocity, before_x, after_x, before_y, after_y, sent, divergence, padded):
    along_y, rim_y, along_z = stencils()
    padded[0:RIM] = before_x[RIM : 2 * RIM].astype(F32)
    padded[RIM : RIM + 32] = velocity[0]
    padded[RIM + 32 : 2 * RIM + 32] = after_x[RIM : 2 * RIM].astype(F32)
    for g in range(4):
        along_one = halves(velocity[1, 8 * g : 8 * g + 8].reshape(256, 256))
        along_two = halves(velocity[2, 8 * g : 8 * g + 8].reshape(256, 256))
        total = (
            difference_x(padded, g)
            + difference_y(along_one, rim_rows(before_y, after_y, RIM, g), along_y, rim_y)
            + difference_z(along_two, along_z)
        )
        divergence[8 * g : 8 * g + 8] = total.reshape(8, 32, 256)


def rims_kernel(state, divergence, sent, native, low_x, high_x, low_y, high_y, folded, turned):
    x_form_to_native(state, folded, turned, native)
    low_x[0:RIM] = native[0:RIM]
    high_x[0:RIM] = native[29:32]
    low_x[RIM : 2 * RIM] = divergence[0:RIM].astype(BF16)
    high_x[RIM : 2 * RIM] = divergence[29:32].astype(BF16)
    put_rims([native[8 * g : 8 * g + 8].reshape(256, 256) for g in range(4)], 0, low_y, high_y)
    put_rims(
        [divergence[8 * g : 8 * g + 8].astype(BF16).reshape(256, 256) for g in range(4)], RIM, low_y, high_y
    )


def gradient_kernel(
    template,
    state,
    divergence,
    adjoint_two,
    adjoint_one,
    b0x,
    a0x,
    b0y,
    a0y,
    b1x,
    a1x,
    b1y,
    a1y,
    sent,
    gradient,
    folded,
    turned,
    weight_two,
    weight_one,
    pad_zero,
    pad_one,
    pad_div,
):
    x_form_to_native(adjoint_one, folded, turned, weight_one)
    for g in range(4):
        to_native(lane_pair(adjoint_two, g), g, weight_two)
    along_y, rim_y, along_z = stencils()
    for padded, before, middle, after, base in (
        (pad_zero, b0x, template, a0x, 0),
        (pad_one, b1x, state, a1x, 0),
        (pad_div, b1x, divergence, a1x, RIM),
    ):
        padded[0:RIM] = before[base : base + RIM].astype(F32)
        padded[RIM : RIM + 32] = middle[...].astype(F32)
        padded[RIM + 32 : 2 * RIM + 32] = after[base : base + RIM].astype(F32)
    for g in range(4):
        zero = (template[8 * g : 8 * g + 8].reshape(256, 256),)
        one = (state[8 * g : 8 * g + 8].reshape(256, 256),)
        div = halves(divergence[8 * g : 8 * g + 8].reshape(256, 256))
        weigh_one = 0.5 * weight_one[8 * g : 8 * g + 8].reshape(256, 256)
        weigh_two = 0.5 * weight_two[8 * g : 8 * g + 8].reshape(256, 256)
        for axis in range(3):
            if axis == 0:
                parts = [difference_x(padded, g) for padded in (pad_zero, pad_one, pad_div)]
            elif axis == 1:
                parts = [
                    difference_y(zero, rim_rows(b0y, a0y, 0, g), along_y, rim_y),
                    difference_y(one, rim_rows(b1y, a1y, 0, g), along_y, rim_y),
                    difference_y(div, rim_rows(b1y, a1y, RIM, g), along_y, rim_y),
                ]
            else:
                parts = [difference_z(value, along_z) for value in (zero, one, div)]
            value = weigh_one * parts[0] + weigh_two * parts[1] - 0.25 * parts[2]
            gradient[axis, 8 * g : 8 * g + 8] = value.reshape(8, 32, 256)


SCALAR = pl.BlockSpec(memory_space=pltpu.SMEM)
WHOLE = pl.BlockSpec(memory_space=pltpu.VMEM)
FAR = pl.BlockSpec(memory_space=pltpu.HBM)
FOLDED = (32, 64, 128)
FLAT = (256, 1024)
NATIVE = (32, 32, 256)
FORM = (8, 256, 128)
TABLES = (3, 32, 256)


def pinned(values):
    return [pltpu.with_memory_space_constraint(value, pltpu.HBM) for value in values]


def call(kernel, out, in_specs, out_specs, scratch, work=1 << 31):
    made = pl.pallas_call(
        kernel,
        out_shape=out,
        in_specs=in_specs,
        out_specs=out_specs,
        scratch_shapes=scratch,
        compiler_params=pltpu.CompilerParams(vmem_limit_bytes=48 * 1024 * 1024),
        cost_estimate=pl.CostEstimate(flops=work, bytes_accessed=8 * 1024 * 1024, transcendentals=0),
    )

    def apply(*values):
        specs = in_specs
        return made(*[pinned([v])[0] if spec is FAR else v for v, spec in zip(values, specs, strict=True)])

    return apply


def like(shape, dtype):
    return jax.ShapeDtypeStruct(shape, dtype)


def far(shape, dtype):
    return pltpu.HBM(shape, dtype)


def neighbours(low_x, high_x, low_y, high_y):
    moved = []
    for low, high, axis in ((low_x, high_x, "gx"), (low_y, high_y, "gy")):
        size = lax.axis_size(axis)
        up = [(i, i + 1) for i in range(size - 1)]
        down = [(i + 1, i) for i in range(size - 1)]
        moved += [lax.ppermute(high, axis, up), lax.ppermute(low, axis, down)]
    return moved


def swap_slots(send):
    return lax.all_to_all(send, "gx", split_axis=0, concat_axis=0, tiled=True)


def shards(template, target_image, velocity, operators, route, target_brick, operator_index):
    peers = lax.axis_size("gx")
    sems = pltpu.SemaphoreType.DMA((16,))
    slot_sems = pltpu.SemaphoreType.DMA((peers * CAP,))
    turning = [pltpu.VMEM(FLAT, F32), pltpu.VMEM(FOLDED, F32), pltpu.VMEM(FLAT, F32)]
    form = pltpu.VMEM(FORM, BF16)
    total = pltpu.VMEM(FORM, F32)
    landed = pltpu.SMEM((peers, 8, 128), jnp.int32)
    slots = far((peers, 512, 128), BF16)
    table_rows_count = operators.shape[1] * operators.shape[2] * operators.shape[3]
    listed = operators.transpose(1, 2, 3, 0).reshape(table_rows_count, operators.shape[0])
    route = route.reshape(route.shape[:4])

    send, tables_zero = call(
        first_kernel,
        [far((peers, 528, 128), BF16), like(TABLES, BF16)],
        [FAR] * 5,
        [FAR, WHOLE],
        [pltpu.SMEM(route.shape, jnp.int32)] * 3
        + [pltpu.VMEM(listed.shape, BF16), pltpu.VMEM(NATIVE, BF16)]
        + turning
        + [form, pltpu.VMEM((peers, 16, 128), F32), pltpu.VMEM((peers, 16, 128), BF16), sems],
    )(operator_index, route, target_brick, listed, template)
    arrived = swap_slots(send)

    rim = like((2 * RIM, 32, 256), BF16)
    rim_spec = pl.BlockSpec((2 * RIM, 32, 256), lambda i: (0, 0, 0))
    low_x, high_x, low_y, high_y, target_z, tables_one = pl.pallas_call(
        opening_kernel,
        out_shape=[rim] * 4 + [far(FORM, BF16), like(TABLES, BF16)],
        grid=(1,),
        in_specs=[
            SCALAR,
            pl.BlockSpec(listed.shape, lambda i: (0, 0)),
            pl.BlockSpec(NATIVE, lambda i: (0, 0, 0)),
            pl.BlockSpec(NATIVE, lambda i: (0, 0, 0)),
            pl.BlockSpec((1, 4, 32, 256), lambda i: (0, 0, 0, 0)),
            pl.BlockSpec((1, 4, 32, 256), lambda i: (0, 7, 0, 0)),
            pl.BlockSpec((1, 32, 32, 256), lambda i: (1, 0, 0, 0)),
            FAR,
        ],
        out_specs=[rim_spec] * 4
        + [pl.BlockSpec(FORM, lambda i: (0, 0, 0)), pl.BlockSpec(TABLES, lambda i: (0, 0, 0))],
        compiler_params=pltpu.CompilerParams(vmem_limit_bytes=48 * 1024 * 1024),
        cost_estimate=pl.CostEstimate(flops=1 << 31, bytes_accessed=8 * 1024 * 1024, transcendentals=0),
    )(operator_index, listed, template, target_image, velocity, velocity, velocity, *pinned([send]))
    b0x, a0x, b0y, a0y = neighbours(low_x, high_x, low_y, high_y)
    send, state_x, landing = call(
        second_kernel,
        [slots, far(FORM, BF16), far((peers, 8, 128), jnp.int32)],
        [SCALAR, WHOLE, FAR] + [WHOLE] * 4,
        [FAR] * 3,
        [
            pltpu.VMEM((peers, 512, 128), BF16),
            pltpu.VMEM((peers, 16, 128), BF16),
            pltpu.VMEM((peers, 8, 128), jnp.int32),
            landed,
            form,
            total,
        ]
        + turning
        + [form, sems],
    )(route, tables_one, arrived, b0x, a0x, b0y, a0y)
    arrived = swap_slots(send)

    divergence = call(
        divergence_kernel, like(NATIVE, F32), [WHOLE] * 5 + [FAR], WHOLE, [pltpu.VMEM((38, 32, 256), F32)]
    )(velocity, b0x, a0x, b0y, a0y, send)

    state, low_x, high_x, low_y, high_y = call(
        rims_kernel, [far(NATIVE, BF16)] + [rim] * 4, [WHOLE] * 2 + [FAR], [WHOLE] * 5, turning[1:]
    )(state_x, divergence, send)
    b1x, a1x, b1y, a1y = neighbours(low_x, high_x, low_y, high_y)

    send, adjoint_two = call(
        third_kernel,
        [slots, far(FORM, BF16)],
        [FAR] * 3 + [WHOLE] * 4,
        [FAR] * 2,
        [pltpu.VMEM((peers, 512, 128), BF16), landed, total, form, form, sems, slot_sems],
    )(landing, arrived, target_z, b1x, a1x, b1y, a1y)
    arrived = swap_slots(send)

    send, adjoint_one = call(
        fourth_kernel,
        [slots, far(FORM, BF16)],
        [SCALAR, WHOLE, FAR, FAR],
        [FAR] * 2,
        [form, landed] + turning + [form, sems, slot_sems],
    )(route, tables_one, landing, arrived)
    arrived = swap_slots(send)

    gradient = call(
        gradient_kernel,
        far((3,) + NATIVE, F32),
        [WHOLE] * 13 + [FAR],
        WHOLE,
        turning[1:] + [pltpu.VMEM(NATIVE, F32)] * 2 + [pltpu.VMEM((38, 32, 256), F32)] * 3,
    )(template, state, divergence, adjoint_two, adjoint_one, b0x, a0x, b0y, a0y, b1x, a1x, b1y, a1y, send)

    adjoint = call(
        fifth_kernel, like(NATIVE, BF16), [SCALAR, WHOLE, FAR, FAR], WHOLE, [form] + turning + [sems]
    )(route, tables_zero, arrived, gradient)
    return gradient, adjoint


def solution(mesh):
    placed = (
        P("gx", "gy", None),
        P("gx", "gy", None),
        P(None, "gx", "gy", None),
        P(),
        P(None, "gx", "gy", None, None),
        P(None, "gx", "gy", None),
        P(None, "gx", "gy", None),
    )
    return jax.shard_map(
        shards,
        mesh=mesh,
        in_specs=placed,
        out_specs=(P(None, "gx", "gy", None), P("gx", "gy", None)),
        check_vma=False,
    )
```

```python
import functools

import jax
import jax.numpy as jnp
from jax import lax
from jax.experimental import pallas as pl
from jax.experimental.pallas import tpu as pltpu
from jax.sharding import PartitionSpec as P

STEPS = 2
CAP = 2
RIM = 3
F32 = jnp.float32
BF16 = jnp.bfloat16
NT = (((1,), (1,)), ((), ()))
NN = (((1,), (0,)), ((), ()))
TAPS = ((1, 0.75), (2, -0.15), (3, 1.0 / 60.0))


def iota(shape, dim):
    return lax.broadcasted_iota(jnp.int32, shape, dim)


def mm(left, right, dims=NN):
    return lax.dot_general(left, right, dims, preferred_element_type=F32)


def halves(value):
    high = value.astype(BF16)
    return high, (value - high.astype(F32)).astype(BF16)


def table_rows(operators, picks, axis):
    lane = iota((operators.shape[1], 256), 1)
    chosen = jnp.zeros(lane.shape, jnp.int32)
    for b, pick in enumerate(picks):
        chosen = jnp.where(lane // 32 == b, pick, chosen)
    one_hot = (iota(lane.shape, 0) == chosen).astype(F32).astype(BF16)
    found = mm(operators[axis * 1024 : axis * 1024 + 1024, :], one_hot)
    within = iota((32, 256), 1) % 32
    total = jnp.zeros((32, 256), F32)
    for x in range(32):
        total = jnp.where(within == x, found[x * 32 : x * 32 + 32], total)
    return total


def same_block(size, edge):
    return iota((size, size), 0) // edge == iota((size, size), 1) // edge


def identity():
    return (iota((256, 256), 0) == iota((256, 256), 1)).astype(F32).astype(BF16)


def flipped_diagonal(table):
    return jnp.where(same_block(256, 32), jnp.concatenate([table] * 8, axis=0), 0.0).astype(BF16)


def diagonal(table):
    return mm(identity(), flipped_diagonal(table), NT).astype(BF16)


def spread(table):
    copies = (iota((256, 256), 0) % 32 == iota((256, 256), 1) % 32).astype(F32).astype(BF16)
    return mm(flipped_diagonal(table), copies)


def swap_chunks(parts):
    lane = iota(parts[0].shape, 1)
    for bit, shift in ((1, 32), (2, 64)):
        keep = (lane & shift) == 0
        fresh = list(parts)
        for index in range(4):
            if index & bit:
                continue
            one, two = parts[index], parts[index | bit]
            fresh[index] = jnp.where(keep, one, pltpu.roll(two, shift, 1))
            fresh[index | bit] = jnp.where(keep, pltpu.roll(one, 128 - shift, 1), two)
        parts = fresh
    return parts


def swap_brick(block, folded, turned, brick, parts=2):
    slabs = []
    for ph in range(4):
        slabs.append(
            jnp.concatenate(
                [
                    block[(qs // 2) * 32 + ph * 8 : (qs // 2) * 32 + ph * 8 + 8, (qs % 2) * 128 : (qs % 2) * 128 + 128]
                    for qs in range(8)
                ],
                axis=0,
            )
        )
    slabs = swap_chunks(slabs)
    for qh in range(4):
        folded[brick * 4 + qh] = slabs[qh]
    for ps in range(8):
        value = jnp.concatenate(
            [folded[brick * 4 + qh, pl.ds(ps, 8, stride=8), :] for qh in range(4)], axis=0
        )
        for part, half in enumerate(halves(value)[:parts]):
            turned[part * 256 + brick * 32 : part * 256 + brick * 32 + 32, ps * 128 : ps * 128 + 128] = half


def lane_pair(field, g):
    return jnp.concatenate(
        [
            jnp.concatenate([field[b, qs * 32 : qs * 32 + 32, :] for b in range(8)], axis=0)
            for qs in (2 * g, 2 * g + 1)
        ],
        axis=1,
    )


def put_pair(field, g, value):
    for b in range(8):
        for half in range(2):
            rows = slice((2 * g + half) * 32, (2 * g + half) * 32 + 32)
            field[b, rows, :] = value[b * 32 : b * 32 + 32, half * 128 : half * 128 + 128]


def middle_and_last(start, spread_mid, last, folded, turned, flipped):
    mask = same_block(256, 32)
    for brick in range(8):
        rows = spread_mid[brick * 32 : brick * 32 + 32]
        line = jnp.where(mask, jnp.concatenate([rows] * 8, axis=0), 0.0).astype(BF16)
        block = start[brick * 32 : brick * 32 + 32, :]
        block = jnp.concatenate([block[:, g * 256 : g * 256 + 256] for g in range(4)], axis=0)
        high, low = halves(block)
        both = mm(jnp.concatenate([high, low], axis=0), line, NT if flipped else NN)
        swap_brick(both[:128] + both[128:], folded, turned, brick)
    last = jnp.concatenate([last, last], axis=1)
    for g in range(4):
        yield g, mm(last, turned[:, g * 256 : g * 256 + 256]).astype(BF16)


def slot_numbers(route, step):
    own = [route[step, 0, 0, b] for b in range(8)]
    slots = []
    for b in range(8):
        rank = jnp.int32(0)
        for other in range(b):
            rank = rank + (own[other] == own[b]).astype(jnp.int32)
        slots.append((own[b], rank))
    return slots


def fetch(source, target, sem):
    copy = pltpu.make_async_copy(source, target, sem)
    copy.start()
    return copy


def send_quarter(g, bricks, send, slots, sems):
    copies = []
    for b, (place, rank) in enumerate(slots):
        rows = pl.ds(pl.multiple_of(rank * 256 + g * 64, 64), 64)
        copies.append(fetch(bricks.at[b, g * 64 : g * 64 + 64, :], send.at[place, rows, :], sems.at[g, b]))
    return copies


def first_kernel(*refs):
    picks_in, route_in, landing_in, operators, field, send, tables = refs[:7]
    picks, route, landing, table_mem, field_mem, start, folded, turned, out, meta, meta_half, tables_mem, sems, slot_sems = refs[7:]
    told = [fetch(a, b, sems.at[11 + i]) for i, (a, b) in enumerate(((picks_in, picks), (route_in, route), (landing_in, landing)))]
    loads = [fetch(operators, table_mem, sems.at[8]), fetch(field, field_mem, sems.at[9])]
    for copy in told:
        copy.wait()
    meta[...] = jnp.zeros(meta.shape, F32)
    for step in range(STEPS):
        for b, (place, rank) in enumerate(slot_numbers(route, step)):
            value = jnp.full((1, 128), landing[step, 0, 0, b] + 1, jnp.int32).astype(F32)
            meta[place, pl.ds(step * CAP + rank, 1), :] = value
    meta_half[...] = meta[...].astype(BF16)
    told = fetch(meta_half, send.at[:, 512:528, :], sems.at[10])
    chosen = [picks[0, 0, 0, b] for b in range(8)]
    loads[0].wait()
    found = [table_rows(table_mem, chosen, axis) for axis in range(3)]
    for axis in range(3):
        tables_mem[axis] = found[axis].astype(BF16)
    kept = fetch(tables_mem, tables, sems.at[8])
    begin = diagonal(found[2])
    loads[1].wait()
    for g in range(4):
        block = jnp.concatenate(
            [field_mem[qh * 8 + qs] for qs in (2 * g, 2 * g + 1) for qh in range(4)], axis=0
        )
        start[:, g * 256 : g * 256 + 256] = mm(begin, block, NT)
    slots = slot_numbers(route, 0)
    sent = []
    for g, moved in middle_and_last(start, spread(found[1]), diagonal(found[0]), folded, turned, False):
        put_pair(out, g, moved)
        sent += send_quarter(g, out, send, slots, slot_sems)
    for copy in sent + [told, kept]:
        copy.wait()


def second_kernel(route, tables_in, arrived, *refs):
    send, state, landing_out, meta, landing, tables, state_mem, total, start, folded, turned, out, sems, slot_sems = refs[-14:]
    loads = [fetch(tables_in, tables, sems.at[8])]
    meta[...] = arrived[:, 512:528, :].astype(F32).astype(jnp.int32)[:, 0:8, :]
    told = [fetch(meta, landing, sems.at[9]), fetch(meta, landing_out, sems.at[10])]
    total[...] = jnp.zeros(total.shape, F32)
    loads[0].wait()
    begin = diagonal(tables[0].astype(F32))
    mid = spread(tables[1].astype(F32))
    end = diagonal(tables[2].astype(F32))
    told[0].wait()
    gather_sum(0, landing, arrived, total)
    for b in range(8):
        state_mem[b] = total[b].astype(BF16)
    kept = fetch(state_mem, state, sems.at[9])
    for g in range(4):
        start[:, g * 256 : g * 256 + 256] = mm(begin, lane_pair(state_mem, g))
    slots = slot_numbers(route, 1)
    sent = []
    for g, moved in middle_and_last(start, mid, end, folded, turned, False):
        put_pair(out, g, moved)
        sent += send_quarter(g, out, send, slots, slot_sems)
    for copy in sent + [kept, told[1]]:
        copy.wait()


def gather_sum(step, landing, arrived, total):
    def add(source, carry):
        for rank in range(CAP):
            brick = landing[source, step * CAP + rank, 0]

            @pl.when(brick > 0)
            def _():
                total[brick - 1] += arrived[source, rank * 256 : rank * 256 + 256, :].astype(F32)

        return carry

    lax.fori_loop(0, arrived.shape[0], add, 0)


def hand_out(step, landing, field, send, sems):
    def each(act):
        def body(source, carry):
            for rank in range(CAP):
                brick = landing[source, step * CAP + rank, 0]

                @pl.when(brick > 0)
                def _():
                    act(
                        pltpu.make_async_copy(
                            field.at[brick - 1],
                            send.at[source, rank * 256 : rank * 256 + 256, :],
                            sems.at[source * CAP + rank],
                        )
                    )

            return carry

        lax.fori_loop(0, send.shape[0], body, 0)

    each(lambda copy: copy.start())
    each(lambda copy: copy.wait())


def third_kernel(landing_in, arrived, target, *refs):
    send, adjoint, landing, total, adjoint_mem, target_mem, sems, slot_sems = refs[-8:]
    loads = [fetch(landing_in, landing, sems.at[0]), fetch(target, target_mem, sems.at[2])]
    total[...] = jnp.zeros(total.shape, F32)
    for load in loads:
        load.wait()
    gather_sum(1, landing, arrived, total)
    for b in range(8):
        final = total[b].astype(BF16).astype(F32)
        adjoint_mem[b] = (final - target_mem[b].astype(F32)).astype(BF16)
    kept = fetch(adjoint_mem, adjoint, sems.at[0])
    hand_out(1, landing, adjoint_mem, send, slot_sems)
    kept.wait()


def pulled_pair(arrived, slots, g):
    tiles = []
    for qs in (2 * g, 2 * g + 1):
        rows = [
            arrived[place, pl.ds(pl.multiple_of(rank * 256 + qs * 32, 32), 32), :] for place, rank in slots
        ]
        tiles.append(jnp.concatenate(rows, axis=0))
    return jnp.concatenate(tiles, axis=1)


def fourth_kernel(route, tables_in, landing_in, arrived, *refs):
    send, adjoint, tables, landing, start, folded, turned, out, sems, slot_sems = refs[-10:]
    loads = [fetch(tables_in, tables, sems.at[1]), fetch(landing_in, landing, sems.at[2])]
    slots = slot_numbers(route, 1)
    loads[0].wait()
    begin = flipped_diagonal(tables[2].astype(F32))
    mid = spread(tables[1].astype(F32))
    end = flipped_diagonal(tables[0].astype(F32))
    for g in range(4):
        start[:, g * 256 : g * 256 + 256] = mm(begin, pulled_pair(arrived, slots, g))
    for g, moved in middle_and_last(start, mid, end, folded, turned, True):
        put_pair(out, g, moved)
    kept = fetch(out, adjoint, sems.at[0])
    loads[1].wait()
    hand_out(0, landing, out, send, slot_sems)
    kept.wait()


def fifth_kernel(route, tables_in, arrived, *refs):
    adjoint, tables, start, folded, turned, sems = refs[-6:]
    load = fetch(tables_in, tables, sems.at[0])
    slots = slot_numbers(route, 0)
    load.wait()
    begin = flipped_diagonal(tables[0].astype(F32))
    mid = spread(tables[1].astype(F32))
    end = flipped_diagonal(tables[2].astype(F32))
    for g in range(4):
        start[:, g * 256 : g * 256 + 256] = mm(begin, pulled_pair(arrived, slots, g))
    for g, moved in middle_and_last(start, mid, end, folded, turned, True):
        to_native(moved, g, adjoint)


def to_native(block, g, field):
    flat = mm(identity(), block, NT).astype(field.dtype)
    for index in range(8):
        x = (index % 4) * 8 + 2 * g + index // 4
        field[x] = flat[index * 32 : index * 32 + 32]


def x_form_to_native(source, folded, turned, field):
    for b in range(8):
        block = source[b].astype(F32)
        block = jnp.concatenate(
            [
                jnp.concatenate([block[g * 64 : g * 64 + 32], block[g * 64 + 32 : g * 64 + 64]], axis=1)
                for g in range(4)
            ],
            axis=0,
        )
        swap_brick(block, folded, turned, b, 1)
    for g in range(4):
        to_native(turned[0:256, g * 256 : g * 256 + 256], g, field)


def tap(offset):
    value = jnp.zeros(offset.shape, F32)
    for step, weight in TAPS:
        value = jnp.where(offset == step, weight, value)
        value = jnp.where(offset == -step, -weight, value)
    return value


def stencils():
    size = 256
    row, col = iota((size, size), 0), iota((size, size), 1)
    along_y = halves(jnp.where(row // 32 == col // 32, tap(col - row), 0.0))
    along_z = halves(tap(row - col))
    row, col = iota((size, 48), 0), iota((size, 48), 1)
    layer = col // 8
    place = jnp.where(layer < RIM, layer - RIM, layer - RIM + 32)
    rim_y = halves(jnp.where(row // 32 == col % 8, tap(place - row % 32), 0.0))
    return along_y, rim_y, along_z


def rim_picker():
    row, col = iota((48, 256), 0), iota((48, 256), 1)
    layer = row // 8
    place = jnp.where(layer < RIM, layer, layer - RIM + 29)
    return ((row % 8 == col // 32) & (place == col % 32)).astype(F32).astype(BF16)


def difference_x(padded, g):
    total = None
    for step, weight in TAPS:
        ahead = padded[pl.ds(8 * g + RIM + step, 8)]
        behind = padded[pl.ds(8 * g + RIM - step, 8)]
        term = weight * (ahead - behind)
        total = term if total is None else total + term
    return total.reshape(256, 256)


def difference_y(parts, rims, along_y, rim_y):
    total = mm(along_y[0], parts[0]) + mm(along_y[1], parts[0])
    if len(parts) > 1:
        total = total + mm(along_y[0], parts[1])
    return total + mm(rim_y[0], rims) + mm(rim_y[1], rims)


def difference_z(parts, along_z):
    total = mm(parts[0], along_z[0]) + mm(parts[0], along_z[1])
    if len(parts) > 1:
        total = total + mm(parts[1], along_z[0])
    return total


def rim_rows(before, after, base, g):
    rows = [before[base + h, (g // 2) * 16 : (g // 2) * 16 + 16, :].astype(F32) for h in range(RIM)]
    rows += [after[base + h, (g // 2) * 16 : (g // 2) * 16 + 16, :].astype(F32) for h in range(RIM)]
    half = (g % 2) * 8
    return jnp.concatenate([value[half : half + 8] for value in rows], axis=0).astype(BF16)


def put_rims(blocks, base, low_y, high_y):
    picker = rim_picker()
    for pair in range(2):
        left, right = mm(picker, blocks[2 * pair]), mm(picker, blocks[2 * pair + 1])
        for layer in range(2 * RIM):
            value = jnp.concatenate(
                [left[layer * 8 : layer * 8 + 8], right[layer * 8 : layer * 8 + 8]], axis=0
            ).astype(BF16)
            target = low_y if layer < RIM else high_y
            target[base + layer % RIM, pair * 16 : pair * 16 + 16, :] = value


def opening_kernel(picks, operators, template, target, first_x, last_x, mid_v, sent, low_x, high_x, low_y, high_y, target_z, tables):
    chosen = [picks[1, 0, 0, b] for b in range(8)]
    for axis in range(3):
        tables[axis] = table_rows(operators, chosen, axis).astype(BF16)
    low_x[0:RIM] = template[0:RIM]
    high_x[0:RIM] = template[29:32]
    low_x[RIM : 2 * RIM] = first_x[0, 0:RIM].astype(BF16)
    high_x[RIM : 2 * RIM] = last_x[0, 1:4].astype(BF16)
    put_rims([template[8 * g : 8 * g + 8].reshape(256, 256) for g in range(4)], 0, low_y, high_y)
    put_rims([mid_v[0, 8 * g : 8 * g + 8].astype(BF16).reshape(256, 256) for g in range(4)], RIM, low_y, high_y)
    for g in range(4):
        block = jnp.concatenate(
            [target[qh * 8 + qs] for qs in (2 * g, 2 * g + 1) for qh in range(4)], axis=0
        )
        put_pair(target_z, g, mm(identity(), block, NT).astype(BF16))


def divergence_kernel(velocity, before_x, after_x, before_y, after_y, sent, divergence, padded):
    along_y, rim_y, along_z = stencils()
    padded[0:RIM] = before_x[RIM : 2 * RIM].astype(F32)
    padded[RIM : RIM + 32] = velocity[0]
    padded[RIM + 32 : 2 * RIM + 32] = after_x[RIM : 2 * RIM].astype(F32)
    for g in range(4):
        along_one = halves(velocity[1, 8 * g : 8 * g + 8].reshape(256, 256))
        along_two = halves(velocity[2, 8 * g : 8 * g + 8].reshape(256, 256))
        total = (
            difference_x(padded, g)
            + difference_y(along_one, rim_rows(before_y, after_y, RIM, g), along_y, rim_y)
            + difference_z(along_two, along_z)
        )
        divergence[8 * g : 8 * g + 8] = total.reshape(8, 32, 256)


def rims_kernel(state, divergence, sent, native, low_x, high_x, low_y, high_y, folded, turned):
    x_form_to_native(state, folded, turned, native)
    low_x[0:RIM] = native[0:RIM]
    high_x[0:RIM] = native[29:32]
    low_x[RIM : 2 * RIM] = divergence[0:RIM].astype(BF16)
    high_x[RIM : 2 * RIM] = divergence[29:32].astype(BF16)
    put_rims([native[8 * g : 8 * g + 8].reshape(256, 256) for g in range(4)], 0, low_y, high_y)
    put_rims(
        [divergence[8 * g : 8 * g + 8].astype(BF16).reshape(256, 256) for g in range(4)], RIM, low_y, high_y
    )


def gradient_kernel(
    template,
    state,
    divergence,
    adjoint_two,
    adjoint_one,
    b0x,
    a0x,
    b0y,
    a0y,
    b1x,
    a1x,
    b1y,
    a1y,
    sent,
    gradient,
    folded,
    turned,
    weight_two,
    weight_one,
    pad_zero,
    pad_one,
    pad_div,
):
    x_form_to_native(adjoint_one, folded, turned, weight_one)
    for g in range(4):
        to_native(lane_pair(adjoint_two, g), g, weight_two)
    along_y, rim_y, along_z = stencils()
    for padded, before, middle, after, base in (
        (pad_zero, b0x, template, a0x, 0),
        (pad_one, b1x, state, a1x, 0),
        (pad_div, b1x, divergence, a1x, RIM),
    ):
        padded[0:RIM] = before[base : base + RIM].astype(F32)
        padded[RIM : RIM + 32] = middle[...].astype(F32)
        padded[RIM + 32 : 2 * RIM + 32] = after[base : base + RIM].astype(F32)
    for g in range(4):
        zero = (template[8 * g : 8 * g + 8].reshape(256, 256),)
        one = (state[8 * g : 8 * g + 8].reshape(256, 256),)
        div = halves(divergence[8 * g : 8 * g + 8].reshape(256, 256))
        weigh_one = 0.5 * weight_one[8 * g : 8 * g + 8].reshape(256, 256)
        weigh_two = 0.5 * weight_two[8 * g : 8 * g + 8].reshape(256, 256)
        for axis in range(3):
            if axis == 0:
                parts = [difference_x(padded, g) for padded in (pad_zero, pad_one, pad_div)]
            elif axis == 1:
                parts = [
                    difference_y(zero, rim_rows(b0y, a0y, 0, g), along_y, rim_y),
                    difference_y(one, rim_rows(b1y, a1y, 0, g), along_y, rim_y),
                    difference_y(div, rim_rows(b1y, a1y, RIM, g), along_y, rim_y),
                ]
            else:
                parts = [difference_z(value, along_z) for value in (zero, one, div)]
            value = weigh_one * parts[0] + weigh_two * parts[1] - 0.25 * parts[2]
            gradient[axis, 8 * g : 8 * g + 8] = value.reshape(8, 32, 256)


SCALAR = pl.BlockSpec(memory_space=pltpu.SMEM)
WHOLE = pl.BlockSpec(memory_space=pltpu.VMEM)
NEAR = pl.BlockSpec(memory_space=pltpu.VMEM)
FAR = pl.BlockSpec(memory_space=pltpu.HBM)
FOLDED = (32, 64, 128)
FLAT = (256, 1024)
NATIVE = (32, 32, 256)
FORM = (8, 256, 128)
TABLES = (3, 32, 256)


def pinned(value, spec):
    if spec is FAR:
        return pltpu.with_memory_space_constraint(value, pltpu.HBM)
    if spec is NEAR:
        return pltpu.with_memory_space_constraint(value, pltpu.VMEM)
    return value


def call(kernel, out, in_specs, out_specs, scratch, work=1 << 31):
    made = pl.pallas_call(
        kernel,
        out_shape=out,
        in_specs=in_specs,
        out_specs=out_specs,
        scratch_shapes=scratch,
        compiler_params=pltpu.CompilerParams(vmem_limit_bytes=24 * 1024 * 1024),
        cost_estimate=pl.CostEstimate(flops=work, bytes_accessed=8 * 1024 * 1024, transcendentals=0),
    )

    def apply(*values):
        return made(*[pinned(value, spec) for value, spec in zip(values, in_specs, strict=True)])

    return apply


def like(shape, dtype):
    return jax.ShapeDtypeStruct(shape, dtype)


def far(shape, dtype):
    return pltpu.HBM(shape, dtype)


def neighbours(low_x, high_x, low_y, high_y):
    moved = []
    for low, high, axis in ((low_x, high_x, "gx"), (low_y, high_y, "gy")):
        size = lax.axis_size(axis)
        up = [(i, i + 1) for i in range(size - 1)]
        down = [(i + 1, i) for i in range(size - 1)]
        moved += [lax.ppermute(high, axis, up), lax.ppermute(low, axis, down)]
    return moved


def swap_slots(send):
    return lax.all_to_all(send, "gx", split_axis=0, concat_axis=0, tiled=True)


def shards(template, target_image, velocity, operators, route, target_brick, operator_index):
    peers = lax.axis_size("gx")
    sems = pltpu.SemaphoreType.DMA((16,))
    slot_sems = pltpu.SemaphoreType.DMA((peers * CAP,))
    quarter_sems = pltpu.SemaphoreType.DMA((4, 8))
    turning = [pltpu.VMEM(FLAT, F32), pltpu.VMEM(FOLDED, F32), pltpu.VMEM((512, 1024), BF16)]
    form = pltpu.VMEM(FORM, BF16)
    total = pltpu.VMEM(FORM, F32)
    landed = pltpu.SMEM((peers, 8, 128), jnp.int32)
    slots = far((peers, 512, 128), BF16)
    table_rows_count = operators.shape[1] * operators.shape[2] * operators.shape[3]
    listed = operators.transpose(1, 2, 3, 0).reshape(table_rows_count, operators.shape[0])
    route = route.reshape(route.shape[:4])

    send, tables_zero = call(
        first_kernel,
        [far((peers, 528, 128), BF16), far(TABLES, BF16)],
        [FAR] * 5,
        [FAR, FAR],
        [pltpu.SMEM(route.shape, jnp.int32)] * 3
        + [pltpu.VMEM(listed.shape, BF16), pltpu.VMEM(NATIVE, BF16)]
        + turning
        + [
            form,
            pltpu.VMEM((peers, 16, 128), F32),
            pltpu.VMEM((peers, 16, 128), BF16),
            pltpu.VMEM(TABLES, BF16),
            sems,
            quarter_sems,
        ],
    )(operator_index, route, target_brick, listed, template)
    arrived = swap_slots(send)

    rim = like((2 * RIM, 32, 256), BF16)
    rim_spec = pl.BlockSpec((2 * RIM, 32, 256), lambda i: (0, 0, 0))
    low_x, high_x, low_y, high_y, target_z, tables_one = pl.pallas_call(
        opening_kernel,
        out_shape=[rim] * 4 + [far(FORM, BF16), far(TABLES, BF16)],
        grid=(1,),
        in_specs=[
            SCALAR,
            pl.BlockSpec(listed.shape, lambda i: (0, 0)),
            pl.BlockSpec(NATIVE, lambda i: (0, 0, 0)),
            pl.BlockSpec(NATIVE, lambda i: (0, 0, 0)),
            pl.BlockSpec((1, 4, 32, 256), lambda i: (0, 0, 0, 0)),
            pl.BlockSpec((1, 4, 32, 256), lambda i: (0, 7, 0, 0)),
            pl.BlockSpec((1, 32, 32, 256), lambda i: (1, 0, 0, 0)),
            FAR,
        ],
        out_specs=[rim_spec] * 4
        + [pl.BlockSpec(FORM, lambda i: (0, 0, 0)), pl.BlockSpec(TABLES, lambda i: (0, 0, 0))],
        compiler_params=pltpu.CompilerParams(vmem_limit_bytes=24 * 1024 * 1024),
        cost_estimate=pl.CostEstimate(flops=1 << 31, bytes_accessed=8 * 1024 * 1024, transcendentals=0),
    )(operator_index, listed, template, target_image, velocity, velocity, velocity, pinned(send, FAR))
    b0x, a0x, b0y, a0y = neighbours(low_x, high_x, low_y, high_y)
    send, state_x, landing = call(
        second_kernel,
        [slots, far(FORM, BF16), far((peers, 8, 128), jnp.int32)],
        [SCALAR, FAR, NEAR] + [WHOLE] * 4,
        [FAR] * 3,
        [
            pltpu.VMEM((peers, 8, 128), jnp.int32),
            landed,
            pltpu.VMEM(TABLES, BF16),
            form,
            total,
        ]
        + turning
        + [form, sems, quarter_sems],
    )(route, tables_one, arrived, b0x, a0x, b0y, a0y)
    arrived = swap_slots(send)

    divergence = call(
        divergence_kernel, like(NATIVE, F32), [WHOLE] * 5 + [FAR], WHOLE, [pltpu.VMEM((38, 32, 256), F32)]
    )(velocity, b0x, a0x, b0y, a0y, send)

    state, low_x, high_x, low_y, high_y = call(
        rims_kernel, [far(NATIVE, BF16)] + [rim] * 4, [WHOLE] * 2 + [FAR], [WHOLE] * 5, turning[1:]
    )(state_x, divergence, send)
    b1x, a1x, b1y, a1y = neighbours(low_x, high_x, low_y, high_y)

    send, adjoint_two = call(
        third_kernel,
        [slots, far(FORM, BF16)],
        [FAR, NEAR, FAR] + [WHOLE] * 4,
        [FAR] * 2,
        [landed, total, form, form, sems, slot_sems],
    )(landing, arrived, target_z, b1x, a1x, b1y, a1y)
    arrived = swap_slots(send)

    send, adjoint_one = call(
        fourth_kernel,
        [slots, far(FORM, BF16)],
        [SCALAR, FAR, FAR, NEAR],
        [FAR] * 2,
        [pltpu.VMEM(TABLES, BF16), landed] + turning + [form, sems, slot_sems],
    )(route, tables_one, landing, arrived)
    arrived = swap_slots(send)

    gradient = call(
        gradient_kernel,
        far((3,) + NATIVE, F32),
        [WHOLE] * 13 + [FAR],
        WHOLE,
        turning[1:] + [pltpu.VMEM(NATIVE, F32)] * 2 + [pltpu.VMEM((38, 32, 256), F32)] * 3,
    )(template, state, divergence, adjoint_two, adjoint_one, b0x, a0x, b0y, a0y, b1x, a1x, b1y, a1y, send)

    adjoint = call(
        fifth_kernel, like(NATIVE, BF16), [SCALAR, FAR, NEAR, FAR], WHOLE, [pltpu.VMEM(TABLES, BF16)] + turning + [sems]
    )(route, tables_zero, arrived, gradient)
    return gradient, adjoint


def solution(mesh):
    placed = (
        P("gx", "gy", None),
        P("gx", "gy", None),
        P(None, "gx", "gy", None),
        P(),
        P(None, "gx", "gy", None, None),
        P(None, "gx", "gy", None),
        P(None, "gx", "gy", None),
    )
    return jax.shard_map(
        shards,
        mesh=mesh,
        in_specs=placed,
        out_specs=(P(None, "gx", "gy", None), P("gx", "gy", None)),
        check_vma=False,
    )
```

```python
import functools

import jax
import jax.numpy as jnp
from jax import lax
from jax.experimental import pallas as pl
from jax.experimental.pallas import tpu as pltpu
from jax.sharding import PartitionSpec as P

STEPS = 2
CAP = 2
RIM = 3
F32 = jnp.float32
BF16 = jnp.bfloat16
NT = (((1,), (1,)), ((), ()))
NN = (((1,), (0,)), ((), ()))
TAPS = ((1, 0.75), (2, -0.15), (3, 1.0 / 60.0))


def iota(shape, dim):
    return lax.broadcasted_iota(jnp.int32, shape, dim)


def mm(left, right, dims=NN):
    return lax.dot_general(left, right, dims, preferred_element_type=F32)


def halves(value):
    high = value.astype(BF16)
    return high, (value - high.astype(F32)).astype(BF16)


def table_rows(operators, picks, axis):
    lane = iota((operators.shape[1], 256), 1)
    chosen = jnp.zeros(lane.shape, jnp.int32)
    for b, pick in enumerate(picks):
        chosen = jnp.where(lane // 32 == b, pick, chosen)
    one_hot = (iota(lane.shape, 0) == chosen).astype(F32).astype(BF16)
    found = mm(operators[axis * 1024 : axis * 1024 + 1024, :], one_hot)
    within = iota((32, 256), 1) % 32
    total = jnp.zeros((32, 256), F32)
    for x in range(32):
        total = jnp.where(within == x, found[x * 32 : x * 32 + 32], total)
    return total


def same_block(size, edge):
    return iota((size, size), 0) // edge == iota((size, size), 1) // edge


def identity():
    return (iota((256, 256), 0) == iota((256, 256), 1)).astype(F32).astype(BF16)


def flipped_diagonal(table):
    return jnp.where(same_block(256, 32), jnp.concatenate([table] * 8, axis=0), 0.0).astype(BF16)


def diagonal(table):
    return mm(identity(), flipped_diagonal(table), NT).astype(BF16)


def spread(table):
    copies = (iota((256, 256), 0) % 32 == iota((256, 256), 1) % 32).astype(F32).astype(BF16)
    return mm(flipped_diagonal(table), copies)


def swap_chunks(parts):
    lane = iota(parts[0].shape, 1)
    for bit, shift in ((1, 32), (2, 64)):
        keep = (lane & shift) == 0
        fresh = list(parts)
        for index in range(4):
            if index & bit:
                continue
            one, two = parts[index], parts[index | bit]
            fresh[index] = jnp.where(keep, one, pltpu.roll(two, shift, 1))
            fresh[index | bit] = jnp.where(keep, pltpu.roll(one, 128 - shift, 1), two)
        parts = fresh
    return parts


def swap_brick(block, folded, turned, brick, parts=2):
    slabs = []
    for ph in range(4):
        slabs.append(
            jnp.concatenate(
                [
                    block[(qs // 2) * 32 + ph * 8 : (qs // 2) * 32 + ph * 8 + 8, (qs % 2) * 128 : (qs % 2) * 128 + 128]
                    for qs in range(8)
                ],
                axis=0,
            )
        )
    slabs = swap_chunks(slabs)
    for qh in range(4):
        folded[brick * 4 + qh] = slabs[qh]
    for ps in range(8):
        value = jnp.concatenate(
            [folded[brick * 4 + qh, pl.ds(ps, 8, stride=8), :] for qh in range(4)], axis=0
        )
        for part, half in enumerate(halves(value)[:parts]):
            turned[part * 256 + brick * 32 : part * 256 + brick * 32 + 32, ps * 128 : ps * 128 + 128] = half


def lane_pair(field, g):
    return jnp.concatenate(
        [
            jnp.concatenate([field[b, qs * 32 : qs * 32 + 32, :] for b in range(8)], axis=0)
            for qs in (2 * g, 2 * g + 1)
        ],
        axis=1,
    )


def put_pair(field, g, value):
    for b in range(8):
        for half in range(2):
            rows = slice((2 * g + half) * 32, (2 * g + half) * 32 + 32)
            field[b, rows, :] = value[b * 32 : b * 32 + 32, half * 128 : half * 128 + 128]


def middle_and_last(start, spread_mid, last, folded, turned, flipped):
    mask = same_block(256, 32)
    for brick in range(8):
        rows = spread_mid[brick * 32 : brick * 32 + 32]
        line = jnp.where(mask, jnp.concatenate([rows] * 8, axis=0), 0.0).astype(BF16)
        block = start[brick * 32 : brick * 32 + 32, :]
        block = jnp.concatenate([block[:, g * 256 : g * 256 + 256] for g in range(4)], axis=0)
        high, low = halves(block)
        both = mm(jnp.concatenate([high, low], axis=0), line, NT if flipped else NN)
        swap_brick(both[:128] + both[128:], folded, turned, brick)
    last = jnp.concatenate([last, last], axis=1)
    for g in range(4):
        yield g, mm(last, turned[:, g * 256 : g * 256 + 256]).astype(BF16)


def slot_numbers(route, step):
    own = [route[step, 0, 0, b] for b in range(8)]
    slots = []
    for b in range(8):
        rank = jnp.int32(0)
        for other in range(b):
            rank = rank + (own[other] == own[b]).astype(jnp.int32)
        slots.append((own[b], rank))
    return slots


def fetch(source, target, sem):
    copy = pltpu.make_async_copy(source, target, sem)
    copy.start()
    return copy


def send_quarter(g, bricks, send, slots, sems):
    copies = []
    for b, (place, rank) in enumerate(slots):
        rows = pl.ds(pl.multiple_of(rank * 256 + g * 64, 64), 64)
        copies.append(fetch(bricks.at[b, g * 64 : g * 64 + 64, :], send.at[place, rows, :], sems.at[g, b]))
    return copies


def first_kernel(*refs):
    picks_in, route_in, landing_in, operators, field, send, tables = refs[:7]
    picks, route, landing, table_mem, field_mem, start, folded, turned, out, meta, meta_half, tables_mem, sems, slot_sems = refs[7:]
    told = [fetch(a, b, sems.at[11 + i]) for i, (a, b) in enumerate(((picks_in, picks), (route_in, route), (landing_in, landing)))]
    loads = [fetch(operators, table_mem, sems.at[8]), fetch(field, field_mem, sems.at[9])]
    for copy in told:
        copy.wait()
    meta[...] = jnp.zeros(meta.shape, F32)
    for step in range(STEPS):
        for b, (place, rank) in enumerate(slot_numbers(route, step)):
            value = jnp.full((1, 128), landing[step, 0, 0, b] + 1, jnp.int32).astype(F32)
            meta[place, pl.ds(step * CAP + rank, 1), :] = value
    meta_half[...] = meta[...].astype(BF16)
    told = fetch(meta_half, send.at[:, 512:528, :], sems.at[10])
    chosen = [picks[0, 0, 0, b] for b in range(8)]
    loads[0].wait()
    found = [table_rows(table_mem, chosen, axis) for axis in range(3)]
    for axis in range(3):
        tables_mem[axis] = found[axis].astype(BF16)
    kept = fetch(tables_mem, tables, sems.at[8])
    begin = diagonal(found[2])
    loads[1].wait()
    for g in range(4):
        block = jnp.concatenate(
            [field_mem[qh * 8 + qs] for qs in (2 * g, 2 * g + 1) for qh in range(4)], axis=0
        )
        start[:, g * 256 : g * 256 + 256] = mm(begin, block, NT)
    slots = slot_numbers(route, 0)
    sent = []
    for g, moved in middle_and_last(start, spread(found[1]), diagonal(found[0]), folded, turned, False):
        put_pair(out, g, moved)
        sent += send_quarter(g, out, send, slots, slot_sems)
    for copy in sent + [told, kept]:
        copy.wait()


def second_kernel(route, tables, arrived, *refs):
    send, state, landing_out, arrived_mem, meta_half, meta, landing, state_mem, total, start, folded, turned, out, sems, slot_sems = refs[-15:]
    loads = pull_slots(arrived, arrived_mem, slot_sems)
    heard = fetch(arrived.at[:, 512:528, :], meta_half, sems.at[8])
    total[...] = jnp.zeros(total.shape, F32)
    begin = diagonal(tables[0].astype(F32))
    mid = spread(tables[1].astype(F32))
    end = diagonal(tables[2].astype(F32))
    heard.wait()
    meta[...] = meta_half[...].astype(F32).astype(jnp.int32)[:, 0:8, :]
    told = [fetch(meta, landing, sems.at[9]), fetch(meta, landing_out, sems.at[10])]
    told[0].wait()
    gather_sum(0, landing, arrived_mem, total, loads)
    for b in range(8):
        state_mem[b] = total[b + 1].astype(BF16)
    kept = fetch(state_mem, state, sems.at[9])
    for g in range(4):
        start[:, g * 256 : g * 256 + 256] = mm(begin, lane_pair(state_mem, g))
    slots = slot_numbers(route, 1)
    sent = []
    for g, moved in middle_and_last(start, mid, end, folded, turned, False):
        put_pair(out, g, moved)
        sent += send_quarter(g, out, send, slots, slot_sems)
    for copy in sent + [kept, told[1]]:
        copy.wait()


def pull_slots(arrived, arrived_mem, sems):
    return [
        fetch(arrived.at[source, 0:512, :], arrived_mem.at[source], sems.at[source // 8, source % 8])
        for source in range(arrived.shape[0])
    ]


def gather_sum(step, landing, arrived, total, loads):
    for source, load in enumerate(loads):
        load.wait()
        for rank in range(CAP):
            brick = landing[source, step * CAP + rank, 0]
            total[brick] += arrived[source, rank * 256 : rank * 256 + 256, :].astype(F32)


def hand_out(step, landing, field, send, sems):
    copies = []
    for source in range(send.shape[0]):
        for rank in range(CAP):
            brick = jnp.maximum(landing[source, step * CAP + rank, 0] - 1, 0)
            target = send.at[source, rank * 256 : rank * 256 + 256, :]
            copies.append(fetch(field.at[brick], target, sems.at[source * CAP + rank]))
    return copies


def third_kernel(landing_in, arrived, target, *refs):
    send, adjoint, arrived_mem, landing, total, adjoint_mem, target_mem, sems, load_sems, slot_sems = refs[-10:]
    told = fetch(landing_in, landing, sems.at[0])
    loads = pull_slots(arrived, arrived_mem, load_sems)
    aim = fetch(target, target_mem, sems.at[2])
    total[...] = jnp.zeros(total.shape, F32)
    told.wait()
    gather_sum(1, landing, arrived_mem, total, loads)
    aim.wait()
    for b in range(8):
        final = total[b + 1].astype(BF16).astype(F32)
        adjoint_mem[b] = (final - target_mem[b].astype(F32)).astype(BF16)
    sent = hand_out(1, landing, adjoint_mem, send, slot_sems)
    for copy in sent + [fetch(adjoint_mem, adjoint, sems.at[0])]:
        copy.wait()


def pulled_pair(arrived, slots, g):
    tiles = []
    for qs in (2 * g, 2 * g + 1):
        rows = [
            arrived[place, pl.ds(pl.multiple_of(rank * 256 + qs * 32, 32), 32), :] for place, rank in slots
        ]
        tiles.append(jnp.concatenate(rows, axis=0))
    return jnp.concatenate(tiles, axis=1)


def fourth_kernel(route, tables, landing_in, arrived, *refs):
    send, adjoint, bricks, landing, start, folded, turned, out, sems, slot_sems = refs[-10:]
    loads = []
    for b, (place, rank) in enumerate(slot_numbers(route, 1)):
        source = arrived.at[place, pl.ds(pl.multiple_of(rank * 256, 256), 256), :]
        loads.append(fetch(source, bricks.at[b], sems.at[b]))
    told = fetch(landing_in, landing, sems.at[8])
    begin = flipped_diagonal(tables[2].astype(F32))
    mid = spread(tables[1].astype(F32))
    end = flipped_diagonal(tables[0].astype(F32))
    for load in loads:
        load.wait()
    for g in range(4):
        start[:, g * 256 : g * 256 + 256] = mm(begin, lane_pair(bricks, g))
    for g, moved in middle_and_last(start, mid, end, folded, turned, True):
        put_pair(out, g, moved)
    told.wait()
    sent = hand_out(0, landing, out, send, slot_sems)
    for copy in sent + [fetch(out, adjoint, sems.at[0])]:
        copy.wait()


def fifth_kernel(route, tables, arrived, *refs):
    adjoint, start, folded, turned, out, sems = refs[-6:]
    slots = slot_numbers(route, 0)
    begin = flipped_diagonal(tables[0].astype(F32))
    mid = spread(tables[1].astype(F32))
    end = flipped_diagonal(tables[2].astype(F32))
    for g in range(4):
        start[:, g * 256 : g * 256 + 256] = mm(begin, pulled_pair(arrived, slots, g))
    stored = []
    for g, moved in middle_and_last(start, mid, end, folded, turned, True):
        to_native(moved, g, out)
        for qh in range(4):
            rows = slice(qh * 8 + 2 * g, qh * 8 + 2 * g + 2)
            stored.append(fetch(out.at[rows], adjoint.at[rows], sems.at[g, qh]))
    for copy in stored:
        copy.wait()


def to_native(block, g, field):
    flat = mm(identity(), block, NT).astype(field.dtype)
    for index in range(8):
        x = (index % 4) * 8 + 2 * g + index // 4
        field[x] = flat[index * 32 : index * 32 + 32]


def x_form_to_native(source, folded, turned, field):
    for b in range(8):
        block = source[b].astype(F32)
        block = jnp.concatenate(
            [
                jnp.concatenate([block[g * 64 : g * 64 + 32], block[g * 64 + 32 : g * 64 + 64]], axis=1)
                for g in range(4)
            ],
            axis=0,
        )
        swap_brick(block, folded, turned, b, 1)
    for g in range(4):
        to_native(turned[0:256, g * 256 : g * 256 + 256], g, field)


def tap(offset):
    value = jnp.zeros(offset.shape, F32)
    for step, weight in TAPS:
        value = jnp.where(offset == step, weight, value)
        value = jnp.where(offset == -step, -weight, value)
    return value


def stencils():
    size = 256
    row, col = iota((size, size), 0), iota((size, size), 1)
    along_y = halves(jnp.where(row // 32 == col // 32, tap(col - row), 0.0))
    along_z = halves(tap(row - col))
    row, col = iota((size, 48), 0), iota((size, 48), 1)
    layer = col // 8
    place = jnp.where(layer < RIM, layer - RIM, layer - RIM + 32)
    rim_y = halves(jnp.where(row // 32 == col % 8, tap(place - row % 32), 0.0))
    return along_y, rim_y, along_z


def rim_picker():
    row, col = iota((48, 256), 0), iota((48, 256), 1)
    layer = row // 8
    place = jnp.where(layer < RIM, layer, layer - RIM + 29)
    return ((row % 8 == col // 32) & (place == col % 32)).astype(F32).astype(BF16)


def difference_x(padded, g):
    total = None
    for step, weight in TAPS:
        ahead = padded[pl.ds(8 * g + RIM + step, 8)]
        behind = padded[pl.ds(8 * g + RIM - step, 8)]
        term = weight * (ahead - behind)
        total = term if total is None else total + term
    return total.reshape(256, 256)


def difference_y(parts, rims, along_y, rim_y):
    total = mm(along_y[0], parts[0]) + mm(along_y[1], parts[0])
    if len(parts) > 1:
        total = total + mm(along_y[0], parts[1])
    return total + mm(rim_y[0], rims) + mm(rim_y[1], rims)


def difference_z(parts, along_z):
    total = mm(parts[0], along_z[0]) + mm(parts[0], along_z[1])
    if len(parts) > 1:
        total = total + mm(parts[1], along_z[0])
    return total


def rim_rows(before, after, base, g):
    rows = [before[base + h, (g // 2) * 16 : (g // 2) * 16 + 16, :].astype(F32) for h in range(RIM)]
    rows += [after[base + h, (g // 2) * 16 : (g // 2) * 16 + 16, :].astype(F32) for h in range(RIM)]
    half = (g % 2) * 8
    return jnp.concatenate([value[half : half + 8] for value in rows], axis=0).astype(BF16)


def put_rims(blocks, base, low_y, high_y):
    picker = rim_picker()
    for pair in range(2):
        left, right = mm(picker, blocks[2 * pair]), mm(picker, blocks[2 * pair + 1])
        for layer in range(2 * RIM):
            value = jnp.concatenate(
                [left[layer * 8 : layer * 8 + 8], right[layer * 8 : layer * 8 + 8]], axis=0
            ).astype(BF16)
            target = low_y if layer < RIM else high_y
            target[base + layer % RIM, pair * 16 : pair * 16 + 16, :] = value


def edge_kernel(template, velocity, sent, low_x, high_x, low_y, high_y, field, first_x, last_x, mid_v, sems):
    loads = [
        fetch(template, field, sems.at[0]),
        fetch(velocity.at[0, 0:RIM], first_x, sems.at[1]),
        fetch(velocity.at[0, 29:32], last_x, sems.at[2]),
        fetch(velocity.at[1], mid_v, sems.at[3]),
    ]
    for load in loads:
        load.wait()
    low_x[0:RIM] = field[0:RIM]
    high_x[0:RIM] = field[29:32]
    low_x[RIM : 2 * RIM] = first_x[...].astype(BF16)
    high_x[RIM : 2 * RIM] = last_x[...].astype(BF16)
    put_rims([field[8 * g : 8 * g + 8].reshape(256, 256) for g in range(4)], 0, low_y, high_y)
    put_rims([mid_v[8 * g : 8 * g + 8].astype(BF16).reshape(256, 256) for g in range(4)], RIM, low_y, high_y)


def prepare_kernel(picks, operators, target, edge, target_z, tables):
    chosen = [picks[1, 0, 0, b] for b in range(8)]
    for axis in range(3):
        tables[axis] = table_rows(operators, chosen, axis).astype(BF16)
    for g in range(4):
        block = jnp.concatenate(
            [target[qh * 8 + qs] for qs in (2 * g, 2 * g + 1) for qh in range(4)], axis=0
        )
        put_pair(target_z, g, mm(identity(), block, NT).astype(BF16))


def divergence_kernel(velocity, before_x, after_x, before_y, after_y, sent, divergence, padded):
    along_y, rim_y, along_z = stencils()
    padded[0:RIM] = before_x[RIM : 2 * RIM].astype(F32)
    padded[RIM : RIM + 32] = velocity[0]
    padded[RIM + 32 : 2 * RIM + 32] = after_x[RIM : 2 * RIM].astype(F32)
    for g in range(4):
        along_one = halves(velocity[1, 8 * g : 8 * g + 8].reshape(256, 256))
        along_two = halves(velocity[2, 8 * g : 8 * g + 8].reshape(256, 256))
        total = (
            difference_x(padded, g)
            + difference_y(along_one, rim_rows(before_y, after_y, RIM, g), along_y, rim_y)
            + difference_z(along_two, along_z)
        )
        divergence[8 * g : 8 * g + 8] = total.reshape(8, 32, 256)


def rims_kernel(state, divergence, sent, native, low_x, high_x, low_y, high_y, folded, turned):
    x_form_to_native(state, folded, turned, native)
    low_x[0:RIM] = native[0:RIM]
    high_x[0:RIM] = native[29:32]
    low_x[RIM : 2 * RIM] = divergence[0:RIM].astype(BF16)
    high_x[RIM : 2 * RIM] = divergence[29:32].astype(BF16)
    put_rims([native[8 * g : 8 * g + 8].reshape(256, 256) for g in range(4)], 0, low_y, high_y)
    put_rims(
        [divergence[8 * g : 8 * g + 8].astype(BF16).reshape(256, 256) for g in range(4)], RIM, low_y, high_y
    )


def gradient_kernel(
    template,
    state,
    divergence,
    adjoint_two,
    adjoint_one,
    b0x,
    a0x,
    b0y,
    a0y,
    b1x,
    a1x,
    b1y,
    a1y,
    sent,
    gradient,
    folded,
    turned,
    weight_two,
    weight_one,
    pad_zero,
    pad_one,
    pad_div,
):
    x_form_to_native(adjoint_one, folded, turned, weight_one)
    for g in range(4):
        to_native(lane_pair(adjoint_two, g), g, weight_two)
    along_y, rim_y, along_z = stencils()
    for padded, before, middle, after, base in (
        (pad_zero, b0x, template, a0x, 0),
        (pad_one, b1x, state, a1x, 0),
        (pad_div, b1x, divergence, a1x, RIM),
    ):
        padded[0:RIM] = before[base : base + RIM].astype(F32)
        padded[RIM : RIM + 32] = middle[...].astype(F32)
        padded[RIM + 32 : 2 * RIM + 32] = after[base : base + RIM].astype(F32)
    for g in range(4):
        zero = (template[8 * g : 8 * g + 8].reshape(256, 256),)
        one = (state[8 * g : 8 * g + 8].reshape(256, 256),)
        div = halves(divergence[8 * g : 8 * g + 8].reshape(256, 256))
        weigh_one = 0.5 * weight_one[8 * g : 8 * g + 8].reshape(256, 256)
        weigh_two = 0.5 * weight_two[8 * g : 8 * g + 8].reshape(256, 256)
        for axis in range(3):
            if axis == 0:
                parts = [difference_x(padded, g) for padded in (pad_zero, pad_one, pad_div)]
            elif axis == 1:
                parts = [
                    difference_y(zero, rim_rows(b0y, a0y, 0, g), along_y, rim_y),
                    difference_y(one, rim_rows(b1y, a1y, 0, g), along_y, rim_y),
                    difference_y(div, rim_rows(b1y, a1y, RIM, g), along_y, rim_y),
                ]
            else:
                parts = [difference_z(value, along_z) for value in (zero, one, div)]
            value = weigh_one * parts[0] + weigh_two * parts[1] - 0.25 * parts[2]
            gradient[axis, 8 * g : 8 * g + 8] = value.reshape(8, 32, 256)


SCALAR = pl.BlockSpec(memory_space=pltpu.SMEM)
WHOLE = pl.BlockSpec(memory_space=pltpu.VMEM)
NEAR = pl.BlockSpec(memory_space=pltpu.VMEM)
FAR = pl.BlockSpec(memory_space=pltpu.HBM)
FOLDED = (32, 64, 128)
FLAT = (256, 1024)
NATIVE = (32, 32, 256)
FORM = (8, 256, 128)
TABLES = (3, 32, 256)


def pinned(value, spec):
    if spec is FAR:
        return pltpu.with_memory_space_constraint(value, pltpu.HBM)
    if spec is NEAR:
        return pltpu.with_memory_space_constraint(value, pltpu.VMEM)
    return value


def call(kernel, out, in_specs, out_specs, scratch, work=1 << 31):
    made = pl.pallas_call(
        kernel,
        out_shape=out,
        in_specs=in_specs,
        out_specs=out_specs,
        scratch_shapes=scratch,
        compiler_params=pltpu.CompilerParams(vmem_limit_bytes=24 * 1024 * 1024),
        cost_estimate=pl.CostEstimate(flops=work, bytes_accessed=8 * 1024 * 1024, transcendentals=0),
    )

    def apply(*values):
        return made(*[pinned(value, spec) for value, spec in zip(values, in_specs, strict=True)])

    return apply


def like(shape, dtype):
    return jax.ShapeDtypeStruct(shape, dtype)


def far(shape, dtype):
    return pltpu.HBM(shape, dtype)


def neighbours(low_x, high_x, low_y, high_y):
    moved = []
    for low, high, axis in ((low_x, high_x, "gx"), (low_y, high_y, "gy")):
        size = lax.axis_size(axis)
        up = [(i, i + 1) for i in range(size - 1)]
        down = [(i + 1, i) for i in range(size - 1)]
        moved += [lax.ppermute(high, axis, up), lax.ppermute(low, axis, down)]
    return moved


def swap_slots(send):
    return lax.all_to_all(send, "gx", split_axis=0, concat_axis=0, tiled=True)


def shards(template, target_image, velocity, operators, route, target_brick, operator_index):
    peers = lax.axis_size("gx")
    sems = pltpu.SemaphoreType.DMA((16,))
    slot_sems = pltpu.SemaphoreType.DMA((peers * CAP,))
    quarter_sems = pltpu.SemaphoreType.DMA((4, 8))
    turning = [pltpu.VMEM(FLAT, F32), pltpu.VMEM(FOLDED, F32), pltpu.VMEM((512, 1024), BF16)]
    form = pltpu.VMEM(FORM, BF16)
    total = pltpu.VMEM((9,) + FORM[1:], F32)
    landed = pltpu.SMEM((peers, 8, 128), jnp.int32)
    slots = far((peers, 512, 128), BF16)
    table_rows_count = operators.shape[1] * operators.shape[2] * operators.shape[3]
    listed = operators.transpose(1, 2, 3, 0).reshape(table_rows_count, operators.shape[0])
    route = route.reshape(route.shape[:4])

    send, tables_zero = call(
        first_kernel,
        [far((peers, 528, 128), BF16), far(TABLES, BF16)],
        [FAR] * 5,
        [FAR, FAR],
        [pltpu.SMEM(route.shape, jnp.int32)] * 3
        + [pltpu.VMEM(listed.shape, BF16), pltpu.VMEM(NATIVE, BF16)]
        + turning
        + [
            form,
            pltpu.VMEM((peers, 16, 128), F32),
            pltpu.VMEM((peers, 16, 128), BF16),
            pltpu.VMEM(TABLES, BF16),
            sems,
            quarter_sems,
        ],
    )(operator_index, route, target_brick, listed, template)
    arrived = swap_slots(send)

    rim = like((2 * RIM, 32, 256), BF16)
    low_x, high_x, low_y, high_y = call(
        edge_kernel,
        [rim] * 4,
        [FAR] * 3,
        [WHOLE] * 4,
        [pltpu.VMEM(NATIVE, BF16)] + [pltpu.VMEM((RIM, 32, 256), F32)] * 2 + [pltpu.VMEM(NATIVE, F32), sems],
    )(template, velocity, send)
    target_z, tables_one = call(
        prepare_kernel, [far(FORM, BF16), far(TABLES, BF16)], [SCALAR] + [WHOLE] * 3, [WHOLE] * 2, []
    )(operator_index, listed, target_image, low_x)
    b0x, a0x, b0y, a0y = neighbours(low_x, high_x, low_y, high_y)
    send, state_x, landing = call(
        second_kernel,
        [slots, far(FORM, BF16), far((peers, 8, 128), jnp.int32)],
        [SCALAR, NEAR, FAR] + [WHOLE] * 4,
        [FAR] * 3,
        [
            pltpu.VMEM((peers, 512, 128), BF16),
            pltpu.VMEM((peers, 16, 128), BF16),
            pltpu.VMEM((peers, 8, 128), jnp.int32),
            landed,
            form,
            total,
        ]
        + turning
        + [form, sems, quarter_sems],
    )(route, tables_one, arrived, b0x, a0x, b0y, a0y)
    arrived = swap_slots(send)

    divergence = call(
        divergence_kernel, like(NATIVE, F32), [WHOLE] * 5 + [FAR], WHOLE, [pltpu.VMEM((38, 32, 256), F32)]
    )(velocity, b0x, a0x, b0y, a0y, send)

    state, low_x, high_x, low_y, high_y = call(
        rims_kernel, [far(NATIVE, BF16)] + [rim] * 4, [WHOLE] * 2 + [FAR], [WHOLE] * 5, turning[1:]
    )(state_x, divergence, send)
    send, adjoint_two = call(
        third_kernel,
        [slots, far(FORM, BF16)],
        [FAR, FAR, FAR] + [WHOLE] * 4,
        [FAR] * 2,
        [pltpu.VMEM((peers, 512, 128), BF16), landed, total, form, form, sems, quarter_sems, slot_sems],
    )(landing, arrived, target_z, low_x, high_x, low_y, high_y)
    arrived = swap_slots(send)
    b1x, a1x, b1y, a1y = neighbours(low_x, high_x, low_y, high_y)

    send, adjoint_one = call(
        fourth_kernel,
        [slots, far(FORM, BF16)],
        [SCALAR, NEAR, FAR, FAR] + [WHOLE] * 4,
        [FAR] * 2,
        [form, landed] + turning + [form, sems, slot_sems],
    )(route, tables_one, landing, arrived, b1x, a1x, b1y, a1y)
    arrived = swap_slots(send)

    gradient = call(
        gradient_kernel,
        far((3,) + NATIVE, F32),
        [WHOLE] * 13 + [FAR],
        WHOLE,
        turning[1:] + [pltpu.VMEM(NATIVE, F32)] * 2 + [pltpu.VMEM((38, 32, 256), F32)] * 3,
    )(template, state, divergence, adjoint_two, adjoint_one, b0x, a0x, b0y, a0y, b1x, a1x, b1y, a1y, send)

    adjoint = call(
        fifth_kernel,
        far(NATIVE, BF16),
        [SCALAR, NEAR, NEAR, FAR],
        FAR,
        turning + [pltpu.VMEM(NATIVE, BF16), quarter_sems],
    )(route, tables_zero, arrived, gradient)
    return gradient, adjoint


def solution(mesh):
    placed = (
        P("gx", "gy", None),
        P("gx", "gy", None),
        P(None, "gx", "gy", None),
        P(),
        P(None, "gx", "gy", None, None),
        P(None, "gx", "gy", None),
        P(None, "gx", "gy", None),
    )
    return jax.shard_map(
        shards,
        mesh=mesh,
        in_specs=placed,
        out_specs=(P(None, "gx", "gy", None), P("gx", "gy", None)),
        check_vma=False,
    )
```

```python
import functools

import jax
import jax.numpy as jnp
from jax import lax
from jax.experimental import pallas as pl
from jax.experimental.pallas import tpu as pltpu
from jax.sharding import PartitionSpec as P

STEPS = 2
CAP = 2
RIM = 3
F32 = jnp.float32
BF16 = jnp.bfloat16
NT = (((1,), (1,)), ((), ()))
NN = (((1,), (0,)), ((), ()))
TAPS = ((1, 0.75), (2, -0.15), (3, 1.0 / 60.0))


def iota(shape, dim):
    return lax.broadcasted_iota(jnp.int32, shape, dim)


def mm(left, right, dims=NN):
    return lax.dot_general(left, right, dims, preferred_element_type=F32)


def halves(value):
    high = value.astype(BF16)
    return high, (value - high.astype(F32)).astype(BF16)


def table_rows(operators, picks, axis):
    lane = iota((operators.shape[1], 256), 1)
    chosen = jnp.zeros(lane.shape, jnp.int32)
    for b, pick in enumerate(picks):
        chosen = jnp.where(lane // 32 == b, pick, chosen)
    one_hot = (iota(lane.shape, 0) == chosen).astype(F32).astype(BF16)
    found = mm(operators[axis * 1024 : axis * 1024 + 1024, :], one_hot)
    within = iota((32, 256), 1) % 32
    total = jnp.zeros((32, 256), F32)
    for x in range(32):
        total = jnp.where(within == x, found[x * 32 : x * 32 + 32], total)
    return total


def same_block(size, edge):
    return iota((size, size), 0) // edge == iota((size, size), 1) // edge


def identity():
    return (iota((256, 256), 0) == iota((256, 256), 1)).astype(F32).astype(BF16)


def flipped_diagonal(table):
    return jnp.where(same_block(256, 32), jnp.concatenate([table] * 8, axis=0), 0.0).astype(BF16)


def diagonal(table):
    return mm(identity(), flipped_diagonal(table), NT).astype(BF16)


def spread(table):
    copies = (iota((256, 256), 0) % 32 == iota((256, 256), 1) % 32).astype(F32).astype(BF16)
    return mm(flipped_diagonal(table), copies)


def swap_chunks(parts):
    lane = iota(parts[0].shape, 1)
    for bit, shift in ((1, 32), (2, 64)):
        keep = (lane & shift) == 0
        fresh = list(parts)
        for index in range(4):
            if index & bit:
                continue
            one, two = parts[index], parts[index | bit]
            fresh[index] = jnp.where(keep, one, pltpu.roll(two, shift, 1))
            fresh[index | bit] = jnp.where(keep, pltpu.roll(one, 128 - shift, 1), two)
        parts = fresh
    return parts


def swap_brick(block, folded, turned, brick, parts=2):
    slabs = []
    for ph in range(4):
        slabs.append(
            jnp.concatenate(
                [
                    block[(qs // 2) * 32 + ph * 8 : (qs // 2) * 32 + ph * 8 + 8, (qs % 2) * 128 : (qs % 2) * 128 + 128]
                    for qs in range(8)
                ],
                axis=0,
            )
        )
    slabs = swap_chunks(slabs)
    for qh in range(4):
        folded[brick * 4 + qh] = slabs[qh]
    for ps in range(8):
        value = jnp.concatenate(
            [folded[brick * 4 + qh, pl.ds(ps, 8, stride=8), :] for qh in range(4)], axis=0
        )
        for part, half in enumerate(halves(value)[:parts]):
            turned[part * 256 + brick * 32 : part * 256 + brick * 32 + 32, ps * 128 : ps * 128 + 128] = half


def lane_pair(field, g):
    return jnp.concatenate(
        [
            jnp.concatenate([field[b, qs * 32 : qs * 32 + 32, :] for b in range(8)], axis=0)
            for qs in (2 * g, 2 * g + 1)
        ],
        axis=1,
    )


def put_pair(field, g, value):
    for b in range(8):
        for half in range(2):
            rows = slice((2 * g + half) * 32, (2 * g + half) * 32 + 32)
            field[b, rows, :] = value[b * 32 : b * 32 + 32, half * 128 : half * 128 + 128]


def middle_and_last(start, spread_mid, last, folded, turned, flipped):
    mask = same_block(256, 32)
    for brick in range(8):
        rows = spread_mid[brick * 32 : brick * 32 + 32]
        line = jnp.where(mask, jnp.concatenate([rows] * 8, axis=0), 0.0).astype(BF16)
        block = start[brick * 32 : brick * 32 + 32, :]
        block = jnp.concatenate([block[:, g * 256 : g * 256 + 256] for g in range(4)], axis=0)
        high, low = halves(block)
        both = mm(jnp.concatenate([high, low], axis=0), line, NT if flipped else NN)
        swap_brick(both[:128] + both[128:], folded, turned, brick)
    last = jnp.concatenate([last, last], axis=1)
    for g in range(4):
        yield g, mm(last, turned[:, g * 256 : g * 256 + 256]).astype(BF16)


def slot_numbers(route, step):
    own = [route[step, 0, 0, b] for b in range(8)]
    slots = []
    for b in range(8):
        rank = jnp.int32(0)
        for other in range(b):
            rank = rank + (own[other] == own[b]).astype(jnp.int32)
        slots.append((own[b], rank))
    return slots


def fetch(source, target, sem):
    copy = pltpu.make_async_copy(source, target, sem)
    copy.start()
    return copy


def send_quarter(g, bricks, send, slots, sems):
    copies = []
    for b, (place, rank) in enumerate(slots):
        rows = pl.ds(pl.multiple_of(rank * 256 + g * 64, 64), 64)
        copies.append(fetch(bricks.at[b, g * 64 : g * 64 + 64, :], send.at[place, rows, :], sems.at[g, b]))
    return copies


def first_kernel(*refs):
    picks_in, route_in, landing_in, operators, field, send, tables = refs[:7]
    picks, route, landing, table_mem, field_mem, start, folded, turned, out, meta, meta_half, tables_mem, sems, slot_sems = refs[7:]
    told = [fetch(a, b, sems.at[11 + i]) for i, (a, b) in enumerate(((picks_in, picks), (route_in, route), (landing_in, landing)))]
    loads = [fetch(operators, table_mem, sems.at[8]), fetch(field, field_mem, sems.at[9])]
    for copy in told:
        copy.wait()
    meta[...] = jnp.zeros(meta.shape, F32)
    for step in range(STEPS):
        for b, (place, rank) in enumerate(slot_numbers(route, step)):
            value = jnp.full((1, 128), landing[step, 0, 0, b] + 1, jnp.int32).astype(F32)
            meta[place, pl.ds(step * CAP + rank, 1), :] = value
    meta_half[...] = meta[...].astype(BF16)
    told = fetch(meta_half, send.at[:, 512:528, :], sems.at[10])
    chosen = [picks[0, 0, 0, b] for b in range(8)]
    loads[0].wait()
    found = [table_rows(table_mem, chosen, axis) for axis in range(3)]
    for axis in range(3):
        tables_mem[axis] = found[axis].astype(BF16)
    kept = fetch(tables_mem, tables, sems.at[8])
    begin = diagonal(found[2])
    loads[1].wait()
    for g in range(4):
        block = jnp.concatenate(
            [field_mem[qh * 8 + qs] for qs in (2 * g, 2 * g + 1) for qh in range(4)], axis=0
        )
        start[:, g * 256 : g * 256 + 256] = mm(begin, block, NT)
    slots = slot_numbers(route, 0)
    sent = []
    for g, moved in middle_and_last(start, spread(found[1]), diagonal(found[0]), folded, turned, False):
        put_pair(out, g, moved)
        sent += send_quarter(g, out, send, slots, slot_sems)
    for copy in sent + [told, kept]:
        copy.wait()


def second_kernel(route, tables_in, arrived, *refs):
    send, state, landing_out, arrived_mem, meta_half, meta, tables, landing, state_mem, total, start, folded, turned, out, sems, slot_sems = refs[-16:]
    heard = fetch(arrived.at[:, 512:528, :], meta_half, sems.at[8])
    listed = fetch(tables_in, tables, sems.at[11])
    load = fetch(arrived.at[:, 0:512, :], arrived_mem, sems.at[12])
    total[...] = jnp.zeros(total.shape, F32)
    listed.wait()
    begin = diagonal(tables[0].astype(F32))
    mid = spread(tables[1].astype(F32))
    end = diagonal(tables[2].astype(F32))
    heard.wait()
    meta[...] = meta_half[...].astype(F32).astype(jnp.int32)[:, 0:8, :]
    told = [fetch(meta, landing, sems.at[9]), fetch(meta, landing_out, sems.at[10])]
    load.wait()
    told[0].wait()
    gather_sum(0, landing, arrived_mem, total)
    for b in range(8):
        state_mem[b] = total[b].astype(BF16)
    kept = fetch(state_mem, state, sems.at[9])
    for g in range(4):
        start[:, g * 256 : g * 256 + 256] = mm(begin, lane_pair(state_mem, g))
    slots = slot_numbers(route, 1)
    sent = []
    for g, moved in middle_and_last(start, mid, end, folded, turned, False):
        put_pair(out, g, moved)
        sent += send_quarter(g, out, send, slots, slot_sems)
    for copy in sent + [kept, told[1]]:
        copy.wait()


def gather_sum(step, landing, arrived, total):
    def add(source, carry):
        for rank in range(CAP):
            brick = landing[source, step * CAP + rank, 0]

            @pl.when(brick > 0)
            def _():
                total[brick - 1] += arrived[source, rank * 256 : rank * 256 + 256, :].astype(F32)

        return carry

    lax.fori_loop(0, arrived.shape[0], add, 0)


def hand_out(step, landing, field, send, sems):
    copies = []
    for source in range(send.shape[0]):
        for rank in range(CAP):
            brick = jnp.maximum(landing[source, step * CAP + rank, 0] - 1, 0)
            target = send.at[source, rank * 256 : rank * 256 + 256, :]
            copies.append(fetch(field.at[brick], target, sems.at[source * CAP + rank]))
    return copies


def third_kernel(landing_in, arrived, target, *refs):
    send, adjoint, arrived_mem, landing, total, adjoint_mem, target_mem, sems, slot_sems = refs[-9:]
    told = fetch(landing_in, landing, sems.at[0])
    load = fetch(arrived, arrived_mem, sems.at[1])
    aim = fetch(target, target_mem, sems.at[2])
    total[...] = jnp.zeros(total.shape, F32)
    told.wait()
    load.wait()
    gather_sum(1, landing, arrived_mem, total)
    aim.wait()
    for b in range(8):
        final = total[b].astype(BF16).astype(F32)
        adjoint_mem[b] = (final - target_mem[b].astype(F32)).astype(BF16)
    sent = hand_out(1, landing, adjoint_mem, send, slot_sems)
    for copy in sent + [fetch(adjoint_mem, adjoint, sems.at[0])]:
        copy.wait()


def pulled_pair(arrived, slots, g):
    tiles = []
    for qs in (2 * g, 2 * g + 1):
        rows = [
            arrived[place, pl.ds(pl.multiple_of(rank * 256 + qs * 32, 32), 32), :] for place, rank in slots
        ]
        tiles.append(jnp.concatenate(rows, axis=0))
    return jnp.concatenate(tiles, axis=1)


def fourth_kernel(route, tables_in, landing_in, arrived, *refs):
    send, adjoint, bricks, tables, landing, start, folded, turned, out, sems, slot_sems = refs[-11:]
    loads = [fetch(tables_in, tables, sems.at[9])]
    for b, (place, rank) in enumerate(slot_numbers(route, 1)):
        source = arrived.at[place, pl.ds(pl.multiple_of(rank * 256, 256), 256), :]
        loads.append(fetch(source, bricks.at[b], sems.at[b]))
    told = fetch(landing_in, landing, sems.at[8])
    loads[0].wait()
    begin = flipped_diagonal(tables[2].astype(F32))
    mid = spread(tables[1].astype(F32))
    end = flipped_diagonal(tables[0].astype(F32))
    for load in loads[1:]:
        load.wait()
    for g in range(4):
        start[:, g * 256 : g * 256 + 256] = mm(begin, lane_pair(bricks, g))
    for g, moved in middle_and_last(start, mid, end, folded, turned, True):
        put_pair(out, g, moved)
    told.wait()
    sent = hand_out(0, landing, out, send, slot_sems)
    for copy in sent + [fetch(out, adjoint, sems.at[0])]:
        copy.wait()


def fifth_kernel(route, tables_in, arrived, *refs):
    adjoint, tables, start, folded, turned, out, sems = refs[-7:]
    load = fetch(tables_in, tables, sems.at[0, 7])
    slots = slot_numbers(route, 0)
    load.wait()
    begin = flipped_diagonal(tables[0].astype(F32))
    mid = spread(tables[1].astype(F32))
    end = flipped_diagonal(tables[2].astype(F32))
    for g in range(4):
        start[:, g * 256 : g * 256 + 256] = mm(begin, pulled_pair(arrived, slots, g))
    stored = []
    for g, moved in middle_and_last(start, mid, end, folded, turned, True):
        to_native(moved, g, out)
        for qh in range(4):
            rows = slice(qh * 8 + 2 * g, qh * 8 + 2 * g + 2)
            stored.append(fetch(out.at[rows], adjoint.at[rows], sems.at[g, qh]))
    for copy in stored:
        copy.wait()


def to_native(block, g, field):
    flat = mm(identity(), block, NT).astype(field.dtype)
    for index in range(8):
        x = (index % 4) * 8 + 2 * g + index // 4
        field[x] = flat[index * 32 : index * 32 + 32]


def x_form_to_native(source, folded, turned, field):
    for b in range(8):
        block = source[b].astype(F32)
        block = jnp.concatenate(
            [
                jnp.concatenate([block[g * 64 : g * 64 + 32], block[g * 64 + 32 : g * 64 + 64]], axis=1)
                for g in range(4)
            ],
            axis=0,
        )
        swap_brick(block, folded, turned, b, 1)
    for g in range(4):
        to_native(turned[0:256, g * 256 : g * 256 + 256], g, field)


def tap(offset):
    value = jnp.zeros(offset.shape, F32)
    for step, weight in TAPS:
        value = jnp.where(offset == step, weight, value)
        value = jnp.where(offset == -step, -weight, value)
    return value


def stencils():
    size = 256
    row, col = iota((size, size), 0), iota((size, size), 1)
    along_y = halves(jnp.where(row // 32 == col // 32, tap(col - row), 0.0))
    along_z = halves(tap(row - col))
    row, col = iota((size, 48), 0), iota((size, 48), 1)
    layer = col // 8
    place = jnp.where(layer < RIM, layer - RIM, layer - RIM + 32)
    rim_y = halves(jnp.where(row // 32 == col % 8, tap(place - row % 32), 0.0))
    return along_y, rim_y, along_z


def rim_picker():
    row, col = iota((48, 256), 0), iota((48, 256), 1)
    layer = row // 8
    place = jnp.where(layer < RIM, layer, layer - RIM + 29)
    return ((row % 8 == col // 32) & (place == col % 32)).astype(F32).astype(BF16)


def difference_x(padded, g):
    total = None
    for step, weight in TAPS:
        ahead = padded[pl.ds(8 * g + RIM + step, 8)]
        behind = padded[pl.ds(8 * g + RIM - step, 8)]
        term = weight * (ahead - behind)
        total = term if total is None else total + term
    return total.reshape(256, 256)


def difference_y(parts, rims, along_y, rim_y):
    total = mm(along_y[0], parts[0]) + mm(along_y[1], parts[0])
    if len(parts) > 1:
        total = total + mm(along_y[0], parts[1])
    return total + mm(rim_y[0], rims) + mm(rim_y[1], rims)


def difference_z(parts, along_z):
    total = mm(parts[0], along_z[0]) + mm(parts[0], along_z[1])
    if len(parts) > 1:
        total = total + mm(parts[1], along_z[0])
    return total


def rim_rows(before, after, base, g):
    rows = [before[base + h, (g // 2) * 16 : (g // 2) * 16 + 16, :].astype(F32) for h in range(RIM)]
    rows += [after[base + h, (g // 2) * 16 : (g // 2) * 16 + 16, :].astype(F32) for h in range(RIM)]
    half = (g % 2) * 8
    return jnp.concatenate([value[half : half + 8] for value in rows], axis=0).astype(BF16)


def put_rims(blocks, base, low_y, high_y):
    picker = rim_picker()
    for pair in range(2):
        left, right = mm(picker, blocks[2 * pair]), mm(picker, blocks[2 * pair + 1])
        for layer in range(2 * RIM):
            value = jnp.concatenate(
                [left[layer * 8 : layer * 8 + 8], right[layer * 8 : layer * 8 + 8]], axis=0
            ).astype(BF16)
            target = low_y if layer < RIM else high_y
            target[base + layer % RIM, pair * 16 : pair * 16 + 16, :] = value


def edge_kernel(template, velocity, sent, low_x, high_x, low_y, high_y, field, first_x, last_x, mid_v, sems):
    loads = [
        fetch(template, field, sems.at[0]),
        fetch(velocity.at[0, 0:RIM], first_x, sems.at[1]),
        fetch(velocity.at[0, 29:32], last_x, sems.at[2]),
        fetch(velocity.at[1], mid_v, sems.at[3]),
    ]
    for load in loads:
        load.wait()
    low_x[0:RIM] = field[0:RIM]
    high_x[0:RIM] = field[29:32]
    low_x[RIM : 2 * RIM] = first_x[...].astype(BF16)
    high_x[RIM : 2 * RIM] = last_x[...].astype(BF16)
    put_rims([field[8 * g : 8 * g + 8].reshape(256, 256) for g in range(4)], 0, low_y, high_y)
    put_rims([mid_v[8 * g : 8 * g + 8].astype(BF16).reshape(256, 256) for g in range(4)], RIM, low_y, high_y)


def prepare_kernel(picks, operators, target, edge, target_z, tables):
    chosen = [picks[1, 0, 0, b] for b in range(8)]
    for axis in range(3):
        tables[axis] = table_rows(operators, chosen, axis).astype(BF16)
    for g in range(4):
        block = jnp.concatenate(
            [target[qh * 8 + qs] for qs in (2 * g, 2 * g + 1) for qh in range(4)], axis=0
        )
        put_pair(target_z, g, mm(identity(), block, NT).astype(BF16))


def divergence_kernel(velocity, before_x, after_x, before_y, after_y, sent, divergence, padded):
    along_y, rim_y, along_z = stencils()
    padded[0:RIM] = before_x[RIM : 2 * RIM].astype(F32)
    padded[RIM : RIM + 32] = velocity[0]
    padded[RIM + 32 : 2 * RIM + 32] = after_x[RIM : 2 * RIM].astype(F32)
    for g in range(4):
        along_one = halves(velocity[1, 8 * g : 8 * g + 8].reshape(256, 256))
        along_two = halves(velocity[2, 8 * g : 8 * g + 8].reshape(256, 256))
        total = (
            difference_x(padded, g)
            + difference_y(along_one, rim_rows(before_y, after_y, RIM, g), along_y, rim_y)
            + difference_z(along_two, along_z)
        )
        divergence[8 * g : 8 * g + 8] = total.reshape(8, 32, 256)


def rims_kernel(state, divergence, sent, native, low_x, high_x, low_y, high_y, folded, turned):
    x_form_to_native(state, folded, turned, native)
    low_x[0:RIM] = native[0:RIM]
    high_x[0:RIM] = native[29:32]
    low_x[RIM : 2 * RIM] = divergence[0:RIM].astype(BF16)
    high_x[RIM : 2 * RIM] = divergence[29:32].astype(BF16)
    put_rims([native[8 * g : 8 * g + 8].reshape(256, 256) for g in range(4)], 0, low_y, high_y)
    put_rims(
        [divergence[8 * g : 8 * g + 8].astype(BF16).reshape(256, 256) for g in range(4)], RIM, low_y, high_y
    )


def gradient_kernel(
    template,
    state,
    divergence,
    adjoint_two,
    adjoint_one,
    b0x,
    a0x,
    b0y,
    a0y,
    b1x,
    a1x,
    b1y,
    a1y,
    sent,
    gradient,
    folded,
    turned,
    weight_two,
    weight_one,
    pad_zero,
    pad_one,
    pad_div,
):
    x_form_to_native(adjoint_one, folded, turned, weight_one)
    for g in range(4):
        to_native(lane_pair(adjoint_two, g), g, weight_two)
    along_y, rim_y, along_z = stencils()
    for padded, before, middle, after, base in (
        (pad_zero, b0x, template, a0x, 0),
        (pad_one, b1x, state, a1x, 0),
        (pad_div, b1x, divergence, a1x, RIM),
    ):
        padded[0:RIM] = before[base : base + RIM].astype(F32)
        padded[RIM : RIM + 32] = middle[...].astype(F32)
        padded[RIM + 32 : 2 * RIM + 32] = after[base : base + RIM].astype(F32)
    for g in range(4):
        zero = (template[8 * g : 8 * g + 8].reshape(256, 256),)
        one = (state[8 * g : 8 * g + 8].reshape(256, 256),)
        div = halves(divergence[8 * g : 8 * g + 8].reshape(256, 256))
        weigh_one = 0.5 * weight_one[8 * g : 8 * g + 8].reshape(256, 256)
        weigh_two = 0.5 * weight_two[8 * g : 8 * g + 8].reshape(256, 256)
        for axis in range(3):
            if axis == 0:
                parts = [difference_x(padded, g) for padded in (pad_zero, pad_one, pad_div)]
            elif axis == 1:
                parts = [
                    difference_y(zero, rim_rows(b0y, a0y, 0, g), along_y, rim_y),
                    difference_y(one, rim_rows(b1y, a1y, 0, g), along_y, rim_y),
                    difference_y(div, rim_rows(b1y, a1y, RIM, g), along_y, rim_y),
                ]
            else:
                parts = [difference_z(value, along_z) for value in (zero, one, div)]
            value = weigh_one * parts[0] + weigh_two * parts[1] - 0.25 * parts[2]
            gradient[axis, 8 * g : 8 * g + 8] = value.reshape(8, 32, 256)


SCALAR = pl.BlockSpec(memory_space=pltpu.SMEM)
WHOLE = pl.BlockSpec(memory_space=pltpu.VMEM)
NEAR = pl.BlockSpec(memory_space=pltpu.VMEM)
FAR = pl.BlockSpec(memory_space=pltpu.HBM)
FOLDED = (32, 64, 128)
FLAT = (256, 1024)
NATIVE = (32, 32, 256)
FORM = (8, 256, 128)
TABLES = (3, 32, 256)


def pinned(value, spec):
    if spec is FAR:
        return pltpu.with_memory_space_constraint(value, pltpu.HBM)
    if spec is NEAR:
        return pltpu.with_memory_space_constraint(value, pltpu.VMEM)
    return value


SHORT, LONG = 1 << 20, 1 << 36


def call(kernel, out, in_specs, out_specs, scratch, work=LONG):
    made = pl.pallas_call(
        kernel,
        out_shape=out,
        in_specs=in_specs,
        out_specs=out_specs,
        scratch_shapes=scratch,
        compiler_params=pltpu.CompilerParams(vmem_limit_bytes=24 * 1024 * 1024),
        cost_estimate=pl.CostEstimate(flops=work, bytes_accessed=1024 * 1024, transcendentals=0),
    )

    def apply(*values):
        return made(*[pinned(value, spec) for value, spec in zip(values, in_specs, strict=True)])

    return apply


def like(shape, dtype):
    return jax.ShapeDtypeStruct(shape, dtype)


def far(shape, dtype):
    return pltpu.HBM(shape, dtype)


def neighbours(low_x, high_x, low_y, high_y):
    moved = []
    for low, high, axis in ((low_x, high_x, "gx"), (low_y, high_y, "gy")):
        size = lax.axis_size(axis)
        up = [(i, i + 1) for i in range(size - 1)]
        down = [(i + 1, i) for i in range(size - 1)]
        moved += [lax.ppermute(high, axis, up), lax.ppermute(low, axis, down)]
    return moved


def swap_slots(send):
    return lax.all_to_all(send, "gx", split_axis=0, concat_axis=0, tiled=True)


def shards(template, target_image, velocity, operators, route, target_brick, operator_index):
    peers = lax.axis_size("gx")
    sems = pltpu.SemaphoreType.DMA((16,))
    slot_sems = pltpu.SemaphoreType.DMA((peers * CAP,))
    quarter_sems = pltpu.SemaphoreType.DMA((4, 8))
    turning = [pltpu.VMEM(FLAT, F32), pltpu.VMEM(FOLDED, F32), pltpu.VMEM((512, 1024), BF16)]
    form = pltpu.VMEM(FORM, BF16)
    total = pltpu.VMEM(FORM, F32)
    landed = pltpu.SMEM((peers, 8, 128), jnp.int32)
    slots = far((peers, 512, 128), BF16)
    table_rows_count = operators.shape[1] * operators.shape[2] * operators.shape[3]
    listed = operators.transpose(1, 2, 3, 0).reshape(table_rows_count, operators.shape[0])
    route = route.reshape(route.shape[:4])

    send, tables_zero = call(
        first_kernel,
        [far((peers, 528, 128), BF16), far(TABLES, BF16)],
        [FAR] * 5,
        [FAR, FAR],
        [pltpu.SMEM(route.shape, jnp.int32)] * 3
        + [pltpu.VMEM(listed.shape, BF16), pltpu.VMEM(NATIVE, BF16)]
        + turning
        + [
            form,
            pltpu.VMEM((peers, 16, 128), F32),
            pltpu.VMEM((peers, 16, 128), BF16),
            pltpu.VMEM(TABLES, BF16),
            sems,
            quarter_sems,
        ],
        SHORT,
    )(operator_index, route, target_brick, listed, template)
    arrived = swap_slots(send)

    rim = like((2 * RIM, 32, 256), BF16)
    low_x, high_x, low_y, high_y = call(
        edge_kernel,
        [rim] * 4,
        [FAR] * 3,
        [WHOLE] * 4,
        [pltpu.VMEM(NATIVE, BF16)] + [pltpu.VMEM((RIM, 32, 256), F32)] * 2 + [pltpu.VMEM(NATIVE, F32), sems],
    )(template, velocity, send)
    target_z, tables_one = call(
        prepare_kernel, [far(FORM, BF16), far(TABLES, BF16)], [SCALAR] + [WHOLE] * 3, [WHOLE] * 2, []
    )(operator_index, listed, target_image, low_x)
    b0x, a0x, b0y, a0y = neighbours(low_x, high_x, low_y, high_y)
    send, state_x, landing = call(
        second_kernel,
        [slots, far(FORM, BF16), far((peers, 8, 128), jnp.int32)],
        [SCALAR, FAR, FAR],
        [FAR] * 3,
        [
            pltpu.VMEM((peers, 512, 128), BF16),
            pltpu.VMEM((peers, 16, 128), BF16),
            pltpu.VMEM((peers, 8, 128), jnp.int32),
            pltpu.VMEM(TABLES, BF16),
            landed,
            form,
            total,
        ]
        + turning
        + [form, sems, quarter_sems],
        SHORT,
    )(route, tables_one, arrived)
    arrived = swap_slots(send)

    divergence = call(
        divergence_kernel, like(NATIVE, F32), [WHOLE] * 5 + [FAR], WHOLE, [pltpu.VMEM((38, 32, 256), F32)]
    )(velocity, b0x, a0x, b0y, a0y, send)

    state, low_x, high_x, low_y, high_y = call(
        rims_kernel, [far(NATIVE, BF16)] + [rim] * 4, [WHOLE] * 2 + [FAR], [WHOLE] * 5, turning[1:]
    )(state_x, divergence, send)
    send, adjoint_two = call(
        third_kernel,
        [slots, far(FORM, BF16)],
        [FAR, FAR, FAR, FAR],
        [FAR] * 2,
        [pltpu.VMEM((peers, 512, 128), BF16), landed, total, form, form, sems, slot_sems],
        SHORT,
    )(landing, arrived, target_z, state)
    arrived = swap_slots(send)
    b1x, a1x, b1y, a1y = neighbours(low_x, high_x, low_y, high_y)

    send, adjoint_one = call(
        fourth_kernel,
        [slots, far(FORM, BF16)],
        [SCALAR, FAR, FAR, FAR],
        [FAR] * 2,
        [form, pltpu.VMEM(TABLES, BF16), landed] + turning + [form, sems, slot_sems],
        SHORT,
    )(route, tables_one, landing, arrived)
    arrived = swap_slots(send)

    gradient = call(
        gradient_kernel,
        far((3,) + NATIVE, F32),
        [WHOLE] * 13 + [FAR],
        WHOLE,
        turning[1:] + [pltpu.VMEM(NATIVE, F32)] * 2 + [pltpu.VMEM((38, 32, 256), F32)] * 3,
    )(template, state, divergence, adjoint_two, adjoint_one, b0x, a0x, b0y, a0y, b1x, a1x, b1y, a1y, send)

    adjoint = call(
        fifth_kernel,
        far(NATIVE, BF16),
        [SCALAR, FAR, NEAR, FAR],
        FAR,
        [pltpu.VMEM(TABLES, BF16)] + turning + [pltpu.VMEM(NATIVE, BF16), quarter_sems],
        SHORT,
    )(route, tables_zero, arrived, gradient)
    return gradient, adjoint


def solution(mesh):
    placed = (
        P("gx", "gy", None),
        P("gx", "gy", None),
        P(None, "gx", "gy", None),
        P(),
        P(None, "gx", "gy", None, None),
        P(None, "gx", "gy", None),
        P(None, "gx", "gy", None),
    )
    return jax.shard_map(
        shards,
        mesh=mesh,
        in_specs=placed,
        out_specs=(P(None, "gx", "gy", None), P("gx", "gy", None)),
        check_vma=False,
    )
```

```python
import functools

import jax
import jax.numpy as jnp
from jax import lax
from jax.experimental import pallas as pl
from jax.experimental.pallas import tpu as pltpu
from jax.sharding import PartitionSpec as P

STEPS = 2
CAP = 2
RIM = 3
F32 = jnp.float32
BF16 = jnp.bfloat16
NT = (((1,), (1,)), ((), ()))
NN = (((1,), (0,)), ((), ()))
TAPS = ((1, 0.75), (2, -0.15), (3, 1.0 / 60.0))


def iota(shape, dim):
    return lax.broadcasted_iota(jnp.int32, shape, dim)


def mm(left, right, dims=NN):
    return lax.dot_general(left, right, dims, preferred_element_type=F32)


def halves(value):
    high = value.astype(BF16)
    return high, (value - high.astype(F32)).astype(BF16)


def table_rows(operators, picks, axis):
    lane = iota((operators.shape[1], 256), 1)
    chosen = jnp.zeros(lane.shape, jnp.int32)
    for b, pick in enumerate(picks):
        chosen = jnp.where(lane // 32 == b, pick, chosen)
    one_hot = (iota(lane.shape, 0) == chosen).astype(F32).astype(BF16)
    found = mm(operators[axis * 1024 : axis * 1024 + 1024, :], one_hot)
    within = iota((32, 256), 1) % 32
    total = jnp.zeros((32, 256), F32)
    for x in range(32):
        total = jnp.where(within == x, found[x * 32 : x * 32 + 32], total)
    return total


def same_block(size, edge):
    return iota((size, size), 0) // edge == iota((size, size), 1) // edge


def identity():
    return (iota((256, 256), 0) == iota((256, 256), 1)).astype(F32).astype(BF16)


def flipped_diagonal(table):
    return jnp.where(same_block(256, 32), jnp.concatenate([table] * 8, axis=0), 0.0).astype(BF16)


def diagonal(table):
    return mm(identity(), flipped_diagonal(table), NT).astype(BF16)


def spread(table):
    copies = (iota((256, 256), 0) % 32 == iota((256, 256), 1) % 32).astype(F32).astype(BF16)
    return mm(flipped_diagonal(table), copies)


def swap_chunks(parts):
    lane = iota(parts[0].shape, 1)
    for bit, shift in ((1, 32), (2, 64)):
        keep = (lane & shift) == 0
        fresh = list(parts)
        for index in range(4):
            if index & bit:
                continue
            one, two = parts[index], parts[index | bit]
            fresh[index] = jnp.where(keep, one, pltpu.roll(two, shift, 1))
            fresh[index | bit] = jnp.where(keep, pltpu.roll(one, 128 - shift, 1), two)
        parts = fresh
    return parts


def swap_brick(block, folded, turned, brick, parts=2):
    slabs = []
    for ph in range(4):
        slabs.append(
            jnp.concatenate(
                [
                    block[(qs // 2) * 32 + ph * 8 : (qs // 2) * 32 + ph * 8 + 8, (qs % 2) * 128 : (qs % 2) * 128 + 128]
                    for qs in range(8)
                ],
                axis=0,
            )
        )
    slabs = swap_chunks(slabs)
    for qh in range(4):
        folded[brick * 4 + qh] = slabs[qh]
    for ps in range(8):
        value = jnp.concatenate(
            [folded[brick * 4 + qh, pl.ds(ps, 8, stride=8), :] for qh in range(4)], axis=0
        )
        for part, half in enumerate(halves(value)[:parts]):
            turned[part * 256 + brick * 32 : part * 256 + brick * 32 + 32, ps * 128 : ps * 128 + 128] = half


def lane_pair(field, g):
    return jnp.concatenate(
        [
            jnp.concatenate([field[b, qs * 32 : qs * 32 + 32, :] for b in range(8)], axis=0)
            for qs in (2 * g, 2 * g + 1)
        ],
        axis=1,
    )


def put_pair(field, g, value):
    for b in range(8):
        for half in range(2):
            rows = slice((2 * g + half) * 32, (2 * g + half) * 32 + 32)
            field[b, rows, :] = value[b * 32 : b * 32 + 32, half * 128 : half * 128 + 128]


def middle_and_last(start, spread_mid, last, folded, turned, flipped):
    mask = same_block(256, 32)
    for brick in range(8):
        rows = spread_mid[brick * 32 : brick * 32 + 32]
        line = jnp.where(mask, jnp.concatenate([rows] * 8, axis=0), 0.0).astype(BF16)
        block = start[brick * 32 : brick * 32 + 32, :]
        block = jnp.concatenate([block[:, g * 256 : g * 256 + 256] for g in range(4)], axis=0)
        high, low = halves(block)
        both = mm(jnp.concatenate([high, low], axis=0), line, NT if flipped else NN)
        swap_brick(both[:128] + both[128:], folded, turned, brick)
    last = jnp.concatenate([last, last], axis=1)
    for g in range(4):
        yield g, mm(last, turned[:, g * 256 : g * 256 + 256]).astype(BF16)


def slot_numbers(route, step):
    own = [route[step, 0, 0, b] for b in range(8)]
    slots = []
    for b in range(8):
        rank = jnp.int32(0)
        for other in range(b):
            rank = rank + (own[other] == own[b]).astype(jnp.int32)
        slots.append((own[b], rank))
    return slots


def fetch(source, target, sem):
    copy = pltpu.make_async_copy(source, target, sem)
    copy.start()
    return copy


def send_quarter(g, bricks, send, slots, sems):
    copies = []
    for b, (place, rank) in enumerate(slots):
        rows = pl.ds(pl.multiple_of(rank * 256 + g * 64, 64), 64)
        copies.append(fetch(bricks.at[b, g * 64 : g * 64 + 64, :], send.at[place, rows, :], sems.at[g, b]))
    return copies


def first_kernel(*refs):
    picks_in, route_in, landing_in, operators, field, send, tables = refs[:7]
    picks, route, landing, table_mem, field_mem, start, folded, turned, out, meta, meta_half, tables_mem, sems, slot_sems = refs[7:]
    told = [fetch(a, b, sems.at[11 + i]) for i, (a, b) in enumerate(((picks_in, picks), (route_in, route), (landing_in, landing)))]
    loads = [fetch(operators, table_mem, sems.at[8]), fetch(field, field_mem, sems.at[9])]
    for copy in told:
        copy.wait()
    meta[...] = jnp.zeros(meta.shape, F32)
    for step in range(STEPS):
        for b, (place, rank) in enumerate(slot_numbers(route, step)):
            value = jnp.full((1, 128), landing[step, 0, 0, b] + 1, jnp.int32).astype(F32)
            meta[place, pl.ds(step * CAP + rank, 1), :] = value
    meta_half[...] = meta[...].astype(BF16)
    told = fetch(meta_half, send.at[:, 512:528, :], sems.at[10])
    chosen = [picks[0, 0, 0, b] for b in range(8)]
    loads[0].wait()
    found = [table_rows(table_mem, chosen, axis) for axis in range(3)]
    for axis in range(3):
        tables_mem[axis] = found[axis].astype(BF16)
    kept = fetch(tables_mem, tables, sems.at[8])
    begin = diagonal(found[2])
    loads[1].wait()
    for g in range(4):
        block = jnp.concatenate(
            [field_mem[qh * 8 + qs] for qs in (2 * g, 2 * g + 1) for qh in range(4)], axis=0
        )
        start[:, g * 256 : g * 256 + 256] = mm(begin, block, NT)
    slots = slot_numbers(route, 0)
    sent = []
    for g, moved in middle_and_last(start, spread(found[1]), diagonal(found[0]), folded, turned, False):
        put_pair(out, g, moved)
        sent += send_quarter(g, out, send, slots, slot_sems)
    for copy in sent + [told, kept]:
        copy.wait()


def second_kernel(route, tables_in, arrived, *refs):
    send, state, landing_out, meta, tables, landing, state_mem, total, start, folded, turned, out, sems, slot_sems = refs[-14:]
    meta[...] = arrived[:, 512:528, :].astype(F32).astype(jnp.int32)[:, 0:8, :]
    told = [fetch(meta, landing, sems.at[9]), fetch(meta, landing_out, sems.at[10])]
    listed = fetch(tables_in, tables, sems.at[11])
    total[...] = jnp.zeros(total.shape, F32)
    told[0].wait()
    gather_sum(0, landing, arrived, total)
    for b in range(8):
        state_mem[b] = total[b].astype(BF16)
    kept = fetch(state_mem, state, sems.at[9])
    listed.wait()
    begin = diagonal(tables[0].astype(F32))
    mid = spread(tables[1].astype(F32))
    end = diagonal(tables[2].astype(F32))
    for g in range(4):
        start[:, g * 256 : g * 256 + 256] = mm(begin, lane_pair(state_mem, g))
    slots = slot_numbers(route, 1)
    sent = []
    for g, moved in middle_and_last(start, mid, end, folded, turned, False):
        put_pair(out, g, moved)
        sent += send_quarter(g, out, send, slots, slot_sems)
    for copy in sent + [kept, told[1]]:
        copy.wait()


def gather_sum(step, landing, arrived, total):
    def add(source, carry):
        for rank in range(CAP):
            brick = landing[source, step * CAP + rank, 0]

            @pl.when(brick > 0)
            def _():
                total[brick - 1] += arrived[source, rank * 256 : rank * 256 + 256, :].astype(F32)

        return carry

    lax.fori_loop(0, arrived.shape[0], add, 0)


def hand_out(step, landing, field, send, sems):
    copies = []
    for source in range(send.shape[0]):
        for rank in range(CAP):
            brick = jnp.maximum(landing[source, step * CAP + rank, 0] - 1, 0)
            target = send.at[source, rank * 256 : rank * 256 + 256, :]
            copies.append(fetch(field.at[brick], target, sems.at[source * CAP + rank]))
    return copies


def third_kernel(landing_in, arrived, target, *refs):
    send, adjoint, arrived_mem, landing, total, adjoint_mem, target_mem, sems, slot_sems = refs[-9:]
    told = fetch(landing_in, landing, sems.at[0])
    load = fetch(arrived, arrived_mem, sems.at[1])
    aim = fetch(target, target_mem, sems.at[2])
    total[...] = jnp.zeros(total.shape, F32)
    told.wait()
    load.wait()
    gather_sum(1, landing, arrived_mem, total)
    aim.wait()
    for b in range(8):
        final = total[b].astype(BF16).astype(F32)
        adjoint_mem[b] = (final - target_mem[b].astype(F32)).astype(BF16)
    sent = hand_out(1, landing, adjoint_mem, send, slot_sems)
    for copy in sent + [fetch(adjoint_mem, adjoint, sems.at[0])]:
        copy.wait()


def pulled_pair(arrived, slots, g):
    tiles = []
    for qs in (2 * g, 2 * g + 1):
        rows = [
            arrived[place, pl.ds(pl.multiple_of(rank * 256 + qs * 32, 32), 32), :] for place, rank in slots
        ]
        tiles.append(jnp.concatenate(rows, axis=0))
    return jnp.concatenate(tiles, axis=1)


def fourth_kernel(route, tables_in, landing_in, arrived, *refs):
    send, adjoint, tables, landing, start, folded, turned, out, sems, slot_sems = refs[-10:]
    listed = fetch(tables_in, tables, sems.at[1])
    told = fetch(landing_in, landing, sems.at[2])
    slots = slot_numbers(route, 1)
    listed.wait()
    begin = flipped_diagonal(tables[2].astype(F32))
    mid = spread(tables[1].astype(F32))
    end = flipped_diagonal(tables[0].astype(F32))
    for g in range(4):
        start[:, g * 256 : g * 256 + 256] = mm(begin, pulled_pair(arrived, slots, g))
    for g, moved in middle_and_last(start, mid, end, folded, turned, True):
        put_pair(out, g, moved)
    told.wait()
    sent = hand_out(0, landing, out, send, slot_sems)
    for copy in sent + [fetch(out, adjoint, sems.at[0])]:
        copy.wait()


def fifth_kernel(route, tables_in, arrived, *refs):
    adjoint, tables, start, folded, turned, out, sems = refs[-7:]
    load = fetch(tables_in, tables, sems.at[0, 7])
    slots = slot_numbers(route, 0)
    load.wait()
    begin = flipped_diagonal(tables[0].astype(F32))
    mid = spread(tables[1].astype(F32))
    end = flipped_diagonal(tables[2].astype(F32))
    for g in range(4):
        start[:, g * 256 : g * 256 + 256] = mm(begin, pulled_pair(arrived, slots, g))
    stored = []
    for g, moved in middle_and_last(start, mid, end, folded, turned, True):
        to_native(moved, g, out)
        for qh in range(4):
            rows = slice(qh * 8 + 2 * g, qh * 8 + 2 * g + 2)
            stored.append(fetch(out.at[rows], adjoint.at[rows], sems.at[g, qh]))
    for copy in stored:
        copy.wait()


def to_native(block, g, field):
    flat = mm(identity(), block, NT).astype(field.dtype)
    for index in range(8):
        x = (index % 4) * 8 + 2 * g + index // 4
        field[x] = flat[index * 32 : index * 32 + 32]


def x_form_to_native(source, folded, turned, field):
    for b in range(8):
        block = source[b].astype(F32)
        block = jnp.concatenate(
            [
                jnp.concatenate([block[g * 64 : g * 64 + 32], block[g * 64 + 32 : g * 64 + 64]], axis=1)
                for g in range(4)
            ],
            axis=0,
        )
        swap_brick(block, folded, turned, b, 1)
    for g in range(4):
        to_native(turned[0:256, g * 256 : g * 256 + 256], g, field)


def tap(offset):
    value = jnp.zeros(offset.shape, F32)
    for step, weight in TAPS:
        value = jnp.where(offset == step, weight, value)
        value = jnp.where(offset == -step, -weight, value)
    return value


def stencils():
    size = 256
    row, col = iota((size, size), 0), iota((size, size), 1)
    along_y = halves(jnp.where(row // 32 == col // 32, tap(col - row), 0.0))
    along_z = halves(tap(row - col))
    row, col = iota((size, 48), 0), iota((size, 48), 1)
    layer = col // 8
    place = jnp.where(layer < RIM, layer - RIM, layer - RIM + 32)
    rim_y = halves(jnp.where(row // 32 == col % 8, tap(place - row % 32), 0.0))
    return along_y, rim_y, along_z


def rim_picker():
    row, col = iota((48, 256), 0), iota((48, 256), 1)
    layer = row // 8
    place = jnp.where(layer < RIM, layer, layer - RIM + 29)
    return ((row % 8 == col // 32) & (place == col % 32)).astype(F32).astype(BF16)


def difference_x(padded, g):
    total = None
    for step, weight in TAPS:
        ahead = padded[pl.ds(8 * g + RIM + step, 8)]
        behind = padded[pl.ds(8 * g + RIM - step, 8)]
        term = weight * (ahead - behind)
        total = term if total is None else total + term
    return total.reshape(256, 256)


def difference_y(parts, rims, along_y, rim_y):
    total = mm(along_y[0], parts[0]) + mm(along_y[1], parts[0])
    if len(parts) > 1:
        total = total + mm(along_y[0], parts[1])
    return total + mm(rim_y[0], rims) + mm(rim_y[1], rims)


def difference_z(parts, along_z):
    total = mm(parts[0], along_z[0]) + mm(parts[0], along_z[1])
    if len(parts) > 1:
        total = total + mm(parts[1], along_z[0])
    return total


def rim_rows(before, after, base, g):
    rows = [before[base + h, (g // 2) * 16 : (g // 2) * 16 + 16, :].astype(F32) for h in range(RIM)]
    rows += [after[base + h, (g // 2) * 16 : (g // 2) * 16 + 16, :].astype(F32) for h in range(RIM)]
    half = (g % 2) * 8
    return jnp.concatenate([value[half : half + 8] for value in rows], axis=0).astype(BF16)


def put_rims(blocks, base, low_y, high_y):
    picker = rim_picker()
    for pair in range(2):
        left, right = mm(picker, blocks[2 * pair]), mm(picker, blocks[2 * pair + 1])
        for layer in range(2 * RIM):
            value = jnp.concatenate(
                [left[layer * 8 : layer * 8 + 8], right[layer * 8 : layer * 8 + 8]], axis=0
            ).astype(BF16)
            target = low_y if layer < RIM else high_y
            target[base + layer % RIM, pair * 16 : pair * 16 + 16, :] = value


def edge_kernel(template, velocity, sent, low_x, high_x, low_y, high_y, field, first_x, last_x, mid_v, sems):
    loads = [
        fetch(template, field, sems.at[0]),
        fetch(velocity.at[0, 0:RIM], first_x, sems.at[1]),
        fetch(velocity.at[0, 29:32], last_x, sems.at[2]),
        fetch(velocity.at[1], mid_v, sems.at[3]),
    ]
    for load in loads:
        load.wait()
    low_x[0:RIM] = field[0:RIM]
    high_x[0:RIM] = field[29:32]
    low_x[RIM : 2 * RIM] = first_x[...].astype(BF16)
    high_x[RIM : 2 * RIM] = last_x[...].astype(BF16)
    put_rims([field[8 * g : 8 * g + 8].reshape(256, 256) for g in range(4)], 0, low_y, high_y)
    put_rims([mid_v[8 * g : 8 * g + 8].astype(BF16).reshape(256, 256) for g in range(4)], RIM, low_y, high_y)


def prepare_kernel(picks, operators, target, edge, target_z, tables):
    chosen = [picks[1, 0, 0, b] for b in range(8)]
    for axis in range(3):
        tables[axis] = table_rows(operators, chosen, axis).astype(BF16)
    for g in range(4):
        block = jnp.concatenate(
            [target[qh * 8 + qs] for qs in (2 * g, 2 * g + 1) for qh in range(4)], axis=0
        )
        put_pair(target_z, g, mm(identity(), block, NT).astype(BF16))


def divergence_kernel(velocity, before_x, after_x, before_y, after_y, sent, divergence, padded):
    along_y, rim_y, along_z = stencils()
    padded[0:RIM] = before_x[RIM : 2 * RIM].astype(F32)
    padded[RIM : RIM + 32] = velocity[0]
    padded[RIM + 32 : 2 * RIM + 32] = after_x[RIM : 2 * RIM].astype(F32)
    for g in range(4):
        along_one = halves(velocity[1, 8 * g : 8 * g + 8].reshape(256, 256))
        along_two = halves(velocity[2, 8 * g : 8 * g + 8].reshape(256, 256))
        total = (
            difference_x(padded, g)
            + difference_y(along_one, rim_rows(before_y, after_y, RIM, g), along_y, rim_y)
            + difference_z(along_two, along_z)
        )
        divergence[8 * g : 8 * g + 8] = total.reshape(8, 32, 256)


def rims_kernel(state, divergence, sent, native, low_x, high_x, low_y, high_y, folded, turned):
    x_form_to_native(state, folded, turned, native)
    low_x[0:RIM] = native[0:RIM]
    high_x[0:RIM] = native[29:32]
    low_x[RIM : 2 * RIM] = divergence[0:RIM].astype(BF16)
    high_x[RIM : 2 * RIM] = divergence[29:32].astype(BF16)
    put_rims([native[8 * g : 8 * g + 8].reshape(256, 256) for g in range(4)], 0, low_y, high_y)
    put_rims(
        [divergence[8 * g : 8 * g + 8].astype(BF16).reshape(256, 256) for g in range(4)], RIM, low_y, high_y
    )


def gradient_kernel(
    template,
    state,
    divergence,
    adjoint_two,
    adjoint_one,
    b0x,
    a0x,
    b0y,
    a0y,
    b1x,
    a1x,
    b1y,
    a1y,
    sent,
    gradient,
    folded,
    turned,
    weight_two,
    weight_one,
    pad_zero,
    pad_one,
    pad_div,
):
    x_form_to_native(adjoint_one, folded, turned, weight_one)
    for g in range(4):
        to_native(lane_pair(adjoint_two, g), g, weight_two)
    along_y, rim_y, along_z = stencils()
    for padded, before, middle, after, base in (
        (pad_zero, b0x, template, a0x, 0),
        (pad_one, b1x, state, a1x, 0),
        (pad_div, b1x, divergence, a1x, RIM),
    ):
        padded[0:RIM] = before[base : base + RIM].astype(F32)
        padded[RIM : RIM + 32] = middle[...].astype(F32)
        padded[RIM + 32 : 2 * RIM + 32] = after[base : base + RIM].astype(F32)
    for g in range(4):
        zero = (template[8 * g : 8 * g + 8].reshape(256, 256),)
        one = (state[8 * g : 8 * g + 8].reshape(256, 256),)
        div = halves(divergence[8 * g : 8 * g + 8].reshape(256, 256))
        weigh_one = 0.5 * weight_one[8 * g : 8 * g + 8].reshape(256, 256)
        weigh_two = 0.5 * weight_two[8 * g : 8 * g + 8].reshape(256, 256)
        for axis in range(3):
            if axis == 0:
                parts = [difference_x(padded, g) for padded in (pad_zero, pad_one, pad_div)]
            elif axis == 1:
                parts = [
                    difference_y(zero, rim_rows(b0y, a0y, 0, g), along_y, rim_y),
                    difference_y(one, rim_rows(b1y, a1y, 0, g), along_y, rim_y),
                    difference_y(div, rim_rows(b1y, a1y, RIM, g), along_y, rim_y),
                ]
            else:
                parts = [difference_z(value, along_z) for value in (zero, one, div)]
            value = weigh_one * parts[0] + weigh_two * parts[1] - 0.25 * parts[2]
            gradient[axis, 8 * g : 8 * g + 8] = value.reshape(8, 32, 256)


SCALAR = pl.BlockSpec(memory_space=pltpu.SMEM)
WHOLE = pl.BlockSpec(memory_space=pltpu.VMEM)
NEAR = pl.BlockSpec(memory_space=pltpu.VMEM)
FAR = pl.BlockSpec(memory_space=pltpu.HBM)
FOLDED = (32, 64, 128)
FLAT = (256, 1024)
NATIVE = (32, 32, 256)
FORM = (8, 256, 128)
TABLES = (3, 32, 256)


def pinned(value, spec):
    if spec is FAR:
        return pltpu.with_memory_space_constraint(value, pltpu.HBM)
    if spec is NEAR:
        return pltpu.with_memory_space_constraint(value, pltpu.VMEM)
    return value


SHORT, LONG = 1 << 20, 1 << 36


def call(kernel, out, in_specs, out_specs, scratch, work=LONG):
    made = pl.pallas_call(
        kernel,
        out_shape=out,
        in_specs=in_specs,
        out_specs=out_specs,
        scratch_shapes=scratch,
        compiler_params=pltpu.CompilerParams(vmem_limit_bytes=24 * 1024 * 1024),
        cost_estimate=pl.CostEstimate(flops=work, bytes_accessed=1024 * 1024, transcendentals=0),
    )

    def apply(*values):
        return made(*[pinned(value, spec) for value, spec in zip(values, in_specs, strict=True)])

    return apply


def like(shape, dtype):
    return jax.ShapeDtypeStruct(shape, dtype)


def far(shape, dtype):
    return pltpu.HBM(shape, dtype)


def neighbours(low_x, high_x, low_y, high_y):
    moved = []
    for low, high, axis in ((low_x, high_x, "gx"), (low_y, high_y, "gy")):
        size = lax.axis_size(axis)
        up = [(i, i + 1) for i in range(size - 1)]
        down = [(i + 1, i) for i in range(size - 1)]
        moved += [lax.ppermute(high, axis, up), lax.ppermute(low, axis, down)]
    return moved


def swap_slots(send):
    return lax.all_to_all(send, "gx", split_axis=0, concat_axis=0, tiled=True)


def shards(template, target_image, velocity, operators, route, target_brick, operator_index):
    peers = lax.axis_size("gx")
    sems = pltpu.SemaphoreType.DMA((16,))
    slot_sems = pltpu.SemaphoreType.DMA((peers * CAP,))
    quarter_sems = pltpu.SemaphoreType.DMA((4, 8))
    turning = [pltpu.VMEM(FLAT, F32), pltpu.VMEM(FOLDED, F32), pltpu.VMEM((512, 1024), BF16)]
    form = pltpu.VMEM(FORM, BF16)
    total = pltpu.VMEM(FORM, F32)
    landed = pltpu.SMEM((peers, 8, 128), jnp.int32)
    slots = far((peers, 512, 128), BF16)
    table_rows_count = operators.shape[1] * operators.shape[2] * operators.shape[3]
    listed = operators.transpose(1, 2, 3, 0).reshape(table_rows_count, operators.shape[0])
    route = route.reshape(route.shape[:4])

    send, tables_zero = call(
        first_kernel,
        [far((peers, 528, 128), BF16), far(TABLES, BF16)],
        [FAR] * 5,
        [FAR, FAR],
        [pltpu.SMEM(route.shape, jnp.int32)] * 3
        + [pltpu.VMEM(listed.shape, BF16), pltpu.VMEM(NATIVE, BF16)]
        + turning
        + [
            form,
            pltpu.VMEM((peers, 16, 128), F32),
            pltpu.VMEM((peers, 16, 128), BF16),
            pltpu.VMEM(TABLES, BF16),
            sems,
            quarter_sems,
        ],
        SHORT,
    )(operator_index, route, target_brick, listed, template)
    arrived = swap_slots(send)

    rim = like((2 * RIM, 32, 256), BF16)
    low_x, high_x, low_y, high_y = call(
        edge_kernel,
        [rim] * 4,
        [FAR] * 3,
        [WHOLE] * 4,
        [pltpu.VMEM(NATIVE, BF16)] + [pltpu.VMEM((RIM, 32, 256), F32)] * 2 + [pltpu.VMEM(NATIVE, F32), sems],
    )(template, velocity, send)
    target_z, tables_one = call(
        prepare_kernel, [far(FORM, BF16), far(TABLES, BF16)], [SCALAR] + [WHOLE] * 3, [WHOLE] * 2, []
    )(operator_index, listed, target_image, low_x)
    b0x, a0x, b0y, a0y = neighbours(low_x, high_x, low_y, high_y)
    send, state_x, landing = call(
        second_kernel,
        [slots, far(FORM, BF16), far((peers, 8, 128), jnp.int32)],
        [SCALAR, FAR, NEAR],
        [FAR] * 3,
        [
            pltpu.VMEM((peers, 8, 128), jnp.int32),
            pltpu.VMEM(TABLES, BF16),
            landed,
            form,
            total,
        ]
        + turning
        + [form, sems, quarter_sems],
        SHORT,
    )(route, tables_one, arrived)
    arrived = swap_slots(send)

    divergence = call(
        divergence_kernel, like(NATIVE, F32), [WHOLE] * 5 + [FAR], WHOLE, [pltpu.VMEM((38, 32, 256), F32)]
    )(velocity, b0x, a0x, b0y, a0y, send)

    state, low_x, high_x, low_y, high_y = call(
        rims_kernel, [far(NATIVE, BF16)] + [rim] * 4, [WHOLE] * 2 + [FAR], [WHOLE] * 5, turning[1:]
    )(state_x, divergence, send)
    send, adjoint_two = call(
        third_kernel,
        [slots, far(FORM, BF16)],
        [FAR, pl.BlockSpec(memory_space=pl.ANY), FAR, FAR],
        [FAR] * 2,
        [pltpu.VMEM((peers, 512, 128), BF16), landed, total, form, form, sems, slot_sems],
        SHORT,
    )(landing, arrived, target_z, state)
    arrived = swap_slots(send)
    b1x, a1x, b1y, a1y = neighbours(low_x, high_x, low_y, high_y)

    send, adjoint_one = call(
        fourth_kernel,
        [slots, far(FORM, BF16)],
        [SCALAR, FAR, FAR, NEAR],
        [FAR] * 2,
        [pltpu.VMEM(TABLES, BF16), landed] + turning + [form, sems, slot_sems],
        SHORT,
    )(route, tables_one, landing, arrived)
    arrived = swap_slots(send)

    gradient = call(
        gradient_kernel,
        far((3,) + NATIVE, F32),
        [WHOLE] * 13 + [FAR],
        WHOLE,
        turning[1:] + [pltpu.VMEM(NATIVE, F32)] * 2 + [pltpu.VMEM((38, 32, 256), F32)] * 3,
    )(template, state, divergence, adjoint_two, adjoint_one, b0x, a0x, b0y, a0y, b1x, a1x, b1y, a1y, send)

    adjoint = call(
        fifth_kernel,
        far(NATIVE, BF16),
        [SCALAR, FAR, NEAR, FAR],
        FAR,
        [pltpu.VMEM(TABLES, BF16)] + turning + [pltpu.VMEM(NATIVE, BF16), quarter_sems],
        SHORT,
    )(route, tables_zero, arrived, gradient)
    return gradient, adjoint


def solution(mesh):
    placed = (
        P("gx", "gy", None),
        P("gx", "gy", None),
        P(None, "gx", "gy", None),
        P(),
        P(None, "gx", "gy", None, None),
        P(None, "gx", "gy", None),
        P(None, "gx", "gy", None),
    )
    return jax.shard_map(
        shards,
        mesh=mesh,
        in_specs=placed,
        out_specs=(P(None, "gx", "gy", None), P("gx", "gy", None)),
        check_vma=False,
    )
```

```python
import functools

import jax
import jax.numpy as jnp
from jax import lax
from jax.experimental import pallas as pl
from jax.experimental.pallas import tpu as pltpu
from jax.sharding import PartitionSpec as P

STEPS = 2
CAP = 2
RIM = 3
F32 = jnp.float32
BF16 = jnp.bfloat16
NT = (((1,), (1,)), ((), ()))
NN = (((1,), (0,)), ((), ()))
TAPS = ((1, 0.75), (2, -0.15), (3, 1.0 / 60.0))


def iota(shape, dim):
    return lax.broadcasted_iota(jnp.int32, shape, dim)


def mm(left, right, dims=NN):
    return lax.dot_general(left, right, dims, preferred_element_type=F32)


def halves(value):
    high = value.astype(BF16)
    return high, (value - high.astype(F32)).astype(BF16)


def table_rows(operators, picks, axis):
    lane = iota((operators.shape[1], 256), 1)
    chosen = jnp.zeros(lane.shape, jnp.int32)
    for b, pick in enumerate(picks):
        chosen = jnp.where(lane // 32 == b, pick, chosen)
    one_hot = (iota(lane.shape, 0) == chosen).astype(F32).astype(BF16)
    found = mm(operators[axis * 1024 : axis * 1024 + 1024, :], one_hot)
    within = iota((32, 256), 1) % 32
    total = jnp.zeros((32, 256), F32)
    for x in range(32):
        total = jnp.where(within == x, found[x * 32 : x * 32 + 32], total)
    return total


def same_block(size, edge):
    return iota((size, size), 0) // edge == iota((size, size), 1) // edge


def identity():
    return (iota((256, 256), 0) == iota((256, 256), 1)).astype(F32).astype(BF16)


def flipped_diagonal(table):
    return jnp.where(same_block(256, 32), jnp.concatenate([table] * 8, axis=0), 0.0).astype(BF16)


def diagonal(table):
    return mm(identity(), flipped_diagonal(table), NT).astype(BF16)


def spread(table):
    copies = (iota((256, 256), 0) % 32 == iota((256, 256), 1) % 32).astype(F32).astype(BF16)
    return mm(flipped_diagonal(table), copies)


def swap_chunks(parts):
    lane = iota(parts[0].shape, 1)
    for bit, shift in ((1, 32), (2, 64)):
        keep = (lane & shift) == 0
        fresh = list(parts)
        for index in range(4):
            if index & bit:
                continue
            one, two = parts[index], parts[index | bit]
            fresh[index] = jnp.where(keep, one, pltpu.roll(two, shift, 1))
            fresh[index | bit] = jnp.where(keep, pltpu.roll(one, 128 - shift, 1), two)
        parts = fresh
    return parts


def swap_brick(block, folded, turned, brick, parts=2):
    slabs = []
    for ph in range(4):
        slabs.append(
            jnp.concatenate(
                [
                    block[(qs // 2) * 32 + ph * 8 : (qs // 2) * 32 + ph * 8 + 8, (qs % 2) * 128 : (qs % 2) * 128 + 128]
                    for qs in range(8)
                ],
                axis=0,
            )
        )
    slabs = swap_chunks(slabs)
    for qh in range(4):
        folded[brick * 4 + qh] = slabs[qh]
    for ps in range(8):
        value = jnp.concatenate(
            [folded[brick * 4 + qh, pl.ds(ps, 8, stride=8), :] for qh in range(4)], axis=0
        )
        for part, half in enumerate(halves(value)[:parts]):
            turned[part * 256 + brick * 32 : part * 256 + brick * 32 + 32, ps * 128 : ps * 128 + 128] = half


def lane_pair(field, g):
    return jnp.concatenate(
        [
            jnp.concatenate([field[b, qs * 32 : qs * 32 + 32, :] for b in range(8)], axis=0)
            for qs in (2 * g, 2 * g + 1)
        ],
        axis=1,
    )


def put_pair(field, g, value):
    for b in range(8):
        for half in range(2):
            rows = slice((2 * g + half) * 32, (2 * g + half) * 32 + 32)
            field[b, rows, :] = value[b * 32 : b * 32 + 32, half * 128 : half * 128 + 128]


def middle_and_last(start, spread_mid, last, folded, turned, flipped):
    mask = same_block(256, 32)
    for brick in range(8):
        rows = spread_mid[brick * 32 : brick * 32 + 32]
        line = jnp.where(mask, jnp.concatenate([rows] * 8, axis=0), 0.0).astype(BF16)
        block = start[brick * 32 : brick * 32 + 32, :]
        block = jnp.concatenate([block[:, g * 256 : g * 256 + 256] for g in range(4)], axis=0)
        high, low = halves(block)
        both = mm(jnp.concatenate([high, low], axis=0), line, NT if flipped else NN)
        swap_brick(both[:128] + both[128:], folded, turned, brick)
    last = jnp.concatenate([last, last], axis=1)
    for g in range(4):
        yield g, mm(last, turned[:, g * 256 : g * 256 + 256]).astype(BF16)


def slot_numbers(route, step):
    own = [route[step, 0, 0, b] for b in range(8)]
    slots = []
    for b in range(8):
        rank = jnp.int32(0)
        for other in range(b):
            rank = rank + (own[other] == own[b]).astype(jnp.int32)
        slots.append((own[b], rank))
    return slots


def fetch(source, target, sem):
    copy = pltpu.make_async_copy(source, target, sem)
    copy.start()
    return copy


def put_pieces(stage, g, value, rows):
    parts = 32 // rows
    for half in range(2):
        tile = value[:, half * 128 : half * 128 + 128]
        for part in range(parts):
            share = (2 * g + half) * parts + part
            if parts == 1:
                stage[share] = tile
            else:
                for b in range(8):
                    at = b * 32 + part * rows
                    stage[share, b * rows : b * rows + rows, :] = tile[at : at + rows]


def pieces_pair(pieces, kind, g, rows):
    parts = 32 // rows
    base = kind * 8 * rows
    tiles = []
    for tile in (2 * g, 2 * g + 1):
        if parts == 1:
            tiles.append(pieces[tile, base : base + 256, :])
        else:
            tiles.append(
                jnp.concatenate(
                    [
                        pieces[tile * parts + part, base + b * rows : base + b * rows + rows, :]
                        for b in range(8)
                        for part in range(parts)
                    ],
                    axis=0,
                )
            )
    return jnp.concatenate(tiles, axis=1)


def target_kernel(picks_in, route_in, brick_in, target, send, *refs):
    picks, route, landing, field, stage, meta, meta_half, sems = refs
    told = [
        fetch(source, place, sems.at[index])
        for index, (source, place) in enumerate(((picks_in, picks), (route_in, route), (brick_in, landing)))
    ]
    load = fetch(target, field, sems.at[3])
    for copy in told:
        copy.wait()
    lane = iota((1, 128), 1)
    meta[...] = jnp.zeros(meta.shape, F32)
    for b in range(8):
        codes = [route[step, 0, 0, b] * 8 + landing[step, 0, 0, b] for step in range(STEPS)]
        value = jnp.zeros((1, 128), jnp.int32)
        for index, number in enumerate(codes + [picks[1, 0, 0, b]]):
            value = jnp.where(lane == index, number, value)
        meta[b : b + 1, :] = value.astype(F32)
    meta_half[...] = jnp.broadcast_to(meta[...].astype(BF16)[None], meta_half.shape)
    shared = stage.shape[1]
    sent = [fetch(meta_half, send.at[:, shared : shared + 16, :], sems.at[4])]
    load.wait()
    for g in range(4):
        block = jnp.concatenate(
            [field[qh * 8 + qs] for qs in (2 * g, 2 * g + 1) for qh in range(4)], axis=0
        )
        put_pieces(stage, g, mm(identity(), block, NT).astype(BF16), shared // 8)
    for copy in sent + [fetch(stage, send.at[:, 0:shared, :], sems.at[5])]:
        copy.wait()


def first_kernel(picks, operators, field, sent, moved_out, tables, table_mem, field_mem, start, folded, turned, out, tables_mem, sems):
    loads = [fetch(operators, table_mem, sems.at[0]), fetch(field, field_mem, sems.at[1])]
    chosen = [picks[0, 0, 0, b] for b in range(8)]
    loads[0].wait()
    found = [table_rows(table_mem, chosen, axis) for axis in range(3)]
    for axis in range(3):
        tables_mem[axis] = found[axis].astype(BF16)
    kept = fetch(tables_mem, tables, sems.at[0])
    begin = diagonal(found[2])
    loads[1].wait()
    for g in range(4):
        block = jnp.concatenate(
            [field_mem[qh * 8 + qs] for qs in (2 * g, 2 * g + 1) for qh in range(4)], axis=0
        )
        start[:, g * 256 : g * 256 + 256] = mm(begin, block, NT)
    for g, moved in middle_and_last(start, spread(found[1]), diagonal(found[0]), folded, turned, False):
        put_pair(out, g, moved)
    for copy in [kept, fetch(out, moved_out, sems.at[1])]:
        copy.wait()


def second_kernel(route, landing, operators, moved, arrived, *refs):
    send, tables, codes_out, table_mem, moved_mem, meta_half, meta, codes, start, folded, turned, stage, tables_mem, sems, slot_sems = refs
    shared = stage.shape[1]
    heard = fetch(arrived.at[:, shared : shared + 16, :], meta_half, sems.at[0])
    loads = [fetch(operators, table_mem, sems.at[1]), fetch(moved, moved_mem, sems.at[2])]
    heard.wait()
    meta[...] = meta_half[...].astype(F32).astype(jnp.int32)[:, 0:8, :]
    told = [fetch(meta, codes, sems.at[3]), fetch(meta, codes_out, sems.at[4])]
    loads[1].wait()
    sent = []
    for b, (place, rank) in enumerate(slot_numbers(route, 0)):
        rows = pl.ds(pl.multiple_of(rank * 256, 256), 256)
        sent.append(fetch(moved_mem.at[b], send.at[place, rows, :], slot_sems.at[b]))
    told[0].wait()
    chosen = [codes[route[0, 0, 0, b], landing[0, 0, 0, b], 2] for b in range(8)]
    loads[0].wait()
    found = [table_rows(table_mem, chosen, axis) for axis in range(3)]
    for axis in range(3):
        tables_mem[axis] = found[axis].astype(BF16)
    kept = fetch(tables_mem, tables, sems.at[5])
    begin = diagonal(found[0])
    for g in range(4):
        start[:, g * 256 : g * 256 + 256] = mm(begin, lane_pair(moved_mem, g))
    for g, value in middle_and_last(start, spread(found[1]), diagonal(found[2]), folded, turned, False):
        put_pieces(stage, g, value, shared // 8)
    sent.append(fetch(stage, send.at[:, 512 : 512 + shared, :], sems.at[6]))
    for copy in sent + [kept, told[1]]:
        copy.wait()


def share_kernel(codes_in, arrived, targets, send, codes, moved, aims, total, stage, sems):
    peers, shared = moved.shape[0], moved.shape[1]
    rows = shared // 8
    loads = [
        fetch(codes_in, codes, sems.at[0]),
        fetch(arrived.at[:, 512 : 512 + shared, :], moved, sems.at[1]),
        fetch(targets.at[:, 0:shared, :], aims, sems.at[2]),
    ]
    total[...] = jnp.zeros(total.shape, F32)
    for load in loads:
        load.wait()

    def add(source, carry):
        for b in range(8):
            first = codes[source, b, 0]
            final = codes[first >> 3, first & 7, 1]
            place = pl.ds(pl.multiple_of((final & 7) * rows, rows), rows)
            total[final >> 3, place, :] += moved[source, b * rows : b * rows + rows, :].astype(F32)
        return carry

    lax.fori_loop(0, peers, add, 0)
    for source in range(peers):
        final = total[source].astype(BF16).astype(F32)
        stage[source, 0:shared, :] = (final - aims[source].astype(F32)).astype(BF16)

    def give(source, carry):
        for b in range(8):
            first = codes[source, b, 0]
            for kind, code in ((1, codes[source, b, 1]), (2, codes[first >> 3, first & 7, 1])):
                place = pl.ds(pl.multiple_of((code & 7) * rows, rows), rows)
                stage[source, kind * shared + b * rows : kind * shared + b * rows + rows, :] = stage[code >> 3, place, :]
        return carry

    lax.fori_loop(0, peers, give, 0)
    fetch(stage, send, sems.at[0]).wait()


def final_kernel(tables_one_in, tables_far_in, tables_zero_in, arrived, *refs):
    adjoint_one, adjoint, tables, start, folded, turned, out, later, field, sems, quarter_sems = refs
    loads = [
        fetch(source, tables.at[index], sems.at[index])
        for index, source in enumerate((tables_one_in, tables_far_in, tables_zero_in))
    ]
    rows = arrived.shape[1] // 24
    for load in loads:
        load.wait()
    kept = None
    for index in range(2):
        begin = flipped_diagonal(tables[index, 2].astype(F32))
        mid = spread(tables[index, 1].astype(F32))
        end = flipped_diagonal(tables[index, 0].astype(F32))
        for g in range(4):
            start[:, g * 256 : g * 256 + 256] = mm(begin, pieces_pair(arrived, index + 1, g, rows))
        for g, moved in middle_and_last(start, mid, end, folded, turned, True):
            put_pair((out, later)[index], g, moved)
        if index == 0:
            kept = fetch(out, adjoint_one, sems.at[0])
    begin = flipped_diagonal(tables[2, 0].astype(F32))
    mid = spread(tables[2, 1].astype(F32))
    end = flipped_diagonal(tables[2, 2].astype(F32))
    for g in range(4):
        start[:, g * 256 : g * 256 + 256] = mm(begin, lane_pair(later, g))
    stored = [kept]
    for g, moved in middle_and_last(start, mid, end, folded, turned, True):
        to_native(moved, g, field)
        for qh in range(4):
            at = slice(qh * 8 + 2 * g, qh * 8 + 2 * g + 2)
            stored.append(fetch(field.at[at], adjoint.at[at], quarter_sems.at[g, qh]))
    for copy in stored:
        copy.wait()


def to_native(block, g, field):
    flat = mm(identity(), block, NT).astype(field.dtype)
    for index in range(8):
        x = (index % 4) * 8 + 2 * g + index // 4
        field[x] = flat[index * 32 : index * 32 + 32]


def x_form_to_native(source, folded, turned, field):
    for b in range(8):
        block = source[b].astype(F32)
        block = jnp.concatenate(
            [
                jnp.concatenate([block[g * 64 : g * 64 + 32], block[g * 64 + 32 : g * 64 + 64]], axis=1)
                for g in range(4)
            ],
            axis=0,
        )
        swap_brick(block, folded, turned, b, 1)
    for g in range(4):
        to_native(turned[0:256, g * 256 : g * 256 + 256], g, field)


def tap(offset):
    value = jnp.zeros(offset.shape, F32)
    for step, weight in TAPS:
        value = jnp.where(offset == step, weight, value)
        value = jnp.where(offset == -step, -weight, value)
    return value


def stencils():
    size = 256
    row, col = iota((size, size), 0), iota((size, size), 1)
    along_y = halves(jnp.where(row // 32 == col // 32, tap(col - row), 0.0))
    along_z = halves(tap(row - col))
    row, col = iota((size, 48), 0), iota((size, 48), 1)
    layer = col // 8
    place = jnp.where(layer < RIM, layer - RIM, layer - RIM + 32)
    rim_y = halves(jnp.where(row // 32 == col % 8, tap(place - row % 32), 0.0))
    return along_y, rim_y, along_z


def rim_picker():
    row, col = iota((48, 256), 0), iota((48, 256), 1)
    layer = row // 8
    place = jnp.where(layer < RIM, layer, layer - RIM + 29)
    return ((row % 8 == col // 32) & (place == col % 32)).astype(F32).astype(BF16)


def difference_x(padded, g):
    total = None
    for step, weight in TAPS:
        ahead = padded[pl.ds(8 * g + RIM + step, 8)]
        behind = padded[pl.ds(8 * g + RIM - step, 8)]
        term = weight * (ahead - behind)
        total = term if total is None else total + term
    return total.reshape(256, 256)


def difference_y(parts, rims, along_y, rim_y):
    total = mm(along_y[0], parts[0]) + mm(along_y[1], parts[0])
    if len(parts) > 1:
        total = total + mm(along_y[0], parts[1])
    return total + mm(rim_y[0], rims) + mm(rim_y[1], rims)


def difference_z(parts, along_z):
    total = mm(parts[0], along_z[0]) + mm(parts[0], along_z[1])
    if len(parts) > 1:
        total = total + mm(parts[1], along_z[0])
    return total


def rim_rows(before, after, base, g):
    rows = [before[base + h, (g // 2) * 16 : (g // 2) * 16 + 16, :].astype(F32) for h in range(RIM)]
    rows += [after[base + h, (g // 2) * 16 : (g // 2) * 16 + 16, :].astype(F32) for h in range(RIM)]
    half = (g % 2) * 8
    return jnp.concatenate([value[half : half + 8] for value in rows], axis=0).astype(BF16)


def put_rims(blocks, base, low_y, high_y):
    picker = rim_picker()
    for pair in range(2):
        left, right = mm(picker, blocks[2 * pair]), mm(picker, blocks[2 * pair + 1])
        for layer in range(2 * RIM):
            value = jnp.concatenate(
                [left[layer * 8 : layer * 8 + 8], right[layer * 8 : layer * 8 + 8]], axis=0
            ).astype(BF16)
            target = low_y if layer < RIM else high_y
            target[base + layer % RIM, pair * 16 : pair * 16 + 16, :] = value


def edge_kernel(template, velocity, sent, low_x, high_x, low_y, high_y, field, first_x, last_x, mid_v, sems):
    loads = [
        fetch(template, field, sems.at[0]),
        fetch(velocity.at[0, 0:RIM], first_x, sems.at[1]),
        fetch(velocity.at[0, 29:32], last_x, sems.at[2]),
        fetch(velocity.at[1], mid_v, sems.at[3]),
    ]
    for load in loads:
        load.wait()
    low_x[0:RIM] = field[0:RIM]
    high_x[0:RIM] = field[29:32]
    low_x[RIM : 2 * RIM] = first_x[...].astype(BF16)
    high_x[RIM : 2 * RIM] = last_x[...].astype(BF16)
    put_rims([field[8 * g : 8 * g + 8].reshape(256, 256) for g in range(4)], 0, low_y, high_y)
    put_rims([mid_v[8 * g : 8 * g + 8].astype(BF16).reshape(256, 256) for g in range(4)], RIM, low_y, high_y)


def prepare_kernel(picks, operators, edge, tables):
    chosen = [picks[1, 0, 0, b] for b in range(8)]
    for axis in range(3):
        tables[axis] = table_rows(operators, chosen, axis).astype(BF16)


def divergence_kernel(velocity, before_x, after_x, before_y, after_y, sent, divergence, padded):
    along_y, rim_y, along_z = stencils()
    padded[0:RIM] = before_x[RIM : 2 * RIM].astype(F32)
    padded[RIM : RIM + 32] = velocity[0]
    padded[RIM + 32 : 2 * RIM + 32] = after_x[RIM : 2 * RIM].astype(F32)
    for g in range(4):
        along_one = halves(velocity[1, 8 * g : 8 * g + 8].reshape(256, 256))
        along_two = halves(velocity[2, 8 * g : 8 * g + 8].reshape(256, 256))
        total = (
            difference_x(padded, g)
            + difference_y(along_one, rim_rows(before_y, after_y, RIM, g), along_y, rim_y)
            + difference_z(along_two, along_z)
        )
        divergence[8 * g : 8 * g + 8] = total.reshape(8, 32, 256)


def rims_kernel(codes_in, arrived, divergence, sent, native, low_x, high_x, low_y, high_y, codes, slots, total, state, folded, turned, sems):
    loads = [fetch(codes_in, codes, sems.at[0]), fetch(arrived.at[:, 0:512, :], slots, sems.at[1])]
    total[...] = jnp.zeros(total.shape, F32)
    for load in loads:
        load.wait()
    me = lax.axis_index("gx")

    def add(source, carry):
        rank = jnp.int32(0)
        for b in range(8):
            code = codes[source, b, 0]
            hit = (code >> 3) == me

            @pl.when(hit)
            def _():
                place = pl.ds(pl.multiple_of(rank * 256, 256), 256)
                total[code & 7] += slots[source, place, :].astype(F32)

            rank = rank + hit.astype(jnp.int32)
        return carry

    lax.fori_loop(0, slots.shape[0], add, 0)
    for b in range(8):
        state[b] = total[b].astype(BF16)
    x_form_to_native(state, folded, turned, native)
    low_x[0:RIM] = native[0:RIM]
    high_x[0:RIM] = native[29:32]
    low_x[RIM : 2 * RIM] = divergence[0:RIM].astype(BF16)
    high_x[RIM : 2 * RIM] = divergence[29:32].astype(BF16)
    put_rims([native[8 * g : 8 * g + 8].reshape(256, 256) for g in range(4)], 0, low_y, high_y)
    put_rims(
        [divergence[8 * g : 8 * g + 8].astype(BF16).reshape(256, 256) for g in range(4)], RIM, low_y, high_y
    )


def gradient_kernel(
    template,
    state,
    divergence,
    adjoint_two,
    adjoint_one,
    b0x,
    a0x,
    b0y,
    a0y,
    b1x,
    a1x,
    b1y,
    a1y,
    gradient,
    folded,
    turned,
    weight_two,
    weight_one,
    pad_zero,
    pad_one,
    pad_div,
):
    x_form_to_native(adjoint_one, folded, turned, weight_one)
    for g in range(4):
        to_native(pieces_pair(adjoint_two, 0, g, adjoint_two.shape[1] // 24), g, weight_two)
    along_y, rim_y, along_z = stencils()
    for padded, before, middle, after, base in (
        (pad_zero, b0x, template, a0x, 0),
        (pad_one, b1x, state, a1x, 0),
        (pad_div, b1x, divergence, a1x, RIM),
    ):
        padded[0:RIM] = before[base : base + RIM].astype(F32)
        padded[RIM : RIM + 32] = middle[...].astype(F32)
        padded[RIM + 32 : 2 * RIM + 32] = after[base : base + RIM].astype(F32)
    for g in range(4):
        zero = (template[8 * g : 8 * g + 8].reshape(256, 256),)
        one = (state[8 * g : 8 * g + 8].reshape(256, 256),)
        div = halves(divergence[8 * g : 8 * g + 8].reshape(256, 256))
        weigh_one = 0.5 * weight_one[8 * g : 8 * g + 8].reshape(256, 256)
        weigh_two = 0.5 * weight_two[8 * g : 8 * g + 8].reshape(256, 256)
        for axis in range(3):
            if axis == 0:
                parts = [difference_x(padded, g) for padded in (pad_zero, pad_one, pad_div)]
            elif axis == 1:
                parts = [
                    difference_y(zero, rim_rows(b0y, a0y, 0, g), along_y, rim_y),
                    difference_y(one, rim_rows(b1y, a1y, 0, g), along_y, rim_y),
                    difference_y(div, rim_rows(b1y, a1y, RIM, g), along_y, rim_y),
                ]
            else:
                parts = [difference_z(value, along_z) for value in (zero, one, div)]
            value = weigh_one * parts[0] + weigh_two * parts[1] - 0.25 * parts[2]
            gradient[axis, 8 * g : 8 * g + 8] = value.reshape(8, 32, 256)


SCALAR = pl.BlockSpec(memory_space=pltpu.SMEM)
WHOLE = pl.BlockSpec(memory_space=pltpu.VMEM)
NEAR = pl.BlockSpec(memory_space=pltpu.VMEM)
ANYWHERE = pl.BlockSpec(memory_space=pl.ANY)
FAR = pl.BlockSpec(memory_space=pltpu.HBM)
FOLDED = (32, 64, 128)
FLAT = (256, 1024)
NATIVE = (32, 32, 256)
FORM = (8, 256, 128)
TABLES = (3, 32, 256)


def pinned(value, spec):
    if spec is FAR:
        return pltpu.with_memory_space_constraint(value, pltpu.HBM)
    if spec is NEAR:
        return pltpu.with_memory_space_constraint(value, pltpu.VMEM)
    return value


SHORT, LONG = 1 << 20, 1 << 36


def call(kernel, out, in_specs, out_specs, scratch, work=LONG):
    made = pl.pallas_call(
        kernel,
        out_shape=out,
        in_specs=in_specs,
        out_specs=out_specs,
        scratch_shapes=scratch,
        compiler_params=pltpu.CompilerParams(vmem_limit_bytes=24 * 1024 * 1024),
        cost_estimate=pl.CostEstimate(flops=work, bytes_accessed=1024 * 1024, transcendentals=0),
    )

    def apply(*values):
        return made(*[pinned(value, spec) for value, spec in zip(values, in_specs, strict=True)])

    return apply


def like(shape, dtype):
    return jax.ShapeDtypeStruct(shape, dtype)


def far(shape, dtype):
    return pltpu.HBM(shape, dtype)


def neighbours(low_x, high_x, low_y, high_y):
    moved = []
    for low, high, axis in ((low_x, high_x, "gx"), (low_y, high_y, "gy")):
        size = lax.axis_size(axis)
        up = [(i, i + 1) for i in range(size - 1)]
        down = [(i + 1, i) for i in range(size - 1)]
        moved += [lax.ppermute(high, axis, up), lax.ppermute(low, axis, down)]
    return moved


def swap_slots(send):
    return lax.all_to_all(send, "gx", split_axis=0, concat_axis=0, tiled=True)


def shards(template, target_image, velocity, operators, route, target_brick, operator_index):
    peers = lax.axis_size("gx")
    shared = 8 * (256 // peers)
    sems = pltpu.SemaphoreType.DMA((16,))
    quarter_sems = pltpu.SemaphoreType.DMA((4, 4))
    turning = [pltpu.VMEM(FLAT, F32), pltpu.VMEM(FOLDED, F32), pltpu.VMEM((512, 1024), BF16)]
    form = pltpu.VMEM(FORM, BF16)
    tables = pltpu.VMEM(TABLES, BF16)
    codes_mem = pltpu.SMEM((peers, 8, 128), jnp.int32)
    stage = pltpu.VMEM((peers, shared, 128), BF16)
    meta_half = pltpu.VMEM((peers, 16, 128), BF16)
    table_rows_count = operators.shape[1] * operators.shape[2] * operators.shape[3]
    listed = operators.transpose(1, 2, 3, 0).reshape(table_rows_count, operators.shape[0])
    listed_mem = pltpu.VMEM(listed.shape, BF16)
    route = route.reshape(route.shape[:4])

    send = call(
        target_kernel,
        far((peers, shared + 16, 128), BF16),
        [FAR] * 4,
        FAR,
        [pltpu.SMEM(route.shape, jnp.int32)] * 3
        + [pltpu.VMEM(NATIVE, BF16), stage, pltpu.VMEM((16, 128), F32), meta_half, sems],
        SHORT,
    )(operator_index, route, target_brick, target_image)
    targets = swap_slots(send)

    moved, tables_zero = call(
        first_kernel,
        [far(FORM, BF16), far(TABLES, BF16)],
        [SCALAR, FAR, FAR, FAR],
        [FAR] * 2,
        [listed_mem, pltpu.VMEM(NATIVE, BF16)] + turning + [form, tables, sems],
    )(operator_index, listed, template, send)

    send, tables_far, codes = call(
        second_kernel,
        [far((peers, 512 + shared, 128), BF16), far(TABLES, BF16), far((peers, 8, 128), jnp.int32)],
        [SCALAR, SCALAR, FAR, FAR, ANYWHERE],
        [FAR] * 3,
        [listed_mem, form, meta_half, pltpu.VMEM((peers, 8, 128), jnp.int32), codes_mem]
        + turning
        + [stage, tables, sems, pltpu.SemaphoreType.DMA((8,))],
        SHORT,
    )(route, target_brick, listed, moved, targets)
    arrived = swap_slots(send)

    rim = like((2 * RIM, 32, 256), BF16)
    low_x, high_x, low_y, high_y = call(
        edge_kernel,
        [rim] * 4,
        [FAR] * 3,
        [WHOLE] * 4,
        [pltpu.VMEM(NATIVE, BF16)] + [pltpu.VMEM((RIM, 32, 256), F32)] * 2 + [pltpu.VMEM(NATIVE, F32), sems],
    )(template, velocity, send)
    tables_one = call(prepare_kernel, far(TABLES, BF16), [SCALAR] + [WHOLE] * 2, WHOLE, [])(
        operator_index, listed, low_x
    )
    b0x, a0x, b0y, a0y = neighbours(low_x, high_x, low_y, high_y)

    send = call(
        share_kernel,
        far((peers, 3 * shared, 128), BF16),
        [FAR, ANYWHERE, ANYWHERE],
        FAR,
        [codes_mem, stage, stage, pltpu.VMEM((peers, shared, 128), F32), pltpu.VMEM((peers, 3 * shared, 128), BF16), sems],
        SHORT,
    )(codes, arrived, targets)
    pulled = swap_slots(send)

    divergence = call(
        divergence_kernel, like(NATIVE, F32), [WHOLE] * 5 + [FAR], WHOLE, [pltpu.VMEM((38, 32, 256), F32)]
    )(velocity, b0x, a0x, b0y, a0y, send)
    state, low_x, high_x, low_y, high_y = call(
        rims_kernel,
        [like(NATIVE, BF16)] + [rim] * 4,
        [FAR, ANYWHERE, WHOLE, FAR],
        [WHOLE] * 5,
        [codes_mem, pltpu.VMEM((peers, 512, 128), BF16), pltpu.VMEM(FORM, F32), form] + turning[1:] + [sems],
    )(codes, arrived, divergence, send)
    b1x, a1x, b1y, a1y = neighbours(low_x, high_x, low_y, high_y)

    adjoint_one, adjoint = call(
        final_kernel,
        [far(FORM, BF16), far(NATIVE, BF16)],
        [FAR, FAR, FAR, NEAR],
        [FAR] * 2,
        [pltpu.VMEM((3,) + TABLES, BF16)] + turning + [form, form, pltpu.VMEM(NATIVE, BF16), sems, quarter_sems],
        SHORT,
    )(tables_one, tables_far, tables_zero, pulled)

    gradient = call(
        gradient_kernel,
        far((3,) + NATIVE, F32),
        [WHOLE] * 13,
        WHOLE,
        turning[1:] + [pltpu.VMEM(NATIVE, F32)] * 2 + [pltpu.VMEM((38, 32, 256), F32)] * 3,
    )(template, state, divergence, pulled, adjoint_one, b0x, a0x, b0y, a0y, b1x, a1x, b1y, a1y)
    return gradient, adjoint


def solution(mesh):
    placed = (
        P("gx", "gy", None),
        P("gx", "gy", None),
        P(None, "gx", "gy", None),
        P(),
        P(None, "gx", "gy", None, None),
        P(None, "gx", "gy", None),
        P(None, "gx", "gy", None),
    )
    return jax.shard_map(
        shards,
        mesh=mesh,
        in_specs=placed,
        out_specs=(P(None, "gx", "gy", None), P("gx", "gy", None)),
        check_vma=False,
    )
```

```python
import functools

import jax
import jax.numpy as jnp
from jax import lax
from jax.experimental import pallas as pl
from jax.experimental.pallas import tpu as pltpu
from jax.sharding import PartitionSpec as P

STEPS = 2
CAP = 2
RIM = 3
F32 = jnp.float32
BF16 = jnp.bfloat16
NT = (((1,), (1,)), ((), ()))
NN = (((1,), (0,)), ((), ()))
TAPS = ((1, 0.75), (2, -0.15), (3, 1.0 / 60.0))


def iota(shape, dim):
    return lax.broadcasted_iota(jnp.int32, shape, dim)


def mm(left, right, dims=NN):
    return lax.dot_general(left, right, dims, preferred_element_type=F32)


def halves(value):
    high = value.astype(BF16)
    return high, (value - high.astype(F32)).astype(BF16)


def on_lanes(picks):
    lane = iota((1, 256), 1)
    chosen = jnp.zeros(lane.shape, jnp.int32)
    for b, pick in enumerate(picks):
        chosen = jnp.where(lane // 32 == b, pick, chosen)
    return chosen


def table_rows(operators, chosen, axis):
    shape = (operators.shape[1], 256)
    one_hot = (iota(shape, 0) == jnp.broadcast_to(chosen, shape)).astype(F32).astype(BF16)
    found = mm(operators[axis * 1024 : axis * 1024 + 1024, :], one_hot)
    within = iota((32, 256), 1) % 32
    total = jnp.zeros((32, 256), F32)
    for x in range(32):
        total = jnp.where(within == x, found[x * 32 : x * 32 + 32], total)
    return total


def same_block(size, edge):
    return iota((size, size), 0) // edge == iota((size, size), 1) // edge


def identity():
    return (iota((256, 256), 0) == iota((256, 256), 1)).astype(F32).astype(BF16)


def flipped_diagonal(table):
    return jnp.where(same_block(256, 32), jnp.concatenate([table] * 8, axis=0), 0.0).astype(BF16)


def diagonal(table):
    return mm(identity(), flipped_diagonal(table), NT).astype(BF16)


def spread(table):
    copies = (iota((256, 256), 0) % 32 == iota((256, 256), 1) % 32).astype(F32).astype(BF16)
    return mm(flipped_diagonal(table), copies)


def swap_chunks(parts):
    lane = iota(parts[0].shape, 1)
    for bit, shift in ((1, 32), (2, 64)):
        keep = (lane & shift) == 0
        fresh = list(parts)
        for index in range(4):
            if index & bit:
                continue
            one, two = parts[index], parts[index | bit]
            fresh[index] = jnp.where(keep, one, pltpu.roll(two, shift, 1))
            fresh[index | bit] = jnp.where(keep, pltpu.roll(one, 128 - shift, 1), two)
        parts = fresh
    return parts


def swap_brick(block, folded, turned, brick, parts=2):
    slabs = []
    for ph in range(4):
        slabs.append(
            jnp.concatenate(
                [
                    block[(qs // 2) * 32 + ph * 8 : (qs // 2) * 32 + ph * 8 + 8, (qs % 2) * 128 : (qs % 2) * 128 + 128]
                    for qs in range(8)
                ],
                axis=0,
            )
        )
    slabs = swap_chunks(slabs)
    for qh in range(4):
        folded[brick * 4 + qh] = slabs[qh]
    for ps in range(8):
        value = jnp.concatenate(
            [folded[brick * 4 + qh, pl.ds(ps, 8, stride=8), :] for qh in range(4)], axis=0
        )
        for part, half in enumerate(halves(value)[:parts]):
            turned[part * 256 + brick * 32 : part * 256 + brick * 32 + 32, ps * 128 : ps * 128 + 128] = half


def lane_pair(field, g):
    return jnp.concatenate(
        [
            jnp.concatenate([field[b, qs * 32 : qs * 32 + 32, :] for b in range(8)], axis=0)
            for qs in (2 * g, 2 * g + 1)
        ],
        axis=1,
    )


def put_pair(field, g, value):
    for b in range(8):
        for half in range(2):
            rows = slice((2 * g + half) * 32, (2 * g + half) * 32 + 32)
            field[b, rows, :] = value[b * 32 : b * 32 + 32, half * 128 : half * 128 + 128]


def middle_and_last(start, spread_mid, last, folded, turned, flipped):
    mask = same_block(256, 32)
    for brick in range(8):
        rows = spread_mid[brick * 32 : brick * 32 + 32]
        line = jnp.where(mask, jnp.concatenate([rows] * 8, axis=0), 0.0).astype(BF16)
        block = start[brick * 32 : brick * 32 + 32, :]
        block = jnp.concatenate([block[:, g * 256 : g * 256 + 256] for g in range(4)], axis=0)
        high, low = halves(block)
        both = mm(jnp.concatenate([high, low], axis=0), line, NT if flipped else NN)
        swap_brick(both[:128] + both[128:], folded, turned, brick)
    last = jnp.concatenate([last, last], axis=1)
    for g in range(4):
        yield g, mm(last, turned[:, g * 256 : g * 256 + 256]).astype(BF16)


def slot_numbers(route, step):
    own = [route[step, 0, 0, b] for b in range(8)]
    slots = []
    for b in range(8):
        rank = jnp.int32(0)
        for other in range(b):
            rank = rank + (own[other] == own[b]).astype(jnp.int32)
        slots.append((own[b], rank))
    return slots


def fetch(source, target, sem):
    copy = pltpu.make_async_copy(source, target, sem)
    copy.start()
    return copy


def put_pieces(stage, g, value, rows):
    parts = 32 // rows
    for half in range(2):
        tile = value[:, half * 128 : half * 128 + 128]
        for part in range(parts):
            share = (2 * g + half) * parts + part
            if parts == 1:
                stage[share] = tile
            else:
                for b in range(8):
                    at = b * 32 + part * rows
                    stage[share, b * rows : b * rows + rows, :] = tile[at : at + rows]


def pieces_pair(pieces, kind, g, rows):
    parts = 32 // rows
    base = kind * 8 * rows
    tiles = []
    for tile in (2 * g, 2 * g + 1):
        if parts == 1:
            tiles.append(pieces[tile, base : base + 256, :])
        else:
            tiles.append(
                jnp.concatenate(
                    [
                        pieces[tile * parts + part, base + b * rows : base + b * rows + rows, :]
                        for b in range(8)
                        for part in range(parts)
                    ],
                    axis=0,
                )
            )
    return jnp.concatenate(tiles, axis=1)


def target_kernel(picks_in, route_in, brick_in, target, send, *refs):
    picks, route, landing, field, stage, meta, meta_half, sems = refs
    told = [
        fetch(source, place, sems.at[index])
        for index, (source, place) in enumerate(((picks_in, picks), (route_in, route), (brick_in, landing)))
    ]
    load = fetch(target, field, sems.at[3])
    for copy in told:
        copy.wait()
    lane = iota((1, 128), 1)
    meta[...] = jnp.zeros(meta.shape, F32)
    for b in range(8):
        codes = [route[step, 0, 0, b] * 8 + landing[step, 0, 0, b] for step in range(STEPS)]
        value = jnp.zeros((1, 128), jnp.int32)
        for index, number in enumerate(codes):
            value = jnp.where(lane == index, number, value)
        meta[b : b + 1, :] = value.astype(F32)
        meta[8 + b : 9 + b, :] = jnp.full((1, 128), picks[1, 0, 0, b], jnp.int32).astype(F32)
    meta_half[...] = jnp.broadcast_to(meta[...].astype(BF16)[None], meta_half.shape)
    shared = stage.shape[1]
    sent = [fetch(meta_half, send.at[:, shared : shared + 16, :], sems.at[4])]
    load.wait()
    for g in range(4):
        block = jnp.concatenate(
            [field[qh * 8 + qs] for qs in (2 * g, 2 * g + 1) for qh in range(4)], axis=0
        )
        put_pieces(stage, g, mm(identity(), block, NT).astype(BF16), shared // 8)
    for copy in sent + [fetch(stage, send.at[:, 0:shared, :], sems.at[5])]:
        copy.wait()


def first_kernel(picks, operators, field, sent, moved_out, tables, table_mem, field_mem, start, folded, turned, out, tables_mem, sems):
    loads = [fetch(operators, table_mem, sems.at[0]), fetch(field, field_mem, sems.at[1])]
    chosen = on_lanes([picks[0, 0, 0, b] for b in range(8)])
    loads[0].wait()
    found = [table_rows(table_mem, chosen, axis) for axis in range(3)]
    for axis in range(3):
        tables_mem[axis] = found[axis].astype(BF16)
    kept = fetch(tables_mem, tables, sems.at[0])
    begin = diagonal(found[2])
    loads[1].wait()
    for g in range(4):
        block = jnp.concatenate(
            [field_mem[qh * 8 + qs] for qs in (2 * g, 2 * g + 1) for qh in range(4)], axis=0
        )
        start[:, g * 256 : g * 256 + 256] = mm(begin, block, NT)
    for g, moved in middle_and_last(start, spread(found[1]), diagonal(found[0]), folded, turned, False):
        put_pair(out, g, moved)
    for copy in [kept, fetch(out, moved_out, sems.at[1])]:
        copy.wait()


def second_kernel(route, landing, operators, moved, arrived, *refs):
    send, tables, codes_out, table_mem, moved_mem, meta_half, meta, codes, start, folded, turned, stage, tables_mem, sems, slot_sems = refs
    shared = stage.shape[1]
    heard = fetch(arrived.at[:, shared : shared + 16, :], meta_half, sems.at[0])
    loads = [fetch(operators, table_mem, sems.at[1]), fetch(moved, moved_mem, sems.at[2])]
    heard.wait()
    meta[...] = meta_half[...].astype(F32)
    codes[...] = meta[:, 0:8, :].astype(jnp.int32)
    told = fetch(codes, codes_out, sems.at[3])
    lane = iota((1, 128), 1) // 32
    chosen = []
    for part in range(2):
        row = jnp.zeros((1, 128), F32)
        for b in range(4):
            own = part * 4 + b
            found = meta[route[0, 0, 0, own], pl.ds(8 + landing[0, 0, 0, own], 1), :]
            row = jnp.where(lane == b, found, row)
        chosen.append(row)
    chosen = jnp.concatenate(chosen, axis=1).astype(jnp.int32)
    loads[1].wait()
    sent = []
    for b, (place, rank) in enumerate(slot_numbers(route, 0)):
        rows = pl.ds(pl.multiple_of(rank * 256, 256), 256)
        sent.append(fetch(moved_mem.at[b], send.at[place, rows, :], slot_sems.at[b]))
    loads[0].wait()
    found = [table_rows(table_mem, chosen, axis) for axis in range(3)]
    for axis in range(3):
        tables_mem[axis] = found[axis].astype(BF16)
    kept = fetch(tables_mem, tables, sems.at[5])
    begin = diagonal(found[0])
    for g in range(4):
        start[:, g * 256 : g * 256 + 256] = mm(begin, lane_pair(moved_mem, g))
    for g, value in middle_and_last(start, spread(found[1]), diagonal(found[2]), folded, turned, False):
        put_pieces(stage, g, value, shared // 8)
    sent.append(fetch(stage, send.at[:, 512 : 512 + shared, :], sems.at[6]))
    for copy in sent + [kept, told]:
        copy.wait()


def share_kernel(codes_in, arrived, targets, send, codes, moved, aims, total, stage, sems, chunk_sems):
    peers, shared = moved.shape[0], moved.shape[1]
    rows = shared // 8
    loads = [
        fetch(codes_in, codes, sems.at[0]),
        fetch(arrived.at[:, 512 : 512 + shared, :], moved, sems.at[1]),
        fetch(targets.at[:, 0:shared, :], aims, sems.at[2]),
    ]
    total[...] = jnp.zeros(total.shape, F32)
    for load in loads:
        load.wait()

    def add(source, carry):
        for b in range(8):
            first = codes[source, b, 0]
            final = codes[first >> 3, first & 7, 1]
            place = pl.ds(pl.multiple_of((final & 7) * rows, rows), rows)
            total[final >> 3, place, :] += moved[source, b * rows : b * rows + rows, :].astype(F32)
        return carry

    lax.fori_loop(0, peers, add, 0)
    for source in range(peers):
        final = total[source].astype(BF16).astype(F32)
        stage[source, 0:shared, :] = (final - aims[source].astype(F32)).astype(BF16)
    sent = []
    for source in range(peers):
        for b in range(8):
            code = codes[source, b, 1]
            place = pl.ds(pl.multiple_of((code & 7) * rows, rows), rows)
            stage[source, shared + b * rows : shared + b * rows + rows, :] = stage[code >> 3, place, :]
        sent.append(fetch(stage.at[source], send.at[source], chunk_sems.at[source]))
    for copy in sent:
        copy.wait()


def composed_kernel(codes_in, shares, edge, send, codes, own, stage, sems):
    peers, shared = own.shape[0], own.shape[1]
    rows = shared // 8
    loads = [fetch(codes_in, codes, sems.at[0]), fetch(shares.at[:, 0:shared, :], own, sems.at[1])]
    for load in loads:
        load.wait()

    def give(source, carry):
        for b in range(8):
            first = codes[source, b, 0]
            code = codes[first >> 3, first & 7, 1]
            place = pl.ds(pl.multiple_of((code & 7) * rows, rows), rows)
            stage[source, b * rows : b * rows + rows, :] = own[code >> 3, place, :]
        return carry

    lax.fori_loop(0, peers, give, 0)
    fetch(stage, send, sems.at[0]).wait()


def adjoint_kernel(tables_in, arrived, *refs):
    adjoint, tables, start, folded, turned, sems = refs
    load = fetch(tables_in, tables, sems.at[0])
    rows = arrived.shape[1] // 16
    load.wait()
    begin = flipped_diagonal(tables[2].astype(F32))
    mid = spread(tables[1].astype(F32))
    end = flipped_diagonal(tables[0].astype(F32))
    for g in range(4):
        start[:, g * 256 : g * 256 + 256] = mm(begin, pieces_pair(arrived, 1, g, rows))
    for g, moved in middle_and_last(start, mid, end, folded, turned, True):
        put_pair(adjoint, g, moved)


def final_kernel(tables_far_in, tables_zero_in, gradient, arrived, *refs):
    adjoint, tables, start, folded, turned, later, field, sems, quarter_sems = refs
    loads = [
        fetch(source, tables.at[index], sems.at[index])
        for index, source in enumerate((tables_far_in, tables_zero_in))
    ]
    rows = arrived.shape[1] // 8
    for load in loads:
        load.wait()
    begin = flipped_diagonal(tables[0, 2].astype(F32))
    mid = spread(tables[0, 1].astype(F32))
    end = flipped_diagonal(tables[0, 0].astype(F32))
    for g in range(4):
        start[:, g * 256 : g * 256 + 256] = mm(begin, pieces_pair(arrived, 0, g, rows))
    for g, moved in middle_and_last(start, mid, end, folded, turned, True):
        put_pair(later, g, moved)
    begin = flipped_diagonal(tables[1, 0].astype(F32))
    mid = spread(tables[1, 1].astype(F32))
    end = flipped_diagonal(tables[1, 2].astype(F32))
    for g in range(4):
        start[:, g * 256 : g * 256 + 256] = mm(begin, lane_pair(later, g))
    stored = []
    for g, moved in middle_and_last(start, mid, end, folded, turned, True):
        to_native(moved, g, field)
        for qh in range(4):
            at = slice(qh * 8 + 2 * g, qh * 8 + 2 * g + 2)
            stored.append(fetch(field.at[at], adjoint.at[at], quarter_sems.at[g, qh]))
    for copy in stored:
        copy.wait()


def to_native(block, g, field):
    flat = mm(identity(), block, NT).astype(field.dtype)
    for index in range(8):
        x = (index % 4) * 8 + 2 * g + index // 4
        field[x] = flat[index * 32 : index * 32 + 32]


def x_form_to_native(source, folded, turned, field):
    for b in range(8):
        block = source[b].astype(F32)
        block = jnp.concatenate(
            [
                jnp.concatenate([block[g * 64 : g * 64 + 32], block[g * 64 + 32 : g * 64 + 64]], axis=1)
                for g in range(4)
            ],
            axis=0,
        )
        swap_brick(block, folded, turned, b, 1)
    for g in range(4):
        to_native(turned[0:256, g * 256 : g * 256 + 256], g, field)


def tap(offset):
    value = jnp.zeros(offset.shape, F32)
    for step, weight in TAPS:
        value = jnp.where(offset == step, weight, value)
        value = jnp.where(offset == -step, -weight, value)
    return value


def stencils():
    size = 256
    row, col = iota((size, size), 0), iota((size, size), 1)
    along_y = halves(jnp.where(row // 32 == col // 32, tap(col - row), 0.0))
    along_z = halves(tap(row - col))
    row, col = iota((size, 48), 0), iota((size, 48), 1)
    layer = col // 8
    place = jnp.where(layer < RIM, layer - RIM, layer - RIM + 32)
    rim_y = halves(jnp.where(row // 32 == col % 8, tap(place - row % 32), 0.0))
    return along_y, rim_y, along_z


def rim_picker():
    row, col = iota((48, 256), 0), iota((48, 256), 1)
    layer = row // 8
    place = jnp.where(layer < RIM, layer, layer - RIM + 29)
    return ((row % 8 == col // 32) & (place == col % 32)).astype(F32).astype(BF16)


def difference_x(padded, g):
    total = None
    for step, weight in TAPS:
        ahead = padded[pl.ds(8 * g + RIM + step, 8)]
        behind = padded[pl.ds(8 * g + RIM - step, 8)]
        term = weight * (ahead - behind)
        total = term if total is None else total + term
    return total.reshape(256, 256)


def difference_y(parts, rims, along_y, rim_y):
    total = mm(along_y[0], parts[0]) + mm(along_y[1], parts[0])
    if len(parts) > 1:
        total = total + mm(along_y[0], parts[1])
    return total + mm(rim_y[0], rims) + mm(rim_y[1], rims)


def difference_z(parts, along_z):
    total = mm(parts[0], along_z[0]) + mm(parts[0], along_z[1])
    if len(parts) > 1:
        total = total + mm(parts[1], along_z[0])
    return total


def rim_rows(before, after, base, g):
    rows = [before[base + h, (g // 2) * 16 : (g // 2) * 16 + 16, :].astype(F32) for h in range(RIM)]
    rows += [after[base + h, (g // 2) * 16 : (g // 2) * 16 + 16, :].astype(F32) for h in range(RIM)]
    half = (g % 2) * 8
    return jnp.concatenate([value[half : half + 8] for value in rows], axis=0).astype(BF16)


def put_rims(blocks, base, low_y, high_y):
    picker = rim_picker()
    for pair in range(2):
        left, right = mm(picker, blocks[2 * pair]), mm(picker, blocks[2 * pair + 1])
        for layer in range(2 * RIM):
            value = jnp.concatenate(
                [left[layer * 8 : layer * 8 + 8], right[layer * 8 : layer * 8 + 8]], axis=0
            ).astype(BF16)
            target = low_y if layer < RIM else high_y
            target[base + layer % RIM, pair * 16 : pair * 16 + 16, :] = value


def edge_kernel(template, velocity, sent, low_x, high_x, low_y, high_y, field, first_x, last_x, mid_v, sems):
    loads = [
        fetch(template, field, sems.at[0]),
        fetch(velocity.at[0, 0:RIM], first_x, sems.at[1]),
        fetch(velocity.at[0, 29:32], last_x, sems.at[2]),
        fetch(velocity.at[1], mid_v, sems.at[3]),
    ]
    for load in loads:
        load.wait()
    low_x[0:RIM] = field[0:RIM]
    high_x[0:RIM] = field[29:32]
    low_x[RIM : 2 * RIM] = first_x[...].astype(BF16)
    high_x[RIM : 2 * RIM] = last_x[...].astype(BF16)
    put_rims([field[8 * g : 8 * g + 8].reshape(256, 256) for g in range(4)], 0, low_y, high_y)
    put_rims([mid_v[8 * g : 8 * g + 8].astype(BF16).reshape(256, 256) for g in range(4)], RIM, low_y, high_y)


def prepare_kernel(picks, operators, edge, tables):
    chosen = on_lanes([picks[1, 0, 0, b] for b in range(8)])
    for axis in range(3):
        tables[axis] = table_rows(operators, chosen, axis).astype(BF16)


def divergence_kernel(velocity, before_x, after_x, before_y, after_y, sent, divergence, padded):
    along_y, rim_y, along_z = stencils()
    padded[0:RIM] = before_x[RIM : 2 * RIM].astype(F32)
    padded[RIM : RIM + 32] = velocity[0]
    padded[RIM + 32 : 2 * RIM + 32] = after_x[RIM : 2 * RIM].astype(F32)
    for g in range(4):
        along_one = halves(velocity[1, 8 * g : 8 * g + 8].reshape(256, 256))
        along_two = halves(velocity[2, 8 * g : 8 * g + 8].reshape(256, 256))
        total = (
            difference_x(padded, g)
            + difference_y(along_one, rim_rows(before_y, after_y, RIM, g), along_y, rim_y)
            + difference_z(along_two, along_z)
        )
        divergence[8 * g : 8 * g + 8] = total.reshape(8, 32, 256)


def rims_kernel(codes_in, arrived, divergence, sent, native, low_x, high_x, low_y, high_y, codes, slots, total, state, folded, turned, sems):
    loads = [fetch(codes_in, codes, sems.at[0]), fetch(arrived.at[:, 0:512, :], slots, sems.at[1])]
    total[...] = jnp.zeros(total.shape, F32)
    for load in loads:
        load.wait()
    me = lax.axis_index("gx")

    def add(source, carry):
        rank = jnp.int32(0)
        for b in range(8):
            code = codes[source, b, 0]
            hit = (code >> 3) == me

            @pl.when(hit)
            def _():
                place = pl.ds(pl.multiple_of(rank * 256, 256), 256)
                total[code & 7] += slots[source, place, :].astype(F32)

            rank = rank + hit.astype(jnp.int32)
        return carry

    lax.fori_loop(0, slots.shape[0], add, 0)
    for b in range(8):
        state[b] = total[b].astype(BF16)
    x_form_to_native(state, folded, turned, native)
    low_x[0:RIM] = native[0:RIM]
    high_x[0:RIM] = native[29:32]
    low_x[RIM : 2 * RIM] = divergence[0:RIM].astype(BF16)
    high_x[RIM : 2 * RIM] = divergence[29:32].astype(BF16)
    put_rims([native[8 * g : 8 * g + 8].reshape(256, 256) for g in range(4)], 0, low_y, high_y)
    put_rims(
        [divergence[8 * g : 8 * g + 8].astype(BF16).reshape(256, 256) for g in range(4)], RIM, low_y, high_y
    )


def gradient_kernel(
    template,
    state,
    divergence,
    adjoint_two,
    adjoint_one,
    b0x,
    a0x,
    b0y,
    a0y,
    b1x,
    a1x,
    b1y,
    a1y,
    gradient,
    folded,
    turned,
    weight_two,
    weight_one,
    pad_zero,
    pad_one,
    pad_div,
):
    x_form_to_native(adjoint_one, folded, turned, weight_one)
    for g in range(4):
        to_native(pieces_pair(adjoint_two, 0, g, adjoint_two.shape[1] // 16), g, weight_two)
    along_y, rim_y, along_z = stencils()
    for padded, before, middle, after, base in (
        (pad_zero, b0x, template, a0x, 0),
        (pad_one, b1x, state, a1x, 0),
        (pad_div, b1x, divergence, a1x, RIM),
    ):
        padded[0:RIM] = before[base : base + RIM].astype(F32)
        padded[RIM : RIM + 32] = middle[...].astype(F32)
        padded[RIM + 32 : 2 * RIM + 32] = after[base : base + RIM].astype(F32)
    for g in range(4):
        zero = (template[8 * g : 8 * g + 8].reshape(256, 256),)
        one = (state[8 * g : 8 * g + 8].reshape(256, 256),)
        div = halves(divergence[8 * g : 8 * g + 8].reshape(256, 256))
        weigh_one = 0.5 * weight_one[8 * g : 8 * g + 8].reshape(256, 256)
        weigh_two = 0.5 * weight_two[8 * g : 8 * g + 8].reshape(256, 256)
        for axis in range(3):
            if axis == 0:
                parts = [difference_x(padded, g) for padded in (pad_zero, pad_one, pad_div)]
            elif axis == 1:
                parts = [
                    difference_y(zero, rim_rows(b0y, a0y, 0, g), along_y, rim_y),
                    difference_y(one, rim_rows(b1y, a1y, 0, g), along_y, rim_y),
                    difference_y(div, rim_rows(b1y, a1y, RIM, g), along_y, rim_y),
                ]
            else:
                parts = [difference_z(value, along_z) for value in (zero, one, div)]
            value = weigh_one * parts[0] + weigh_two * parts[1] - 0.25 * parts[2]
            gradient[axis, 8 * g : 8 * g + 8] = value.reshape(8, 32, 256)


SCALAR = pl.BlockSpec(memory_space=pltpu.SMEM)
WHOLE = pl.BlockSpec(memory_space=pltpu.VMEM)
NEAR = pl.BlockSpec(memory_space=pltpu.VMEM)
ANYWHERE = pl.BlockSpec(memory_space=pl.ANY)
FAR = pl.BlockSpec(memory_space=pltpu.HBM)
FOLDED = (32, 64, 128)
FLAT = (256, 1024)
NATIVE = (32, 32, 256)
FORM = (8, 256, 128)
TABLES = (3, 32, 256)


def pinned(value, spec):
    if spec is FAR:
        return pltpu.with_memory_space_constraint(value, pltpu.HBM)
    if spec is NEAR:
        return pltpu.with_memory_space_constraint(value, pltpu.VMEM)
    return value


SHORT, LONG = 1 << 20, 1 << 36


def call(kernel, out, in_specs, out_specs, scratch, work=LONG):
    made = pl.pallas_call(
        kernel,
        out_shape=out,
        in_specs=in_specs,
        out_specs=out_specs,
        scratch_shapes=scratch,
        compiler_params=pltpu.CompilerParams(vmem_limit_bytes=24 * 1024 * 1024),
        cost_estimate=pl.CostEstimate(flops=work, bytes_accessed=1024 * 1024, transcendentals=0),
    )

    def apply(*values):
        return made(*[pinned(value, spec) for value, spec in zip(values, in_specs, strict=True)])

    return apply


def like(shape, dtype):
    return jax.ShapeDtypeStruct(shape, dtype)


def far(shape, dtype):
    return pltpu.HBM(shape, dtype)


def neighbours(low_x, high_x, low_y, high_y):
    moved = []
    for low, high, axis in ((low_x, high_x, "gx"), (low_y, high_y, "gy")):
        size = lax.axis_size(axis)
        up = [(i, i + 1) for i in range(size - 1)]
        down = [(i + 1, i) for i in range(size - 1)]
        moved += [lax.ppermute(high, axis, up), lax.ppermute(low, axis, down)]
    return moved


def swap_slots(send):
    return lax.all_to_all(send, "gx", split_axis=0, concat_axis=0, tiled=True)


def shards(template, target_image, velocity, operators, route, target_brick, operator_index):
    peers = lax.axis_size("gx")
    shared = 8 * (256 // peers)
    sems = pltpu.SemaphoreType.DMA((16,))
    quarter_sems = pltpu.SemaphoreType.DMA((4, 4))
    turning = [pltpu.VMEM(FLAT, F32), pltpu.VMEM(FOLDED, F32), pltpu.VMEM((512, 1024), BF16)]
    form = pltpu.VMEM(FORM, BF16)
    tables = pltpu.VMEM(TABLES, BF16)
    codes_mem = pltpu.SMEM((peers, 8, 128), jnp.int32)
    stage = pltpu.VMEM((peers, shared, 128), BF16)
    meta_half = pltpu.VMEM((peers, 16, 128), BF16)
    table_rows_count = operators.shape[1] * operators.shape[2] * operators.shape[3]
    listed = operators.transpose(1, 2, 3, 0).reshape(table_rows_count, operators.shape[0])
    listed_mem = pltpu.VMEM(listed.shape, BF16)
    route = route.reshape(route.shape[:4])

    send = call(
        target_kernel,
        far((peers, shared + 16, 128), BF16),
        [FAR] * 4,
        FAR,
        [pltpu.SMEM(route.shape, jnp.int32)] * 3
        + [pltpu.VMEM(NATIVE, BF16), stage, pltpu.VMEM((16, 128), F32), meta_half, sems],
        SHORT,
    )(operator_index, route, target_brick, target_image)
    targets = swap_slots(send)

    moved, tables_zero = call(
        first_kernel,
        [far(FORM, BF16), far(TABLES, BF16)],
        [SCALAR, FAR, FAR, FAR],
        [FAR] * 2,
        [listed_mem, pltpu.VMEM(NATIVE, BF16)] + turning + [form, tables, sems],
    )(operator_index, listed, template, send)

    send, tables_far, codes = call(
        second_kernel,
        [far((peers, 512 + shared, 128), BF16), far(TABLES, BF16), far((peers, 8, 128), jnp.int32)],
        [SCALAR, SCALAR, FAR, FAR, ANYWHERE],
        [FAR] * 3,
        [listed_mem, form, meta_half, pltpu.VMEM((peers, 16, 128), F32), pltpu.VMEM((peers, 8, 128), jnp.int32)]
        + turning
        + [stage, tables, sems, pltpu.SemaphoreType.DMA((8,))],
        SHORT,
    )(route, target_brick, listed, moved, targets)
    arrived = swap_slots(send)

    rim = like((2 * RIM, 32, 256), BF16)
    low_x, high_x, low_y, high_y = call(
        edge_kernel,
        [rim] * 4,
        [FAR] * 3,
        [WHOLE] * 4,
        [pltpu.VMEM(NATIVE, BF16)] + [pltpu.VMEM((RIM, 32, 256), F32)] * 2 + [pltpu.VMEM(NATIVE, F32), sems],
    )(template, velocity, send)
    tables_one = call(prepare_kernel, far(TABLES, BF16), [SCALAR] + [WHOLE] * 2, WHOLE, [])(
        operator_index, listed, low_x
    )
    b0x, a0x, b0y, a0y = neighbours(low_x, high_x, low_y, high_y)

    send = call(
        share_kernel,
        far((peers, 2 * shared, 128), BF16),
        [FAR, ANYWHERE, ANYWHERE],
        FAR,
        [codes_mem, stage, stage, pltpu.VMEM((peers, shared, 128), F32), pltpu.VMEM((peers, 2 * shared, 128), BF16)]
        + [sems, pltpu.SemaphoreType.DMA((peers,))],
        SHORT,
    )(codes, arrived, targets)
    pulled = swap_slots(send)
    divergence = call(
        divergence_kernel, like(NATIVE, F32), [WHOLE] * 5 + [FAR], WHOLE, [pltpu.VMEM((38, 32, 256), F32)]
    )(velocity, b0x, a0x, b0y, a0y, send)
    state, low_x, high_x, low_y, high_y = call(
        rims_kernel,
        [like(NATIVE, BF16)] + [rim] * 4,
        [FAR, ANYWHERE, WHOLE, FAR],
        [WHOLE] * 5,
        [codes_mem, pltpu.VMEM((peers, 512, 128), BF16), pltpu.VMEM(FORM, F32), form] + turning[1:] + [sems],
    )(codes, arrived, divergence, send)
    b1x, a1x, b1y, a1y = neighbours(low_x, high_x, low_y, high_y)
    composed = call(
        composed_kernel, far((peers, shared, 128), BF16), [FAR, FAR, WHOLE], FAR, [codes_mem, stage, stage, sems]
    )(codes, send, low_x)

    composed = swap_slots(composed)

    adjoint_one = call(
        adjoint_kernel, like(FORM, BF16), [FAR, NEAR], WHOLE, [tables] + turning + [sems]
    )(tables_one, pulled)
    gradient = call(
        gradient_kernel,
        far((3,) + NATIVE, F32),
        [WHOLE] * 13,
        WHOLE,
        turning[1:] + [pltpu.VMEM(NATIVE, F32)] * 2 + [pltpu.VMEM((38, 32, 256), F32)] * 3,
    )(template, state, divergence, pulled, adjoint_one, b0x, a0x, b0y, a0y, b1x, a1x, b1y, a1y)

    adjoint = call(
        final_kernel,
        far(NATIVE, BF16),
        [FAR, FAR, FAR, NEAR],
        FAR,
        [pltpu.VMEM((2,) + TABLES, BF16)] + turning + [form, pltpu.VMEM(NATIVE, BF16), sems, quarter_sems],
        SHORT,
    )(tables_far, tables_zero, gradient, composed)
    return gradient, adjoint


def solution(mesh):
    placed = (
        P("gx", "gy", None),
        P("gx", "gy", None),
        P(None, "gx", "gy", None),
        P(),
        P(None, "gx", "gy", None, None),
        P(None, "gx", "gy", None),
        P(None, "gx", "gy", None),
    )
    return jax.shard_map(
        shards,
        mesh=mesh,
        in_specs=placed,
        out_specs=(P(None, "gx", "gy", None), P("gx", "gy", None)),
        check_vma=False,
    )
```

```python
import functools

import jax
import jax.numpy as jnp
from jax import lax
from jax.experimental import pallas as pl
from jax.experimental.pallas import tpu as pltpu
from jax.sharding import PartitionSpec as P

STEPS = 2
CAP = 2
RIM = 3
F32 = jnp.float32
BF16 = jnp.bfloat16
NT = (((1,), (1,)), ((), ()))
NN = (((1,), (0,)), ((), ()))
TAPS = ((1, 0.75), (2, -0.15), (3, 1.0 / 60.0))


def iota(shape, dim):
    return lax.broadcasted_iota(jnp.int32, shape, dim)


def mm(left, right, dims=NN):
    return lax.dot_general(left, right, dims, preferred_element_type=F32)


def halves(value):
    high = value.astype(BF16)
    return high, (value - high.astype(F32)).astype(BF16)


def on_lanes(picks):
    lane = iota((1, 256), 1)
    chosen = jnp.zeros(lane.shape, jnp.int32)
    for b, pick in enumerate(picks):
        chosen = jnp.where(lane // 32 == b, pick, chosen)
    return chosen


def table_rows(operators, chosen, axis):
    shape = (operators.shape[1], 256)
    one_hot = (iota(shape, 0) == jnp.broadcast_to(chosen, shape)).astype(F32).astype(BF16)
    found = mm(operators[axis * 1024 : axis * 1024 + 1024, :], one_hot)
    within = iota((32, 256), 1) % 32
    total = jnp.zeros((32, 256), F32)
    for x in range(32):
        total = jnp.where(within == x, found[x * 32 : x * 32 + 32], total)
    return total


def same_block(size, edge):
    return iota((size, size), 0) // edge == iota((size, size), 1) // edge


def identity():
    return (iota((256, 256), 0) == iota((256, 256), 1)).astype(F32).astype(BF16)


def flipped_diagonal(table):
    return jnp.where(same_block(256, 32), jnp.concatenate([table] * 8, axis=0), 0.0).astype(BF16)


def diagonal(table):
    return mm(identity(), flipped_diagonal(table), NT).astype(BF16)


def spread(table):
    copies = (iota((256, 256), 0) % 32 == iota((256, 256), 1) % 32).astype(F32).astype(BF16)
    return mm(flipped_diagonal(table), copies)


def swap_chunks(parts):
    lane = iota(parts[0].shape, 1)
    for bit, shift in ((1, 32), (2, 64)):
        keep = (lane & shift) == 0
        fresh = list(parts)
        for index in range(4):
            if index & bit:
                continue
            one, two = parts[index], parts[index | bit]
            fresh[index] = jnp.where(keep, one, pltpu.roll(two, shift, 1))
            fresh[index | bit] = jnp.where(keep, pltpu.roll(one, 128 - shift, 1), two)
        parts = fresh
    return parts


def swap_brick(block, folded, turned, brick, parts=2):
    slabs = []
    for ph in range(4):
        slabs.append(
            jnp.concatenate(
                [
                    block[(qs // 2) * 32 + ph * 8 : (qs // 2) * 32 + ph * 8 + 8, (qs % 2) * 128 : (qs % 2) * 128 + 128]
                    for qs in range(8)
                ],
                axis=0,
            )
        )
    slabs = swap_chunks(slabs)
    for qh in range(4):
        folded[brick * 4 + qh] = slabs[qh]
    for ps in range(8):
        value = jnp.concatenate(
            [folded[brick * 4 + qh, pl.ds(ps, 8, stride=8), :] for qh in range(4)], axis=0
        )
        for part, half in enumerate(halves(value)[:parts]):
            turned[part * 256 + brick * 32 : part * 256 + brick * 32 + 32, ps * 128 : ps * 128 + 128] = half


def lane_pair(field, g):
    return jnp.concatenate(
        [
            jnp.concatenate([field[b, qs * 32 : qs * 32 + 32, :] for b in range(8)], axis=0)
            for qs in (2 * g, 2 * g + 1)
        ],
        axis=1,
    )


def put_pair(field, g, value):
    for b in range(8):
        for half in range(2):
            rows = slice((2 * g + half) * 32, (2 * g + half) * 32 + 32)
            field[b, rows, :] = value[b * 32 : b * 32 + 32, half * 128 : half * 128 + 128]


def middle_and_last(start, spread_mid, last, folded, turned, flipped):
    mask = same_block(256, 32)
    for brick in range(8):
        rows = spread_mid[brick * 32 : brick * 32 + 32]
        line = jnp.where(mask, jnp.concatenate([rows] * 8, axis=0), 0.0).astype(BF16)
        block = start[brick * 32 : brick * 32 + 32, :]
        block = jnp.concatenate([block[:, g * 256 : g * 256 + 256] for g in range(4)], axis=0)
        high, low = halves(block)
        both = mm(jnp.concatenate([high, low], axis=0), line, NT if flipped else NN)
        swap_brick(both[:128] + both[128:], folded, turned, brick)
    last = jnp.concatenate([last, last], axis=1)
    for g in range(4):
        yield g, mm(last, turned[:, g * 256 : g * 256 + 256]).astype(BF16)


def slot_numbers(route, step):
    own = [route[step, 0, 0, b] for b in range(8)]
    slots = []
    for b in range(8):
        rank = jnp.int32(0)
        for other in range(b):
            rank = rank + (own[other] == own[b]).astype(jnp.int32)
        slots.append((own[b], rank))
    return slots


def fetch(source, target, sem):
    copy = pltpu.make_async_copy(source, target, sem)
    copy.start()
    return copy


def put_pieces(stage, g, value, rows):
    parts = 32 // rows
    for half in range(2):
        tile = value[:, half * 128 : half * 128 + 128]
        for part in range(parts):
            share = (2 * g + half) * parts + part
            if parts == 1:
                stage[share] = tile
            else:
                for b in range(8):
                    at = b * 32 + part * rows
                    stage[share, b * rows : b * rows + rows, :] = tile[at : at + rows]


def pieces_pair(pieces, kind, g, rows):
    parts = 32 // rows
    base = kind * 8 * rows
    tiles = []
    for tile in (2 * g, 2 * g + 1):
        if parts == 1:
            tiles.append(pieces[tile, base : base + 256, :])
        else:
            tiles.append(
                jnp.concatenate(
                    [
                        pieces[tile * parts + part, base + b * rows : base + b * rows + rows, :]
                        for b in range(8)
                        for part in range(parts)
                    ],
                    axis=0,
                )
            )
    return jnp.concatenate(tiles, axis=1)


def tell_kernel(picks_in, route_in, brick_in, send, picks, route, landing, meta, meta_half, sems):
    told = [
        fetch(source, place, sems.at[index])
        for index, (source, place) in enumerate(((picks_in, picks), (route_in, route), (brick_in, landing)))
    ]
    for copy in told:
        copy.wait()
    lane = iota((1, 128), 1)
    meta[...] = jnp.zeros(meta.shape, F32)
    value = jnp.zeros((1, 128), jnp.int32)
    for b in range(8):
        for step in range(STEPS):
            code = route[step, 0, 0, b] * 8 + landing[step, 0, 0, b]
            value = jnp.where(lane == 2 * b + step, code, value)
        meta[8 + b : 9 + b, :] = jnp.full((1, 128), picks[1, 0, 0, b], jnp.int32).astype(F32)
    meta[0:1, :] = value.astype(F32)
    meta_half[...] = jnp.broadcast_to(meta[...].astype(BF16)[None], meta_half.shape)
    fetch(meta_half, send, sems.at[0]).wait()


def target_kernel(target, told, send, field, stage, sems):
    fetch(target, field, sems.at[0]).wait()
    for g in range(4):
        block = jnp.concatenate(
            [field[qh * 8 + qs] for qs in (2 * g, 2 * g + 1) for qh in range(4)], axis=0
        )
        put_pieces(stage, g, mm(identity(), block, NT).astype(BF16), stage.shape[1] // 8)
    fetch(stage, send, sems.at[0]).wait()


def pass_kernel(send, targets, same):
    del send, targets, same


def first_kernel(picks, operators, field, sent, moved_out, tables, table_mem, field_mem, start, folded, turned, out, tables_mem, sems):
    loads = [fetch(operators, table_mem, sems.at[0]), fetch(field, field_mem, sems.at[1])]
    chosen = on_lanes([picks[0, 0, 0, b] for b in range(8)])
    loads[0].wait()
    found = [table_rows(table_mem, chosen, axis) for axis in range(3)]
    for axis in range(3):
        tables_mem[axis] = found[axis].astype(BF16)
    kept = fetch(tables_mem, tables, sems.at[0])
    begin = diagonal(found[2])
    loads[1].wait()
    for g in range(4):
        block = jnp.concatenate(
            [field_mem[qh * 8 + qs] for qs in (2 * g, 2 * g + 1) for qh in range(4)], axis=0
        )
        start[:, g * 256 : g * 256 + 256] = mm(begin, block, NT)
    for g, moved in middle_and_last(start, spread(found[1]), diagonal(found[0]), folded, turned, False):
        put_pair(out, g, moved)
    for copy in [kept, fetch(out, moved_out, sems.at[1])]:
        copy.wait()


def second_kernel(route, landing, operators, moved, arrived, *refs):
    send, tables, codes_out, table_mem, moved_mem, meta_half, meta, codes, start, folded, turned, stage, tables_mem, sems, slot_sems = refs
    shared = stage.shape[1]
    heard = fetch(arrived, meta_half, sems.at[0])
    loads = [fetch(operators, table_mem, sems.at[1]), fetch(moved, moved_mem, sems.at[2])]
    heard.wait()
    meta[...] = meta_half[...].astype(F32)
    for source in range(meta.shape[0]):
        codes[source : source + 1, :] = meta[source, 0:1, :].astype(jnp.int32)
    told = fetch(codes, codes_out, sems.at[3])
    lane = iota((1, 128), 1) // 32
    chosen = []
    for part in range(2):
        row = jnp.zeros((1, 128), F32)
        for b in range(4):
            own = part * 4 + b
            found = meta[route[0, 0, 0, own], pl.ds(8 + landing[0, 0, 0, own], 1), :]
            row = jnp.where(lane == b, found, row)
        chosen.append(row)
    chosen = jnp.concatenate(chosen, axis=1).astype(jnp.int32)
    loads[1].wait()
    sent = []
    for b, (place, rank) in enumerate(slot_numbers(route, 0)):
        rows = pl.ds(pl.multiple_of(rank * 256, 256), 256)
        sent.append(fetch(moved_mem.at[b], send.at[place, rows, :], slot_sems.at[b]))
    loads[0].wait()
    found = [table_rows(table_mem, chosen, axis) for axis in range(3)]
    for axis in range(3):
        tables_mem[axis] = found[axis].astype(BF16)
    kept = fetch(tables_mem, tables, sems.at[5])
    begin = diagonal(found[0])
    for g in range(4):
        start[:, g * 256 : g * 256 + 256] = mm(begin, lane_pair(moved_mem, g))
    for g, value in middle_and_last(start, spread(found[1]), diagonal(found[2]), folded, turned, False):
        put_pieces(stage, g, value, shared // 8)
    sent.append(fetch(stage, send.at[:, 512 : 512 + shared, :], sems.at[6]))
    for copy in sent + [kept, told]:
        copy.wait()


def share_kernel(plan_in, arrived, targets, send, plan, total, stage, sems, chunk_sems):
    peers, shared = targets.shape[0], targets.shape[1]
    rows = shared // 8
    load = fetch(plan_in, plan, sems.at[0])
    total[...] = jnp.zeros(total.shape, F32)
    load.wait()

    def add(source, carry):
        for b in range(8):
            final = plan[source, 8 + b]
            place = pl.ds(pl.multiple_of((final & 7) * rows, rows), rows)
            at = 512 + b * rows
            total[final >> 3, place, :] += arrived[source, at : at + rows, :].astype(F32)
        return carry

    lax.fori_loop(0, peers, add, 0)
    for source in range(peers):
        final = total[source].astype(BF16).astype(F32)
        stage[source, 0:shared, :] = (final - targets[source].astype(F32)).astype(BF16)
    sent = []
    for source in range(peers):
        for b in range(8):
            code = plan[source, b]
            place = pl.ds(pl.multiple_of((code & 7) * rows, rows), rows)
            stage[source, shared + b * rows : shared + b * rows + rows, :] = stage[code >> 3, place, :]
        sent.append(fetch(stage.at[source], send.at[source], chunk_sems.at[source]))
    for copy in sent:
        copy.wait()


def composed_kernel(plan_in, shares, edge, send, plan, own, stage, sems):
    peers, shared = own.shape[0], own.shape[1]
    rows = shared // 8
    loads = [fetch(plan_in, plan, sems.at[0]), fetch(shares.at[:, 0:shared, :], own, sems.at[1])]
    for load in loads:
        load.wait()

    def give(source, carry):
        for b in range(8):
            code = plan[source, 8 + b]
            place = pl.ds(pl.multiple_of((code & 7) * rows, rows), rows)
            stage[source, b * rows : b * rows + rows, :] = own[code >> 3, place, :]
        return carry

    lax.fori_loop(0, peers, give, 0)
    fetch(stage, send, sems.at[0]).wait()


def adjoint_kernel(tables_in, arrived, *refs):
    adjoint, tables, start, folded, turned, sems = refs
    load = fetch(tables_in, tables, sems.at[0])
    rows = arrived.shape[1] // 16
    load.wait()
    begin = flipped_diagonal(tables[2].astype(F32))
    mid = spread(tables[1].astype(F32))
    end = flipped_diagonal(tables[0].astype(F32))
    for g in range(4):
        start[:, g * 256 : g * 256 + 256] = mm(begin, pieces_pair(arrived, 1, g, rows))
    for g, moved in middle_and_last(start, mid, end, folded, turned, True):
        put_pair(adjoint, g, moved)


def final_kernel(tables_far, tables_zero, gradient, arrived, *refs):
    adjoint, start, folded, turned, later, field, quarter_sems = refs
    rows = arrived.shape[1] // 8
    begin = flipped_diagonal(tables_far[2].astype(F32))
    mid = spread(tables_far[1].astype(F32))
    end = flipped_diagonal(tables_far[0].astype(F32))
    for g in range(4):
        start[:, g * 256 : g * 256 + 256] = mm(begin, pieces_pair(arrived, 0, g, rows))
    for g, moved in middle_and_last(start, mid, end, folded, turned, True):
        put_pair(later, g, moved)
    begin = flipped_diagonal(tables_zero[0].astype(F32))
    mid = spread(tables_zero[1].astype(F32))
    end = flipped_diagonal(tables_zero[2].astype(F32))
    for g in range(4):
        start[:, g * 256 : g * 256 + 256] = mm(begin, lane_pair(later, g))
    stored = []
    for g, moved in middle_and_last(start, mid, end, folded, turned, True):
        to_native(moved, g, field)
        for qh in range(4):
            at = slice(qh * 8 + 2 * g, qh * 8 + 2 * g + 2)
            stored.append(fetch(field.at[at], adjoint.at[at], quarter_sems.at[g, qh]))
    for copy in stored:
        copy.wait()


def to_native(block, g, field):
    flat = mm(identity(), block, NT).astype(field.dtype)
    for index in range(8):
        x = (index % 4) * 8 + 2 * g + index // 4
        field[x] = flat[index * 32 : index * 32 + 32]


def x_form_to_native(source, folded, turned, field):
    for b in range(8):
        block = source[b].astype(F32)
        block = jnp.concatenate(
            [
                jnp.concatenate([block[g * 64 : g * 64 + 32], block[g * 64 + 32 : g * 64 + 64]], axis=1)
                for g in range(4)
            ],
            axis=0,
        )
        swap_brick(block, folded, turned, b, 1)
    for g in range(4):
        to_native(turned[0:256, g * 256 : g * 256 + 256], g, field)


def tap(offset):
    value = jnp.zeros(offset.shape, F32)
    for step, weight in TAPS:
        value = jnp.where(offset == step, weight, value)
        value = jnp.where(offset == -step, -weight, value)
    return value


def stencils():
    size = 256
    row, col = iota((size, size), 0), iota((size, size), 1)
    along_y = halves(jnp.where(row // 32 == col // 32, tap(col - row), 0.0))
    along_z = halves(tap(row - col))
    row, col = iota((size, 48), 0), iota((size, 48), 1)
    layer = col // 8
    place = jnp.where(layer < RIM, layer - RIM, layer - RIM + 32)
    rim_y = halves(jnp.where(row // 32 == col % 8, tap(place - row % 32), 0.0))
    return along_y, rim_y, along_z


def rim_picker():
    row, col = iota((48, 256), 0), iota((48, 256), 1)
    layer = row // 8
    place = jnp.where(layer < RIM, layer, layer - RIM + 29)
    return ((row % 8 == col // 32) & (place == col % 32)).astype(F32).astype(BF16)


def difference_x(padded, g):
    total = None
    for step, weight in TAPS:
        ahead = padded[pl.ds(8 * g + RIM + step, 8)]
        behind = padded[pl.ds(8 * g + RIM - step, 8)]
        term = weight * (ahead - behind)
        total = term if total is None else total + term
    return total.reshape(256, 256)


def difference_y(parts, rims, along_y, rim_y):
    total = mm(along_y[0], parts[0]) + mm(along_y[1], parts[0])
    if len(parts) > 1:
        total = total + mm(along_y[0], parts[1])
    return total + mm(rim_y[0], rims) + mm(rim_y[1], rims)


def difference_z(parts, along_z):
    total = mm(parts[0], along_z[0]) + mm(parts[0], along_z[1])
    if len(parts) > 1:
        total = total + mm(parts[1], along_z[0])
    return total


def rim_rows(before, after, base, g):
    rows = [before[base + h, (g // 2) * 16 : (g // 2) * 16 + 16, :].astype(F32) for h in range(RIM)]
    rows += [after[base + h, (g // 2) * 16 : (g // 2) * 16 + 16, :].astype(F32) for h in range(RIM)]
    half = (g % 2) * 8
    return jnp.concatenate([value[half : half + 8] for value in rows], axis=0).astype(BF16)


def put_rims(blocks, base, low_y, high_y):
    picker = rim_picker()
    for pair in range(2):
        left, right = mm(picker, blocks[2 * pair]), mm(picker, blocks[2 * pair + 1])
        for layer in range(2 * RIM):
            value = jnp.concatenate(
                [left[layer * 8 : layer * 8 + 8], right[layer * 8 : layer * 8 + 8]], axis=0
            ).astype(BF16)
            target = low_y if layer < RIM else high_y
            target[base + layer % RIM, pair * 16 : pair * 16 + 16, :] = value


def edge_kernel(template, velocity, sent, low_x, high_x, low_y, high_y, field, first_x, last_x, mid_v, sems):
    loads = [
        fetch(template, field, sems.at[0]),
        fetch(velocity.at[0, 0:RIM], first_x, sems.at[1]),
        fetch(velocity.at[0, 29:32], last_x, sems.at[2]),
        fetch(velocity.at[1], mid_v, sems.at[3]),
    ]
    for load in loads:
        load.wait()
    low_x[0:RIM] = field[0:RIM]
    high_x[0:RIM] = field[29:32]
    low_x[RIM : 2 * RIM] = first_x[...].astype(BF16)
    high_x[RIM : 2 * RIM] = last_x[...].astype(BF16)
    put_rims([field[8 * g : 8 * g + 8].reshape(256, 256) for g in range(4)], 0, low_y, high_y)
    put_rims([mid_v[8 * g : 8 * g + 8].astype(BF16).reshape(256, 256) for g in range(4)], RIM, low_y, high_y)


def prepare_kernel(picks, codes_in, operators, edge, tables, plan_out, codes, plan, sems):
    load = fetch(codes_in, codes, sems.at[0])
    chosen = on_lanes([picks[1, 0, 0, b] for b in range(8)])
    for axis in range(3):
        tables[axis] = table_rows(operators, chosen, axis).astype(BF16)
    load.wait()

    def row(source, carry):
        for b in range(8):
            first = codes[source, 2 * b]
            plan[source, b] = codes[source, 2 * b + 1]
            plan[source, 8 + b] = codes[first >> 3, 2 * (first & 7) + 1]
        return carry

    lax.fori_loop(0, codes.shape[0], row, 0)
    fetch(plan, plan_out, sems.at[0]).wait()


def divergence_kernel(velocity, before_x, after_x, before_y, after_y, sent, divergence, padded):
    along_y, rim_y, along_z = stencils()
    padded[0:RIM] = before_x[RIM : 2 * RIM].astype(F32)
    padded[RIM : RIM + 32] = velocity[0]
    padded[RIM + 32 : 2 * RIM + 32] = after_x[RIM : 2 * RIM].astype(F32)
    for g in range(4):
        along_one = halves(velocity[1, 8 * g : 8 * g + 8].reshape(256, 256))
        along_two = halves(velocity[2, 8 * g : 8 * g + 8].reshape(256, 256))
        total = (
            difference_x(padded, g)
            + difference_y(along_one, rim_rows(before_y, after_y, RIM, g), along_y, rim_y)
            + difference_z(along_two, along_z)
        )
        divergence[8 * g : 8 * g + 8] = total.reshape(8, 32, 256)


def rims_kernel(codes_in, arrived, divergence, sent, native, low_x, high_x, low_y, high_y, codes, slots, total, state, folded, turned, sems):
    loads = [fetch(codes_in, codes, sems.at[0]), fetch(arrived.at[:, 0:512, :], slots, sems.at[1])]
    total[...] = jnp.zeros(total.shape, F32)
    for load in loads:
        load.wait()
    me = lax.axis_index("gx")

    def add(source, carry):
        rank = jnp.int32(0)
        for b in range(8):
            code = codes[source, 2 * b]
            hit = (code >> 3) == me

            @pl.when(hit)
            def _():
                place = pl.ds(pl.multiple_of(rank * 256, 256), 256)
                total[code & 7] += slots[source, place, :].astype(F32)

            rank = rank + hit.astype(jnp.int32)
        return carry

    lax.fori_loop(0, slots.shape[0], add, 0)
    for b in range(8):
        state[b] = total[b].astype(BF16)
    x_form_to_native(state, folded, turned, native)
    low_x[0:RIM] = native[0:RIM]
    high_x[0:RIM] = native[29:32]
    low_x[RIM : 2 * RIM] = divergence[0:RIM].astype(BF16)
    high_x[RIM : 2 * RIM] = divergence[29:32].astype(BF16)
    put_rims([native[8 * g : 8 * g + 8].reshape(256, 256) for g in range(4)], 0, low_y, high_y)
    put_rims(
        [divergence[8 * g : 8 * g + 8].astype(BF16).reshape(256, 256) for g in range(4)], RIM, low_y, high_y
    )


def gradient_kernel(
    template,
    state,
    divergence,
    adjoint_two,
    adjoint_one,
    b0x,
    a0x,
    b0y,
    a0y,
    b1x,
    a1x,
    b1y,
    a1y,
    gradient,
    folded,
    turned,
    weight_two,
    weight_one,
    pad_zero,
    pad_one,
    pad_div,
):
    x_form_to_native(adjoint_one, folded, turned, weight_one)
    for g in range(4):
        to_native(pieces_pair(adjoint_two, 0, g, adjoint_two.shape[1] // 16), g, weight_two)
    along_y, rim_y, along_z = stencils()
    for padded, before, middle, after, base in (
        (pad_zero, b0x, template, a0x, 0),
        (pad_one, b1x, state, a1x, 0),
        (pad_div, b1x, divergence, a1x, RIM),
    ):
        padded[0:RIM] = before[base : base + RIM].astype(F32)
        padded[RIM : RIM + 32] = middle[...].astype(F32)
        padded[RIM + 32 : 2 * RIM + 32] = after[base : base + RIM].astype(F32)
    for g in range(4):
        zero = (template[8 * g : 8 * g + 8].reshape(256, 256),)
        one = (state[8 * g : 8 * g + 8].reshape(256, 256),)
        div = halves(divergence[8 * g : 8 * g + 8].reshape(256, 256))
        weigh_one = 0.5 * weight_one[8 * g : 8 * g + 8].reshape(256, 256)
        weigh_two = 0.5 * weight_two[8 * g : 8 * g + 8].reshape(256, 256)
        for axis in range(3):
            if axis == 0:
                parts = [difference_x(padded, g) for padded in (pad_zero, pad_one, pad_div)]
            elif axis == 1:
                parts = [
                    difference_y(zero, rim_rows(b0y, a0y, 0, g), along_y, rim_y),
                    difference_y(one, rim_rows(b1y, a1y, 0, g), along_y, rim_y),
                    difference_y(div, rim_rows(b1y, a1y, RIM, g), along_y, rim_y),
                ]
            else:
                parts = [difference_z(value, along_z) for value in (zero, one, div)]
            value = weigh_one * parts[0] + weigh_two * parts[1] - 0.25 * parts[2]
            gradient[axis, 8 * g : 8 * g + 8] = value.reshape(8, 32, 256)


SCALAR = pl.BlockSpec(memory_space=pltpu.SMEM)
WHOLE = pl.BlockSpec(memory_space=pltpu.VMEM)
NEAR = pl.BlockSpec(memory_space=pltpu.VMEM)
ANYWHERE = pl.BlockSpec(memory_space=pl.ANY)
FAR = pl.BlockSpec(memory_space=pltpu.HBM)
FOLDED = (32, 64, 128)
FLAT = (256, 1024)
NATIVE = (32, 32, 256)
FORM = (8, 256, 128)
TABLES = (3, 32, 256)


def pinned(value, spec):
    if spec is FAR:
        return pltpu.with_memory_space_constraint(value, pltpu.HBM)
    if spec is NEAR:
        return pltpu.with_memory_space_constraint(value, pltpu.VMEM)
    return value


SHORT, LONG = 1 << 20, 1 << 36


def call(kernel, out, in_specs, out_specs, scratch, work=LONG):
    made = pl.pallas_call(
        kernel,
        out_shape=out,
        in_specs=in_specs,
        out_specs=out_specs,
        scratch_shapes=scratch,
        compiler_params=pltpu.CompilerParams(vmem_limit_bytes=24 * 1024 * 1024),
        cost_estimate=pl.CostEstimate(flops=work, bytes_accessed=1024 * 1024, transcendentals=0),
    )

    def apply(*values):
        return made(*[pinned(value, spec) for value, spec in zip(values, in_specs, strict=True)])

    return apply


def like(shape, dtype):
    return jax.ShapeDtypeStruct(shape, dtype)


def far(shape, dtype):
    return pltpu.HBM(shape, dtype)


def neighbours(low_x, high_x, low_y, high_y):
    moved = []
    for low, high, axis in ((low_x, high_x, "gx"), (low_y, high_y, "gy")):
        size = lax.axis_size(axis)
        up = [(i, i + 1) for i in range(size - 1)]
        down = [(i + 1, i) for i in range(size - 1)]
        moved += [lax.ppermute(high, axis, up), lax.ppermute(low, axis, down)]
    return moved


def swap_slots(send):
    return lax.all_to_all(send, "gx", split_axis=0, concat_axis=0, tiled=True)


def shards(template, target_image, velocity, operators, route, target_brick, operator_index):
    peers = lax.axis_size("gx")
    shared = 8 * (256 // peers)
    sems = pltpu.SemaphoreType.DMA((16,))
    quarter_sems = pltpu.SemaphoreType.DMA((4, 4))
    turning = [pltpu.VMEM(FLAT, F32), pltpu.VMEM(FOLDED, F32), pltpu.VMEM((512, 1024), BF16)]
    form = pltpu.VMEM(FORM, BF16)
    tables = pltpu.VMEM(TABLES, BF16)
    routes_mem = pltpu.SMEM((peers, 128), jnp.int32)
    stage = pltpu.VMEM((peers, shared, 128), BF16)
    meta_half = pltpu.VMEM((peers, 16, 128), BF16)
    table_rows_count = operators.shape[1] * operators.shape[2] * operators.shape[3]
    listed = operators.transpose(1, 2, 3, 0).reshape(table_rows_count, operators.shape[0])
    listed_mem = pltpu.VMEM(listed.shape, BF16)
    route = route.reshape(route.shape[:4])

    told = call(
        tell_kernel,
        far((peers, 16, 128), BF16),
        [FAR] * 3,
        FAR,
        [pltpu.SMEM(route.shape, jnp.int32)] * 3 + [pltpu.VMEM((16, 128), F32), meta_half, sems],
        SHORT,
    )(operator_index, route, target_brick)
    heard = swap_slots(told)
    send = call(
        target_kernel, far((peers, shared, 128), BF16), [FAR, FAR], FAR, [pltpu.VMEM(NATIVE, BF16), stage, sems]
    )(target_image, told)
    targets = swap_slots(send)

    moved, tables_zero = call(
        first_kernel,
        [far(FORM, BF16), far(TABLES, BF16)],
        [SCALAR, FAR, FAR, FAR],
        [FAR] * 2,
        [listed_mem, pltpu.VMEM(NATIVE, BF16)] + turning + [form, tables, sems],
    )(operator_index, listed, template, send)
    send, tables_far, codes = call(
        second_kernel,
        [far((peers, 512 + shared, 128), BF16), far(TABLES, BF16), far((peers, 128), jnp.int32)],
        [SCALAR, SCALAR, FAR, FAR, ANYWHERE],
        [FAR] * 3,
        [listed_mem, form, meta_half, pltpu.VMEM((peers, 16, 128), F32), pltpu.VMEM((peers, 128), jnp.int32)]
        + turning
        + [stage, tables, sems, pltpu.SemaphoreType.DMA((8,))],
    )(route, target_brick, listed, moved, heard)
    send = pl.pallas_call(
        pass_kernel,
        out_shape=far(send.shape, BF16),
        in_specs=[FAR, ANYWHERE],
        out_specs=FAR,
        input_output_aliases={0: 0},
        cost_estimate=pl.CostEstimate(flops=SHORT, bytes_accessed=1024, transcendentals=0),
    )(pinned(send, FAR), targets)
    arrived = swap_slots(send)

    rim = like((2 * RIM, 32, 256), BF16)
    low_x, high_x, low_y, high_y = call(
        edge_kernel,
        [rim] * 4,
        [FAR] * 3,
        [WHOLE] * 4,
        [pltpu.VMEM(NATIVE, BF16)] + [pltpu.VMEM((RIM, 32, 256), F32)] * 2 + [pltpu.VMEM(NATIVE, F32), sems],
    )(template, velocity, send)
    tables_one, plan = call(
        prepare_kernel,
        [far(TABLES, BF16), far((peers, 128), jnp.int32)],
        [SCALAR, FAR, WHOLE, WHOLE],
        [WHOLE, FAR],
        [routes_mem, routes_mem, sems],
    )(operator_index, codes, listed, low_x)
    b0x, a0x, b0y, a0y = neighbours(low_x, high_x, low_y, high_y)

    send = call(
        share_kernel,
        far((peers, 2 * shared, 128), BF16),
        [FAR, WHOLE, WHOLE],
        FAR,
        [routes_mem, pltpu.VMEM((peers, shared, 128), F32), pltpu.VMEM((peers, 2 * shared, 128), BF16)]
        + [sems, pltpu.SemaphoreType.DMA((peers,))],
        SHORT,
    )(plan, arrived, targets)
    pulled = swap_slots(send)

    divergence = call(
        divergence_kernel, like(NATIVE, F32), [WHOLE] * 5 + [FAR], WHOLE, [pltpu.VMEM((38, 32, 256), F32)]
    )(velocity, b0x, a0x, b0y, a0y, send)
    state, low_x, high_x, low_y, high_y = call(
        rims_kernel,
        [like(NATIVE, BF16)] + [rim] * 4,
        [FAR, ANYWHERE, WHOLE, FAR],
        [WHOLE] * 5,
        [routes_mem, pltpu.VMEM((peers, 512, 128), BF16), pltpu.VMEM(FORM, F32), form] + turning[1:] + [sems],
    )(codes, arrived, divergence, send)
    b1x, a1x, b1y, a1y = neighbours(low_x, high_x, low_y, high_y)
    composed = call(
        composed_kernel, far((peers, shared, 128), BF16), [FAR, FAR, WHOLE], FAR, [routes_mem, stage, stage, sems]
    )(plan, send, low_x)

    composed = swap_slots(composed)

    adjoint_one = call(
        adjoint_kernel, like(FORM, BF16), [FAR, NEAR], WHOLE, [tables] + turning + [sems]
    )(tables_one, pulled)
    gradient = call(
        gradient_kernel,
        far((3,) + NATIVE, F32),
        [WHOLE] * 13,
        WHOLE,
        turning[1:] + [pltpu.VMEM(NATIVE, F32)] * 2 + [pltpu.VMEM((38, 32, 256), F32)] * 3,
    )(template, state, divergence, pulled, adjoint_one, b0x, a0x, b0y, a0y, b1x, a1x, b1y, a1y)

    adjoint = call(
        final_kernel,
        far(NATIVE, BF16),
        [WHOLE, WHOLE, FAR, NEAR],
        FAR,
        turning + [form, pltpu.VMEM(NATIVE, BF16), quarter_sems],
        SHORT,
    )(tables_far, tables_zero, gradient, composed)
    return gradient, adjoint


def solution(mesh):
    placed = (
        P("gx", "gy", None),
        P("gx", "gy", None),
        P(None, "gx", "gy", None),
        P(),
        P(None, "gx", "gy", None, None),
        P(None, "gx", "gy", None),
        P(None, "gx", "gy", None),
    )
    return jax.shard_map(
        shards,
        mesh=mesh,
        in_specs=placed,
        out_specs=(P(None, "gx", "gy", None), P("gx", "gy", None)),
        check_vma=False,
    )
```

```python
import functools

import jax
import jax.numpy as jnp
from jax import lax
from jax.experimental import pallas as pl
from jax.experimental.pallas import tpu as pltpu
from jax.sharding import PartitionSpec as P

STEPS = 2
CAP = 2
RIM = 3
F32 = jnp.float32
BF16 = jnp.bfloat16
NT = (((1,), (1,)), ((), ()))
NN = (((1,), (0,)), ((), ()))
TAPS = ((1, 0.75), (2, -0.15), (3, 1.0 / 60.0))


def iota(shape, dim):
    return lax.broadcasted_iota(jnp.int32, shape, dim)


def mm(left, right, dims=NN):
    return lax.dot_general(left, right, dims, preferred_element_type=F32)


def halves(value):
    high = value.astype(BF16)
    return high, (value - high.astype(F32)).astype(BF16)


def on_lanes(picks):
    lane = iota((1, 256), 1)
    chosen = jnp.zeros(lane.shape, jnp.int32)
    for b, pick in enumerate(picks):
        chosen = jnp.where(lane // 32 == b, pick, chosen)
    return chosen


def table_rows(operators, chosen, axis):
    shape = (operators.shape[1], 256)
    one_hot = (iota(shape, 0) == jnp.broadcast_to(chosen, shape)).astype(F32).astype(BF16)
    found = mm(operators[axis * 1024 : axis * 1024 + 1024, :], one_hot)
    within = iota((32, 256), 1) % 32
    total = jnp.zeros((32, 256), F32)
    for x in range(32):
        total = jnp.where(within == x, found[x * 32 : x * 32 + 32], total)
    return total


def same_block(size, edge):
    return iota((size, size), 0) // edge == iota((size, size), 1) // edge


def identity():
    return (iota((256, 256), 0) == iota((256, 256), 1)).astype(F32).astype(BF16)


def flipped_diagonal(table):
    return jnp.where(same_block(256, 32), jnp.concatenate([table] * 8, axis=0), 0.0).astype(BF16)


def diagonal(table):
    return mm(identity(), flipped_diagonal(table), NT).astype(BF16)


def spread(table):
    copies = (iota((256, 256), 0) % 32 == iota((256, 256), 1) % 32).astype(F32).astype(BF16)
    return mm(flipped_diagonal(table), copies)


def swap_chunks(parts):
    lane = iota(parts[0].shape, 1)
    for bit, shift in ((1, 32), (2, 64)):
        keep = (lane & shift) == 0
        fresh = list(parts)
        for index in range(4):
            if index & bit:
                continue
            one, two = parts[index], parts[index | bit]
            fresh[index] = jnp.where(keep, one, pltpu.roll(two, shift, 1))
            fresh[index | bit] = jnp.where(keep, pltpu.roll(one, 128 - shift, 1), two)
        parts = fresh
    return parts


def swap_brick(block, folded, turned, brick, parts=2):
    slabs = []
    for ph in range(4):
        slabs.append(
            jnp.concatenate(
                [
                    block[(qs // 2) * 32 + ph * 8 : (qs // 2) * 32 + ph * 8 + 8, (qs % 2) * 128 : (qs % 2) * 128 + 128]
                    for qs in range(8)
                ],
                axis=0,
            )
        )
    slabs = swap_chunks(slabs)
    for qh in range(4):
        folded[brick * 4 + qh] = slabs[qh]
    for ps in range(8):
        value = jnp.concatenate(
            [folded[brick * 4 + qh, pl.ds(ps, 8, stride=8), :] for qh in range(4)], axis=0
        )
        for part, half in enumerate(halves(value)[:parts]):
            turned[part * 256 + brick * 32 : part * 256 + brick * 32 + 32, ps * 128 : ps * 128 + 128] = half


def lane_pair(field, g):
    return jnp.concatenate(
        [
            jnp.concatenate([field[b, qs * 32 : qs * 32 + 32, :] for b in range(8)], axis=0)
            for qs in (2 * g, 2 * g + 1)
        ],
        axis=1,
    )


def put_pair(field, g, value):
    for b in range(8):
        for half in range(2):
            rows = slice((2 * g + half) * 32, (2 * g + half) * 32 + 32)
            field[b, rows, :] = value[b * 32 : b * 32 + 32, half * 128 : half * 128 + 128]


def middle_and_last(start, spread_mid, last, folded, turned, flipped):
    mask = same_block(256, 32)
    for brick in range(8):
        rows = spread_mid[brick * 32 : brick * 32 + 32]
        line = jnp.where(mask, jnp.concatenate([rows] * 8, axis=0), 0.0).astype(BF16)
        block = start[brick * 32 : brick * 32 + 32, :]
        block = jnp.concatenate([block[:, g * 256 : g * 256 + 256] for g in range(4)], axis=0)
        high, low = halves(block)
        both = mm(jnp.concatenate([high, low], axis=0), line, NT if flipped else NN)
        swap_brick(both[:128] + both[128:], folded, turned, brick)
    last = jnp.concatenate([last, last], axis=1)
    for g in range(4):
        yield g, mm(last, turned[:, g * 256 : g * 256 + 256]).astype(BF16)


def slot_numbers(route, step):
    own = [route[step, 0, 0, b] for b in range(8)]
    slots = []
    for b in range(8):
        rank = jnp.int32(0)
        for other in range(b):
            rank = rank + (own[other] == own[b]).astype(jnp.int32)
        slots.append((own[b], rank))
    return slots


def fetch(source, target, sem):
    copy = pltpu.make_async_copy(source, target, sem)
    copy.start()
    return copy


def put_pieces(stage, g, value, rows):
    parts = 32 // rows
    for half in range(2):
        tile = value[:, half * 128 : half * 128 + 128]
        for part in range(parts):
            share = (2 * g + half) * parts + part
            if parts == 1:
                stage[share] = tile
            else:
                for b in range(8):
                    at = b * 32 + part * rows
                    stage[share, b * rows : b * rows + rows, :] = tile[at : at + rows]


def pieces_pair(pieces, kind, g, rows):
    parts = 32 // rows
    base = kind * 8 * rows
    tiles = []
    for tile in (2 * g, 2 * g + 1):
        if parts == 1:
            tiles.append(pieces[tile, base : base + 256, :])
        else:
            tiles.append(
                jnp.concatenate(
                    [
                        pieces[tile * parts + part, base + b * rows : base + b * rows + rows, :]
                        for b in range(8)
                        for part in range(parts)
                    ],
                    axis=0,
                )
            )
    return jnp.concatenate(tiles, axis=1)


def target_kernel(picks_in, route_in, brick_in, target, send, *refs):
    picks, route, landing, field, stage, meta, meta_half, sems = refs
    told = [
        fetch(source, place, sems.at[index])
        for index, (source, place) in enumerate(((picks_in, picks), (route_in, route), (brick_in, landing)))
    ]
    load = fetch(target, field, sems.at[3])
    for copy in told:
        copy.wait()
    lane = iota((1, 128), 1)
    meta[...] = jnp.zeros(meta.shape, F32)
    value = jnp.zeros((1, 128), jnp.int32)
    for b in range(8):
        for step in range(STEPS):
            code = route[step, 0, 0, b] * 8 + landing[step, 0, 0, b]
            value = jnp.where(lane == 2 * b + step, code, value)
        meta[8 + b : 9 + b, :] = jnp.full((1, 128), picks[1, 0, 0, b], jnp.int32).astype(F32)
    meta[0:1, :] = value.astype(F32)
    meta_half[...] = jnp.broadcast_to(meta[...].astype(BF16)[None], meta_half.shape)
    shared = stage.shape[1]
    sent = [fetch(meta_half, send.at[:, shared : shared + 16, :], sems.at[4])]
    load.wait()
    for g in range(4):
        block = jnp.concatenate(
            [field[qh * 8 + qs] for qs in (2 * g, 2 * g + 1) for qh in range(4)], axis=0
        )
        put_pieces(stage, g, mm(identity(), block, NT).astype(BF16), shared // 8)
    for copy in sent + [fetch(stage, send.at[:, 0:shared, :], sems.at[5])]:
        copy.wait()


def first_kernel(picks, operators, field, sent, moved_out, tables, table_mem, field_mem, start, folded, turned, out, tables_mem, sems):
    loads = [fetch(operators, table_mem, sems.at[0]), fetch(field, field_mem, sems.at[1])]
    chosen = on_lanes([picks[0, 0, 0, b] for b in range(8)])
    loads[0].wait()
    found = [table_rows(table_mem, chosen, axis) for axis in range(3)]
    for axis in range(3):
        tables_mem[axis] = found[axis].astype(BF16)
    kept = fetch(tables_mem, tables, sems.at[0])
    begin = diagonal(found[2])
    loads[1].wait()
    for g in range(4):
        block = jnp.concatenate(
            [field_mem[qh * 8 + qs] for qs in (2 * g, 2 * g + 1) for qh in range(4)], axis=0
        )
        start[:, g * 256 : g * 256 + 256] = mm(begin, block, NT)
    for g, moved in middle_and_last(start, spread(found[1]), diagonal(found[0]), folded, turned, False):
        put_pair(out, g, moved)
    for copy in [kept, fetch(out, moved_out, sems.at[1])]:
        copy.wait()


def second_kernel(route, landing, operators, moved, arrived, *refs):
    send, tables, codes_out, table_mem, moved_mem, meta_half, meta, codes, start, folded, turned, stage, tables_mem, sems, slot_sems = refs
    shared = stage.shape[1]
    heard = fetch(arrived.at[:, shared : shared + 16, :], meta_half, sems.at[0])
    loads = [fetch(operators, table_mem, sems.at[1]), fetch(moved, moved_mem, sems.at[2])]
    heard.wait()
    meta[...] = meta_half[...].astype(F32)
    for source in range(meta.shape[0]):
        codes[source : source + 1, :] = meta[source, 0:1, :].astype(jnp.int32)
    told = fetch(codes, codes_out, sems.at[3])
    lane = iota((1, 128), 1) // 32
    chosen = []
    for part in range(2):
        row = jnp.zeros((1, 128), F32)
        for b in range(4):
            own = part * 4 + b
            found = meta[route[0, 0, 0, own], pl.ds(8 + landing[0, 0, 0, own], 1), :]
            row = jnp.where(lane == b, found, row)
        chosen.append(row)
    chosen = jnp.concatenate(chosen, axis=1).astype(jnp.int32)
    loads[1].wait()
    sent = []
    for b, (place, rank) in enumerate(slot_numbers(route, 0)):
        rows = pl.ds(pl.multiple_of(rank * 256, 256), 256)
        sent.append(fetch(moved_mem.at[b], send.at[place, rows, :], slot_sems.at[b]))
    loads[0].wait()
    found = [table_rows(table_mem, chosen, axis) for axis in range(3)]
    for axis in range(3):
        tables_mem[axis] = found[axis].astype(BF16)
    kept = fetch(tables_mem, tables, sems.at[5])
    begin = diagonal(found[0])
    for g in range(4):
        start[:, g * 256 : g * 256 + 256] = mm(begin, lane_pair(moved_mem, g))
    for g, value in middle_and_last(start, spread(found[1]), diagonal(found[2]), folded, turned, False):
        put_pieces(stage, g, value, shared // 8)
    sent.append(fetch(stage, send.at[:, 512 : 512 + shared, :], sems.at[6]))
    for copy in sent + [kept, told]:
        copy.wait()


def share_kernel(plan_in, arrived, targets, send, plan, total, stage, sems, chunk_sems):
    peers, shared = total.shape[0], total.shape[1]
    rows = shared // 8
    load = fetch(plan_in, plan, sems.at[0])
    total[...] = jnp.zeros(total.shape, F32)
    load.wait()

    def add(source, carry):
        for b in range(8):
            final = plan[source, 8 + b]
            place = pl.ds(pl.multiple_of((final & 7) * rows, rows), rows)
            at = 512 + b * rows
            total[final >> 3, place, :] += arrived[source, at : at + rows, :].astype(F32)
        return carry

    lax.fori_loop(0, peers, add, 0)
    for source in range(peers):
        final = total[source].astype(BF16).astype(F32)
        stage[source, 0:shared, :] = (final - targets[source, 0:shared, :].astype(F32)).astype(BF16)
    sent = []
    for source in range(peers):
        for b in range(8):
            code = plan[source, b]
            place = pl.ds(pl.multiple_of((code & 7) * rows, rows), rows)
            stage[source, shared + b * rows : shared + b * rows + rows, :] = stage[code >> 3, place, :]
        sent.append(fetch(stage.at[source], send.at[source], chunk_sems.at[source]))
    for copy in sent:
        copy.wait()


def composed_kernel(plan_in, shares, edge, send, plan, own, stage, sems):
    peers, shared = own.shape[0], own.shape[1]
    rows = shared // 8
    loads = [fetch(plan_in, plan, sems.at[0]), fetch(shares.at[:, 0:shared, :], own, sems.at[1])]
    for load in loads:
        load.wait()

    def give(source, carry):
        for b in range(8):
            code = plan[source, 8 + b]
            place = pl.ds(pl.multiple_of((code & 7) * rows, rows), rows)
            stage[source, b * rows : b * rows + rows, :] = own[code >> 3, place, :]
        return carry

    lax.fori_loop(0, peers, give, 0)
    fetch(stage, send, sems.at[0]).wait()


def adjoint_kernel(tables_in, arrived, *refs):
    adjoint, tables, start, folded, turned, sems = refs
    load = fetch(tables_in, tables, sems.at[0])
    rows = arrived.shape[1] // 16
    load.wait()
    begin = flipped_diagonal(tables[2].astype(F32))
    mid = spread(tables[1].astype(F32))
    end = flipped_diagonal(tables[0].astype(F32))
    for g in range(4):
        start[:, g * 256 : g * 256 + 256] = mm(begin, pieces_pair(arrived, 1, g, rows))
    for g, moved in middle_and_last(start, mid, end, folded, turned, True):
        put_pair(adjoint, g, moved)


def final_kernel(tables_far, tables_zero, gradient, arrived, *refs):
    adjoint, start, folded, turned, later, field, quarter_sems = refs
    rows = arrived.shape[1] // 8
    begin = flipped_diagonal(tables_far[2].astype(F32))
    mid = spread(tables_far[1].astype(F32))
    end = flipped_diagonal(tables_far[0].astype(F32))
    for g in range(4):
        start[:, g * 256 : g * 256 + 256] = mm(begin, pieces_pair(arrived, 0, g, rows))
    for g, moved in middle_and_last(start, mid, end, folded, turned, True):
        put_pair(later, g, moved)
    begin = flipped_diagonal(tables_zero[0].astype(F32))
    mid = spread(tables_zero[1].astype(F32))
    end = flipped_diagonal(tables_zero[2].astype(F32))
    for g in range(4):
        start[:, g * 256 : g * 256 + 256] = mm(begin, lane_pair(later, g))
    stored = []
    for g, moved in middle_and_last(start, mid, end, folded, turned, True):
        to_native(moved, g, field)
        for qh in range(4):
            at = slice(qh * 8 + 2 * g, qh * 8 + 2 * g + 2)
            stored.append(fetch(field.at[at], adjoint.at[at], quarter_sems.at[g, qh]))
    for copy in stored:
        copy.wait()


def to_native(block, g, field):
    flat = mm(identity(), block, NT).astype(field.dtype)
    for index in range(8):
        x = (index % 4) * 8 + 2 * g + index // 4
        field[x] = flat[index * 32 : index * 32 + 32]


def x_form_to_native(source, folded, turned, field):
    for b in range(8):
        block = source[b].astype(F32)
        block = jnp.concatenate(
            [
                jnp.concatenate([block[g * 64 : g * 64 + 32], block[g * 64 + 32 : g * 64 + 64]], axis=1)
                for g in range(4)
            ],
            axis=0,
        )
        swap_brick(block, folded, turned, b, 1)
    for g in range(4):
        to_native(turned[0:256, g * 256 : g * 256 + 256], g, field)


def tap(offset):
    value = jnp.zeros(offset.shape, F32)
    for step, weight in TAPS:
        value = jnp.where(offset == step, weight, value)
        value = jnp.where(offset == -step, -weight, value)
    return value


def stencils():
    size = 256
    row, col = iota((size, size), 0), iota((size, size), 1)
    along_y = halves(jnp.where(row // 32 == col // 32, tap(col - row), 0.0))
    along_z = halves(tap(row - col))
    row, col = iota((size, 48), 0), iota((size, 48), 1)
    layer = col // 8
    place = jnp.where(layer < RIM, layer - RIM, layer - RIM + 32)
    rim_y = halves(jnp.where(row // 32 == col % 8, tap(place - row % 32), 0.0))
    return along_y, rim_y, along_z


def rim_picker():
    row, col = iota((48, 256), 0), iota((48, 256), 1)
    layer = row // 8
    place = jnp.where(layer < RIM, layer, layer - RIM + 29)
    return ((row % 8 == col // 32) & (place == col % 32)).astype(F32).astype(BF16)


def difference_x(padded, g):
    total = None
    for step, weight in TAPS:
        ahead = padded[pl.ds(8 * g + RIM + step, 8)]
        behind = padded[pl.ds(8 * g + RIM - step, 8)]
        term = weight * (ahead - behind)
        total = term if total is None else total + term
    return total.reshape(256, 256)


def difference_y(parts, rims, along_y, rim_y):
    total = mm(along_y[0], parts[0]) + mm(along_y[1], parts[0])
    if len(parts) > 1:
        total = total + mm(along_y[0], parts[1])
    return total + mm(rim_y[0], rims) + mm(rim_y[1], rims)


def difference_z(parts, along_z):
    total = mm(parts[0], along_z[0]) + mm(parts[0], along_z[1])
    if len(parts) > 1:
        total = total + mm(parts[1], along_z[0])
    return total


def rim_rows(before, after, base, g):
    rows = [before[base + h, (g // 2) * 16 : (g // 2) * 16 + 16, :].astype(F32) for h in range(RIM)]
    rows += [after[base + h, (g // 2) * 16 : (g // 2) * 16 + 16, :].astype(F32) for h in range(RIM)]
    half = (g % 2) * 8
    return jnp.concatenate([value[half : half + 8] for value in rows], axis=0).astype(BF16)


def put_rims(blocks, base, low_y, high_y):
    picker = rim_picker()
    for pair in range(2):
        left, right = mm(picker, blocks[2 * pair]), mm(picker, blocks[2 * pair + 1])
        for layer in range(2 * RIM):
            value = jnp.concatenate(
                [left[layer * 8 : layer * 8 + 8], right[layer * 8 : layer * 8 + 8]], axis=0
            ).astype(BF16)
            target = low_y if layer < RIM else high_y
            target[base + layer % RIM, pair * 16 : pair * 16 + 16, :] = value


def edge_kernel(template, velocity, sent, low_x, high_x, low_y, high_y, field, first_x, last_x, mid_v, sems):
    loads = [
        fetch(template, field, sems.at[0]),
        fetch(velocity.at[0, 0:RIM], first_x, sems.at[1]),
        fetch(velocity.at[0, 29:32], last_x, sems.at[2]),
        fetch(velocity.at[1], mid_v, sems.at[3]),
    ]
    for load in loads:
        load.wait()
    low_x[0:RIM] = field[0:RIM]
    high_x[0:RIM] = field[29:32]
    low_x[RIM : 2 * RIM] = first_x[...].astype(BF16)
    high_x[RIM : 2 * RIM] = last_x[...].astype(BF16)
    put_rims([field[8 * g : 8 * g + 8].reshape(256, 256) for g in range(4)], 0, low_y, high_y)
    put_rims([mid_v[8 * g : 8 * g + 8].astype(BF16).reshape(256, 256) for g in range(4)], RIM, low_y, high_y)


def prepare_kernel(picks, codes_in, operators, edge, tables, plan_out, codes, plan, sems):
    load = fetch(codes_in, codes, sems.at[0])
    chosen = on_lanes([picks[1, 0, 0, b] for b in range(8)])
    for axis in range(3):
        tables[axis] = table_rows(operators, chosen, axis).astype(BF16)
    load.wait()

    def row(source, carry):
        for b in range(8):
            first = codes[source, 2 * b]
            plan[source, b] = codes[source, 2 * b + 1]
            plan[source, 8 + b] = codes[first >> 3, 2 * (first & 7) + 1]
        return carry

    lax.fori_loop(0, codes.shape[0], row, 0)
    fetch(plan, plan_out, sems.at[0]).wait()


def divergence_kernel(velocity, before_x, after_x, before_y, after_y, sent, divergence, padded):
    along_y, rim_y, along_z = stencils()
    padded[0:RIM] = before_x[RIM : 2 * RIM].astype(F32)
    padded[RIM : RIM + 32] = velocity[0]
    padded[RIM + 32 : 2 * RIM + 32] = after_x[RIM : 2 * RIM].astype(F32)
    for g in range(4):
        along_one = halves(velocity[1, 8 * g : 8 * g + 8].reshape(256, 256))
        along_two = halves(velocity[2, 8 * g : 8 * g + 8].reshape(256, 256))
        total = (
            difference_x(padded, g)
            + difference_y(along_one, rim_rows(before_y, after_y, RIM, g), along_y, rim_y)
            + difference_z(along_two, along_z)
        )
        divergence[8 * g : 8 * g + 8] = total.reshape(8, 32, 256)


def rims_kernel(codes_in, arrived, divergence, sent, native, low_x, high_x, low_y, high_y, codes, slots, total, state, folded, turned, sems):
    loads = [fetch(codes_in, codes, sems.at[0]), fetch(arrived.at[:, 0:512, :], slots, sems.at[1])]
    total[...] = jnp.zeros(total.shape, F32)
    for load in loads:
        load.wait()
    me = lax.axis_index("gx")

    def add(source, carry):
        rank = jnp.int32(0)
        for b in range(8):
            code = codes[source, 2 * b]
            hit = (code >> 3) == me

            @pl.when(hit)
            def _():
                place = pl.ds(pl.multiple_of(rank * 256, 256), 256)
                total[code & 7] += slots[source, place, :].astype(F32)

            rank = rank + hit.astype(jnp.int32)
        return carry

    lax.fori_loop(0, slots.shape[0], add, 0)
    for b in range(8):
        state[b] = total[b].astype(BF16)
    x_form_to_native(state, folded, turned, native)
    low_x[0:RIM] = native[0:RIM]
    high_x[0:RIM] = native[29:32]
    low_x[RIM : 2 * RIM] = divergence[0:RIM].astype(BF16)
    high_x[RIM : 2 * RIM] = divergence[29:32].astype(BF16)
    put_rims([native[8 * g : 8 * g + 8].reshape(256, 256) for g in range(4)], 0, low_y, high_y)
    put_rims(
        [divergence[8 * g : 8 * g + 8].astype(BF16).reshape(256, 256) for g in range(4)], RIM, low_y, high_y
    )


def gradient_kernel(
    template,
    state,
    divergence,
    adjoint_two,
    adjoint_one,
    b0x,
    a0x,
    b0y,
    a0y,
    b1x,
    a1x,
    b1y,
    a1y,
    gradient,
    folded,
    turned,
    weight_two,
    weight_one,
    pad_zero,
    pad_one,
    pad_div,
):
    x_form_to_native(adjoint_one, folded, turned, weight_one)
    for g in range(4):
        to_native(pieces_pair(adjoint_two, 0, g, adjoint_two.shape[1] // 16), g, weight_two)
    along_y, rim_y, along_z = stencils()
    for padded, before, middle, after, base in (
        (pad_zero, b0x, template, a0x, 0),
        (pad_one, b1x, state, a1x, 0),
        (pad_div, b1x, divergence, a1x, RIM),
    ):
        padded[0:RIM] = before[base : base + RIM].astype(F32)
        padded[RIM : RIM + 32] = middle[...].astype(F32)
        padded[RIM + 32 : 2 * RIM + 32] = after[base : base + RIM].astype(F32)
    for g in range(4):
        zero = (template[8 * g : 8 * g + 8].reshape(256, 256),)
        one = (state[8 * g : 8 * g + 8].reshape(256, 256),)
        div = halves(divergence[8 * g : 8 * g + 8].reshape(256, 256))
        weigh_one = 0.5 * weight_one[8 * g : 8 * g + 8].reshape(256, 256)
        weigh_two = 0.5 * weight_two[8 * g : 8 * g + 8].reshape(256, 256)
        for axis in range(3):
            if axis == 0:
                parts = [difference_x(padded, g) for padded in (pad_zero, pad_one, pad_div)]
            elif axis == 1:
                parts = [
                    difference_y(zero, rim_rows(b0y, a0y, 0, g), along_y, rim_y),
                    difference_y(one, rim_rows(b1y, a1y, 0, g), along_y, rim_y),
                    difference_y(div, rim_rows(b1y, a1y, RIM, g), along_y, rim_y),
                ]
            else:
                parts = [difference_z(value, along_z) for value in (zero, one, div)]
            value = weigh_one * parts[0] + weigh_two * parts[1] - 0.25 * parts[2]
            gradient[axis, 8 * g : 8 * g + 8] = value.reshape(8, 32, 256)


SCALAR = pl.BlockSpec(memory_space=pltpu.SMEM)
WHOLE = pl.BlockSpec(memory_space=pltpu.VMEM)
NEAR = pl.BlockSpec(memory_space=pltpu.VMEM)
ANYWHERE = pl.BlockSpec(memory_space=pl.ANY)
FAR = pl.BlockSpec(memory_space=pltpu.HBM)
FOLDED = (32, 64, 128)
FLAT = (256, 1024)
NATIVE = (32, 32, 256)
FORM = (8, 256, 128)
TABLES = (3, 32, 256)


def pinned(value, spec):
    if spec is FAR:
        return pltpu.with_memory_space_constraint(value, pltpu.HBM)
    if spec is NEAR:
        return pltpu.with_memory_space_constraint(value, pltpu.VMEM)
    return value


SHORT, LONG = 1 << 20, 1 << 36


def call(kernel, out, in_specs, out_specs, scratch, work=LONG):
    made = pl.pallas_call(
        kernel,
        out_shape=out,
        in_specs=in_specs,
        out_specs=out_specs,
        scratch_shapes=scratch,
        compiler_params=pltpu.CompilerParams(vmem_limit_bytes=24 * 1024 * 1024),
        cost_estimate=pl.CostEstimate(flops=work, bytes_accessed=1024 * 1024, transcendentals=0),
    )

    def apply(*values):
        return made(*[pinned(value, spec) for value, spec in zip(values, in_specs, strict=True)])

    return apply


def like(shape, dtype):
    return jax.ShapeDtypeStruct(shape, dtype)


def far(shape, dtype):
    return pltpu.HBM(shape, dtype)


def neighbours(low_x, high_x, low_y, high_y):
    moved = []
    for low, high, axis in ((low_x, high_x, "gx"), (low_y, high_y, "gy")):
        size = lax.axis_size(axis)
        up = [(i, i + 1) for i in range(size - 1)]
        down = [(i + 1, i) for i in range(size - 1)]
        moved += [lax.ppermute(high, axis, up), lax.ppermute(low, axis, down)]
    return moved


def swap_slots(send):
    return lax.all_to_all(send, "gx", split_axis=0, concat_axis=0, tiled=True)


def shards(template, target_image, velocity, operators, route, target_brick, operator_index):
    peers = lax.axis_size("gx")
    shared = 8 * (256 // peers)
    sems = pltpu.SemaphoreType.DMA((16,))
    quarter_sems = pltpu.SemaphoreType.DMA((4, 4))
    turning = [pltpu.VMEM(FLAT, F32), pltpu.VMEM(FOLDED, F32), pltpu.VMEM((512, 1024), BF16)]
    form = pltpu.VMEM(FORM, BF16)
    tables = pltpu.VMEM(TABLES, BF16)
    routes_mem = pltpu.SMEM((peers, 128), jnp.int32)
    stage = pltpu.VMEM((peers, shared, 128), BF16)
    meta_half = pltpu.VMEM((peers, 16, 128), BF16)
    table_rows_count = operators.shape[1] * operators.shape[2] * operators.shape[3]
    listed = operators.transpose(1, 2, 3, 0).reshape(table_rows_count, operators.shape[0])
    listed_mem = pltpu.VMEM(listed.shape, BF16)
    route = route.reshape(route.shape[:4])

    send = call(
        target_kernel,
        far((peers, shared + 16, 128), BF16),
        [FAR] * 4,
        FAR,
        [pltpu.SMEM(route.shape, jnp.int32)] * 3
        + [pltpu.VMEM(NATIVE, BF16), stage, pltpu.VMEM((16, 128), F32), meta_half, sems],
        SHORT,
    )(operator_index, route, target_brick, target_image)
    targets = swap_slots(send)

    moved, tables_zero = call(
        first_kernel,
        [far(FORM, BF16), far(TABLES, BF16)],
        [SCALAR, FAR, FAR, FAR],
        [FAR] * 2,
        [listed_mem, pltpu.VMEM(NATIVE, BF16)] + turning + [form, tables, sems],
    )(operator_index, listed, template, send)
    send, tables_far, codes = call(
        second_kernel,
        [far((peers, 512 + shared, 128), BF16), far(TABLES, BF16), far((peers, 128), jnp.int32)],
        [SCALAR, SCALAR, FAR, FAR, ANYWHERE],
        [FAR] * 3,
        [listed_mem, form, meta_half, pltpu.VMEM((peers, 16, 128), F32), pltpu.VMEM((peers, 128), jnp.int32)]
        + turning
        + [stage, tables, sems, pltpu.SemaphoreType.DMA((8,))],
        SHORT,
    )(route, target_brick, listed, moved, targets)
    arrived = swap_slots(send)

    rim = like((2 * RIM, 32, 256), BF16)
    low_x, high_x, low_y, high_y = call(
        edge_kernel,
        [rim] * 4,
        [FAR] * 3,
        [WHOLE] * 4,
        [pltpu.VMEM(NATIVE, BF16)] + [pltpu.VMEM((RIM, 32, 256), F32)] * 2 + [pltpu.VMEM(NATIVE, F32), sems],
    )(template, velocity, send)
    tables_one, plan = call(
        prepare_kernel,
        [far(TABLES, BF16), far((peers, 128), jnp.int32)],
        [SCALAR, FAR, WHOLE, WHOLE],
        [WHOLE, FAR],
        [routes_mem, routes_mem, sems],
    )(operator_index, codes, listed, low_x)
    b0x, a0x, b0y, a0y = neighbours(low_x, high_x, low_y, high_y)

    send = call(
        share_kernel,
        far((peers, 2 * shared, 128), BF16),
        [FAR, WHOLE, WHOLE],
        FAR,
        [routes_mem, pltpu.VMEM((peers, shared, 128), F32), pltpu.VMEM((peers, 2 * shared, 128), BF16)]
        + [sems, pltpu.SemaphoreType.DMA((peers,))],
        SHORT,
    )(plan, arrived, targets)
    pulled = swap_slots(send)

    divergence = call(
        divergence_kernel, like(NATIVE, F32), [WHOLE] * 5 + [FAR], WHOLE, [pltpu.VMEM((38, 32, 256), F32)]
    )(velocity, b0x, a0x, b0y, a0y, send)
    state, low_x, high_x, low_y, high_y = call(
        rims_kernel,
        [like(NATIVE, BF16)] + [rim] * 4,
        [FAR, ANYWHERE, WHOLE, FAR],
        [WHOLE] * 5,
        [routes_mem, pltpu.VMEM((peers, 512, 128), BF16), pltpu.VMEM(FORM, F32), form] + turning[1:] + [sems],
    )(codes, arrived, divergence, send)
    b1x, a1x, b1y, a1y = neighbours(low_x, high_x, low_y, high_y)
    composed = call(
        composed_kernel, far((peers, shared, 128), BF16), [FAR, FAR, WHOLE], FAR, [routes_mem, stage, stage, sems]
    )(plan, send, low_x)

    composed = swap_slots(composed)

    adjoint_one = call(
        adjoint_kernel, like(FORM, BF16), [FAR, NEAR], WHOLE, [tables] + turning + [sems]
    )(tables_one, pulled)
    gradient = call(
        gradient_kernel,
        far((3,) + NATIVE, F32),
        [WHOLE] * 13,
        WHOLE,
        turning[1:] + [pltpu.VMEM(NATIVE, F32)] * 2 + [pltpu.VMEM((38, 32, 256), F32)] * 3,
    )(template, state, divergence, pulled, adjoint_one, b0x, a0x, b0y, a0y, b1x, a1x, b1y, a1y)

    adjoint = call(
        final_kernel,
        far(NATIVE, BF16),
        [WHOLE, WHOLE, FAR, NEAR],
        FAR,
        turning + [form, pltpu.VMEM(NATIVE, BF16), quarter_sems],
        SHORT,
    )(tables_far, tables_zero, gradient, composed)
    return gradient, adjoint


def solution(mesh):
    placed = (
        P("gx", "gy", None),
        P("gx", "gy", None),
        P(None, "gx", "gy", None),
        P(),
        P(None, "gx", "gy", None, None),
        P(None, "gx", "gy", None),
        P(None, "gx", "gy", None),
    )
    return jax.shard_map(
        shards,
        mesh=mesh,
        in_specs=placed,
        out_specs=(P(None, "gx", "gy", None), P("gx", "gy", None)),
        check_vma=False,
    )
```

```python
import functools

import jax
import jax.numpy as jnp
from jax import lax
from jax.experimental import pallas as pl
from jax.experimental.pallas import tpu as pltpu
from jax.sharding import PartitionSpec as P

STEPS = 2
CAP = 2
RIM = 3
F32 = jnp.float32
BF16 = jnp.bfloat16
NT = (((1,), (1,)), ((), ()))
NN = (((1,), (0,)), ((), ()))
TAPS = ((1, 0.75), (2, -0.15), (3, 1.0 / 60.0))


def iota(shape, dim):
    return lax.broadcasted_iota(jnp.int32, shape, dim)


def mm(left, right, dims=NN):
    return lax.dot_general(left, right, dims, preferred_element_type=F32)


def halves(value):
    high = value.astype(BF16)
    return high, (value - high.astype(F32)).astype(BF16)


def on_lanes(picks):
    lane = iota((1, 256), 1)
    chosen = jnp.zeros(lane.shape, jnp.int32)
    for b, pick in enumerate(picks):
        chosen = jnp.where(lane // 32 == b, pick, chosen)
    return chosen


def table_rows(operators, chosen, axis):
    shape = (operators.shape[1], 256)
    one_hot = (iota(shape, 0) == jnp.broadcast_to(chosen, shape)).astype(F32).astype(BF16)
    found = mm(operators[axis * 1024 : axis * 1024 + 1024, :], one_hot)
    within = iota((32, 256), 1) % 32
    total = jnp.zeros((32, 256), F32)
    for x in range(32):
        total = jnp.where(within == x, found[x * 32 : x * 32 + 32], total)
    return total


def same_block(size, edge):
    return iota((size, size), 0) // edge == iota((size, size), 1) // edge


def identity():
    return (iota((256, 256), 0) == iota((256, 256), 1)).astype(F32).astype(BF16)


def flipped_diagonal(table):
    return jnp.where(same_block(256, 32), jnp.concatenate([table] * 8, axis=0), 0.0).astype(BF16)


def diagonal(table):
    return mm(identity(), flipped_diagonal(table), NT).astype(BF16)


def spread(table):
    copies = (iota((256, 256), 0) % 32 == iota((256, 256), 1) % 32).astype(F32).astype(BF16)
    return mm(flipped_diagonal(table), copies)


def swap_chunks(parts):
    lane = iota(parts[0].shape, 1)
    for bit, shift in ((1, 32), (2, 64)):
        keep = (lane & shift) == 0
        fresh = list(parts)
        for index in range(4):
            if index & bit:
                continue
            one, two = parts[index], parts[index | bit]
            fresh[index] = jnp.where(keep, one, pltpu.roll(two, shift, 1))
            fresh[index | bit] = jnp.where(keep, pltpu.roll(one, 128 - shift, 1), two)
        parts = fresh
    return parts


def swap_brick(block, folded, turned, brick, parts=2):
    slabs = []
    for ph in range(4):
        slabs.append(
            jnp.concatenate(
                [
                    block[(qs // 2) * 32 + ph * 8 : (qs // 2) * 32 + ph * 8 + 8, (qs % 2) * 128 : (qs % 2) * 128 + 128]
                    for qs in range(8)
                ],
                axis=0,
            )
        )
    slabs = swap_chunks(slabs)
    for qh in range(4):
        folded[brick * 4 + qh] = slabs[qh]
    for ps in range(8):
        value = jnp.concatenate(
            [folded[brick * 4 + qh, pl.ds(ps, 8, stride=8), :] for qh in range(4)], axis=0
        )
        for part, half in enumerate(halves(value)[:parts]):
            turned[part * 256 + brick * 32 : part * 256 + brick * 32 + 32, ps * 128 : ps * 128 + 128] = half


def lane_pair(field, g):
    return jnp.concatenate(
        [
            jnp.concatenate([field[b, qs * 32 : qs * 32 + 32, :] for b in range(8)], axis=0)
            for qs in (2 * g, 2 * g + 1)
        ],
        axis=1,
    )


def put_pair(field, g, value):
    for b in range(8):
        for half in range(2):
            rows = slice((2 * g + half) * 32, (2 * g + half) * 32 + 32)
            field[b, rows, :] = value[b * 32 : b * 32 + 32, half * 128 : half * 128 + 128]


def middle_and_last(start, spread_mid, last, folded, turned, flipped):
    mask = same_block(256, 32)
    for brick in range(8):
        rows = spread_mid[brick * 32 : brick * 32 + 32]
        line = jnp.where(mask, jnp.concatenate([rows] * 8, axis=0), 0.0).astype(BF16)
        block = start[brick * 32 : brick * 32 + 32, :]
        block = jnp.concatenate([block[:, g * 256 : g * 256 + 256] for g in range(4)], axis=0)
        high, low = halves(block)
        both = mm(jnp.concatenate([high, low], axis=0), line, NT if flipped else NN)
        swap_brick(both[:128] + both[128:], folded, turned, brick)
    last = jnp.concatenate([last, last], axis=1)
    for g in range(4):
        yield g, mm(last, turned[:, g * 256 : g * 256 + 256]).astype(BF16)


def slot_numbers(route, step):
    own = [route[step, 0, 0, b] for b in range(8)]
    slots = []
    for b in range(8):
        rank = jnp.int32(0)
        for other in range(b):
            rank = rank + (own[other] == own[b]).astype(jnp.int32)
        slots.append((own[b], rank))
    return slots


def fetch(source, target, sem):
    copy = pltpu.make_async_copy(source, target, sem)
    copy.start()
    return copy


def put_pieces(stage, g, value, rows):
    parts = 32 // rows
    for half in range(2):
        tile = value[:, half * 128 : half * 128 + 128]
        for part in range(parts):
            share = (2 * g + half) * parts + part
            if parts == 1:
                stage[share] = tile
            else:
                for b in range(8):
                    at = b * 32 + part * rows
                    stage[share, b * rows : b * rows + rows, :] = tile[at : at + rows]


def send_pieces(stage, send, base, g, sem):
    count = stage.shape[0] // 4
    shares = slice(g * count, g * count + count)
    return fetch(stage.at[shares], send.at[shares, base : base + stage.shape[1], :], sem)


def pieces_pair(pieces, kind, g, rows):
    parts = 32 // rows
    base = kind * 8 * rows
    tiles = []
    for tile in (2 * g, 2 * g + 1):
        if parts == 1:
            tiles.append(pieces[tile, base : base + 256, :])
        else:
            tiles.append(
                jnp.concatenate(
                    [
                        pieces[tile * parts + part, base + b * rows : base + b * rows + rows, :]
                        for b in range(8)
                        for part in range(parts)
                    ],
                    axis=0,
                )
            )
    return jnp.concatenate(tiles, axis=1)


def target_kernel(picks_in, route_in, brick_in, target, send, *refs):
    picks, route, landing, field, stage, meta, meta_half, sems = refs
    told = [
        fetch(source, place, sems.at[index])
        for index, (source, place) in enumerate(((picks_in, picks), (route_in, route), (brick_in, landing)))
    ]
    load = fetch(target, field, sems.at[3])
    for copy in told:
        copy.wait()
    lane = iota((1, 128), 1)
    meta[...] = jnp.zeros(meta.shape, F32)
    value = jnp.zeros((1, 128), jnp.int32)
    for b in range(8):
        for step in range(STEPS):
            code = route[step, 0, 0, b] * 8 + landing[step, 0, 0, b]
            value = jnp.where(lane == 2 * b + step, code, value)
        meta[8 + b : 9 + b, :] = jnp.full((1, 128), picks[1, 0, 0, b], jnp.int32).astype(F32)
    meta[0:1, :] = value.astype(F32)
    meta_half[...] = jnp.broadcast_to(meta[...].astype(BF16)[None], meta_half.shape)
    shared = stage.shape[1]
    sent = [fetch(meta_half, send.at[:, shared : shared + 16, :], sems.at[4])]
    load.wait()
    for g in range(4):
        block = jnp.concatenate(
            [field[qh * 8 + qs] for qs in (2 * g, 2 * g + 1) for qh in range(4)], axis=0
        )
        put_pieces(stage, g, mm(identity(), block, NT).astype(BF16), shared // 8)
        sent.append(send_pieces(stage, send, 0, g, sems.at[5 + g]))
    for copy in sent:
        copy.wait()


def first_kernel(picks, operators, field, sent, moved_out, tables, table_mem, field_mem, start, folded, turned, tables_mem, sems):
    loads = [fetch(operators, table_mem, sems.at[0]), fetch(field, field_mem, sems.at[1])]
    chosen = on_lanes([picks[0, 0, 0, b] for b in range(8)])
    loads[0].wait()
    found = [table_rows(table_mem, chosen, axis) for axis in range(3)]
    for axis in range(3):
        tables_mem[axis] = found[axis].astype(BF16)
    kept = fetch(tables_mem, tables, sems.at[0])
    begin = diagonal(found[2])
    loads[1].wait()
    for g in range(4):
        block = jnp.concatenate(
            [field_mem[qh * 8 + qs] for qs in (2 * g, 2 * g + 1) for qh in range(4)], axis=0
        )
        start[:, g * 256 : g * 256 + 256] = mm(begin, block, NT)
    for g, moved in middle_and_last(start, spread(found[1]), diagonal(found[0]), folded, turned, False):
        put_pair(moved_out, g, moved)
    kept.wait()


def second_kernel(route, landing, operators, moved, arrived, *refs):
    send, tables, codes_out, meta, codes, start, folded, turned, stage, tables_mem, sems, slot_sems = refs
    shared = stage.shape[1]
    sent = []
    for b, (place, rank) in enumerate(slot_numbers(route, 0)):
        rows = pl.ds(pl.multiple_of(rank * 256, 256), 256)
        sent.append(fetch(moved.at[b], send.at[place, rows, :], slot_sems.at[b]))
    meta[...] = arrived[:, shared : shared + 16, :].astype(F32)
    for source in range(meta.shape[0]):
        codes[source : source + 1, :] = meta[source, 0:1, :].astype(jnp.int32)
    sent.append(fetch(codes, codes_out, sems.at[0]))
    lane = iota((1, 128), 1) // 32
    chosen = []
    for part in range(2):
        row = jnp.zeros((1, 128), F32)
        for b in range(4):
            own = part * 4 + b
            found = meta[route[0, 0, 0, own], pl.ds(8 + landing[0, 0, 0, own], 1), :]
            row = jnp.where(lane == b, found, row)
        chosen.append(row)
    chosen = jnp.concatenate(chosen, axis=1).astype(jnp.int32)
    found = [table_rows(operators, chosen, axis) for axis in range(3)]
    for axis in range(3):
        tables_mem[axis] = found[axis].astype(BF16)
    sent.append(fetch(tables_mem, tables, sems.at[1]))
    begin = diagonal(found[0])
    for g in range(4):
        start[:, g * 256 : g * 256 + 256] = mm(begin, lane_pair(moved, g))
    for g, value in middle_and_last(start, spread(found[1]), diagonal(found[2]), folded, turned, False):
        put_pieces(stage, g, value, shared // 8)
        sent.append(send_pieces(stage, send, 512, g, sems.at[2 + g]))
    for copy in sent:
        copy.wait()


def share_kernel(plan_in, arrived, targets, send, plan, total, stage, sems, chunk_sems):
    peers, shared = total.shape[0], total.shape[1]
    rows = shared // 8
    load = fetch(plan_in, plan, sems.at[0])
    total[...] = jnp.zeros(total.shape, F32)
    load.wait()

    def add(source, carry):
        for b in range(8):
            final = plan[source, 8 + b]
            place = pl.ds(pl.multiple_of((final & 7) * rows, rows), rows)
            at = 512 + b * rows
            total[final >> 3, place, :] += arrived[source, at : at + rows, :].astype(F32)
        return carry

    lax.fori_loop(0, peers, add, 0)
    for source in range(peers):
        final = total[source].astype(BF16).astype(F32)
        stage[source, 0:shared, :] = (final - targets[source, 0:shared, :].astype(F32)).astype(BF16)
    sent = []
    for source in range(peers):
        for b in range(8):
            code = plan[source, b]
            place = pl.ds(pl.multiple_of((code & 7) * rows, rows), rows)
            stage[source, shared + b * rows : shared + b * rows + rows, :] = stage[code >> 3, place, :]
        sent.append(fetch(stage.at[source], send.at[source], chunk_sems.at[source]))
    for copy in sent:
        copy.wait()


def composed_kernel(plan_in, shares, edge, send, plan, own, stage, sems):
    peers, shared = own.shape[0], own.shape[1]
    rows = shared // 8
    loads = [fetch(plan_in, plan, sems.at[0]), fetch(shares.at[:, 0:shared, :], own, sems.at[1])]
    for load in loads:
        load.wait()

    def give(source, carry):
        for b in range(8):
            code = plan[source, 8 + b]
            place = pl.ds(pl.multiple_of((code & 7) * rows, rows), rows)
            stage[source, b * rows : b * rows + rows, :] = own[code >> 3, place, :]
        return carry

    lax.fori_loop(0, peers, give, 0)
    fetch(stage, send, sems.at[0]).wait()


def adjoint_kernel(tables_in, arrived, *refs):
    adjoint, tables, start, folded, turned, sems = refs
    load = fetch(tables_in, tables, sems.at[0])
    rows = arrived.shape[1] // 16
    load.wait()
    begin = flipped_diagonal(tables[2].astype(F32))
    mid = spread(tables[1].astype(F32))
    end = flipped_diagonal(tables[0].astype(F32))
    for g in range(4):
        start[:, g * 256 : g * 256 + 256] = mm(begin, pieces_pair(arrived, 1, g, rows))
    for g, moved in middle_and_last(start, mid, end, folded, turned, True):
        put_pair(adjoint, g, moved)


def final_kernel(tables_far, tables_zero, gradient, arrived, *refs):
    adjoint, start, folded, turned, later, field, quarter_sems = refs
    rows = arrived.shape[1] // 8
    begin = flipped_diagonal(tables_far[2].astype(F32))
    mid = spread(tables_far[1].astype(F32))
    end = flipped_diagonal(tables_far[0].astype(F32))
    for g in range(4):
        start[:, g * 256 : g * 256 + 256] = mm(begin, pieces_pair(arrived, 0, g, rows))
    for g, moved in middle_and_last(start, mid, end, folded, turned, True):
        put_pair(later, g, moved)
    begin = flipped_diagonal(tables_zero[0].astype(F32))
    mid = spread(tables_zero[1].astype(F32))
    end = flipped_diagonal(tables_zero[2].astype(F32))
    for g in range(4):
        start[:, g * 256 : g * 256 + 256] = mm(begin, lane_pair(later, g))
    stored = []
    for g, moved in middle_and_last(start, mid, end, folded, turned, True):
        to_native(moved, g, field)
        for qh in range(4):
            at = slice(qh * 8 + 2 * g, qh * 8 + 2 * g + 2)
            stored.append(fetch(field.at[at], adjoint.at[at], quarter_sems.at[g, qh]))
    for copy in stored:
        copy.wait()


def to_native(block, g, field):
    flat = mm(identity(), block, NT).astype(field.dtype)
    for index in range(8):
        x = (index % 4) * 8 + 2 * g + index // 4
        field[x] = flat[index * 32 : index * 32 + 32]


def x_form_to_native(source, folded, turned, field):
    for b in range(8):
        block = source[b].astype(F32)
        block = jnp.concatenate(
            [
                jnp.concatenate([block[g * 64 : g * 64 + 32], block[g * 64 + 32 : g * 64 + 64]], axis=1)
                for g in range(4)
            ],
            axis=0,
        )
        swap_brick(block, folded, turned, b, 1)
    for g in range(4):
        to_native(turned[0:256, g * 256 : g * 256 + 256], g, field)


def tap(offset):
    value = jnp.zeros(offset.shape, F32)
    for step, weight in TAPS:
        value = jnp.where(offset == step, weight, value)
        value = jnp.where(offset == -step, -weight, value)
    return value


def stencils():
    size = 256
    row, col = iota((size, size), 0), iota((size, size), 1)
    along_y = halves(jnp.where(row // 32 == col // 32, tap(col - row), 0.0))
    along_z = halves(tap(row - col))
    row, col = iota((size, 48), 0), iota((size, 48), 1)
    layer = col // 8
    place = jnp.where(layer < RIM, layer - RIM, layer - RIM + 32)
    rim_y = halves(jnp.where(row // 32 == col % 8, tap(place - row % 32), 0.0))
    return along_y, rim_y, along_z


def rim_picker():
    row, col = iota((48, 256), 0), iota((48, 256), 1)
    layer = row // 8
    place = jnp.where(layer < RIM, layer, layer - RIM + 29)
    return ((row % 8 == col // 32) & (place == col % 32)).astype(F32).astype(BF16)


def difference_x(padded, g):
    total = None
    for step, weight in TAPS:
        ahead = padded[pl.ds(8 * g + RIM + step, 8)]
        behind = padded[pl.ds(8 * g + RIM - step, 8)]
        term = weight * (ahead - behind)
        total = term if total is None else total + term
    return total.reshape(256, 256)


def difference_y(parts, rims, along_y, rim_y):
    total = mm(along_y[0], parts[0]) + mm(along_y[1], parts[0])
    if len(parts) > 1:
        total = total + mm(along_y[0], parts[1])
    return total + mm(rim_y[0], rims) + mm(rim_y[1], rims)


def difference_z(parts, along_z):
    total = mm(parts[0], along_z[0]) + mm(parts[0], along_z[1])
    if len(parts) > 1:
        total = total + mm(parts[1], along_z[0])
    return total


def rim_rows(before, after, base, g):
    rows = [before[base + h, (g // 2) * 16 : (g // 2) * 16 + 16, :].astype(F32) for h in range(RIM)]
    rows += [after[base + h, (g // 2) * 16 : (g // 2) * 16 + 16, :].astype(F32) for h in range(RIM)]
    half = (g % 2) * 8
    return jnp.concatenate([value[half : half + 8] for value in rows], axis=0).astype(BF16)


def put_rims(blocks, base, low_y, high_y):
    picker = rim_picker()
    for pair in range(2):
        left, right = mm(picker, blocks[2 * pair]), mm(picker, blocks[2 * pair + 1])
        for layer in range(2 * RIM):
            value = jnp.concatenate(
                [left[layer * 8 : layer * 8 + 8], right[layer * 8 : layer * 8 + 8]], axis=0
            ).astype(BF16)
            target = low_y if layer < RIM else high_y
            target[base + layer % RIM, pair * 16 : pair * 16 + 16, :] = value


def edge_kernel(template, velocity, sent, low_x, high_x, low_y, high_y, field, first_x, last_x, mid_v, sems):
    loads = [
        fetch(template, field, sems.at[0]),
        fetch(velocity.at[0, 0:RIM], first_x, sems.at[1]),
        fetch(velocity.at[0, 29:32], last_x, sems.at[2]),
        fetch(velocity.at[1], mid_v, sems.at[3]),
    ]
    for load in loads:
        load.wait()
    low_x[0:RIM] = field[0:RIM]
    high_x[0:RIM] = field[29:32]
    low_x[RIM : 2 * RIM] = first_x[...].astype(BF16)
    high_x[RIM : 2 * RIM] = last_x[...].astype(BF16)
    put_rims([field[8 * g : 8 * g + 8].reshape(256, 256) for g in range(4)], 0, low_y, high_y)
    put_rims([mid_v[8 * g : 8 * g + 8].astype(BF16).reshape(256, 256) for g in range(4)], RIM, low_y, high_y)


def prepare_kernel(picks, codes_in, operators, edge, tables, plan_out, codes, plan, sems):
    load = fetch(codes_in, codes, sems.at[0])
    chosen = on_lanes([picks[1, 0, 0, b] for b in range(8)])
    for axis in range(3):
        tables[axis] = table_rows(operators, chosen, axis).astype(BF16)
    load.wait()

    def row(source, carry):
        for b in range(8):
            first = codes[source, 2 * b]
            plan[source, b] = codes[source, 2 * b + 1]
            plan[source, 8 + b] = codes[first >> 3, 2 * (first & 7) + 1]
        return carry

    lax.fori_loop(0, codes.shape[0], row, 0)
    fetch(plan, plan_out, sems.at[0]).wait()


def divergence_kernel(velocity, before_x, after_x, before_y, after_y, sent, divergence, padded):
    along_y, rim_y, along_z = stencils()
    padded[0:RIM] = before_x[RIM : 2 * RIM].astype(F32)
    padded[RIM : RIM + 32] = velocity[0]
    padded[RIM + 32 : 2 * RIM + 32] = after_x[RIM : 2 * RIM].astype(F32)
    for g in range(4):
        along_one = halves(velocity[1, 8 * g : 8 * g + 8].reshape(256, 256))
        along_two = halves(velocity[2, 8 * g : 8 * g + 8].reshape(256, 256))
        total = (
            difference_x(padded, g)
            + difference_y(along_one, rim_rows(before_y, after_y, RIM, g), along_y, rim_y)
            + difference_z(along_two, along_z)
        )
        divergence[8 * g : 8 * g + 8] = total.reshape(8, 32, 256)


def rims_kernel(codes_in, arrived, divergence, sent, native, low_x, high_x, low_y, high_y, codes, slots, total, state, folded, turned, sems):
    loads = [fetch(codes_in, codes, sems.at[0]), fetch(arrived.at[:, 0:512, :], slots, sems.at[1])]
    total[...] = jnp.zeros(total.shape, F32)
    for load in loads:
        load.wait()
    me = lax.axis_index("gx")

    def add(source, carry):
        rank = jnp.int32(0)
        for b in range(8):
            code = codes[source, 2 * b]
            hit = (code >> 3) == me

            @pl.when(hit)
            def _():
                place = pl.ds(pl.multiple_of(rank * 256, 256), 256)
                total[code & 7] += slots[source, place, :].astype(F32)

            rank = rank + hit.astype(jnp.int32)
        return carry

    lax.fori_loop(0, slots.shape[0], add, 0)
    for b in range(8):
        state[b] = total[b].astype(BF16)
    x_form_to_native(state, folded, turned, native)
    low_x[0:RIM] = native[0:RIM]
    high_x[0:RIM] = native[29:32]
    low_x[RIM : 2 * RIM] = divergence[0:RIM].astype(BF16)
    high_x[RIM : 2 * RIM] = divergence[29:32].astype(BF16)
    put_rims([native[8 * g : 8 * g + 8].reshape(256, 256) for g in range(4)], 0, low_y, high_y)
    put_rims(
        [divergence[8 * g : 8 * g + 8].astype(BF16).reshape(256, 256) for g in range(4)], RIM, low_y, high_y
    )


def gradient_kernel(
    template,
    state,
    divergence,
    adjoint_two,
    adjoint_one,
    b0x,
    a0x,
    b0y,
    a0y,
    b1x,
    a1x,
    b1y,
    a1y,
    gradient,
    folded,
    turned,
    weight_two,
    weight_one,
    pad_zero,
    pad_one,
    pad_div,
):
    x_form_to_native(adjoint_one, folded, turned, weight_one)
    for g in range(4):
        to_native(pieces_pair(adjoint_two, 0, g, adjoint_two.shape[1] // 16), g, weight_two)
    along_y, rim_y, along_z = stencils()
    for padded, before, middle, after, base in (
        (pad_zero, b0x, template, a0x, 0),
        (pad_one, b1x, state, a1x, 0),
        (pad_div, b1x, divergence, a1x, RIM),
    ):
        padded[0:RIM] = before[base : base + RIM].astype(F32)
        padded[RIM : RIM + 32] = middle[...].astype(F32)
        padded[RIM + 32 : 2 * RIM + 32] = after[base : base + RIM].astype(F32)
    for g in range(4):
        zero = (template[8 * g : 8 * g + 8].reshape(256, 256),)
        one = (state[8 * g : 8 * g + 8].reshape(256, 256),)
        div = halves(divergence[8 * g : 8 * g + 8].reshape(256, 256))
        weigh_one = 0.5 * weight_one[8 * g : 8 * g + 8].reshape(256, 256)
        weigh_two = 0.5 * weight_two[8 * g : 8 * g + 8].reshape(256, 256)
        for axis in range(3):
            if axis == 0:
                parts = [difference_x(padded, g) for padded in (pad_zero, pad_one, pad_div)]
            elif axis == 1:
                parts = [
                    difference_y(zero, rim_rows(b0y, a0y, 0, g), along_y, rim_y),
                    difference_y(one, rim_rows(b1y, a1y, 0, g), along_y, rim_y),
                    difference_y(div, rim_rows(b1y, a1y, RIM, g), along_y, rim_y),
                ]
            else:
                parts = [difference_z(value, along_z) for value in (zero, one, div)]
            value = weigh_one * parts[0] + weigh_two * parts[1] - 0.25 * parts[2]
            gradient[axis, 8 * g : 8 * g + 8] = value.reshape(8, 32, 256)


SCALAR = pl.BlockSpec(memory_space=pltpu.SMEM)
WHOLE = pl.BlockSpec(memory_space=pltpu.VMEM)
NEAR = pl.BlockSpec(memory_space=pltpu.VMEM)
ANYWHERE = pl.BlockSpec(memory_space=pl.ANY)
FAR = pl.BlockSpec(memory_space=pltpu.HBM)
FOLDED = (32, 64, 128)
FLAT = (256, 1024)
NATIVE = (32, 32, 256)
FORM = (8, 256, 128)
TABLES = (3, 32, 256)


def pinned(value, spec):
    if spec is FAR:
        return pltpu.with_memory_space_constraint(value, pltpu.HBM)
    if spec is NEAR:
        return pltpu.with_memory_space_constraint(value, pltpu.VMEM)
    return value


SHORT, LONG = 1 << 20, 1 << 36


def call(kernel, out, in_specs, out_specs, scratch, work=LONG):
    made = pl.pallas_call(
        kernel,
        out_shape=out,
        in_specs=in_specs,
        out_specs=out_specs,
        scratch_shapes=scratch,
        compiler_params=pltpu.CompilerParams(vmem_limit_bytes=24 * 1024 * 1024),
        cost_estimate=pl.CostEstimate(flops=work, bytes_accessed=1024 * 1024, transcendentals=0),
    )

    def apply(*values):
        return made(*[pinned(value, spec) for value, spec in zip(values, in_specs, strict=True)])

    return apply


def like(shape, dtype):
    return jax.ShapeDtypeStruct(shape, dtype)


def far(shape, dtype):
    return pltpu.HBM(shape, dtype)


def neighbours(low_x, high_x, low_y, high_y):
    moved = []
    for low, high, axis in ((low_x, high_x, "gx"), (low_y, high_y, "gy")):
        size = lax.axis_size(axis)
        up = [(i, i + 1) for i in range(size - 1)]
        down = [(i + 1, i) for i in range(size - 1)]
        moved += [lax.ppermute(high, axis, up), lax.ppermute(low, axis, down)]
    return moved


def swap_slots(send):
    return lax.all_to_all(send, "gx", split_axis=0, concat_axis=0, tiled=True)


def shards(template, target_image, velocity, operators, route, target_brick, operator_index):
    peers = lax.axis_size("gx")
    shared = 8 * (256 // peers)
    sems = pltpu.SemaphoreType.DMA((16,))
    quarter_sems = pltpu.SemaphoreType.DMA((4, 4))
    turning = [pltpu.VMEM(FLAT, F32), pltpu.VMEM(FOLDED, F32), pltpu.VMEM((512, 1024), BF16)]
    form = pltpu.VMEM(FORM, BF16)
    tables = pltpu.VMEM(TABLES, BF16)
    routes_mem = pltpu.SMEM((peers, 128), jnp.int32)
    stage = pltpu.VMEM((peers, shared, 128), BF16)
    meta_half = pltpu.VMEM((peers, 16, 128), BF16)
    table_rows_count = operators.shape[1] * operators.shape[2] * operators.shape[3]
    listed = operators.transpose(1, 2, 3, 0).reshape(table_rows_count, operators.shape[0])
    listed_mem = pltpu.VMEM(listed.shape, BF16)
    route = route.reshape(route.shape[:4])

    send = call(
        target_kernel,
        far((peers, shared + 16, 128), BF16),
        [FAR] * 4,
        FAR,
        [pltpu.SMEM(route.shape, jnp.int32)] * 3
        + [pltpu.VMEM(NATIVE, BF16), stage, pltpu.VMEM((16, 128), F32), meta_half, sems],
        SHORT,
    )(operator_index, route, target_brick, target_image)
    targets = swap_slots(send)

    moved, tables_zero = call(
        first_kernel,
        [like(FORM, BF16), far(TABLES, BF16)],
        [SCALAR, FAR, FAR, FAR],
        [WHOLE, FAR],
        [listed_mem, pltpu.VMEM(NATIVE, BF16)] + turning + [tables, sems],
    )(operator_index, listed, template, send)
    send, tables_far, codes = call(
        second_kernel,
        [far((peers, 512 + shared, 128), BF16), far(TABLES, BF16), far((peers, 128), jnp.int32)],
        [SCALAR, SCALAR, WHOLE, WHOLE, WHOLE],
        [FAR] * 3,
        [pltpu.VMEM((peers, 16, 128), F32), pltpu.VMEM((peers, 128), jnp.int32)]
        + turning
        + [stage, tables, sems, pltpu.SemaphoreType.DMA((8,))],
        SHORT,
    )(route, target_brick, listed, moved, targets)
    arrived = swap_slots(send)

    rim = like((2 * RIM, 32, 256), BF16)
    low_x, high_x, low_y, high_y = call(
        edge_kernel,
        [rim] * 4,
        [FAR] * 3,
        [WHOLE] * 4,
        [pltpu.VMEM(NATIVE, BF16)] + [pltpu.VMEM((RIM, 32, 256), F32)] * 2 + [pltpu.VMEM(NATIVE, F32), sems],
    )(template, velocity, send)
    tables_one, plan = call(
        prepare_kernel,
        [far(TABLES, BF16), far((peers, 128), jnp.int32)],
        [SCALAR, FAR, WHOLE, WHOLE],
        [WHOLE, FAR],
        [routes_mem, routes_mem, sems],
    )(operator_index, codes, listed, low_x)
    b0x, a0x, b0y, a0y = neighbours(low_x, high_x, low_y, high_y)

    send = call(
        share_kernel,
        far((peers, 2 * shared, 128), BF16),
        [FAR, WHOLE, WHOLE],
        FAR,
        [routes_mem, pltpu.VMEM((peers, shared, 128), F32), pltpu.VMEM((peers, 2 * shared, 128), BF16)]
        + [sems, pltpu.SemaphoreType.DMA((peers,))],
        SHORT,
    )(plan, arrived, targets)
    pulled = swap_slots(send)

    divergence = call(
        divergence_kernel, like(NATIVE, F32), [WHOLE] * 5 + [FAR], WHOLE, [pltpu.VMEM((38, 32, 256), F32)]
    )(velocity, b0x, a0x, b0y, a0y, send)
    state, low_x, high_x, low_y, high_y = call(
        rims_kernel,
        [like(NATIVE, BF16)] + [rim] * 4,
        [FAR, ANYWHERE, WHOLE, FAR],
        [WHOLE] * 5,
        [routes_mem, pltpu.VMEM((peers, 512, 128), BF16), pltpu.VMEM(FORM, F32), form] + turning[1:] + [sems],
    )(codes, arrived, divergence, send)
    b1x, a1x, b1y, a1y = neighbours(low_x, high_x, low_y, high_y)
    composed = call(
        composed_kernel, far((peers, shared, 128), BF16), [FAR, FAR, WHOLE], FAR, [routes_mem, stage, stage, sems]
    )(plan, send, low_x)

    composed = swap_slots(composed)

    adjoint_one = call(
        adjoint_kernel, like(FORM, BF16), [FAR, NEAR], WHOLE, [tables] + turning + [sems]
    )(tables_one, pulled)
    gradient = call(
        gradient_kernel,
        far((3,) + NATIVE, F32),
        [WHOLE] * 13,
        WHOLE,
        turning[1:] + [pltpu.VMEM(NATIVE, F32)] * 2 + [pltpu.VMEM((38, 32, 256), F32)] * 3,
    )(template, state, divergence, pulled, adjoint_one, b0x, a0x, b0y, a0y, b1x, a1x, b1y, a1y)

    adjoint = call(
        final_kernel,
        far(NATIVE, BF16),
        [WHOLE, WHOLE, FAR, NEAR],
        FAR,
        turning + [form, pltpu.VMEM(NATIVE, BF16), quarter_sems],
        SHORT,
    )(tables_far, tables_zero, gradient, composed)
    return gradient, adjoint


def solution(mesh):
    placed = (
        P("gx", "gy", None),
        P("gx", "gy", None),
        P(None, "gx", "gy", None),
        P(),
        P(None, "gx", "gy", None, None),
        P(None, "gx", "gy", None),
        P(None, "gx", "gy", None),
    )
    return jax.shard_map(
        shards,
        mesh=mesh,
        in_specs=placed,
        out_specs=(P(None, "gx", "gy", None), P("gx", "gy", None)),
        check_vma=False,
    )
```

```python
import functools

import jax
import jax.numpy as jnp
from jax import lax
from jax.experimental import pallas as pl
from jax.experimental.pallas import tpu as pltpu
from jax.sharding import PartitionSpec as P

STEPS = 2
CAP = 2
RIM = 3
F32 = jnp.float32
BF16 = jnp.bfloat16
NT = (((1,), (1,)), ((), ()))
NN = (((1,), (0,)), ((), ()))
TN = (((0,), (0,)), ((), ()))
TAPS = ((1, 0.75), (2, -0.15), (3, 1.0 / 60.0))


def iota(shape, dim):
    return lax.broadcasted_iota(jnp.int32, shape, dim)


def mm(left, right, dims=NN):
    return lax.dot_general(left, right, dims, preferred_element_type=F32)


def halves(value):
    high = value.astype(BF16)
    return high, (value - high.astype(F32)).astype(BF16)


def on_lanes(picks):
    lane = iota((1, 256), 1)
    chosen = jnp.zeros(lane.shape, jnp.int32)
    for b, pick in enumerate(picks):
        chosen = jnp.where(lane // 32 == b, pick, chosen)
    return chosen


def table_rows(operators, chosen, axis):
    shape = (operators.shape[1], 256)
    one_hot = (iota(shape, 0) == jnp.broadcast_to(chosen, shape)).astype(F32).astype(BF16)
    found = mm(operators[axis * 1024 : axis * 1024 + 1024, :], one_hot)
    within = iota((32, 256), 1) % 32
    total = jnp.zeros((32, 256), F32)
    for x in range(32):
        total = jnp.where(within == x, found[x * 32 : x * 32 + 32], total)
    return total


def same_block(size, edge):
    return iota((size, size), 0) // edge == iota((size, size), 1) // edge


def identity():
    return (iota((256, 256), 0) == iota((256, 256), 1)).astype(F32).astype(BF16)


def flipped_diagonal(table):
    return jnp.where(same_block(256, 32), jnp.concatenate([table] * 8, axis=0), 0.0).astype(BF16)


def diagonal(table):
    return mm(identity(), flipped_diagonal(table), NT).astype(BF16)


def spread(table):
    copies = (iota((256, 256), 0) % 32 == iota((256, 256), 1) % 32).astype(F32).astype(BF16)
    return mm(flipped_diagonal(table), copies)


def swap_chunks(parts):
    lane = iota(parts[0].shape, 1)
    for bit, shift in ((1, 32), (2, 64)):
        keep = (lane & shift) == 0
        fresh = list(parts)
        for index in range(4):
            if index & bit:
                continue
            one, two = parts[index], parts[index | bit]
            fresh[index] = jnp.where(keep, one, pltpu.roll(two, shift, 1))
            fresh[index | bit] = jnp.where(keep, pltpu.roll(one, 128 - shift, 1), two)
        parts = fresh
    return parts


def swap_brick(block, folded, turned, brick, parts=2):
    slabs = []
    for ph in range(4):
        slabs.append(
            jnp.concatenate(
                [
                    block[(qs // 2) * 32 + ph * 8 : (qs // 2) * 32 + ph * 8 + 8, (qs % 2) * 128 : (qs % 2) * 128 + 128]
                    for qs in range(8)
                ],
                axis=0,
            )
        )
    slabs = swap_chunks(slabs)
    for qh in range(4):
        folded[brick * 4 + qh] = slabs[qh]
    for ps in range(8):
        value = jnp.concatenate(
            [folded[brick * 4 + qh, pl.ds(ps, 8, stride=8), :] for qh in range(4)], axis=0
        )
        for part, half in enumerate(halves(value)[:parts]):
            turned[part * 256 + brick * 32 : part * 256 + brick * 32 + 32, ps * 128 : ps * 128 + 128] = half


def lane_pair(field, g):
    return jnp.concatenate(
        [
            jnp.concatenate([field[b, qs * 32 : qs * 32 + 32, :] for b in range(8)], axis=0)
            for qs in (2 * g, 2 * g + 1)
        ],
        axis=1,
    )


def put_pair(field, g, value):
    for b in range(8):
        for half in range(2):
            rows = slice((2 * g + half) * 32, (2 * g + half) * 32 + 32)
            field[b, rows, :] = value[b * 32 : b * 32 + 32, half * 128 : half * 128 + 128]


def middle(start, spread_mid, folded, turned, flipped):
    mask = same_block(256, 32)
    for brick in range(8):
        rows = spread_mid[brick * 32 : brick * 32 + 32]
        line = jnp.where(mask, jnp.concatenate([rows] * 8, axis=0), 0.0).astype(BF16)
        block = start[brick * 32 : brick * 32 + 32, :]
        block = jnp.concatenate([block[:, g * 256 : g * 256 + 256] for g in range(4)], axis=0)
        high, low = halves(block)
        both = mm(jnp.concatenate([high, low], axis=0), line, NT if flipped else NN)
        swap_brick(both[:128] + both[128:], folded, turned, brick)


def middle_and_last(start, spread_mid, last, folded, turned, flipped):
    middle(start, spread_mid, folded, turned, flipped)
    last = jnp.concatenate([last, last], axis=1)
    for g in range(4):
        yield g, mm(last, turned[:, g * 256 : g * 256 + 256]).astype(BF16)


def slot_numbers(route, step):
    own = [route[step, 0, 0, b] for b in range(8)]
    slots = []
    for b in range(8):
        rank = jnp.int32(0)
        for other in range(b):
            rank = rank + (own[other] == own[b]).astype(jnp.int32)
        slots.append((own[b], rank))
    return slots


def fetch(source, target, sem):
    copy = pltpu.make_async_copy(source, target, sem)
    copy.start()
    return copy


def put_pieces(stage, g, value, rows):
    parts = 32 // rows
    for half in range(2):
        tile = value[:, half * 128 : half * 128 + 128]
        for part in range(parts):
            share = (2 * g + half) * parts + part
            if parts == 1:
                stage[share] = tile
            else:
                for b in range(8):
                    at = b * 32 + part * rows
                    stage[share, b * rows : b * rows + rows, :] = tile[at : at + rows]


def send_pieces(stage, send, base, g, sem):
    count = stage.shape[0] // 4
    shares = slice(g * count, g * count + count)
    return fetch(stage.at[shares], send.at[shares, base : base + stage.shape[1], :], sem)


def pieces_pair(pieces, kind, g, rows):
    parts = 32 // rows
    base = kind * 8 * rows
    tiles = []
    for tile in (2 * g, 2 * g + 1):
        if parts == 1:
            tiles.append(pieces[tile, base : base + 256, :])
        else:
            tiles.append(
                jnp.concatenate(
                    [
                        pieces[tile * parts + part, base + b * rows : base + b * rows + rows, :]
                        for b in range(8)
                        for part in range(parts)
                    ],
                    axis=0,
                )
            )
    return jnp.concatenate(tiles, axis=1)


def target_kernel(picks_in, route_in, brick_in, target, send, *refs):
    picks, route, landing, field, stage, meta, meta_half, sems = refs
    told = [
        fetch(source, place, sems.at[index])
        for index, (source, place) in enumerate(((picks_in, picks), (route_in, route), (brick_in, landing)))
    ]
    load = fetch(target, field, sems.at[3])
    for copy in told:
        copy.wait()
    lane = iota((1, 128), 1)
    meta[...] = jnp.zeros(meta.shape, F32)
    value = jnp.zeros((1, 128), jnp.int32)
    for b in range(8):
        for step in range(STEPS):
            code = route[step, 0, 0, b] * 8 + landing[step, 0, 0, b]
            value = jnp.where(lane == 2 * b + step, code, value)
        meta[8 + b : 9 + b, :] = jnp.full((1, 128), picks[1, 0, 0, b], jnp.int32).astype(F32)
    meta[0:1, :] = value.astype(F32)
    meta_half[...] = jnp.broadcast_to(meta[...].astype(BF16)[None], meta_half.shape)
    shared = stage.shape[1]
    sent = [fetch(meta_half, send.at[:, shared : shared + 16, :], sems.at[4])]
    load.wait()
    for g in range(4):
        block = jnp.concatenate(
            [field[qh * 8 + qs] for qs in (2 * g, 2 * g + 1) for qh in range(4)], axis=0
        )
        put_pieces(stage, g, mm(identity(), block, NT).astype(BF16), shared // 8)
        sent.append(send_pieces(stage, send, 0, g, sems.at[5 + g]))
    for copy in sent:
        copy.wait()


def first_kernel(picks, operators, field, sent, moved_out, tables, table_mem, field_mem, start, folded, turned, tables_mem, sems):
    loads = [fetch(operators, table_mem, sems.at[0]), fetch(field, field_mem, sems.at[1])]
    chosen = on_lanes([picks[0, 0, 0, b] for b in range(8)])
    loads[0].wait()
    found = [table_rows(table_mem, chosen, axis) for axis in range(3)]
    for axis in range(3):
        tables_mem[axis] = found[axis].astype(BF16)
    kept = fetch(tables_mem, tables, sems.at[0])
    begin = diagonal(found[2])
    loads[1].wait()
    for g in range(4):
        block = jnp.concatenate(
            [field_mem[qh * 8 + qs] for qs in (2 * g, 2 * g + 1) for qh in range(4)], axis=0
        )
        start[:, g * 256 : g * 256 + 256] = mm(begin, block, NT)
    for g, moved in middle_and_last(start, spread(found[1]), diagonal(found[0]), folded, turned, False):
        put_pair(moved_out, g, moved)
    kept.wait()


def second_kernel(route, landing, operators, moved, arrived, *refs):
    send, tables, codes_out, meta, codes, start, folded, turned, stage, tables_mem, sems, slot_sems = refs
    shared = stage.shape[1]
    sent = []
    for b, (place, rank) in enumerate(slot_numbers(route, 0)):
        rows = pl.ds(pl.multiple_of(rank * 256, 256), 256)
        sent.append(fetch(moved.at[b], send.at[place, rows, :], slot_sems.at[b]))
    meta[...] = arrived[:, shared : shared + 16, :].astype(F32)
    for source in range(meta.shape[0]):
        codes[source : source + 1, :] = meta[source, 0:1, :].astype(jnp.int32)
    sent.append(fetch(codes, codes_out, sems.at[0]))
    lane = iota((1, 128), 1) // 32
    chosen = []
    for part in range(2):
        row = jnp.zeros((1, 128), F32)
        for b in range(4):
            own = part * 4 + b
            found = meta[route[0, 0, 0, own], pl.ds(8 + landing[0, 0, 0, own], 1), :]
            row = jnp.where(lane == b, found, row)
        chosen.append(row)
    chosen = jnp.concatenate(chosen, axis=1).astype(jnp.int32)
    found = [table_rows(operators, chosen, axis) for axis in range(3)]
    for axis in range(3):
        tables_mem[axis] = found[axis].astype(BF16)
    sent.append(fetch(tables_mem, tables, sems.at[1]))
    begin = diagonal(found[0])
    for g in range(4):
        start[:, g * 256 : g * 256 + 256] = mm(begin, lane_pair(moved, g))
    for g, value in middle_and_last(start, spread(found[1]), diagonal(found[2]), folded, turned, False):
        put_pieces(stage, g, value, shared // 8)
        sent.append(send_pieces(stage, send, 512, g, sems.at[2 + g]))
    for copy in sent:
        copy.wait()


def share_kernel(plan_in, arrived, targets, send, plan, total, stage, sems, chunk_sems):
    peers, shared = total.shape[0], total.shape[1]
    rows = shared // 8
    load = fetch(plan_in, plan, sems.at[0])
    total[...] = jnp.zeros(total.shape, F32)
    load.wait()

    def add(source, carry):
        for b in range(8):
            final = plan[source, 8 + b]
            place = pl.ds(pl.multiple_of((final & 7) * rows, rows), rows)
            at = 512 + b * rows
            total[final >> 3, place, :] += arrived[source, at : at + rows, :].astype(F32)
        return carry

    lax.fori_loop(0, peers, add, 0)
    for source in range(peers):
        final = total[source].astype(BF16).astype(F32)
        stage[source, 0:shared, :] = (final - targets[source, 0:shared, :].astype(F32)).astype(BF16)
    sent = []
    for source in range(peers):
        for b in range(8):
            code = plan[source, b]
            place = pl.ds(pl.multiple_of((code & 7) * rows, rows), rows)
            stage[source, shared + b * rows : shared + b * rows + rows, :] = stage[code >> 3, place, :]
        sent.append(fetch(stage.at[source], send.at[source], chunk_sems.at[source]))
    for copy in sent:
        copy.wait()


def composed_kernel(plan_in, shares, edge, send, plan, own, stage, sems):
    peers, shared = own.shape[0], own.shape[1]
    rows = shared // 8
    loads = [fetch(plan_in, plan, sems.at[0]), fetch(shares.at[:, 0:shared, :], own, sems.at[1])]
    for load in loads:
        load.wait()

    def give(source, carry):
        for b in range(8):
            code = plan[source, 8 + b]
            place = pl.ds(pl.multiple_of((code & 7) * rows, rows), rows)
            stage[source, b * rows : b * rows + rows, :] = own[code >> 3, place, :]
        return carry

    lax.fori_loop(0, peers, give, 0)
    fetch(stage, send, sems.at[0]).wait()


def adjoint_kernel(tables_in, arrived, *refs):
    adjoint, tables, start, folded, turned, sems = refs
    load = fetch(tables_in, tables, sems.at[0])
    rows = arrived.shape[1] // 16
    load.wait()
    begin = flipped_diagonal(tables[2].astype(F32))
    mid = spread(tables[1].astype(F32))
    end = flipped_diagonal(tables[0].astype(F32))
    for g in range(4):
        start[:, g * 256 : g * 256 + 256] = mm(begin, pieces_pair(arrived, 1, g, rows))
    for g, moved in middle_and_last(start, mid, end, folded, turned, True):
        put_pair(adjoint, g, moved)


def final_kernel(tables_far, tables_zero, gradient, arrived, *refs):
    adjoint, start, folded, turned, later, field, quarter_sems = refs
    rows = arrived.shape[1] // 8
    begin = flipped_diagonal(tables_far[2].astype(F32))
    mid = spread(tables_far[1].astype(F32))
    end = flipped_diagonal(tables_far[0].astype(F32))
    for g in range(4):
        start[:, g * 256 : g * 256 + 256] = mm(begin, pieces_pair(arrived, 0, g, rows))
    for g, moved in middle_and_last(start, mid, end, folded, turned, True):
        put_pair(later, g, moved)
    begin = flipped_diagonal(tables_zero[0].astype(F32))
    mid = spread(tables_zero[1].astype(F32))
    end = diagonal(tables_zero[2].astype(F32))
    end = jnp.concatenate([end, end], axis=0)
    for g in range(4):
        start[:, g * 256 : g * 256 + 256] = mm(begin, lane_pair(later, g))
    stored = []
    middle(start, mid, folded, turned, True)
    for g in range(4):
        flat = mm(turned[:, g * 256 : g * 256 + 256], end, TN).astype(BF16)
        for index in range(8):
            field[(index % 4) * 8 + 2 * g + index // 4] = flat[index * 32 : index * 32 + 32]
        for qh in range(4):
            at = slice(qh * 8 + 2 * g, qh * 8 + 2 * g + 2)
            stored.append(fetch(field.at[at], adjoint.at[at], quarter_sems.at[g, qh]))
    for copy in stored:
        copy.wait()


def to_native(block, g, field):
    flat = mm(identity(), block, NT).astype(field.dtype)
    for index in range(8):
        x = (index % 4) * 8 + 2 * g + index // 4
        field[x] = flat[index * 32 : index * 32 + 32]


def x_form_to_native(source, folded, turned, field):
    for b in range(8):
        block = source[b].astype(F32)
        block = jnp.concatenate(
            [
                jnp.concatenate([block[g * 64 : g * 64 + 32], block[g * 64 + 32 : g * 64 + 64]], axis=1)
                for g in range(4)
            ],
            axis=0,
        )
        swap_brick(block, folded, turned, b, 1)
    for g in range(4):
        to_native(turned[0:256, g * 256 : g * 256 + 256], g, field)


def tap(offset):
    value = jnp.zeros(offset.shape, F32)
    for step, weight in TAPS:
        value = jnp.where(offset == step, weight, value)
        value = jnp.where(offset == -step, -weight, value)
    return value


def stencils():
    size = 256
    row, col = iota((size, size), 0), iota((size, size), 1)
    along_y = halves(jnp.where(row // 32 == col // 32, tap(col - row), 0.0))
    along_z = halves(tap(row - col))
    row, col = iota((size, 48), 0), iota((size, 48), 1)
    layer = col // 8
    place = jnp.where(layer < RIM, layer - RIM, layer - RIM + 32)
    rim_y = halves(jnp.where(row // 32 == col % 8, tap(place - row % 32), 0.0))
    return along_y, rim_y, along_z


def rim_picker():
    row, col = iota((48, 256), 0), iota((48, 256), 1)
    layer = row // 8
    place = jnp.where(layer < RIM, layer, layer - RIM + 29)
    return ((row % 8 == col // 32) & (place == col % 32)).astype(F32).astype(BF16)


def difference_x(padded, g):
    total = None
    for step, weight in TAPS:
        ahead = padded[pl.ds(8 * g + RIM + step, 8)]
        behind = padded[pl.ds(8 * g + RIM - step, 8)]
        term = weight * (ahead - behind)
        total = term if total is None else total + term
    return total.reshape(256, 256)


def difference_y(parts, rims, along_y, rim_y):
    total = mm(along_y[0], parts[0]) + mm(along_y[1], parts[0])
    if len(parts) > 1:
        total = total + mm(along_y[0], parts[1])
    return total + mm(rim_y[0], rims) + mm(rim_y[1], rims)


def difference_z(parts, along_z):
    total = mm(parts[0], along_z[0]) + mm(parts[0], along_z[1])
    if len(parts) > 1:
        total = total + mm(parts[1], along_z[0])
    return total


def rim_rows(before, after, base, g):
    rows = [before[base + h, (g // 2) * 16 : (g // 2) * 16 + 16, :].astype(F32) for h in range(RIM)]
    rows += [after[base + h, (g // 2) * 16 : (g // 2) * 16 + 16, :].astype(F32) for h in range(RIM)]
    half = (g % 2) * 8
    return jnp.concatenate([value[half : half + 8] for value in rows], axis=0).astype(BF16)


def put_rims(blocks, base, low_y, high_y):
    picker = rim_picker()
    for pair in range(2):
        left, right = mm(picker, blocks[2 * pair]), mm(picker, blocks[2 * pair + 1])
        for layer in range(2 * RIM):
            value = jnp.concatenate(
                [left[layer * 8 : layer * 8 + 8], right[layer * 8 : layer * 8 + 8]], axis=0
            ).astype(BF16)
            target = low_y if layer < RIM else high_y
            target[base + layer % RIM, pair * 16 : pair * 16 + 16, :] = value


def edge_kernel(template, velocity, sent, low_x, high_x, low_y, high_y, field, first_x, last_x, mid_v, sems):
    loads = [
        fetch(template, field, sems.at[0]),
        fetch(velocity.at[0, 0:RIM], first_x, sems.at[1]),
        fetch(velocity.at[0, 29:32], last_x, sems.at[2]),
        fetch(velocity.at[1], mid_v, sems.at[3]),
    ]
    for load in loads:
        load.wait()
    low_x[0:RIM] = field[0:RIM]
    high_x[0:RIM] = field[29:32]
    low_x[RIM : 2 * RIM] = first_x[...].astype(BF16)
    high_x[RIM : 2 * RIM] = last_x[...].astype(BF16)
    put_rims([field[8 * g : 8 * g + 8].reshape(256, 256) for g in range(4)], 0, low_y, high_y)
    put_rims([mid_v[8 * g : 8 * g + 8].astype(BF16).reshape(256, 256) for g in range(4)], RIM, low_y, high_y)


def prepare_kernel(picks, codes_in, operators, edge, tables, plan_out, codes, plan, sems):
    load = fetch(codes_in, codes, sems.at[0])
    chosen = on_lanes([picks[1, 0, 0, b] for b in range(8)])
    for axis in range(3):
        tables[axis] = table_rows(operators, chosen, axis).astype(BF16)
    load.wait()

    def row(source, carry):
        for b in range(8):
            first = codes[source, 2 * b]
            plan[source, b] = codes[source, 2 * b + 1]
            plan[source, 8 + b] = codes[first >> 3, 2 * (first & 7) + 1]
        return carry

    lax.fori_loop(0, codes.shape[0], row, 0)
    fetch(plan, plan_out, sems.at[0]).wait()


def divergence_kernel(velocity, before_x, after_x, before_y, after_y, sent, divergence, padded):
    along_y, rim_y, along_z = stencils()
    padded[0:RIM] = before_x[RIM : 2 * RIM].astype(F32)
    padded[RIM : RIM + 32] = velocity[0]
    padded[RIM + 32 : 2 * RIM + 32] = after_x[RIM : 2 * RIM].astype(F32)
    for g in range(4):
        along_one = halves(velocity[1, 8 * g : 8 * g + 8].reshape(256, 256))
        along_two = halves(velocity[2, 8 * g : 8 * g + 8].reshape(256, 256))
        total = (
            difference_x(padded, g)
            + difference_y(along_one, rim_rows(before_y, after_y, RIM, g), along_y, rim_y)
            + difference_z(along_two, along_z)
        )
        divergence[8 * g : 8 * g + 8] = total.reshape(8, 32, 256)


def rims_kernel(codes_in, arrived, divergence, sent, native, low_x, high_x, low_y, high_y, codes, slots, total, state, folded, turned, sems):
    loads = [fetch(codes_in, codes, sems.at[0]), fetch(arrived.at[:, 0:512, :], slots, sems.at[1])]
    total[...] = jnp.zeros(total.shape, F32)
    for load in loads:
        load.wait()
    me = lax.axis_index("gx")

    def add(source, carry):
        rank = jnp.int32(0)
        for b in range(8):
            code = codes[source, 2 * b]
            hit = (code >> 3) == me

            @pl.when(hit)
            def _():
                place = pl.ds(pl.multiple_of(rank * 256, 256), 256)
                total[code & 7] += slots[source, place, :].astype(F32)

            rank = rank + hit.astype(jnp.int32)
        return carry

    lax.fori_loop(0, slots.shape[0], add, 0)
    for b in range(8):
        state[b] = total[b].astype(BF16)
    x_form_to_native(state, folded, turned, native)
    low_x[0:RIM] = native[0:RIM]
    high_x[0:RIM] = native[29:32]
    low_x[RIM : 2 * RIM] = divergence[0:RIM].astype(BF16)
    high_x[RIM : 2 * RIM] = divergence[29:32].astype(BF16)
    put_rims([native[8 * g : 8 * g + 8].reshape(256, 256) for g in range(4)], 0, low_y, high_y)
    put_rims(
        [divergence[8 * g : 8 * g + 8].astype(BF16).reshape(256, 256) for g in range(4)], RIM, low_y, high_y
    )


def gradient_kernel(
    template,
    state,
    divergence,
    adjoint_two,
    adjoint_one,
    b0x,
    a0x,
    b0y,
    a0y,
    b1x,
    a1x,
    b1y,
    a1y,
    gradient,
    folded,
    turned,
    weight_two,
    weight_one,
    pad_zero,
    pad_one,
    pad_div,
):
    x_form_to_native(adjoint_one, folded, turned, weight_one)
    for g in range(4):
        to_native(pieces_pair(adjoint_two, 0, g, adjoint_two.shape[1] // 16), g, weight_two)
    along_y, rim_y, along_z = stencils()
    for padded, before, middle, after, base in (
        (pad_zero, b0x, template, a0x, 0),
        (pad_one, b1x, state, a1x, 0),
        (pad_div, b1x, divergence, a1x, RIM),
    ):
        padded[0:RIM] = before[base : base + RIM].astype(F32)
        padded[RIM : RIM + 32] = middle[...].astype(F32)
        padded[RIM + 32 : 2 * RIM + 32] = after[base : base + RIM].astype(F32)
    for g in range(4):
        zero = (template[8 * g : 8 * g + 8].reshape(256, 256),)
        one = (state[8 * g : 8 * g + 8].reshape(256, 256),)
        div = halves(divergence[8 * g : 8 * g + 8].reshape(256, 256))
        weigh_one = 0.5 * weight_one[8 * g : 8 * g + 8].reshape(256, 256)
        weigh_two = 0.5 * weight_two[8 * g : 8 * g + 8].reshape(256, 256)
        for axis in range(3):
            if axis == 0:
                parts = [difference_x(padded, g) for padded in (pad_zero, pad_one, pad_div)]
            elif axis == 1:
                parts = [
                    difference_y(zero, rim_rows(b0y, a0y, 0, g), along_y, rim_y),
                    difference_y(one, rim_rows(b1y, a1y, 0, g), along_y, rim_y),
                    difference_y(div, rim_rows(b1y, a1y, RIM, g), along_y, rim_y),
                ]
            else:
                parts = [difference_z(value, along_z) for value in (zero, one, div)]
            value = weigh_one * parts[0] + weigh_two * parts[1] - 0.25 * parts[2]
            gradient[axis, 8 * g : 8 * g + 8] = value.reshape(8, 32, 256)


SCALAR = pl.BlockSpec(memory_space=pltpu.SMEM)
WHOLE = pl.BlockSpec(memory_space=pltpu.VMEM)
NEAR = pl.BlockSpec(memory_space=pltpu.VMEM)
ANYWHERE = pl.BlockSpec(memory_space=pl.ANY)
FAR = pl.BlockSpec(memory_space=pltpu.HBM)
FOLDED = (32, 64, 128)
FLAT = (256, 1024)
NATIVE = (32, 32, 256)
FORM = (8, 256, 128)
TABLES = (3, 32, 256)


def pinned(value, spec):
    if spec is FAR:
        return pltpu.with_memory_space_constraint(value, pltpu.HBM)
    if spec is NEAR:
        return pltpu.with_memory_space_constraint(value, pltpu.VMEM)
    return value


SHORT, LONG = 1 << 20, 1 << 36


def call(kernel, out, in_specs, out_specs, scratch, work=LONG):
    made = pl.pallas_call(
        kernel,
        out_shape=out,
        in_specs=in_specs,
        out_specs=out_specs,
        scratch_shapes=scratch,
        compiler_params=pltpu.CompilerParams(vmem_limit_bytes=24 * 1024 * 1024),
        cost_estimate=pl.CostEstimate(flops=work, bytes_accessed=1024 * 1024, transcendentals=0),
    )

    def apply(*values):
        return made(*[pinned(value, spec) for value, spec in zip(values, in_specs, strict=True)])

    return apply


def like(shape, dtype):
    return jax.ShapeDtypeStruct(shape, dtype)


def far(shape, dtype):
    return pltpu.HBM(shape, dtype)


def neighbours(low_x, high_x, low_y, high_y):
    moved = []
    for low, high, axis in ((low_x, high_x, "gx"), (low_y, high_y, "gy")):
        size = lax.axis_size(axis)
        up = [(i, i + 1) for i in range(size - 1)]
        down = [(i + 1, i) for i in range(size - 1)]
        moved += [lax.ppermute(high, axis, up), lax.ppermute(low, axis, down)]
    return moved


def swap_slots(send):
    return lax.all_to_all(send, "gx", split_axis=0, concat_axis=0, tiled=True)


def shards(template, target_image, velocity, operators, route, target_brick, operator_index):
    peers = lax.axis_size("gx")
    shared = 8 * (256 // peers)
    sems = pltpu.SemaphoreType.DMA((16,))
    quarter_sems = pltpu.SemaphoreType.DMA((4, 4))
    turning = [pltpu.VMEM(FLAT, F32), pltpu.VMEM(FOLDED, F32), pltpu.VMEM((512, 1024), BF16)]
    form = pltpu.VMEM(FORM, BF16)
    tables = pltpu.VMEM(TABLES, BF16)
    routes_mem = pltpu.SMEM((peers, 128), jnp.int32)
    stage = pltpu.VMEM((peers, shared, 128), BF16)
    meta_half = pltpu.VMEM((peers, 16, 128), BF16)
    table_rows_count = operators.shape[1] * operators.shape[2] * operators.shape[3]
    listed = operators.transpose(1, 2, 3, 0).reshape(table_rows_count, operators.shape[0])
    listed_mem = pltpu.VMEM(listed.shape, BF16)
    route = route.reshape(route.shape[:4])

    send = call(
        target_kernel,
        far((peers, shared + 16, 128), BF16),
        [FAR] * 4,
        FAR,
        [pltpu.SMEM(route.shape, jnp.int32)] * 3
        + [pltpu.VMEM(NATIVE, BF16), stage, pltpu.VMEM((16, 128), F32), meta_half, sems],
        SHORT,
    )(operator_index, route, target_brick, target_image)
    targets = swap_slots(send)

    moved, tables_zero = call(
        first_kernel,
        [like(FORM, BF16), far(TABLES, BF16)],
        [SCALAR, FAR, FAR, FAR],
        [WHOLE, FAR],
        [listed_mem, pltpu.VMEM(NATIVE, BF16)] + turning + [tables, sems],
    )(operator_index, listed, template, send)
    send, tables_far, codes = call(
        second_kernel,
        [far((peers, 512 + shared, 128), BF16), far(TABLES, BF16), far((peers, 128), jnp.int32)],
        [SCALAR, SCALAR, WHOLE, WHOLE, WHOLE],
        [FAR] * 3,
        [pltpu.VMEM((peers, 16, 128), F32), pltpu.VMEM((peers, 128), jnp.int32)]
        + turning
        + [stage, tables, sems, pltpu.SemaphoreType.DMA((8,))],
        SHORT,
    )(route, target_brick, listed, moved, targets)
    arrived = swap_slots(send)

    rim = like((2 * RIM, 32, 256), BF16)
    low_x, high_x, low_y, high_y = call(
        edge_kernel,
        [rim] * 4,
        [FAR] * 3,
        [WHOLE] * 4,
        [pltpu.VMEM(NATIVE, BF16)] + [pltpu.VMEM((RIM, 32, 256), F32)] * 2 + [pltpu.VMEM(NATIVE, F32), sems],
    )(template, velocity, send)
    tables_one, plan = call(
        prepare_kernel,
        [far(TABLES, BF16), far((peers, 128), jnp.int32)],
        [SCALAR, FAR, WHOLE, WHOLE],
        [WHOLE, FAR],
        [routes_mem, routes_mem, sems],
    )(operator_index, codes, listed, low_x)
    b0x, a0x, b0y, a0y = neighbours(low_x, high_x, low_y, high_y)

    send = call(
        share_kernel,
        far((peers, 2 * shared, 128), BF16),
        [FAR, WHOLE, WHOLE],
        FAR,
        [routes_mem, pltpu.VMEM((peers, shared, 128), F32), pltpu.VMEM((peers, 2 * shared, 128), BF16)]
        + [sems, pltpu.SemaphoreType.DMA((peers,))],
        SHORT,
    )(plan, arrived, targets)
    pulled = swap_slots(send)

    divergence = call(
        divergence_kernel, like(NATIVE, F32), [WHOLE] * 5 + [FAR], WHOLE, [pltpu.VMEM((38, 32, 256), F32)]
    )(velocity, b0x, a0x, b0y, a0y, send)
    state, low_x, high_x, low_y, high_y = call(
        rims_kernel,
        [like(NATIVE, BF16)] + [rim] * 4,
        [FAR, ANYWHERE, WHOLE, FAR],
        [WHOLE] * 5,
        [routes_mem, pltpu.VMEM((peers, 512, 128), BF16), pltpu.VMEM(FORM, F32), form] + turning[1:] + [sems],
    )(codes, arrived, divergence, send)
    b1x, a1x, b1y, a1y = neighbours(low_x, high_x, low_y, high_y)
    composed = call(
        composed_kernel, far((peers, shared, 128), BF16), [FAR, FAR, WHOLE], FAR, [routes_mem, stage, stage, sems]
    )(plan, send, low_x)

    composed = swap_slots(composed)

    adjoint_one = call(
        adjoint_kernel, like(FORM, BF16), [FAR, NEAR], WHOLE, [tables] + turning + [sems]
    )(tables_one, pulled)
    gradient = call(
        gradient_kernel,
        far((3,) + NATIVE, F32),
        [WHOLE] * 13,
        WHOLE,
        turning[1:] + [pltpu.VMEM(NATIVE, F32)] * 2 + [pltpu.VMEM((38, 32, 256), F32)] * 3,
    )(template, state, divergence, pulled, adjoint_one, b0x, a0x, b0y, a0y, b1x, a1x, b1y, a1y)

    adjoint = call(
        final_kernel,
        far(NATIVE, BF16),
        [WHOLE, WHOLE, FAR, NEAR],
        FAR,
        turning + [form, pltpu.VMEM(NATIVE, BF16), quarter_sems],
        SHORT,
    )(tables_far, tables_zero, gradient, composed)
    return gradient, adjoint


def solution(mesh):
    placed = (
        P("gx", "gy", None),
        P("gx", "gy", None),
        P(None, "gx", "gy", None),
        P(),
        P(None, "gx", "gy", None, None),
        P(None, "gx", "gy", None),
        P(None, "gx", "gy", None),
    )
    return jax.shard_map(
        shards,
        mesh=mesh,
        in_specs=placed,
        out_specs=(P(None, "gx", "gy", None), P("gx", "gy", None)),
        check_vma=False,
    )
```

```python
import functools

import jax
import jax.numpy as jnp
from jax import lax
from jax.experimental import pallas as pl
from jax.experimental.pallas import tpu as pltpu
from jax.sharding import PartitionSpec as P

STEPS = 2
CAP = 2
RIM = 3
F32 = jnp.float32
BF16 = jnp.bfloat16
NT = (((1,), (1,)), ((), ()))
NN = (((1,), (0,)), ((), ()))
TN = (((0,), (0,)), ((), ()))
TAPS = ((1, 0.75), (2, -0.15), (3, 1.0 / 60.0))


def iota(shape, dim):
    return lax.broadcasted_iota(jnp.int32, shape, dim)


def mm(left, right, dims=NN):
    return lax.dot_general(left, right, dims, preferred_element_type=F32)


def halves(value):
    high = value.astype(BF16)
    return high, (value - high.astype(F32)).astype(BF16)


def on_lanes(picks):
    lane = iota((1, 256), 1)
    chosen = jnp.zeros(lane.shape, jnp.int32)
    for b, pick in enumerate(picks):
        chosen = jnp.where(lane // 32 == b, pick, chosen)
    return chosen


def table_rows(operators, chosen, axis):
    shape = (operators.shape[1], 256)
    one_hot = (iota(shape, 0) == jnp.broadcast_to(chosen, shape)).astype(F32).astype(BF16)
    found = mm(operators[axis * 1024 : axis * 1024 + 1024, :], one_hot)
    within = iota((32, 256), 1) % 32
    total = jnp.zeros((32, 256), F32)
    for x in range(32):
        total = jnp.where(within == x, found[x * 32 : x * 32 + 32], total)
    return total


def same_block(size, edge):
    return iota((size, size), 0) // edge == iota((size, size), 1) // edge


def identity():
    return (iota((256, 256), 0) == iota((256, 256), 1)).astype(F32).astype(BF16)


def flipped_diagonal(table):
    return jnp.where(same_block(256, 32), jnp.concatenate([table] * 8, axis=0), 0.0).astype(BF16)


def diagonal(table):
    return mm(identity(), flipped_diagonal(table), NT).astype(BF16)


def spread(table):
    copies = (iota((256, 256), 0) % 32 == iota((256, 256), 1) % 32).astype(F32).astype(BF16)
    return mm(flipped_diagonal(table), copies)


def swap_chunks(parts):
    lane = iota(parts[0].shape, 1)
    for bit, shift in ((1, 32), (2, 64)):
        keep = (lane & shift) == 0
        fresh = list(parts)
        for index in range(4):
            if index & bit:
                continue
            one, two = parts[index], parts[index | bit]
            fresh[index] = jnp.where(keep, one, pltpu.roll(two, shift, 1))
            fresh[index | bit] = jnp.where(keep, pltpu.roll(one, 128 - shift, 1), two)
        parts = fresh
    return parts


def swap_brick(block, folded, turned, brick, parts=2):
    slabs = []
    for ph in range(4):
        slabs.append(
            jnp.concatenate(
                [
                    block[(qs // 2) * 32 + ph * 8 : (qs // 2) * 32 + ph * 8 + 8, (qs % 2) * 128 : (qs % 2) * 128 + 128]
                    for qs in range(8)
                ],
                axis=0,
            )
        )
    slabs = swap_chunks(slabs)
    for qh in range(4):
        folded[brick * 4 + qh] = slabs[qh]
    for ps in range(8):
        value = jnp.concatenate(
            [folded[brick * 4 + qh, pl.ds(ps, 8, stride=8), :] for qh in range(4)], axis=0
        )
        for part, half in enumerate(halves(value)[:parts]):
            turned[part * 256 + brick * 32 : part * 256 + brick * 32 + 32, ps * 128 : ps * 128 + 128] = half


def lane_pair(field, g):
    return jnp.concatenate(
        [
            jnp.concatenate([field[b, qs * 32 : qs * 32 + 32, :] for b in range(8)], axis=0)
            for qs in (2 * g, 2 * g + 1)
        ],
        axis=1,
    )


def put_pair(field, g, value):
    for b in range(8):
        for half in range(2):
            rows = slice((2 * g + half) * 32, (2 * g + half) * 32 + 32)
            field[b, rows, :] = value[b * 32 : b * 32 + 32, half * 128 : half * 128 + 128]


def middle(start, spread_mid, folded, turned, flipped, parts):
    mask = same_block(256, 32)
    for brick in range(8):
        rows = spread_mid[brick * 32 : brick * 32 + 32]
        line = jnp.where(mask, jnp.concatenate([rows] * 8, axis=0), 0.0).astype(BF16)
        block = start[brick * 32 : brick * 32 + 32, :]
        block = jnp.concatenate([block[:, g * 256 : g * 256 + 256] for g in range(4)], axis=0)
        held = jnp.concatenate(halves(block)[:parts], axis=0)
        both = mm(held, line, NT if flipped else NN)
        swap_brick(both if parts == 1 else both[:128] + both[128:], folded, turned, brick, parts)


def middle_and_last(start, spread_mid, last, folded, turned, flipped, parts=2):
    middle(start, spread_mid, folded, turned, flipped, parts)
    last = jnp.concatenate([last] * parts, axis=1)
    for g in range(4):
        yield g, mm(last, turned[0 : parts * 256, g * 256 : g * 256 + 256]).astype(BF16)


def slot_numbers(route, step):
    own = [route[step, 0, 0, b] for b in range(8)]
    slots = []
    for b in range(8):
        rank = jnp.int32(0)
        for other in range(b):
            rank = rank + (own[other] == own[b]).astype(jnp.int32)
        slots.append((own[b], rank))
    return slots


def fetch(source, target, sem):
    copy = pltpu.make_async_copy(source, target, sem)
    copy.start()
    return copy


def put_pieces(stage, g, value, rows):
    parts = 32 // rows
    for half in range(2):
        tile = value[:, half * 128 : half * 128 + 128]
        for part in range(parts):
            share = (2 * g + half) * parts + part
            if parts == 1:
                stage[share] = tile
            else:
                for b in range(8):
                    at = b * 32 + part * rows
                    stage[share, b * rows : b * rows + rows, :] = tile[at : at + rows]


def send_pieces(stage, send, base, g, sem):
    count = stage.shape[0] // 4
    shares = slice(g * count, g * count + count)
    return fetch(stage.at[shares], send.at[shares, base : base + stage.shape[1], :], sem)


def pieces_pair(pieces, kind, g, rows):
    parts = 32 // rows
    base = kind * 8 * rows
    tiles = []
    for tile in (2 * g, 2 * g + 1):
        if parts == 1:
            tiles.append(pieces[tile, base : base + 256, :])
        else:
            tiles.append(
                jnp.concatenate(
                    [
                        pieces[tile * parts + part, base + b * rows : base + b * rows + rows, :]
                        for b in range(8)
                        for part in range(parts)
                    ],
                    axis=0,
                )
            )
    return jnp.concatenate(tiles, axis=1)


def target_kernel(picks_in, route_in, brick_in, target, send, *refs):
    picks, route, landing, field, stage, meta, meta_half, sems = refs
    told = [
        fetch(source, place, sems.at[index])
        for index, (source, place) in enumerate(((picks_in, picks), (route_in, route), (brick_in, landing)))
    ]
    load = fetch(target, field, sems.at[3])
    for copy in told:
        copy.wait()
    lane = iota((1, 128), 1)
    meta[...] = jnp.zeros(meta.shape, F32)
    value = jnp.zeros((1, 128), jnp.int32)
    for b in range(8):
        for step in range(STEPS):
            code = route[step, 0, 0, b] * 8 + landing[step, 0, 0, b]
            value = jnp.where(lane == 2 * b + step, code, value)
        meta[8 + b : 9 + b, :] = jnp.full((1, 128), picks[1, 0, 0, b], jnp.int32).astype(F32)
    meta[0:1, :] = value.astype(F32)
    meta_half[...] = jnp.broadcast_to(meta[...].astype(BF16)[None], meta_half.shape)
    shared = stage.shape[1]
    sent = [fetch(meta_half, send.at[:, shared : shared + 16, :], sems.at[4])]
    load.wait()
    for g in range(4):
        block = jnp.concatenate(
            [field[qh * 8 + qs] for qs in (2 * g, 2 * g + 1) for qh in range(4)], axis=0
        )
        put_pieces(stage, g, mm(identity(), block, NT).astype(BF16), shared // 8)
        sent.append(send_pieces(stage, send, 0, g, sems.at[5 + g]))
    for copy in sent:
        copy.wait()


def first_kernel(picks, operators, field, sent, moved_out, tables, table_mem, field_mem, start, folded, turned, tables_mem, sems):
    loads = [fetch(operators, table_mem, sems.at[0]), fetch(field, field_mem, sems.at[1])]
    chosen = on_lanes([picks[0, 0, 0, b] for b in range(8)])
    loads[0].wait()
    found = [table_rows(table_mem, chosen, axis) for axis in range(3)]
    for axis in range(3):
        tables_mem[axis] = found[axis].astype(BF16)
    kept = fetch(tables_mem, tables, sems.at[0])
    begin = diagonal(found[2])
    loads[1].wait()
    for g in range(4):
        block = jnp.concatenate(
            [field_mem[qh * 8 + qs] for qs in (2 * g, 2 * g + 1) for qh in range(4)], axis=0
        )
        start[:, g * 256 : g * 256 + 256] = mm(begin, block, NT)
    for g, moved in middle_and_last(start, spread(found[1]), diagonal(found[0]), folded, turned, False):
        put_pair(moved_out, g, moved)
    kept.wait()


def second_kernel(route, landing, operators, moved, arrived, *refs):
    send, tables, codes_out, meta, codes, start, folded, turned, stage, tables_mem, sems, slot_sems = refs
    shared = stage.shape[1]
    sent = []
    for b, (place, rank) in enumerate(slot_numbers(route, 0)):
        rows = pl.ds(pl.multiple_of(rank * 256, 256), 256)
        sent.append(fetch(moved.at[b], send.at[place, rows, :], slot_sems.at[b]))
    meta[...] = arrived[:, shared : shared + 16, :].astype(F32)
    for source in range(meta.shape[0]):
        codes[source : source + 1, :] = meta[source, 0:1, :].astype(jnp.int32)
    sent.append(fetch(codes, codes_out, sems.at[0]))
    lane = iota((1, 128), 1) // 32
    chosen = []
    for part in range(2):
        row = jnp.zeros((1, 128), F32)
        for b in range(4):
            own = part * 4 + b
            found = meta[route[0, 0, 0, own], pl.ds(8 + landing[0, 0, 0, own], 1), :]
            row = jnp.where(lane == b, found, row)
        chosen.append(row)
    chosen = jnp.concatenate(chosen, axis=1).astype(jnp.int32)
    found = [table_rows(operators, chosen, axis) for axis in range(3)]
    for axis in range(3):
        tables_mem[axis] = found[axis].astype(BF16)
    sent.append(fetch(tables_mem, tables, sems.at[1]))
    begin = diagonal(found[0])
    for g in range(4):
        start[:, g * 256 : g * 256 + 256] = mm(begin, lane_pair(moved, g))
    for g, value in middle_and_last(start, spread(found[1]), diagonal(found[2]), folded, turned, False, 1):
        put_pieces(stage, g, value, shared // 8)
        sent.append(send_pieces(stage, send, 512, g, sems.at[2 + g]))
    for copy in sent:
        copy.wait()


def share_kernel(plan_in, arrived, targets, send, plan, total, stage, sems, chunk_sems):
    peers, shared = total.shape[0], total.shape[1]
    rows = shared // 8
    load = fetch(plan_in, plan, sems.at[0])
    total[...] = jnp.zeros(total.shape, F32)
    load.wait()

    def add(source, carry):
        for b in range(8):
            final = plan[source, 8 + b]
            place = pl.ds(pl.multiple_of((final & 7) * rows, rows), rows)
            at = 512 + b * rows
            total[final >> 3, place, :] += arrived[source, at : at + rows, :].astype(F32)
        return carry

    lax.fori_loop(0, peers, add, 0)
    for source in range(peers):
        final = total[source].astype(BF16).astype(F32)
        stage[source, 0:shared, :] = (final - targets[source, 0:shared, :].astype(F32)).astype(BF16)
    sent = []
    for source in range(peers):
        for b in range(8):
            code = plan[source, b]
            place = pl.ds(pl.multiple_of((code & 7) * rows, rows), rows)
            stage[source, shared + b * rows : shared + b * rows + rows, :] = stage[code >> 3, place, :]
        sent.append(fetch(stage.at[source], send.at[source], chunk_sems.at[source]))
    for copy in sent:
        copy.wait()


def composed_kernel(plan_in, shares, edge, send, plan, own, stage, sems):
    peers, shared = own.shape[0], own.shape[1]
    rows = shared // 8
    loads = [fetch(plan_in, plan, sems.at[0]), fetch(shares.at[:, 0:shared, :], own, sems.at[1])]
    for load in loads:
        load.wait()

    def give(source, carry):
        for b in range(8):
            code = plan[source, 8 + b]
            place = pl.ds(pl.multiple_of((code & 7) * rows, rows), rows)
            stage[source, b * rows : b * rows + rows, :] = own[code >> 3, place, :]
        return carry

    lax.fori_loop(0, peers, give, 0)
    fetch(stage, send, sems.at[0]).wait()


def adjoint_kernel(tables_in, arrived, *refs):
    adjoint, tables, start, folded, turned, sems = refs
    load = fetch(tables_in, tables, sems.at[0])
    rows = arrived.shape[1] // 16
    load.wait()
    begin = flipped_diagonal(tables[2].astype(F32))
    mid = spread(tables[1].astype(F32))
    end = flipped_diagonal(tables[0].astype(F32))
    for g in range(4):
        start[:, g * 256 : g * 256 + 256] = mm(begin, pieces_pair(arrived, 1, g, rows))
    for g, moved in middle_and_last(start, mid, end, folded, turned, True):
        put_pair(adjoint, g, moved)


def final_kernel(tables_far, tables_zero, gradient, arrived, *refs):
    adjoint, start, folded, turned, later, field, quarter_sems = refs
    rows = arrived.shape[1] // 8
    begin = flipped_diagonal(tables_far[2].astype(F32))
    mid = spread(tables_far[1].astype(F32))
    end = flipped_diagonal(tables_far[0].astype(F32))
    for g in range(4):
        start[:, g * 256 : g * 256 + 256] = mm(begin, pieces_pair(arrived, 0, g, rows))
    for g, moved in middle_and_last(start, mid, end, folded, turned, True, 1):
        put_pair(later, g, moved)
    begin = flipped_diagonal(tables_zero[0].astype(F32))
    mid = spread(tables_zero[1].astype(F32))
    end = diagonal(tables_zero[2].astype(F32))
    for g in range(4):
        start[:, g * 256 : g * 256 + 256] = mm(begin, lane_pair(later, g))
    stored = []
    middle(start, mid, folded, turned, True, 1)
    for g in range(4):
        flat = mm(turned[0:256, g * 256 : g * 256 + 256], end, TN).astype(BF16)
        for index in range(8):
            field[(index % 4) * 8 + 2 * g + index // 4] = flat[index * 32 : index * 32 + 32]
        for qh in range(4):
            at = slice(qh * 8 + 2 * g, qh * 8 + 2 * g + 2)
            stored.append(fetch(field.at[at], adjoint.at[at], quarter_sems.at[g, qh]))
    for copy in stored:
        copy.wait()


def to_native(block, g, field):
    flat = mm(identity(), block, NT).astype(field.dtype)
    for index in range(8):
        x = (index % 4) * 8 + 2 * g + index // 4
        field[x] = flat[index * 32 : index * 32 + 32]


def x_form_to_native(source, folded, turned, field):
    for b in range(8):
        block = source[b].astype(F32)
        block = jnp.concatenate(
            [
                jnp.concatenate([block[g * 64 : g * 64 + 32], block[g * 64 + 32 : g * 64 + 64]], axis=1)
                for g in range(4)
            ],
            axis=0,
        )
        swap_brick(block, folded, turned, b, 1)
    for g in range(4):
        to_native(turned[0:256, g * 256 : g * 256 + 256], g, field)


def tap(offset):
    value = jnp.zeros(offset.shape, F32)
    for step, weight in TAPS:
        value = jnp.where(offset == step, weight, value)
        value = jnp.where(offset == -step, -weight, value)
    return value


def stencils():
    size = 256
    row, col = iota((size, size), 0), iota((size, size), 1)
    along_y = halves(jnp.where(row // 32 == col // 32, tap(col - row), 0.0))
    along_z = halves(tap(row - col))
    row, col = iota((size, 48), 0), iota((size, 48), 1)
    layer = col // 8
    place = jnp.where(layer < RIM, layer - RIM, layer - RIM + 32)
    rim_y = halves(jnp.where(row // 32 == col % 8, tap(place - row % 32), 0.0))
    return along_y, rim_y, along_z


def rim_picker():
    row, col = iota((48, 256), 0), iota((48, 256), 1)
    layer = row // 8
    place = jnp.where(layer < RIM, layer, layer - RIM + 29)
    return ((row % 8 == col // 32) & (place == col % 32)).astype(F32).astype(BF16)


def difference_x(padded, g):
    total = None
    for step, weight in TAPS:
        ahead = padded[pl.ds(8 * g + RIM + step, 8)]
        behind = padded[pl.ds(8 * g + RIM - step, 8)]
        term = weight * (ahead - behind)
        total = term if total is None else total + term
    return total.reshape(256, 256)


def difference_y(parts, rims, along_y, rim_y):
    total = mm(along_y[0], parts[0]) + mm(along_y[1], parts[0])
    if len(parts) > 1:
        total = total + mm(along_y[0], parts[1])
    return total + mm(rim_y[0], rims) + mm(rim_y[1], rims)


def difference_z(parts, along_z):
    total = mm(parts[0], along_z[0]) + mm(parts[0], along_z[1])
    if len(parts) > 1:
        total = total + mm(parts[1], along_z[0])
    return total


def rim_rows(before, after, base, g):
    rows = [before[base + h, (g // 2) * 16 : (g // 2) * 16 + 16, :].astype(F32) for h in range(RIM)]
    rows += [after[base + h, (g // 2) * 16 : (g // 2) * 16 + 16, :].astype(F32) for h in range(RIM)]
    half = (g % 2) * 8
    return jnp.concatenate([value[half : half + 8] for value in rows], axis=0).astype(BF16)


def put_rims(blocks, base, low_y, high_y):
    picker = rim_picker()
    for pair in range(2):
        left, right = mm(picker, blocks[2 * pair]), mm(picker, blocks[2 * pair + 1])
        for layer in range(2 * RIM):
            value = jnp.concatenate(
                [left[layer * 8 : layer * 8 + 8], right[layer * 8 : layer * 8 + 8]], axis=0
            ).astype(BF16)
            target = low_y if layer < RIM else high_y
            target[base + layer % RIM, pair * 16 : pair * 16 + 16, :] = value


def edge_kernel(template, velocity, sent, low_x, high_x, low_y, high_y, field, first_x, last_x, mid_v, sems):
    loads = [
        fetch(template, field, sems.at[0]),
        fetch(velocity.at[0, 0:RIM], first_x, sems.at[1]),
        fetch(velocity.at[0, 29:32], last_x, sems.at[2]),
        fetch(velocity.at[1], mid_v, sems.at[3]),
    ]
    for load in loads:
        load.wait()
    low_x[0:RIM] = field[0:RIM]
    high_x[0:RIM] = field[29:32]
    low_x[RIM : 2 * RIM] = first_x[...].astype(BF16)
    high_x[RIM : 2 * RIM] = last_x[...].astype(BF16)
    put_rims([field[8 * g : 8 * g + 8].reshape(256, 256) for g in range(4)], 0, low_y, high_y)
    put_rims([mid_v[8 * g : 8 * g + 8].astype(BF16).reshape(256, 256) for g in range(4)], RIM, low_y, high_y)


def prepare_kernel(picks, codes_in, operators, edge, tables, plan_out, codes, plan, sems):
    load = fetch(codes_in, codes, sems.at[0])
    chosen = on_lanes([picks[1, 0, 0, b] for b in range(8)])
    for axis in range(3):
        tables[axis] = table_rows(operators, chosen, axis).astype(BF16)
    load.wait()

    def row(source, carry):
        for b in range(8):
            first = codes[source, 2 * b]
            plan[source, b] = codes[source, 2 * b + 1]
            plan[source, 8 + b] = codes[first >> 3, 2 * (first & 7) + 1]
        return carry

    lax.fori_loop(0, codes.shape[0], row, 0)
    fetch(plan, plan_out, sems.at[0]).wait()


def divergence_kernel(velocity, before_x, after_x, before_y, after_y, sent, divergence, padded):
    along_y, rim_y, along_z = stencils()
    padded[0:RIM] = before_x[RIM : 2 * RIM].astype(F32)
    padded[RIM : RIM + 32] = velocity[0]
    padded[RIM + 32 : 2 * RIM + 32] = after_x[RIM : 2 * RIM].astype(F32)
    for g in range(4):
        along_one = halves(velocity[1, 8 * g : 8 * g + 8].reshape(256, 256))
        along_two = halves(velocity[2, 8 * g : 8 * g + 8].reshape(256, 256))
        total = (
            difference_x(padded, g)
            + difference_y(along_one, rim_rows(before_y, after_y, RIM, g), along_y, rim_y)
            + difference_z(along_two, along_z)
        )
        divergence[8 * g : 8 * g + 8] = total.reshape(8, 32, 256)


def rims_kernel(codes_in, arrived, divergence, sent, native, low_x, high_x, low_y, high_y, codes, slots, total, state, folded, turned, sems):
    loads = [fetch(codes_in, codes, sems.at[0]), fetch(arrived.at[:, 0:512, :], slots, sems.at[1])]
    total[...] = jnp.zeros(total.shape, F32)
    for load in loads:
        load.wait()
    me = lax.axis_index("gx")

    def add(source, carry):
        rank = jnp.int32(0)
        for b in range(8):
            code = codes[source, 2 * b]
            hit = (code >> 3) == me

            @pl.when(hit)
            def _():
                place = pl.ds(pl.multiple_of(rank * 256, 256), 256)
                total[code & 7] += slots[source, place, :].astype(F32)

            rank = rank + hit.astype(jnp.int32)
        return carry

    lax.fori_loop(0, slots.shape[0], add, 0)
    for b in range(8):
        state[b] = total[b].astype(BF16)
    x_form_to_native(state, folded, turned, native)
    low_x[0:RIM] = native[0:RIM]
    high_x[0:RIM] = native[29:32]
    low_x[RIM : 2 * RIM] = divergence[0:RIM].astype(BF16)
    high_x[RIM : 2 * RIM] = divergence[29:32].astype(BF16)
    put_rims([native[8 * g : 8 * g + 8].reshape(256, 256) for g in range(4)], 0, low_y, high_y)
    put_rims(
        [divergence[8 * g : 8 * g + 8].astype(BF16).reshape(256, 256) for g in range(4)], RIM, low_y, high_y
    )


def gradient_kernel(
    template,
    state,
    divergence,
    adjoint_two,
    adjoint_one,
    b0x,
    a0x,
    b0y,
    a0y,
    b1x,
    a1x,
    b1y,
    a1y,
    gradient,
    folded,
    turned,
    weight_two,
    weight_one,
    pad_zero,
    pad_one,
    pad_div,
):
    x_form_to_native(adjoint_one, folded, turned, weight_one)
    for g in range(4):
        to_native(pieces_pair(adjoint_two, 0, g, adjoint_two.shape[1] // 16), g, weight_two)
    along_y, rim_y, along_z = stencils()
    for padded, before, middle, after, base in (
        (pad_zero, b0x, template, a0x, 0),
        (pad_one, b1x, state, a1x, 0),
        (pad_div, b1x, divergence, a1x, RIM),
    ):
        padded[0:RIM] = before[base : base + RIM].astype(F32)
        padded[RIM : RIM + 32] = middle[...].astype(F32)
        padded[RIM + 32 : 2 * RIM + 32] = after[base : base + RIM].astype(F32)
    for g in range(4):
        zero = (template[8 * g : 8 * g + 8].reshape(256, 256),)
        one = (state[8 * g : 8 * g + 8].reshape(256, 256),)
        div = halves(divergence[8 * g : 8 * g + 8].reshape(256, 256))
        weigh_one = 0.5 * weight_one[8 * g : 8 * g + 8].reshape(256, 256)
        weigh_two = 0.5 * weight_two[8 * g : 8 * g + 8].reshape(256, 256)
        for axis in range(3):
            if axis == 0:
                parts = [difference_x(padded, g) for padded in (pad_zero, pad_one, pad_div)]
            elif axis == 1:
                parts = [
                    difference_y(zero, rim_rows(b0y, a0y, 0, g), along_y, rim_y),
                    difference_y(one, rim_rows(b1y, a1y, 0, g), along_y, rim_y),
                    difference_y(div, rim_rows(b1y, a1y, RIM, g), along_y, rim_y),
                ]
            else:
                parts = [difference_z(value, along_z) for value in (zero, one, div)]
            value = weigh_one * parts[0] + weigh_two * parts[1] - 0.25 * parts[2]
            gradient[axis, 8 * g : 8 * g + 8] = value.reshape(8, 32, 256)


SCALAR = pl.BlockSpec(memory_space=pltpu.SMEM)
WHOLE = pl.BlockSpec(memory_space=pltpu.VMEM)
NEAR = pl.BlockSpec(memory_space=pltpu.VMEM)
ANYWHERE = pl.BlockSpec(memory_space=pl.ANY)
FAR = pl.BlockSpec(memory_space=pltpu.HBM)
FOLDED = (32, 64, 128)
FLAT = (256, 1024)
NATIVE = (32, 32, 256)
FORM = (8, 256, 128)
TABLES = (3, 32, 256)


def pinned(value, spec):
    if spec is FAR:
        return pltpu.with_memory_space_constraint(value, pltpu.HBM)
    if spec is NEAR:
        return pltpu.with_memory_space_constraint(value, pltpu.VMEM)
    return value


SHORT, LONG = 1 << 20, 1 << 36


def call(kernel, out, in_specs, out_specs, scratch, work=LONG):
    made = pl.pallas_call(
        kernel,
        out_shape=out,
        in_specs=in_specs,
        out_specs=out_specs,
        scratch_shapes=scratch,
        compiler_params=pltpu.CompilerParams(vmem_limit_bytes=24 * 1024 * 1024),
        cost_estimate=pl.CostEstimate(flops=work, bytes_accessed=1024 * 1024, transcendentals=0),
    )

    def apply(*values):
        return made(*[pinned(value, spec) for value, spec in zip(values, in_specs, strict=True)])

    return apply


def like(shape, dtype):
    return jax.ShapeDtypeStruct(shape, dtype)


def far(shape, dtype):
    return pltpu.HBM(shape, dtype)


def neighbours(low_x, high_x, low_y, high_y):
    moved = []
    for low, high, axis in ((low_x, high_x, "gx"), (low_y, high_y, "gy")):
        size = lax.axis_size(axis)
        up = [(i, i + 1) for i in range(size - 1)]
        down = [(i + 1, i) for i in range(size - 1)]
        moved += [lax.ppermute(high, axis, up), lax.ppermute(low, axis, down)]
    return moved


def swap_slots(send):
    return lax.all_to_all(send, "gx", split_axis=0, concat_axis=0, tiled=True)


def shards(template, target_image, velocity, operators, route, target_brick, operator_index):
    peers = lax.axis_size("gx")
    shared = 8 * (256 // peers)
    sems = pltpu.SemaphoreType.DMA((16,))
    quarter_sems = pltpu.SemaphoreType.DMA((4, 4))
    turning = [pltpu.VMEM(FLAT, F32), pltpu.VMEM(FOLDED, F32), pltpu.VMEM((512, 1024), BF16)]
    form = pltpu.VMEM(FORM, BF16)
    tables = pltpu.VMEM(TABLES, BF16)
    routes_mem = pltpu.SMEM((peers, 128), jnp.int32)
    stage = pltpu.VMEM((peers, shared, 128), BF16)
    meta_half = pltpu.VMEM((peers, 16, 128), BF16)
    table_rows_count = operators.shape[1] * operators.shape[2] * operators.shape[3]
    listed = operators.transpose(1, 2, 3, 0).reshape(table_rows_count, operators.shape[0])
    listed_mem = pltpu.VMEM(listed.shape, BF16)
    route = route.reshape(route.shape[:4])

    send = call(
        target_kernel,
        far((peers, shared + 16, 128), BF16),
        [FAR] * 4,
        FAR,
        [pltpu.SMEM(route.shape, jnp.int32)] * 3
        + [pltpu.VMEM(NATIVE, BF16), stage, pltpu.VMEM((16, 128), F32), meta_half, sems],
        SHORT,
    )(operator_index, route, target_brick, target_image)
    targets = swap_slots(send)

    moved, tables_zero = call(
        first_kernel,
        [like(FORM, BF16), far(TABLES, BF16)],
        [SCALAR, FAR, FAR, FAR],
        [WHOLE, FAR],
        [listed_mem, pltpu.VMEM(NATIVE, BF16)] + turning + [tables, sems],
    )(operator_index, listed, template, send)
    send, tables_far, codes = call(
        second_kernel,
        [far((peers, 512 + shared, 128), BF16), far(TABLES, BF16), far((peers, 128), jnp.int32)],
        [SCALAR, SCALAR, WHOLE, WHOLE, WHOLE],
        [FAR] * 3,
        [pltpu.VMEM((peers, 16, 128), F32), pltpu.VMEM((peers, 128), jnp.int32)]
        + turning
        + [stage, tables, sems, pltpu.SemaphoreType.DMA((8,))],
        SHORT,
    )(route, target_brick, listed, moved, targets)
    arrived = swap_slots(send)

    rim = like((2 * RIM, 32, 256), BF16)
    low_x, high_x, low_y, high_y = call(
        edge_kernel,
        [rim] * 4,
        [FAR] * 3,
        [WHOLE] * 4,
        [pltpu.VMEM(NATIVE, BF16)] + [pltpu.VMEM((RIM, 32, 256), F32)] * 2 + [pltpu.VMEM(NATIVE, F32), sems],
    )(template, velocity, send)
    tables_one, plan = call(
        prepare_kernel,
        [far(TABLES, BF16), far((peers, 128), jnp.int32)],
        [SCALAR, FAR, WHOLE, WHOLE],
        [WHOLE, FAR],
        [routes_mem, routes_mem, sems],
    )(operator_index, codes, listed, low_x)
    b0x, a0x, b0y, a0y = neighbours(low_x, high_x, low_y, high_y)

    send = call(
        share_kernel,
        far((peers, 2 * shared, 128), BF16),
        [FAR, WHOLE, WHOLE],
        FAR,
        [routes_mem, pltpu.VMEM((peers, shared, 128), F32), pltpu.VMEM((peers, 2 * shared, 128), BF16)]
        + [sems, pltpu.SemaphoreType.DMA((peers,))],
        SHORT,
    )(plan, arrived, targets)
    pulled = swap_slots(send)

    divergence = call(
        divergence_kernel, like(NATIVE, F32), [WHOLE] * 5 + [FAR], WHOLE, [pltpu.VMEM((38, 32, 256), F32)]
    )(velocity, b0x, a0x, b0y, a0y, send)
    state, low_x, high_x, low_y, high_y = call(
        rims_kernel,
        [like(NATIVE, BF16)] + [rim] * 4,
        [FAR, ANYWHERE, WHOLE, FAR],
        [WHOLE] * 5,
        [routes_mem, pltpu.VMEM((peers, 512, 128), BF16), pltpu.VMEM(FORM, F32), form] + turning[1:] + [sems],
    )(codes, arrived, divergence, send)
    b1x, a1x, b1y, a1y = neighbours(low_x, high_x, low_y, high_y)
    composed = call(
        composed_kernel, far((peers, shared, 128), BF16), [FAR, FAR, WHOLE], FAR, [routes_mem, stage, stage, sems]
    )(plan, send, low_x)

    composed = swap_slots(composed)

    adjoint_one = call(
        adjoint_kernel, like(FORM, BF16), [FAR, NEAR], WHOLE, [tables] + turning + [sems]
    )(tables_one, pulled)
    gradient = call(
        gradient_kernel,
        far((3,) + NATIVE, F32),
        [WHOLE] * 13,
        WHOLE,
        turning[1:] + [pltpu.VMEM(NATIVE, F32)] * 2 + [pltpu.VMEM((38, 32, 256), F32)] * 3,
    )(template, state, divergence, pulled, adjoint_one, b0x, a0x, b0y, a0y, b1x, a1x, b1y, a1y)

    adjoint = call(
        final_kernel,
        far(NATIVE, BF16),
        [WHOLE, WHOLE, FAR, NEAR],
        FAR,
        turning + [form, pltpu.VMEM(NATIVE, BF16), quarter_sems],
        SHORT,
    )(tables_far, tables_zero, gradient, composed)
    return gradient, adjoint


def solution(mesh):
    placed = (
        P("gx", "gy", None),
        P("gx", "gy", None),
        P(None, "gx", "gy", None),
        P(),
        P(None, "gx", "gy", None, None),
        P(None, "gx", "gy", None),
        P(None, "gx", "gy", None),
    )
    return jax.shard_map(
        shards,
        mesh=mesh,
        in_specs=placed,
        out_specs=(P(None, "gx", "gy", None), P("gx", "gy", None)),
        check_vma=False,
    )
```

```python
import functools

import jax
import jax.numpy as jnp
from jax import lax
from jax.experimental import pallas as pl
from jax.experimental.pallas import tpu as pltpu
from jax.sharding import PartitionSpec as P

STEPS = 2
CAP = 2
RIM = 3
F32 = jnp.float32
BF16 = jnp.bfloat16
NT = (((1,), (1,)), ((), ()))
NN = (((1,), (0,)), ((), ()))
TN = (((0,), (0,)), ((), ()))
TAPS = ((1, 0.75), (2, -0.15), (3, 1.0 / 60.0))


def iota(shape, dim):
    return lax.broadcasted_iota(jnp.int32, shape, dim)


def mm(left, right, dims=NN):
    return lax.dot_general(left, right, dims, preferred_element_type=F32)


def halves(value):
    high = value.astype(BF16)
    return high, (value - high.astype(F32)).astype(BF16)


def on_lanes(picks):
    lane = iota((1, 256), 1)
    chosen = jnp.zeros(lane.shape, jnp.int32)
    for b, pick in enumerate(picks):
        chosen = jnp.where(lane // 32 == b, pick, chosen)
    return chosen


def table_rows(operators, chosen, axis):
    shape = (operators.shape[1], 256)
    one_hot = (iota(shape, 0) == jnp.broadcast_to(chosen, shape)).astype(F32).astype(BF16)
    found = mm(operators[axis * 1024 : axis * 1024 + 1024, :], one_hot)
    within = iota((32, 256), 1) % 32
    total = jnp.zeros((32, 256), F32)
    for x in range(32):
        total = jnp.where(within == x, found[x * 32 : x * 32 + 32], total)
    return total


def same_block(size, edge):
    return iota((size, size), 0) // edge == iota((size, size), 1) // edge


def identity():
    return (iota((256, 256), 0) == iota((256, 256), 1)).astype(F32).astype(BF16)


def flipped_diagonal(table):
    return jnp.where(same_block(256, 32), jnp.concatenate([table] * 8, axis=0), 0.0).astype(BF16)


def diagonal(table):
    return mm(identity(), flipped_diagonal(table), NT).astype(BF16)


def spread(table):
    copies = (iota((256, 256), 0) % 32 == iota((256, 256), 1) % 32).astype(F32).astype(BF16)
    return mm(flipped_diagonal(table), copies)


def swap_chunks(parts):
    lane = iota(parts[0].shape, 1)
    for bit, shift in ((1, 32), (2, 64)):
        keep = (lane & shift) == 0
        fresh = list(parts)
        for index in range(4):
            if index & bit:
                continue
            one, two = parts[index], parts[index | bit]
            fresh[index] = jnp.where(keep, one, pltpu.roll(two, shift, 1))
            fresh[index | bit] = jnp.where(keep, pltpu.roll(one, 128 - shift, 1), two)
        parts = fresh
    return parts


def swap_brick(block, folded, turned, brick, parts=2):
    slabs = []
    for ph in range(4):
        slabs.append(
            jnp.concatenate(
                [
                    block[(qs // 2) * 32 + ph * 8 : (qs // 2) * 32 + ph * 8 + 8, (qs % 2) * 128 : (qs % 2) * 128 + 128]
                    for qs in range(8)
                ],
                axis=0,
            )
        )
    slabs = swap_chunks(slabs)
    for qh in range(4):
        folded[brick * 4 + qh] = slabs[qh]
    for ps in range(8):
        value = jnp.concatenate(
            [folded[brick * 4 + qh, pl.ds(ps, 8, stride=8), :] for qh in range(4)], axis=0
        )
        for part, half in enumerate(halves(value)[:parts]):
            turned[part * 256 + brick * 32 : part * 256 + brick * 32 + 32, ps * 128 : ps * 128 + 128] = half


def lane_pair(field, g):
    return jnp.concatenate(
        [
            jnp.concatenate([field[b, qs * 32 : qs * 32 + 32, :] for b in range(8)], axis=0)
            for qs in (2 * g, 2 * g + 1)
        ],
        axis=1,
    )


def put_pair(field, g, value):
    for b in range(8):
        for half in range(2):
            rows = slice((2 * g + half) * 32, (2 * g + half) * 32 + 32)
            field[b, rows, :] = value[b * 32 : b * 32 + 32, half * 128 : half * 128 + 128]


def middle(start, spread_mid, folded, turned, flipped, parts):
    mask = same_block(256, 32)
    for brick in range(8):
        rows = spread_mid[brick * 32 : brick * 32 + 32]
        line = jnp.where(mask, jnp.concatenate([rows] * 8, axis=0), 0.0).astype(BF16)
        block = start[brick * 32 : brick * 32 + 32, :]
        block = jnp.concatenate([block[:, g * 256 : g * 256 + 256] for g in range(4)], axis=0)
        held = jnp.concatenate(halves(block)[:parts], axis=0)
        both = mm(held, line, NT if flipped else NN)
        swap_brick(both if parts == 1 else both[:128] + both[128:], folded, turned, brick, parts)


def middle_and_last(start, spread_mid, last, folded, turned, flipped, parts=2):
    middle(start, spread_mid, folded, turned, flipped, parts)
    last = jnp.concatenate([last] * parts, axis=1)
    for g in range(4):
        yield g, mm(last, turned[0 : parts * 256, g * 256 : g * 256 + 256]).astype(BF16)


def slot_numbers(route, step):
    own = [route[step, 0, 0, b] for b in range(8)]
    slots = []
    for b in range(8):
        rank = jnp.int32(0)
        for other in range(b):
            rank = rank + (own[other] == own[b]).astype(jnp.int32)
        slots.append((own[b], rank))
    return slots


def fetch(source, target, sem):
    copy = pltpu.make_async_copy(source, target, sem)
    copy.start()
    return copy


def put_pieces(stage, g, value, rows):
    parts = 32 // rows
    for half in range(2):
        tile = value[:, half * 128 : half * 128 + 128]
        for part in range(parts):
            share = (2 * g + half) * parts + part
            if parts == 1:
                stage[share] = tile
            else:
                for b in range(8):
                    at = b * 32 + part * rows
                    stage[share, b * rows : b * rows + rows, :] = tile[at : at + rows]


def send_pieces(stage, send, base, g, sem):
    count = stage.shape[0] // 4
    shares = slice(g * count, g * count + count)
    return fetch(stage.at[shares], send.at[shares, base : base + stage.shape[1], :], sem)


def pieces_pair(pieces, kind, g, rows):
    parts = 32 // rows
    base = kind * 8 * rows
    tiles = []
    for tile in (2 * g, 2 * g + 1):
        if parts == 1:
            tiles.append(pieces[tile, base : base + 256, :])
        else:
            tiles.append(
                jnp.concatenate(
                    [
                        pieces[tile * parts + part, base + b * rows : base + b * rows + rows, :]
                        for b in range(8)
                        for part in range(parts)
                    ],
                    axis=0,
                )
            )
    return jnp.concatenate(tiles, axis=1)


def target_kernel(picks_in, route_in, brick_in, target, send, *refs):
    picks, route, landing, field, stage, meta, meta_half, sems = refs
    told = [
        fetch(source, place, sems.at[index])
        for index, (source, place) in enumerate(((picks_in, picks), (route_in, route), (brick_in, landing)))
    ]
    load = fetch(target, field, sems.at[3])
    for copy in told:
        copy.wait()
    lane = iota((1, 128), 1)
    meta[...] = jnp.zeros(meta.shape, F32)
    value = jnp.zeros((1, 128), jnp.int32)
    for b in range(8):
        for step in range(STEPS):
            code = route[step, 0, 0, b] * 8 + landing[step, 0, 0, b]
            value = jnp.where(lane == 2 * b + step, code, value)
        meta[8 + b : 9 + b, :] = jnp.full((1, 128), picks[1, 0, 0, b], jnp.int32).astype(F32)
    meta[0:1, :] = value.astype(F32)
    meta_half[...] = jnp.broadcast_to(meta[...].astype(BF16)[None], meta_half.shape)
    shared = stage.shape[1]
    sent = [fetch(meta_half, send.at[:, shared : shared + 16, :], sems.at[4])]
    load.wait()
    for g in range(4):
        block = jnp.concatenate(
            [field[qh * 8 + qs] for qs in (2 * g, 2 * g + 1) for qh in range(4)], axis=0
        )
        put_pieces(stage, g, block.T, shared // 8)
        sent.append(send_pieces(stage, send, 0, g, sems.at[5 + g]))
    for copy in sent:
        copy.wait()


def first_kernel(picks, operators, field, sent, moved_out, tables, table_mem, field_mem, start, folded, turned, tables_mem, sems):
    loads = [fetch(operators, table_mem, sems.at[0]), fetch(field, field_mem, sems.at[1])]
    chosen = on_lanes([picks[0, 0, 0, b] for b in range(8)])
    loads[0].wait()
    found = [table_rows(table_mem, chosen, axis) for axis in range(3)]
    for axis in range(3):
        tables_mem[axis] = found[axis].astype(BF16)
    kept = fetch(tables_mem, tables, sems.at[0])
    begin = diagonal(found[2])
    loads[1].wait()
    for g in range(4):
        block = jnp.concatenate(
            [field_mem[qh * 8 + qs] for qs in (2 * g, 2 * g + 1) for qh in range(4)], axis=0
        )
        start[:, g * 256 : g * 256 + 256] = mm(begin, block, NT)
    for g, moved in middle_and_last(start, spread(found[1]), diagonal(found[0]), folded, turned, False):
        put_pair(moved_out, g, moved)
    kept.wait()


def second_kernel(route, landing, operators, moved, arrived, *refs):
    send, tables, codes_out, meta, codes, start, folded, turned, stage, tables_mem, sems, slot_sems = refs
    shared = stage.shape[1]
    sent = []
    for b, (place, rank) in enumerate(slot_numbers(route, 0)):
        rows = pl.ds(pl.multiple_of(rank * 256, 256), 256)
        sent.append(fetch(moved.at[b], send.at[place, rows, :], slot_sems.at[b]))
    meta[...] = arrived[:, shared : shared + 16, :].astype(F32)
    for source in range(meta.shape[0]):
        codes[source : source + 1, :] = meta[source, 0:1, :].astype(jnp.int32)
    sent.append(fetch(codes, codes_out, sems.at[0]))
    lane = iota((1, 128), 1) // 32
    chosen = []
    for part in range(2):
        row = jnp.zeros((1, 128), F32)
        for b in range(4):
            own = part * 4 + b
            found = meta[route[0, 0, 0, own], pl.ds(8 + landing[0, 0, 0, own], 1), :]
            row = jnp.where(lane == b, found, row)
        chosen.append(row)
    chosen = jnp.concatenate(chosen, axis=1).astype(jnp.int32)
    found = [table_rows(operators, chosen, axis) for axis in range(3)]
    for axis in range(3):
        tables_mem[axis] = found[axis].astype(BF16)
    sent.append(fetch(tables_mem, tables, sems.at[1]))
    begin = diagonal(found[0])
    for g in range(4):
        start[:, g * 256 : g * 256 + 256] = mm(begin, lane_pair(moved, g))
    for g, value in middle_and_last(start, spread(found[1]), diagonal(found[2]), folded, turned, False, 1):
        put_pieces(stage, g, value, shared // 8)
        sent.append(send_pieces(stage, send, 512, g, sems.at[2 + g]))
    for copy in sent:
        copy.wait()


def share_kernel(plan_in, arrived, targets, send, plan, total, stage, sems, chunk_sems):
    peers, shared = total.shape[0], total.shape[1]
    rows = shared // 8
    load = fetch(plan_in, plan, sems.at[0])
    total[...] = jnp.zeros(total.shape, F32)
    load.wait()

    def add(source, carry):
        for b in range(8):
            final = plan[source, 8 + b]
            place = pl.ds(pl.multiple_of((final & 7) * rows, rows), rows)
            at = 512 + b * rows
            total[final >> 3, place, :] += arrived[source, at : at + rows, :].astype(F32)
        return carry

    lax.fori_loop(0, peers, add, 0)
    for source in range(peers):
        final = total[source].astype(BF16).astype(F32)
        stage[source, 0:shared, :] = (final - targets[source, 0:shared, :].astype(F32)).astype(BF16)
    sent = []
    for source in range(peers):
        for b in range(8):
            code = plan[source, b]
            place = pl.ds(pl.multiple_of((code & 7) * rows, rows), rows)
            stage[source, shared + b * rows : shared + b * rows + rows, :] = stage[code >> 3, place, :]
        sent.append(fetch(stage.at[source], send.at[source], chunk_sems.at[source]))
    for copy in sent:
        copy.wait()


def composed_kernel(plan_in, shares, edge, send, plan, own, stage, sems):
    peers, shared = own.shape[0], own.shape[1]
    rows = shared // 8
    loads = [fetch(plan_in, plan, sems.at[0]), fetch(shares.at[:, 0:shared, :], own, sems.at[1])]
    for load in loads:
        load.wait()

    def give(source, carry):
        for b in range(8):
            code = plan[source, 8 + b]
            place = pl.ds(pl.multiple_of((code & 7) * rows, rows), rows)
            stage[source, b * rows : b * rows + rows, :] = own[code >> 3, place, :]
        return carry

    lax.fori_loop(0, peers, give, 0)
    fetch(stage, send, sems.at[0]).wait()


def adjoint_kernel(tables_in, arrived, *refs):
    adjoint, tables, start, folded, turned, sems = refs
    load = fetch(tables_in, tables, sems.at[0])
    rows = arrived.shape[1] // 16
    load.wait()
    begin = flipped_diagonal(tables[2].astype(F32))
    mid = spread(tables[1].astype(F32))
    end = flipped_diagonal(tables[0].astype(F32))
    for g in range(4):
        start[:, g * 256 : g * 256 + 256] = mm(begin, pieces_pair(arrived, 1, g, rows))
    for g, moved in middle_and_last(start, mid, end, folded, turned, True):
        put_pair(adjoint, g, moved)


def final_kernel(tables_far, tables_zero, gradient, arrived, *refs):
    adjoint, start, folded, turned, later, field, quarter_sems = refs
    rows = arrived.shape[1] // 8
    begin = flipped_diagonal(tables_far[2].astype(F32))
    mid = spread(tables_far[1].astype(F32))
    end = flipped_diagonal(tables_far[0].astype(F32))
    for g in range(4):
        start[:, g * 256 : g * 256 + 256] = mm(begin, pieces_pair(arrived, 0, g, rows))
    for g, moved in middle_and_last(start, mid, end, folded, turned, True, 1):
        put_pair(later, g, moved)
    begin = flipped_diagonal(tables_zero[0].astype(F32))
    mid = spread(tables_zero[1].astype(F32))
    end = diagonal(tables_zero[2].astype(F32))
    for g in range(4):
        start[:, g * 256 : g * 256 + 256] = mm(begin, lane_pair(later, g))
    stored = []
    middle(start, mid, folded, turned, True, 1)
    for g in range(4):
        flat = mm(turned[0:256, g * 256 : g * 256 + 256], end, TN).astype(BF16)
        for index in range(8):
            field[(index % 4) * 8 + 2 * g + index // 4] = flat[index * 32 : index * 32 + 32]
        for qh in range(4):
            at = slice(qh * 8 + 2 * g, qh * 8 + 2 * g + 2)
            stored.append(fetch(field.at[at], adjoint.at[at], quarter_sems.at[g, qh]))
    for copy in stored:
        copy.wait()


def to_native(block, g, field):
    flat = block.T.astype(field.dtype)
    for index in range(8):
        x = (index % 4) * 8 + 2 * g + index // 4
        field[x] = flat[index * 32 : index * 32 + 32]


def x_form_to_native(source, folded, turned, field):
    for b in range(8):
        block = source[b].astype(F32)
        block = jnp.concatenate(
            [
                jnp.concatenate([block[g * 64 : g * 64 + 32], block[g * 64 + 32 : g * 64 + 64]], axis=1)
                for g in range(4)
            ],
            axis=0,
        )
        swap_brick(block, folded, turned, b, 1)
    for g in range(4):
        to_native(turned[0:256, g * 256 : g * 256 + 256], g, field)


def tap(offset):
    value = jnp.zeros(offset.shape, F32)
    for step, weight in TAPS:
        value = jnp.where(offset == step, weight, value)
        value = jnp.where(offset == -step, -weight, value)
    return value


def stencils():
    size = 256
    row, col = iota((size, size), 0), iota((size, size), 1)
    along_y = halves(jnp.where(row // 32 == col // 32, tap(col - row), 0.0))
    along_z = halves(tap(row - col))
    row, col = iota((size, 48), 0), iota((size, 48), 1)
    layer = col // 8
    place = jnp.where(layer < RIM, layer - RIM, layer - RIM + 32)
    rim_y = halves(jnp.where(row // 32 == col % 8, tap(place - row % 32), 0.0))
    return along_y, rim_y, along_z


def rim_picker():
    row, col = iota((48, 256), 0), iota((48, 256), 1)
    layer = row // 8
    place = jnp.where(layer < RIM, layer, layer - RIM + 29)
    return ((row % 8 == col // 32) & (place == col % 32)).astype(F32).astype(BF16)


def difference_x(padded, g):
    total = None
    for step, weight in TAPS:
        ahead = padded[pl.ds(8 * g + RIM + step, 8)]
        behind = padded[pl.ds(8 * g + RIM - step, 8)]
        term = weight * (ahead - behind)
        total = term if total is None else total + term
    return total.reshape(256, 256)


def difference_y(parts, rims, along_y, rim_y):
    total = mm(along_y[0], parts[0]) + mm(along_y[1], parts[0])
    if len(parts) > 1:
        total = total + mm(along_y[0], parts[1])
    return total + mm(rim_y[0], rims) + mm(rim_y[1], rims)


def difference_z(parts, along_z):
    total = mm(parts[0], along_z[0]) + mm(parts[0], along_z[1])
    if len(parts) > 1:
        total = total + mm(parts[1], along_z[0])
    return total


def rim_rows(before, after, base, g):
    rows = [before[base + h, (g // 2) * 16 : (g // 2) * 16 + 16, :].astype(F32) for h in range(RIM)]
    rows += [after[base + h, (g // 2) * 16 : (g // 2) * 16 + 16, :].astype(F32) for h in range(RIM)]
    half = (g % 2) * 8
    return jnp.concatenate([value[half : half + 8] for value in rows], axis=0).astype(BF16)


def put_rims(blocks, base, low_y, high_y):
    picker = rim_picker()
    for pair in range(2):
        left, right = mm(picker, blocks[2 * pair]), mm(picker, blocks[2 * pair + 1])
        for layer in range(2 * RIM):
            value = jnp.concatenate(
                [left[layer * 8 : layer * 8 + 8], right[layer * 8 : layer * 8 + 8]], axis=0
            ).astype(BF16)
            target = low_y if layer < RIM else high_y
            target[base + layer % RIM, pair * 16 : pair * 16 + 16, :] = value


def edge_kernel(template, velocity, sent, low_x, high_x, low_y, high_y, field, first_x, last_x, mid_v, sems):
    loads = [
        fetch(template, field, sems.at[0]),
        fetch(velocity.at[0, 0:RIM], first_x, sems.at[1]),
        fetch(velocity.at[0, 29:32], last_x, sems.at[2]),
        fetch(velocity.at[1], mid_v, sems.at[3]),
    ]
    for load in loads:
        load.wait()
    low_x[0:RIM] = field[0:RIM]
    high_x[0:RIM] = field[29:32]
    low_x[RIM : 2 * RIM] = first_x[...].astype(BF16)
    high_x[RIM : 2 * RIM] = last_x[...].astype(BF16)
    put_rims([field[8 * g : 8 * g + 8].reshape(256, 256) for g in range(4)], 0, low_y, high_y)
    put_rims([mid_v[8 * g : 8 * g + 8].astype(BF16).reshape(256, 256) for g in range(4)], RIM, low_y, high_y)


def prepare_kernel(picks, codes_in, operators, edge, tables, plan_out, codes, plan, sems):
    load = fetch(codes_in, codes, sems.at[0])
    chosen = on_lanes([picks[1, 0, 0, b] for b in range(8)])
    for axis in range(3):
        tables[axis] = table_rows(operators, chosen, axis).astype(BF16)
    load.wait()

    def row(source, carry):
        for b in range(8):
            first = codes[source, 2 * b]
            plan[source, b] = codes[source, 2 * b + 1]
            plan[source, 8 + b] = codes[first >> 3, 2 * (first & 7) + 1]
        return carry

    lax.fori_loop(0, codes.shape[0], row, 0)
    fetch(plan, plan_out, sems.at[0]).wait()


def divergence_kernel(velocity, before_x, after_x, before_y, after_y, sent, divergence, padded):
    along_y, rim_y, along_z = stencils()
    padded[0:RIM] = before_x[RIM : 2 * RIM].astype(F32)
    padded[RIM : RIM + 32] = velocity[0]
    padded[RIM + 32 : 2 * RIM + 32] = after_x[RIM : 2 * RIM].astype(F32)
    for g in range(4):
        along_one = halves(velocity[1, 8 * g : 8 * g + 8].reshape(256, 256))
        along_two = halves(velocity[2, 8 * g : 8 * g + 8].reshape(256, 256))
        total = (
            difference_x(padded, g)
            + difference_y(along_one, rim_rows(before_y, after_y, RIM, g), along_y, rim_y)
            + difference_z(along_two, along_z)
        )
        divergence[8 * g : 8 * g + 8] = total.reshape(8, 32, 256)


def rims_kernel(codes_in, arrived, divergence, sent, native, low_x, high_x, low_y, high_y, codes, slots, total, state, folded, turned, sems):
    loads = [fetch(codes_in, codes, sems.at[0]), fetch(arrived.at[:, 0:512, :], slots, sems.at[1])]
    total[...] = jnp.zeros(total.shape, F32)
    for load in loads:
        load.wait()
    me = lax.axis_index("gx")

    def add(source, carry):
        rank = jnp.int32(0)
        for b in range(8):
            code = codes[source, 2 * b]
            hit = (code >> 3) == me

            @pl.when(hit)
            def _():
                place = pl.ds(pl.multiple_of(rank * 256, 256), 256)
                total[code & 7] += slots[source, place, :].astype(F32)

            rank = rank + hit.astype(jnp.int32)
        return carry

    lax.fori_loop(0, slots.shape[0], add, 0)
    for b in range(8):
        state[b] = total[b].astype(BF16)
    x_form_to_native(state, folded, turned, native)
    low_x[0:RIM] = native[0:RIM]
    high_x[0:RIM] = native[29:32]
    low_x[RIM : 2 * RIM] = divergence[0:RIM].astype(BF16)
    high_x[RIM : 2 * RIM] = divergence[29:32].astype(BF16)
    put_rims([native[8 * g : 8 * g + 8].reshape(256, 256) for g in range(4)], 0, low_y, high_y)
    put_rims(
        [divergence[8 * g : 8 * g + 8].astype(BF16).reshape(256, 256) for g in range(4)], RIM, low_y, high_y
    )


def gradient_kernel(
    template,
    state,
    divergence,
    adjoint_two,
    adjoint_one,
    b0x,
    a0x,
    b0y,
    a0y,
    b1x,
    a1x,
    b1y,
    a1y,
    gradient,
    folded,
    turned,
    weight_two,
    weight_one,
    pad_zero,
    pad_one,
    pad_div,
):
    x_form_to_native(adjoint_one, folded, turned, weight_one)
    for g in range(4):
        to_native(pieces_pair(adjoint_two, 0, g, adjoint_two.shape[1] // 16), g, weight_two)
    along_y, rim_y, along_z = stencils()
    for padded, before, middle, after, base in (
        (pad_zero, b0x, template, a0x, 0),
        (pad_one, b1x, state, a1x, 0),
        (pad_div, b1x, divergence, a1x, RIM),
    ):
        padded[0:RIM] = before[base : base + RIM].astype(F32)
        padded[RIM : RIM + 32] = middle[...].astype(F32)
        padded[RIM + 32 : 2 * RIM + 32] = after[base : base + RIM].astype(F32)
    for g in range(4):
        zero = (template[8 * g : 8 * g + 8].reshape(256, 256),)
        one = (state[8 * g : 8 * g + 8].reshape(256, 256),)
        div = halves(divergence[8 * g : 8 * g + 8].reshape(256, 256))
        weigh_one = 0.5 * weight_one[8 * g : 8 * g + 8].reshape(256, 256)
        weigh_two = 0.5 * weight_two[8 * g : 8 * g + 8].reshape(256, 256)
        for axis in range(3):
            if axis == 0:
                parts = [difference_x(padded, g) for padded in (pad_zero, pad_one, pad_div)]
            elif axis == 1:
                parts = [
                    difference_y(zero, rim_rows(b0y, a0y, 0, g), along_y, rim_y),
                    difference_y(one, rim_rows(b1y, a1y, 0, g), along_y, rim_y),
                    difference_y(div, rim_rows(b1y, a1y, RIM, g), along_y, rim_y),
                ]
            else:
                parts = [difference_z(value, along_z) for value in (zero, one, div)]
            value = weigh_one * parts[0] + weigh_two * parts[1] - 0.25 * parts[2]
            gradient[axis, 8 * g : 8 * g + 8] = value.reshape(8, 32, 256)


SCALAR = pl.BlockSpec(memory_space=pltpu.SMEM)
WHOLE = pl.BlockSpec(memory_space=pltpu.VMEM)
NEAR = pl.BlockSpec(memory_space=pltpu.VMEM)
ANYWHERE = pl.BlockSpec(memory_space=pl.ANY)
FAR = pl.BlockSpec(memory_space=pltpu.HBM)
FOLDED = (32, 64, 128)
FLAT = (256, 1024)
NATIVE = (32, 32, 256)
FORM = (8, 256, 128)
TABLES = (3, 32, 256)


def pinned(value, spec):
    if spec is FAR:
        return pltpu.with_memory_space_constraint(value, pltpu.HBM)
    if spec is NEAR:
        return pltpu.with_memory_space_constraint(value, pltpu.VMEM)
    return value


SHORT, LONG = 1 << 20, 1 << 36


def call(kernel, out, in_specs, out_specs, scratch, work=LONG):
    made = pl.pallas_call(
        kernel,
        out_shape=out,
        in_specs=in_specs,
        out_specs=out_specs,
        scratch_shapes=scratch,
        compiler_params=pltpu.CompilerParams(vmem_limit_bytes=24 * 1024 * 1024),
        cost_estimate=pl.CostEstimate(flops=work, bytes_accessed=1024 * 1024, transcendentals=0),
    )

    def apply(*values):
        return made(*[pinned(value, spec) for value, spec in zip(values, in_specs, strict=True)])

    return apply


def like(shape, dtype):
    return jax.ShapeDtypeStruct(shape, dtype)


def far(shape, dtype):
    return pltpu.HBM(shape, dtype)


def neighbours(low_x, high_x, low_y, high_y):
    moved = []
    for low, high, axis in ((low_x, high_x, "gx"), (low_y, high_y, "gy")):
        size = lax.axis_size(axis)
        up = [(i, i + 1) for i in range(size - 1)]
        down = [(i + 1, i) for i in range(size - 1)]
        moved += [lax.ppermute(high, axis, up), lax.ppermute(low, axis, down)]
    return moved


def swap_slots(send):
    return lax.all_to_all(send, "gx", split_axis=0, concat_axis=0, tiled=True)


def shards(template, target_image, velocity, operators, route, target_brick, operator_index):
    peers = lax.axis_size("gx")
    shared = 8 * (256 // peers)
    sems = pltpu.SemaphoreType.DMA((16,))
    quarter_sems = pltpu.SemaphoreType.DMA((4, 4))
    turning = [pltpu.VMEM(FLAT, F32), pltpu.VMEM(FOLDED, F32), pltpu.VMEM((512, 1024), BF16)]
    form = pltpu.VMEM(FORM, BF16)
    tables = pltpu.VMEM(TABLES, BF16)
    routes_mem = pltpu.SMEM((peers, 128), jnp.int32)
    stage = pltpu.VMEM((peers, shared, 128), BF16)
    meta_half = pltpu.VMEM((peers, 16, 128), BF16)
    table_rows_count = operators.shape[1] * operators.shape[2] * operators.shape[3]
    listed = operators.transpose(1, 2, 3, 0).reshape(table_rows_count, operators.shape[0])
    listed_mem = pltpu.VMEM(listed.shape, BF16)
    route = route.reshape(route.shape[:4])

    send = call(
        target_kernel,
        far((peers, shared + 16, 128), BF16),
        [FAR] * 4,
        FAR,
        [pltpu.SMEM(route.shape, jnp.int32)] * 3
        + [pltpu.VMEM(NATIVE, BF16), stage, pltpu.VMEM((16, 128), F32), meta_half, sems],
        SHORT,
    )(operator_index, route, target_brick, target_image)
    targets = swap_slots(send)

    moved, tables_zero = call(
        first_kernel,
        [like(FORM, BF16), far(TABLES, BF16)],
        [SCALAR, FAR, FAR, FAR],
        [WHOLE, FAR],
        [listed_mem, pltpu.VMEM(NATIVE, BF16)] + turning + [tables, sems],
    )(operator_index, listed, template, send)
    send, tables_far, codes = call(
        second_kernel,
        [far((peers, 512 + shared, 128), BF16), far(TABLES, BF16), far((peers, 128), jnp.int32)],
        [SCALAR, SCALAR, WHOLE, WHOLE, WHOLE],
        [FAR] * 3,
        [pltpu.VMEM((peers, 16, 128), F32), pltpu.VMEM((peers, 128), jnp.int32)]
        + turning
        + [stage, tables, sems, pltpu.SemaphoreType.DMA((8,))],
        SHORT,
    )(route, target_brick, listed, moved, targets)
    arrived = swap_slots(send)

    rim = like((2 * RIM, 32, 256), BF16)
    low_x, high_x, low_y, high_y = call(
        edge_kernel,
        [rim] * 4,
        [FAR] * 3,
        [WHOLE] * 4,
        [pltpu.VMEM(NATIVE, BF16)] + [pltpu.VMEM((RIM, 32, 256), F32)] * 2 + [pltpu.VMEM(NATIVE, F32), sems],
    )(template, velocity, send)
    tables_one, plan = call(
        prepare_kernel,
        [far(TABLES, BF16), far((peers, 128), jnp.int32)],
        [SCALAR, FAR, WHOLE, WHOLE],
        [WHOLE, FAR],
        [routes_mem, routes_mem, sems],
    )(operator_index, codes, listed, low_x)
    b0x, a0x, b0y, a0y = neighbours(low_x, high_x, low_y, high_y)

    send = call(
        share_kernel,
        far((peers, 2 * shared, 128), BF16),
        [FAR, WHOLE, WHOLE],
        FAR,
        [routes_mem, pltpu.VMEM((peers, shared, 128), F32), pltpu.VMEM((peers, 2 * shared, 128), BF16)]
        + [sems, pltpu.SemaphoreType.DMA((peers,))],
        SHORT,
    )(plan, arrived, targets)
    pulled = swap_slots(send)

    divergence = call(
        divergence_kernel, like(NATIVE, F32), [WHOLE] * 5 + [FAR], WHOLE, [pltpu.VMEM((38, 32, 256), F32)]
    )(velocity, b0x, a0x, b0y, a0y, send)
    state, low_x, high_x, low_y, high_y = call(
        rims_kernel,
        [like(NATIVE, BF16)] + [rim] * 4,
        [FAR, ANYWHERE, WHOLE, FAR],
        [WHOLE] * 5,
        [routes_mem, pltpu.VMEM((peers, 512, 128), BF16), pltpu.VMEM(FORM, F32), form] + turning[1:] + [sems],
    )(codes, arrived, divergence, send)
    b1x, a1x, b1y, a1y = neighbours(low_x, high_x, low_y, high_y)
    composed = call(
        composed_kernel, far((peers, shared, 128), BF16), [FAR, FAR, WHOLE], FAR, [routes_mem, stage, stage, sems]
    )(plan, send, low_x)

    composed = swap_slots(composed)

    adjoint_one = call(
        adjoint_kernel, like(FORM, BF16), [FAR, NEAR], WHOLE, [tables] + turning + [sems]
    )(tables_one, pulled)
    gradient = call(
        gradient_kernel,
        far((3,) + NATIVE, F32),
        [WHOLE] * 13,
        WHOLE,
        turning[1:] + [pltpu.VMEM(NATIVE, F32)] * 2 + [pltpu.VMEM((38, 32, 256), F32)] * 3,
    )(template, state, divergence, pulled, adjoint_one, b0x, a0x, b0y, a0y, b1x, a1x, b1y, a1y)

    adjoint = call(
        final_kernel,
        far(NATIVE, BF16),
        [WHOLE, WHOLE, FAR, NEAR],
        FAR,
        turning + [form, pltpu.VMEM(NATIVE, BF16), quarter_sems],
        SHORT,
    )(tables_far, tables_zero, gradient, composed)
    return gradient, adjoint


def solution(mesh):
    placed = (
        P("gx", "gy", None),
        P("gx", "gy", None),
        P(None, "gx", "gy", None),
        P(),
        P(None, "gx", "gy", None, None),
        P(None, "gx", "gy", None),
        P(None, "gx", "gy", None),
    )
    return jax.shard_map(
        shards,
        mesh=mesh,
        in_specs=placed,
        out_specs=(P(None, "gx", "gy", None), P("gx", "gy", None)),
        check_vma=False,
    )
```

```python
import functools

import jax
import jax.numpy as jnp
from jax import lax
from jax.experimental import pallas as pl
from jax.experimental.pallas import tpu as pltpu
from jax.sharding import PartitionSpec as P

STEPS = 2
CAP = 2
RIM = 3
F32 = jnp.float32
BF16 = jnp.bfloat16
NT = (((1,), (1,)), ((), ()))
NN = (((1,), (0,)), ((), ()))
TN = (((0,), (0,)), ((), ()))
TAPS = ((1, 0.75), (2, -0.15), (3, 1.0 / 60.0))


def iota(shape, dim):
    return lax.broadcasted_iota(jnp.int32, shape, dim)


def mm(left, right, dims=NN):
    return lax.dot_general(left, right, dims, preferred_element_type=F32)


def halves(value):
    high = value.astype(BF16)
    return high, (value - high.astype(F32)).astype(BF16)


def on_lanes(picks):
    lane = iota((1, 256), 1)
    chosen = jnp.zeros(lane.shape, jnp.int32)
    for b, pick in enumerate(picks):
        chosen = jnp.where(lane // 32 == b, pick, chosen)
    return chosen


def table_rows(operators, chosen, axis):
    shape = (operators.shape[1], 256)
    one_hot = (iota(shape, 0) == jnp.broadcast_to(chosen, shape)).astype(F32).astype(BF16)
    found = mm(operators[axis * 1024 : axis * 1024 + 1024, :], one_hot)
    within = iota((32, 256), 1) % 32
    total = jnp.zeros((32, 256), F32)
    for x in range(32):
        total = jnp.where(within == x, found[x * 32 : x * 32 + 32], total)
    return total


def same_block(size, edge):
    return iota((size, size), 0) // edge == iota((size, size), 1) // edge


def identity():
    return (iota((256, 256), 0) == iota((256, 256), 1)).astype(F32).astype(BF16)


def flipped_diagonal(table):
    return jnp.where(same_block(256, 32), jnp.concatenate([table] * 8, axis=0), 0.0).astype(BF16)


def diagonal(table):
    return mm(identity(), flipped_diagonal(table), NT).astype(BF16)


def spread(table):
    copies = (iota((256, 256), 0) % 32 == iota((256, 256), 1) % 32).astype(F32).astype(BF16)
    return mm(flipped_diagonal(table), copies)


def swap_chunks(parts):
    lane = iota(parts[0].shape, 1)
    for bit, shift in ((1, 32), (2, 64)):
        keep = (lane & shift) == 0
        fresh = list(parts)
        for index in range(4):
            if index & bit:
                continue
            one, two = parts[index], parts[index | bit]
            fresh[index] = jnp.where(keep, one, pltpu.roll(two, shift, 1))
            fresh[index | bit] = jnp.where(keep, pltpu.roll(one, 128 - shift, 1), two)
        parts = fresh
    return parts


def swap_brick(block, folded, turned, brick, parts=2):
    slabs = []
    for ph in range(4):
        slabs.append(
            jnp.concatenate(
                [
                    block[(qs // 2) * 32 + ph * 8 : (qs // 2) * 32 + ph * 8 + 8, (qs % 2) * 128 : (qs % 2) * 128 + 128]
                    for qs in range(8)
                ],
                axis=0,
            )
        )
    slabs = swap_chunks(slabs)
    for qh in range(4):
        folded[brick * 4 + qh] = slabs[qh]
    for ps in range(8):
        value = jnp.concatenate(
            [folded[brick * 4 + qh, pl.ds(ps, 8, stride=8), :] for qh in range(4)], axis=0
        )
        for part, half in enumerate(halves(value)[:parts]):
            turned[part * 256 + brick * 32 : part * 256 + brick * 32 + 32, ps * 128 : ps * 128 + 128] = half


def lane_pair(field, g):
    return jnp.concatenate(
        [
            jnp.concatenate([field[b, qs * 32 : qs * 32 + 32, :] for b in range(8)], axis=0)
            for qs in (2 * g, 2 * g + 1)
        ],
        axis=1,
    )


def put_pair(field, g, value):
    for b in range(8):
        for half in range(2):
            rows = slice((2 * g + half) * 32, (2 * g + half) * 32 + 32)
            field[b, rows, :] = value[b * 32 : b * 32 + 32, half * 128 : half * 128 + 128]


def middle(start, spread_mid, folded, turned, flipped, parts):
    mask = same_block(256, 32)
    for brick in range(8):
        rows = spread_mid[brick * 32 : brick * 32 + 32]
        line = jnp.where(mask, jnp.concatenate([rows] * 8, axis=0), 0.0).astype(BF16)
        block = start[brick * 32 : brick * 32 + 32, :]
        block = jnp.concatenate([block[:, g * 256 : g * 256 + 256] for g in range(4)], axis=0)
        held = jnp.concatenate(halves(block)[:parts], axis=0)
        both = mm(held, line, NT if flipped else NN)
        swap_brick(both if parts == 1 else both[:128] + both[128:], folded, turned, brick, parts)


def middle_and_last(start, spread_mid, last, folded, turned, flipped, parts=2):
    middle(start, spread_mid, folded, turned, flipped, parts)
    last = jnp.concatenate([last] * parts, axis=1)
    for g in range(4):
        yield g, mm(last, turned[0 : parts * 256, g * 256 : g * 256 + 256]).astype(BF16)


def slot_numbers(route, step):
    own = [route[step, 0, 0, b] for b in range(8)]
    slots = []
    for b in range(8):
        rank = jnp.int32(0)
        for other in range(b):
            rank = rank + (own[other] == own[b]).astype(jnp.int32)
        slots.append((own[b], rank))
    return slots


def fetch(source, target, sem):
    copy = pltpu.make_async_copy(source, target, sem)
    copy.start()
    return copy


def put_pieces(stage, g, value, rows):
    parts = 32 // rows
    for half in range(2):
        tile = value[:, half * 128 : half * 128 + 128]
        for part in range(parts):
            share = (2 * g + half) * parts + part
            if parts == 1:
                stage[share] = tile
            else:
                for b in range(8):
                    at = b * 32 + part * rows
                    stage[share, b * rows : b * rows + rows, :] = tile[at : at + rows]


def send_pieces(stage, send, base, g, sem):
    count = stage.shape[0] // 4
    shares = slice(g * count, g * count + count)
    return fetch(stage.at[shares], send.at[shares, base : base + stage.shape[1], :], sem)


def pieces_pair(pieces, kind, g, rows):
    parts = 32 // rows
    base = kind * 8 * rows
    tiles = []
    for tile in (2 * g, 2 * g + 1):
        if parts == 1:
            tiles.append(pieces[tile, base : base + 256, :])
        else:
            tiles.append(
                jnp.concatenate(
                    [
                        pieces[tile * parts + part, base + b * rows : base + b * rows + rows, :]
                        for b in range(8)
                        for part in range(parts)
                    ],
                    axis=0,
                )
            )
    return jnp.concatenate(tiles, axis=1)


def target_kernel(picks_in, route_in, brick_in, target, send, *refs):
    picks, route, landing, field, stage, meta, meta_half, sems = refs
    told = [
        fetch(source, place, sems.at[index])
        for index, (source, place) in enumerate(((picks_in, picks), (route_in, route), (brick_in, landing)))
    ]
    load = fetch(target, field, sems.at[3])
    for copy in told:
        copy.wait()
    lane = iota((1, 128), 1)
    meta[...] = jnp.zeros(meta.shape, F32)
    value = jnp.zeros((1, 128), jnp.int32)
    for b in range(8):
        for step in range(STEPS):
            code = route[step, 0, 0, b] * 8 + landing[step, 0, 0, b]
            value = jnp.where(lane == 2 * b + step, code, value)
        meta[8 + b : 9 + b, :] = jnp.full((1, 128), picks[1, 0, 0, b], jnp.int32).astype(F32)
    meta[0:1, :] = value.astype(F32)
    meta_half[...] = jnp.broadcast_to(meta[...].astype(BF16)[None], meta_half.shape)
    shared = stage.shape[1]
    sent = [fetch(meta_half, send.at[:, shared : shared + 16, :], sems.at[4])]
    load.wait()
    for g in range(4):
        block = jnp.concatenate(
            [field[qh * 8 + qs] for qs in (2 * g, 2 * g + 1) for qh in range(4)], axis=0
        )
        put_pieces(stage, g, block.T, shared // 8)
        sent.append(send_pieces(stage, send, 0, g, sems.at[5 + g]))
    for copy in sent:
        copy.wait()


def first_kernel(picks, operators, field, sent, moved_out, tables, table_mem, field_mem, start, folded, turned, tables_mem, sems):
    loads = [fetch(operators, table_mem, sems.at[0]), fetch(field, field_mem, sems.at[1])]
    chosen = on_lanes([picks[0, 0, 0, b] for b in range(8)])
    loads[0].wait()
    found = [table_rows(table_mem, chosen, axis) for axis in range(3)]
    for axis in range(3):
        tables_mem[axis] = found[axis].astype(BF16)
    kept = fetch(tables_mem, tables, sems.at[0])
    begin = diagonal(found[2])
    loads[1].wait()
    for g in range(4):
        block = jnp.concatenate(
            [field_mem[qh * 8 + qs] for qs in (2 * g, 2 * g + 1) for qh in range(4)], axis=0
        )
        start[:, g * 256 : g * 256 + 256] = mm(begin, block, NT).astype(start.dtype)
    for g, moved in middle_and_last(start, spread(found[1]), diagonal(found[0]), folded, turned, False):
        put_pair(moved_out, g, moved)
    kept.wait()


def second_kernel(route, landing, operators, moved, arrived, *refs):
    send, tables, codes_out, meta, codes, start, folded, turned, stage, tables_mem, sems, slot_sems = refs
    shared = stage.shape[1]
    sent = []
    for b, (place, rank) in enumerate(slot_numbers(route, 0)):
        rows = pl.ds(pl.multiple_of(rank * 256, 256), 256)
        sent.append(fetch(moved.at[b], send.at[place, rows, :], slot_sems.at[b]))
    meta[...] = arrived[:, shared : shared + 16, :].astype(F32)
    for source in range(meta.shape[0]):
        codes[source : source + 1, :] = meta[source, 0:1, :].astype(jnp.int32)
    sent.append(fetch(codes, codes_out, sems.at[0]))
    lane = iota((1, 128), 1) // 32
    chosen = []
    for part in range(2):
        row = jnp.zeros((1, 128), F32)
        for b in range(4):
            own = part * 4 + b
            found = meta[route[0, 0, 0, own], pl.ds(8 + landing[0, 0, 0, own], 1), :]
            row = jnp.where(lane == b, found, row)
        chosen.append(row)
    chosen = jnp.concatenate(chosen, axis=1).astype(jnp.int32)
    found = [table_rows(operators, chosen, axis) for axis in range(3)]
    for axis in range(3):
        tables_mem[axis] = found[axis].astype(BF16)
    sent.append(fetch(tables_mem, tables, sems.at[1]))
    begin = diagonal(found[0])
    for g in range(4):
        start[:, g * 256 : g * 256 + 256] = mm(begin, lane_pair(moved, g)).astype(start.dtype)
    for g, value in middle_and_last(start, spread(found[1]), diagonal(found[2]), folded, turned, False, 1):
        put_pieces(stage, g, value, shared // 8)
        sent.append(send_pieces(stage, send, 512, g, sems.at[2 + g]))
    for copy in sent:
        copy.wait()


def share_kernel(plan, arrived, targets, send, total, stage, chunk_sems):
    peers, shared = total.shape[0], total.shape[1]
    rows = shared // 8
    total[...] = jnp.zeros(total.shape, F32)

    def add(source, carry):
        for b in range(8):
            final = plan[source, 8 + b]
            place = pl.ds(pl.multiple_of((final & 7) * rows, rows), rows)
            at = 512 + b * rows
            total[final >> 3, place, :] += arrived[source, at : at + rows, :].astype(F32)
        return carry

    lax.fori_loop(0, peers, add, 0)
    for source in range(peers):
        final = total[source].astype(BF16).astype(F32)
        stage[source, 0:shared, :] = (final - targets[source, 0:shared, :].astype(F32)).astype(BF16)
    sent = []
    for source in range(peers):
        for b in range(8):
            code = plan[source, b]
            place = pl.ds(pl.multiple_of((code & 7) * rows, rows), rows)
            stage[source, shared + b * rows : shared + b * rows + rows, :] = stage[code >> 3, place, :]
        sent.append(fetch(stage.at[source], send.at[source], chunk_sems.at[source]))
    for copy in sent:
        copy.wait()


def composed_kernel(plan_in, shares, edge, send, plan, own, stage, sems):
    peers, shared = own.shape[0], own.shape[1]
    rows = shared // 8
    loads = [fetch(plan_in, plan, sems.at[0]), fetch(shares.at[:, 0:shared, :], own, sems.at[1])]
    for load in loads:
        load.wait()

    def give(source, carry):
        for b in range(8):
            code = plan[source, 8 + b]
            place = pl.ds(pl.multiple_of((code & 7) * rows, rows), rows)
            stage[source, b * rows : b * rows + rows, :] = own[code >> 3, place, :]
        return carry

    lax.fori_loop(0, peers, give, 0)
    fetch(stage, send, sems.at[0]).wait()


def adjoint_kernel(tables_in, arrived, *refs):
    adjoint, tables, start, folded, turned, sems = refs
    load = fetch(tables_in, tables, sems.at[0])
    rows = arrived.shape[1] // 16
    load.wait()
    begin = flipped_diagonal(tables[2].astype(F32))
    mid = spread(tables[1].astype(F32))
    end = flipped_diagonal(tables[0].astype(F32))
    for g in range(4):
        start[:, g * 256 : g * 256 + 256] = mm(begin, pieces_pair(arrived, 1, g, rows)).astype(start.dtype)
    for g, moved in middle_and_last(start, mid, end, folded, turned, True):
        put_pair(adjoint, g, moved)


def final_kernel(tables_far, tables_zero, gradient, arrived, *refs):
    adjoint, start, folded, turned, later, field, quarter_sems = refs
    rows = arrived.shape[1] // 8
    begin = flipped_diagonal(tables_far[2].astype(F32))
    mid = spread(tables_far[1].astype(F32))
    end = flipped_diagonal(tables_far[0].astype(F32))
    for g in range(4):
        start[:, g * 256 : g * 256 + 256] = mm(begin, pieces_pair(arrived, 0, g, rows)).astype(start.dtype)
    for g, moved in middle_and_last(start, mid, end, folded, turned, True, 1):
        put_pair(later, g, moved)
    begin = flipped_diagonal(tables_zero[0].astype(F32))
    mid = spread(tables_zero[1].astype(F32))
    end = diagonal(tables_zero[2].astype(F32))
    for g in range(4):
        start[:, g * 256 : g * 256 + 256] = mm(begin, lane_pair(later, g)).astype(start.dtype)
    stored = []
    middle(start, mid, folded, turned, True, 1)
    for g in range(4):
        flat = mm(turned[0:256, g * 256 : g * 256 + 256], end, TN).astype(BF16)
        for index in range(8):
            field[(index % 4) * 8 + 2 * g + index // 4] = flat[index * 32 : index * 32 + 32]
        for qh in range(4):
            at = slice(qh * 8 + 2 * g, qh * 8 + 2 * g + 2)
            stored.append(fetch(field.at[at], adjoint.at[at], quarter_sems.at[g, qh]))
    for copy in stored:
        copy.wait()


def to_native(block, g, field):
    flat = block.T.astype(field.dtype)
    for index in range(8):
        x = (index % 4) * 8 + 2 * g + index // 4
        field[x] = flat[index * 32 : index * 32 + 32]


def x_form_to_native(source, folded, turned, field):
    for b in range(8):
        block = source[b].astype(F32)
        block = jnp.concatenate(
            [
                jnp.concatenate([block[g * 64 : g * 64 + 32], block[g * 64 + 32 : g * 64 + 64]], axis=1)
                for g in range(4)
            ],
            axis=0,
        )
        swap_brick(block, folded, turned, b, 1)
    for g in range(4):
        to_native(turned[0:256, g * 256 : g * 256 + 256], g, field)


def tap(offset):
    value = jnp.zeros(offset.shape, F32)
    for step, weight in TAPS:
        value = jnp.where(offset == step, weight, value)
        value = jnp.where(offset == -step, -weight, value)
    return value


def stencils():
    size = 256
    row, col = iota((size, size), 0), iota((size, size), 1)
    along_y = halves(jnp.where(row // 32 == col // 32, tap(col - row), 0.0))
    along_z = halves(tap(row - col))
    row, col = iota((size, 48), 0), iota((size, 48), 1)
    layer = col // 8
    place = jnp.where(layer < RIM, layer - RIM, layer - RIM + 32)
    rim_y = halves(jnp.where(row // 32 == col % 8, tap(place - row % 32), 0.0))
    return along_y, rim_y, along_z


def rim_picker():
    row, col = iota((48, 256), 0), iota((48, 256), 1)
    layer = row // 8
    place = jnp.where(layer < RIM, layer, layer - RIM + 29)
    return ((row % 8 == col // 32) & (place == col % 32)).astype(F32).astype(BF16)


def difference_x(padded, g):
    total = None
    for step, weight in TAPS:
        ahead = padded[pl.ds(8 * g + RIM + step, 8)]
        behind = padded[pl.ds(8 * g + RIM - step, 8)]
        term = weight * (ahead - behind)
        total = term if total is None else total + term
    return total.reshape(256, 256)


def difference_y(parts, rims, along_y, rim_y):
    total = mm(along_y[0], parts[0]) + mm(along_y[1], parts[0])
    if len(parts) > 1:
        total = total + mm(along_y[0], parts[1])
    return total + mm(rim_y[0], rims) + mm(rim_y[1], rims)


def difference_z(parts, along_z):
    total = mm(parts[0], along_z[0]) + mm(parts[0], along_z[1])
    if len(parts) > 1:
        total = total + mm(parts[1], along_z[0])
    return total


def rim_rows(before, after, base, g):
    rows = [before[base + h, (g // 2) * 16 : (g // 2) * 16 + 16, :].astype(F32) for h in range(RIM)]
    rows += [after[base + h, (g // 2) * 16 : (g // 2) * 16 + 16, :].astype(F32) for h in range(RIM)]
    half = (g % 2) * 8
    return jnp.concatenate([value[half : half + 8] for value in rows], axis=0).astype(BF16)


def put_rims(blocks, base, low_y, high_y):
    picker = rim_picker()
    for pair in range(2):
        left, right = mm(picker, blocks[2 * pair]), mm(picker, blocks[2 * pair + 1])
        for layer in range(2 * RIM):
            value = jnp.concatenate(
                [left[layer * 8 : layer * 8 + 8], right[layer * 8 : layer * 8 + 8]], axis=0
            ).astype(BF16)
            target = low_y if layer < RIM else high_y
            target[base + layer % RIM, pair * 16 : pair * 16 + 16, :] = value


def edge_kernel(template, velocity, sent, low_x, high_x, low_y, high_y, field, first_x, last_x, mid_v, sems):
    loads = [
        fetch(template, field, sems.at[0]),
        fetch(velocity.at[0, 0:RIM], first_x, sems.at[1]),
        fetch(velocity.at[0, 29:32], last_x, sems.at[2]),
        fetch(velocity.at[1], mid_v, sems.at[3]),
    ]
    for load in loads:
        load.wait()
    low_x[0:RIM] = field[0:RIM]
    high_x[0:RIM] = field[29:32]
    low_x[RIM : 2 * RIM] = first_x[...].astype(BF16)
    high_x[RIM : 2 * RIM] = last_x[...].astype(BF16)
    put_rims([field[8 * g : 8 * g + 8].reshape(256, 256) for g in range(4)], 0, low_y, high_y)
    put_rims([mid_v[8 * g : 8 * g + 8].astype(BF16).reshape(256, 256) for g in range(4)], RIM, low_y, high_y)


def prepare_kernel(picks, codes_in, operators, edge, tables, plan_out, codes, plan, sems):
    load = fetch(codes_in, codes, sems.at[0])
    chosen = on_lanes([picks[1, 0, 0, b] for b in range(8)])
    for axis in range(3):
        tables[axis] = table_rows(operators, chosen, axis).astype(BF16)
    load.wait()

    def row(source, carry):
        for b in range(8):
            first = codes[source, 2 * b]
            plan[source, b] = codes[source, 2 * b + 1]
            plan[source, 8 + b] = codes[first >> 3, 2 * (first & 7) + 1]
        return carry

    lax.fori_loop(0, codes.shape[0], row, 0)
    fetch(plan, plan_out, sems.at[0]).wait()


def divergence_kernel(velocity, before_x, after_x, before_y, after_y, sent, divergence, padded):
    along_y, rim_y, along_z = stencils()
    padded[0:RIM] = before_x[RIM : 2 * RIM].astype(F32)
    padded[RIM : RIM + 32] = velocity[0]
    padded[RIM + 32 : 2 * RIM + 32] = after_x[RIM : 2 * RIM].astype(F32)
    for g in range(4):
        along_one = halves(velocity[1, 8 * g : 8 * g + 8].reshape(256, 256))
        along_two = halves(velocity[2, 8 * g : 8 * g + 8].reshape(256, 256))
        total = (
            difference_x(padded, g)
            + difference_y(along_one, rim_rows(before_y, after_y, RIM, g), along_y, rim_y)
            + difference_z(along_two, along_z)
        )
        divergence[8 * g : 8 * g + 8] = total.reshape(8, 32, 256)


def rims_kernel(codes_in, arrived, divergence, sent, native, low_x, high_x, low_y, high_y, codes, slots, total, state, folded, turned, sems):
    loads = [fetch(codes_in, codes, sems.at[0]), fetch(arrived.at[:, 0:512, :], slots, sems.at[1])]
    total[...] = jnp.zeros(total.shape, F32)
    for load in loads:
        load.wait()
    me = lax.axis_index("gx")

    def add(source, carry):
        rank = jnp.int32(0)
        for b in range(8):
            code = codes[source, 2 * b]
            hit = (code >> 3) == me

            @pl.when(hit)
            def _():
                place = pl.ds(pl.multiple_of(rank * 256, 256), 256)
                total[code & 7] += slots[source, place, :].astype(F32)

            rank = rank + hit.astype(jnp.int32)
        return carry

    lax.fori_loop(0, slots.shape[0], add, 0)
    for b in range(8):
        state[b] = total[b].astype(BF16)
    x_form_to_native(state, folded, turned, native)
    low_x[0:RIM] = native[0:RIM]
    high_x[0:RIM] = native[29:32]
    low_x[RIM : 2 * RIM] = divergence[0:RIM].astype(BF16)
    high_x[RIM : 2 * RIM] = divergence[29:32].astype(BF16)
    put_rims([native[8 * g : 8 * g + 8].reshape(256, 256) for g in range(4)], 0, low_y, high_y)
    put_rims(
        [divergence[8 * g : 8 * g + 8].astype(BF16).reshape(256, 256) for g in range(4)], RIM, low_y, high_y
    )


def gradient_kernel(
    template,
    state,
    divergence,
    adjoint_two,
    adjoint_one,
    b0x,
    a0x,
    b0y,
    a0y,
    b1x,
    a1x,
    b1y,
    a1y,
    gradient,
    folded,
    turned,
    weight_two,
    weight_one,
    pad_zero,
    pad_one,
    pad_div,
):
    x_form_to_native(adjoint_one, folded, turned, weight_one)
    for g in range(4):
        to_native(pieces_pair(adjoint_two, 0, g, adjoint_two.shape[1] // 16), g, weight_two)
    along_y, rim_y, along_z = stencils()
    for padded, before, middle, after, base in (
        (pad_zero, b0x, template, a0x, 0),
        (pad_one, b1x, state, a1x, 0),
        (pad_div, b1x, divergence, a1x, RIM),
    ):
        padded[0:RIM] = before[base : base + RIM].astype(F32)
        padded[RIM : RIM + 32] = middle[...].astype(F32)
        padded[RIM + 32 : 2 * RIM + 32] = after[base : base + RIM].astype(F32)
    for g in range(4):
        zero = (template[8 * g : 8 * g + 8].reshape(256, 256),)
        one = (state[8 * g : 8 * g + 8].reshape(256, 256),)
        div = halves(divergence[8 * g : 8 * g + 8].reshape(256, 256))
        weigh_one = 0.5 * weight_one[8 * g : 8 * g + 8].reshape(256, 256)
        weigh_two = 0.5 * weight_two[8 * g : 8 * g + 8].reshape(256, 256)
        for axis in range(3):
            if axis == 0:
                parts = [difference_x(padded, g) for padded in (pad_zero, pad_one, pad_div)]
            elif axis == 1:
                parts = [
                    difference_y(zero, rim_rows(b0y, a0y, 0, g), along_y, rim_y),
                    difference_y(one, rim_rows(b1y, a1y, 0, g), along_y, rim_y),
                    difference_y(div, rim_rows(b1y, a1y, RIM, g), along_y, rim_y),
                ]
            else:
                parts = [difference_z(value, along_z) for value in (zero, one, div)]
            value = weigh_one * parts[0] + weigh_two * parts[1] - 0.25 * parts[2]
            gradient[axis, 8 * g : 8 * g + 8] = value.reshape(8, 32, 256)


SCALAR = pl.BlockSpec(memory_space=pltpu.SMEM)
WHOLE = pl.BlockSpec(memory_space=pltpu.VMEM)
NEAR = pl.BlockSpec(memory_space=pltpu.VMEM)
ANYWHERE = pl.BlockSpec(memory_space=pl.ANY)
FAR = pl.BlockSpec(memory_space=pltpu.HBM)
FOLDED = (32, 64, 128)
FLAT = (256, 1024)
NATIVE = (32, 32, 256)
FORM = (8, 256, 128)
TABLES = (3, 32, 256)


def pinned(value, spec):
    if spec is FAR:
        return pltpu.with_memory_space_constraint(value, pltpu.HBM)
    if spec is NEAR:
        return pltpu.with_memory_space_constraint(value, pltpu.VMEM)
    return value


SHORT, LONG = 1 << 20, 1 << 36


def call(kernel, out, in_specs, out_specs, scratch, work=LONG):
    made = pl.pallas_call(
        kernel,
        out_shape=out,
        in_specs=in_specs,
        out_specs=out_specs,
        scratch_shapes=scratch,
        compiler_params=pltpu.CompilerParams(vmem_limit_bytes=24 * 1024 * 1024),
        cost_estimate=pl.CostEstimate(flops=work, bytes_accessed=1024 * 1024, transcendentals=0),
    )

    def apply(*values):
        return made(*[pinned(value, spec) for value, spec in zip(values, in_specs, strict=True)])

    return apply


def like(shape, dtype):
    return jax.ShapeDtypeStruct(shape, dtype)


def far(shape, dtype):
    return pltpu.HBM(shape, dtype)


def neighbours(low_x, high_x, low_y, high_y):
    moved = []
    for low, high, axis in ((low_x, high_x, "gx"), (low_y, high_y, "gy")):
        size = lax.axis_size(axis)
        up = [(i, i + 1) for i in range(size - 1)]
        down = [(i + 1, i) for i in range(size - 1)]
        moved += [lax.ppermute(high, axis, up), lax.ppermute(low, axis, down)]
    return moved


def swap_slots(send):
    return lax.all_to_all(send, "gx", split_axis=0, concat_axis=0, tiled=True)


def shards(template, target_image, velocity, operators, route, target_brick, operator_index):
    peers = lax.axis_size("gx")
    shared = 8 * (256 // peers)
    sems = pltpu.SemaphoreType.DMA((16,))
    quarter_sems = pltpu.SemaphoreType.DMA((4, 4))
    turning = [pltpu.VMEM(FLAT, F32), pltpu.VMEM(FOLDED, F32), pltpu.VMEM((512, 1024), BF16)]
    form = pltpu.VMEM(FORM, BF16)
    tables = pltpu.VMEM(TABLES, BF16)
    routes_mem = pltpu.SMEM((peers, 128), jnp.int32)
    stage = pltpu.VMEM((peers, shared, 128), BF16)
    meta_half = pltpu.VMEM((peers, 16, 128), BF16)
    table_rows_count = operators.shape[1] * operators.shape[2] * operators.shape[3]
    listed = operators.transpose(1, 2, 3, 0).reshape(table_rows_count, operators.shape[0])
    listed_mem = pltpu.VMEM(listed.shape, BF16)
    route = route.reshape(route.shape[:4])

    send = call(
        target_kernel,
        far((peers, shared + 16, 128), BF16),
        [FAR] * 4,
        FAR,
        [pltpu.SMEM(route.shape, jnp.int32)] * 3
        + [pltpu.VMEM(NATIVE, BF16), stage, pltpu.VMEM((16, 128), F32), meta_half, sems],
        SHORT,
    )(operator_index, route, target_brick, target_image)
    targets = swap_slots(send)

    moved, tables_zero = call(
        first_kernel,
        [like(FORM, BF16), far(TABLES, BF16)],
        [SCALAR, FAR, FAR, FAR],
        [WHOLE, FAR],
        [listed_mem, pltpu.VMEM(NATIVE, BF16)] + turning + [tables, sems],
    )(operator_index, listed, template, send)
    send, tables_far, codes = call(
        second_kernel,
        [far((peers, 512 + shared, 128), BF16), far(TABLES, BF16), far((peers, 128), jnp.int32)],
        [SCALAR, SCALAR, WHOLE, WHOLE, WHOLE],
        [FAR] * 3,
        [pltpu.VMEM((peers, 16, 128), F32), pltpu.VMEM((peers, 128), jnp.int32), pltpu.VMEM(FLAT, BF16)]
        + turning[1:]
        + [stage, tables, sems, pltpu.SemaphoreType.DMA((8,))],
        SHORT,
    )(route, target_brick, listed, moved, targets)
    arrived = swap_slots(send)

    rim = like((2 * RIM, 32, 256), BF16)
    low_x, high_x, low_y, high_y = call(
        edge_kernel,
        [rim] * 4,
        [FAR] * 3,
        [WHOLE] * 4,
        [pltpu.VMEM(NATIVE, BF16)] + [pltpu.VMEM((RIM, 32, 256), F32)] * 2 + [pltpu.VMEM(NATIVE, F32), sems],
    )(template, velocity, send)
    tables_one, plan = call(
        prepare_kernel,
        [far(TABLES, BF16), far((peers, 128), jnp.int32)],
        [SCALAR, FAR, WHOLE, WHOLE],
        [WHOLE, FAR],
        [routes_mem, routes_mem, sems],
    )(operator_index, codes, listed, low_x)
    b0x, a0x, b0y, a0y = neighbours(low_x, high_x, low_y, high_y)

    send = call(
        share_kernel,
        far((peers, 2 * shared, 128), BF16),
        [SCALAR, WHOLE, WHOLE],
        FAR,
        [pltpu.VMEM((peers, shared, 128), F32), pltpu.VMEM((peers, 2 * shared, 128), BF16)]
        + [pltpu.SemaphoreType.DMA((peers,))],
        SHORT,
    )(plan, arrived, targets)
    pulled = swap_slots(send)

    divergence = call(
        divergence_kernel, like(NATIVE, F32), [WHOLE] * 5 + [FAR], WHOLE, [pltpu.VMEM((38, 32, 256), F32)]
    )(velocity, b0x, a0x, b0y, a0y, send)
    state, low_x, high_x, low_y, high_y = call(
        rims_kernel,
        [like(NATIVE, BF16)] + [rim] * 4,
        [FAR, ANYWHERE, WHOLE, FAR],
        [WHOLE] * 5,
        [routes_mem, pltpu.VMEM((peers, 512, 128), BF16), pltpu.VMEM(FORM, F32), form] + turning[1:] + [sems],
    )(codes, arrived, divergence, send)
    b1x, a1x, b1y, a1y = neighbours(low_x, high_x, low_y, high_y)
    composed = call(
        composed_kernel, far((peers, shared, 128), BF16), [FAR, FAR, WHOLE], FAR, [routes_mem, stage, stage, sems]
    )(plan, send, low_x)

    composed = swap_slots(composed)

    adjoint_one = call(
        adjoint_kernel, like(FORM, BF16), [FAR, NEAR], WHOLE, [tables] + turning + [sems]
    )(tables_one, pulled)
    gradient = call(
        gradient_kernel,
        far((3,) + NATIVE, F32),
        [WHOLE] * 13,
        WHOLE,
        turning[1:] + [pltpu.VMEM(NATIVE, F32)] * 2 + [pltpu.VMEM((38, 32, 256), F32)] * 3,
    )(template, state, divergence, pulled, adjoint_one, b0x, a0x, b0y, a0y, b1x, a1x, b1y, a1y)

    adjoint = call(
        final_kernel,
        far(NATIVE, BF16),
        [WHOLE, WHOLE, FAR, NEAR],
        FAR,
        [pltpu.VMEM(FLAT, BF16)] + turning[1:] + [form, pltpu.VMEM(NATIVE, BF16), quarter_sems],
        SHORT,
    )(tables_far, tables_zero, gradient, composed)
    return gradient, adjoint


def solution(mesh):
    placed = (
        P("gx", "gy", None),
        P("gx", "gy", None),
        P(None, "gx", "gy", None),
        P(),
        P(None, "gx", "gy", None, None),
        P(None, "gx", "gy", None),
        P(None, "gx", "gy", None),
    )
    return jax.shard_map(
        shards,
        mesh=mesh,
        in_specs=placed,
        out_specs=(P(None, "gx", "gy", None), P("gx", "gy", None)),
        check_vma=False,
    )
```

```python
import functools

import jax
import jax.numpy as jnp
from jax import lax
from jax.experimental import pallas as pl
from jax.experimental.pallas import tpu as pltpu
from jax.sharding import PartitionSpec as P

STEPS = 2
CAP = 2
RIM = 3
F32 = jnp.float32
BF16 = jnp.bfloat16
NT = (((1,), (1,)), ((), ()))
NN = (((1,), (0,)), ((), ()))
TN = (((0,), (0,)), ((), ()))
TAPS = ((1, 0.75), (2, -0.15), (3, 1.0 / 60.0))


def iota(shape, dim):
    return lax.broadcasted_iota(jnp.int32, shape, dim)


def mm(left, right, dims=NN):
    return lax.dot_general(left, right, dims, preferred_element_type=F32)


def halves(value):
    high = value.astype(BF16)
    return high, (value - high.astype(F32)).astype(BF16)


def on_lanes(picks):
    lane = iota((1, 256), 1)
    chosen = jnp.zeros(lane.shape, jnp.int32)
    for b, pick in enumerate(picks):
        chosen = jnp.where(lane // 32 == b, pick, chosen)
    return chosen


def table_rows(operators, chosen, axis):
    shape = (operators.shape[1], 256)
    one_hot = (iota(shape, 0) == jnp.broadcast_to(chosen, shape)).astype(F32).astype(BF16)
    found = mm(operators[axis * 1024 : axis * 1024 + 1024, :], one_hot)
    within = iota((32, 256), 1) % 32
    total = jnp.zeros((32, 256), F32)
    for x in range(32):
        total = jnp.where(within == x, found[x * 32 : x * 32 + 32], total)
    return total


def same_block(size, edge):
    return iota((size, size), 0) // edge == iota((size, size), 1) // edge


def identity():
    return (iota((256, 256), 0) == iota((256, 256), 1)).astype(F32).astype(BF16)


def flipped_diagonal(table):
    return jnp.where(same_block(256, 32), jnp.concatenate([table] * 8, axis=0), 0.0).astype(BF16)


def diagonal(table):
    return mm(identity(), flipped_diagonal(table), NT).astype(BF16)


def spread(table):
    copies = (iota((256, 256), 0) % 32 == iota((256, 256), 1) % 32).astype(F32).astype(BF16)
    return mm(flipped_diagonal(table), copies)


def swap_chunks(parts):
    lane = iota(parts[0].shape, 1)
    for bit, shift in ((1, 32), (2, 64)):
        keep = (lane & shift) == 0
        fresh = list(parts)
        for index in range(4):
            if index & bit:
                continue
            one, two = parts[index], parts[index | bit]
            fresh[index] = jnp.where(keep, one, pltpu.roll(two, shift, 1))
            fresh[index | bit] = jnp.where(keep, pltpu.roll(one, 128 - shift, 1), two)
        parts = fresh
    return parts


def swap_brick(block, folded, turned, brick, parts=2):
    slabs = []
    for ph in range(4):
        slabs.append(
            jnp.concatenate(
                [
                    block[(qs // 2) * 32 + ph * 8 : (qs // 2) * 32 + ph * 8 + 8, (qs % 2) * 128 : (qs % 2) * 128 + 128]
                    for qs in range(8)
                ],
                axis=0,
            )
        )
    slabs = swap_chunks(slabs)
    for qh in range(4):
        folded[brick * 4 + qh] = slabs[qh]
    for ps in range(8):
        value = jnp.concatenate(
            [folded[brick * 4 + qh, pl.ds(ps, 8, stride=8), :] for qh in range(4)], axis=0
        )
        for part, half in enumerate(halves(value)[:parts]):
            turned[part * 256 + brick * 32 : part * 256 + brick * 32 + 32, ps * 128 : ps * 128 + 128] = half


def lane_pair(field, g):
    return jnp.concatenate(
        [
            jnp.concatenate([field[b, qs * 32 : qs * 32 + 32, :] for b in range(8)], axis=0)
            for qs in (2 * g, 2 * g + 1)
        ],
        axis=1,
    )


def put_pair(field, g, value):
    for b in range(8):
        for half in range(2):
            rows = slice((2 * g + half) * 32, (2 * g + half) * 32 + 32)
            field[b, rows, :] = value[b * 32 : b * 32 + 32, half * 128 : half * 128 + 128]


def middle(start, spread_mid, folded, turned, flipped, parts):
    mask = same_block(256, 32)
    for brick in range(8):
        rows = spread_mid[brick * 32 : brick * 32 + 32]
        line = jnp.where(mask, jnp.concatenate([rows] * 8, axis=0), 0.0).astype(BF16)
        block = start[brick * 32 : brick * 32 + 32, :]
        block = jnp.concatenate([block[:, g * 256 : g * 256 + 256] for g in range(4)], axis=0)
        held = jnp.concatenate(halves(block)[:parts], axis=0)
        both = mm(held, line, NT if flipped else NN)
        swap_brick(both if parts == 1 else both[:128] + both[128:], folded, turned, brick, parts)


def middle_and_last(start, spread_mid, last, folded, turned, flipped, parts=2):
    middle(start, spread_mid, folded, turned, flipped, parts)
    last = jnp.concatenate([last] * parts, axis=1)
    for g in range(4):
        yield g, mm(last, turned[0 : parts * 256, g * 256 : g * 256 + 256]).astype(BF16)


def slot_numbers(route, step):
    own = [route[step, 0, 0, b] for b in range(8)]
    slots = []
    for b in range(8):
        rank = jnp.int32(0)
        for other in range(b):
            rank = rank + (own[other] == own[b]).astype(jnp.int32)
        slots.append((own[b], rank))
    return slots


def fetch(source, target, sem):
    copy = pltpu.make_async_copy(source, target, sem)
    copy.start()
    return copy


def put_pieces(stage, g, value, rows):
    parts = 32 // rows
    for half in range(2):
        tile = value[:, half * 128 : half * 128 + 128]
        for part in range(parts):
            share = (2 * g + half) * parts + part
            if parts == 1:
                stage[share] = tile
            else:
                for b in range(8):
                    at = b * 32 + part * rows
                    stage[share, b * rows : b * rows + rows, :] = tile[at : at + rows]


def send_pieces(stage, send, base, g, sem):
    count = stage.shape[0] // 4
    shares = slice(g * count, g * count + count)
    return fetch(stage.at[shares], send.at[shares, base : base + stage.shape[1], :], sem)


def pieces_pair(pieces, kind, g, rows):
    parts = 32 // rows
    base = kind * 8 * rows
    tiles = []
    for tile in (2 * g, 2 * g + 1):
        if parts == 1:
            tiles.append(pieces[tile, base : base + 256, :])
        else:
            tiles.append(
                jnp.concatenate(
                    [
                        pieces[tile * parts + part, base + b * rows : base + b * rows + rows, :]
                        for b in range(8)
                        for part in range(parts)
                    ],
                    axis=0,
                )
            )
    return jnp.concatenate(tiles, axis=1)


def target_kernel(picks_in, route_in, brick_in, target, send, *refs):
    picks, route, landing, field, stage, meta, meta_half, sems = refs
    load = fetch(target, field, sems.at[3])
    told = [
        fetch(source, place, sems.at[index])
        for index, (source, place) in enumerate(((picks_in, picks), (route_in, route), (brick_in, landing)))
    ]
    for copy in told:
        copy.wait()
    lane = iota((1, 128), 1)
    meta[...] = jnp.zeros(meta.shape, F32)
    value = jnp.zeros((1, 128), jnp.int32)
    for b in range(8):
        for step in range(STEPS):
            code = route[step, 0, 0, b] * 8 + landing[step, 0, 0, b]
            value = jnp.where(lane == 2 * b + step, code, value)
        meta[8 + b : 9 + b, :] = jnp.full((1, 128), picks[1, 0, 0, b], jnp.int32).astype(F32)
    meta[0:1, :] = value.astype(F32)
    meta_half[...] = jnp.broadcast_to(meta[...].astype(BF16)[None], meta_half.shape)
    shared = stage.shape[1]
    sent = [fetch(meta_half, send.at[:, shared : shared + 16, :], sems.at[4])]
    load.wait()
    for g in range(4):
        block = jnp.concatenate(
            [field[qh * 8 + qs] for qs in (2 * g, 2 * g + 1) for qh in range(4)], axis=0
        )
        put_pieces(stage, g, block.T, shared // 8)
        sent.append(send_pieces(stage, send, 0, g, sems.at[5 + g]))
    for copy in sent:
        copy.wait()


def first_kernel(picks, operators, field, sent, moved_out, tables, table_mem, field_mem, start, folded, turned, tables_mem, sems):
    loads = [fetch(operators, table_mem, sems.at[0]), fetch(field, field_mem, sems.at[1])]
    chosen = on_lanes([picks[0, 0, 0, b] for b in range(8)])
    loads[0].wait()
    found = [table_rows(table_mem, chosen, axis) for axis in range(3)]
    for axis in range(3):
        tables_mem[axis] = found[axis].astype(BF16)
    kept = fetch(tables_mem, tables, sems.at[0])
    begin = diagonal(found[2])
    loads[1].wait()
    for g in range(4):
        block = jnp.concatenate(
            [field_mem[qh * 8 + qs] for qs in (2 * g, 2 * g + 1) for qh in range(4)], axis=0
        )
        start[:, g * 256 : g * 256 + 256] = mm(begin, block, NT).astype(start.dtype)
    for g, moved in middle_and_last(start, spread(found[1]), diagonal(found[0]), folded, turned, False):
        put_pair(moved_out, g, moved)
    kept.wait()


def second_kernel(route, landing, operators, moved, arrived, *refs):
    send, tables, codes_out, meta, codes, start, folded, turned, stage, tables_mem, sems, slot_sems = refs
    shared = stage.shape[1]
    sent = []
    for b, (place, rank) in enumerate(slot_numbers(route, 0)):
        rows = pl.ds(pl.multiple_of(rank * 256, 256), 256)
        sent.append(fetch(moved.at[b], send.at[place, rows, :], slot_sems.at[b]))
    meta[...] = arrived[:, shared : shared + 16, :].astype(F32)
    for source in range(meta.shape[0]):
        codes[source : source + 1, :] = meta[source, 0:1, :].astype(jnp.int32)
    sent.append(fetch(codes, codes_out, sems.at[0]))
    lane = iota((1, 128), 1) // 32
    chosen = []
    for part in range(2):
        row = jnp.zeros((1, 128), F32)
        for b in range(4):
            own = part * 4 + b
            found = meta[route[0, 0, 0, own], pl.ds(8 + landing[0, 0, 0, own], 1), :]
            row = jnp.where(lane == b, found, row)
        chosen.append(row)
    chosen = jnp.concatenate(chosen, axis=1).astype(jnp.int32)
    found = [table_rows(operators, chosen, axis) for axis in range(3)]
    for axis in range(3):
        tables_mem[axis] = found[axis].astype(BF16)
    sent.append(fetch(tables_mem, tables, sems.at[1]))
    begin = diagonal(found[0])
    for g in range(4):
        start[:, g * 256 : g * 256 + 256] = mm(begin, lane_pair(moved, g)).astype(start.dtype)
    for g, value in middle_and_last(start, spread(found[1]), diagonal(found[2]), folded, turned, False, 1):
        put_pieces(stage, g, value, shared // 8)
        sent.append(send_pieces(stage, send, 512, g, sems.at[2 + g]))
    for copy in sent:
        copy.wait()


def share_kernel(plan, arrived, targets, send, total, stage, chunk_sems):
    peers, shared = total.shape[0], total.shape[1]
    rows = shared // 8
    total[...] = jnp.zeros(total.shape, F32)

    def add(source, carry):
        for b in range(8):
            final = plan[source, 8 + b]
            place = pl.ds(pl.multiple_of((final & 7) * rows, rows), rows)
            at = 512 + b * rows
            total[final >> 3, place, :] += arrived[source, at : at + rows, :].astype(F32)
        return carry

    lax.fori_loop(0, peers, add, 0)
    for source in range(peers):
        final = total[source].astype(BF16).astype(F32)
        stage[source, 0:shared, :] = (final - targets[source, 0:shared, :].astype(F32)).astype(BF16)
    sent = []
    for source in range(peers):
        for b in range(8):
            code = plan[source, b]
            place = pl.ds(pl.multiple_of((code & 7) * rows, rows), rows)
            stage[source, shared + b * rows : shared + b * rows + rows, :] = stage[code >> 3, place, :]
        sent.append(fetch(stage.at[source], send.at[source], chunk_sems.at[source]))
    for copy in sent:
        copy.wait()


def composed_kernel(plan_in, shares, edge, send, plan, own, stage, sems):
    peers, shared = own.shape[0], own.shape[1]
    rows = shared // 8
    loads = [fetch(plan_in, plan, sems.at[0]), fetch(shares.at[:, 0:shared, :], own, sems.at[1])]
    for load in loads:
        load.wait()

    def give(source, carry):
        for b in range(8):
            code = plan[source, 8 + b]
            place = pl.ds(pl.multiple_of((code & 7) * rows, rows), rows)
            stage[source, b * rows : b * rows + rows, :] = own[code >> 3, place, :]
        return carry

    lax.fori_loop(0, peers, give, 0)
    fetch(stage, send, sems.at[0]).wait()


def adjoint_kernel(tables_in, arrived, *refs):
    adjoint, tables, start, folded, turned, sems = refs
    load = fetch(tables_in, tables, sems.at[0])
    rows = arrived.shape[1] // 16
    load.wait()
    begin = flipped_diagonal(tables[2].astype(F32))
    mid = spread(tables[1].astype(F32))
    end = flipped_diagonal(tables[0].astype(F32))
    for g in range(4):
        start[:, g * 256 : g * 256 + 256] = mm(begin, pieces_pair(arrived, 1, g, rows)).astype(start.dtype)
    for g, moved in middle_and_last(start, mid, end, folded, turned, True):
        put_pair(adjoint, g, moved)


def final_kernel(tables_far, tables_zero, gradient, arrived, *refs):
    adjoint, start, folded, turned, later, field, quarter_sems = refs
    rows = arrived.shape[1] // 8
    begin = flipped_diagonal(tables_far[2].astype(F32))
    mid = spread(tables_far[1].astype(F32))
    end = flipped_diagonal(tables_far[0].astype(F32))
    for g in range(4):
        start[:, g * 256 : g * 256 + 256] = mm(begin, pieces_pair(arrived, 0, g, rows)).astype(start.dtype)
    for g, moved in middle_and_last(start, mid, end, folded, turned, True, 1):
        put_pair(later, g, moved)
    begin = flipped_diagonal(tables_zero[0].astype(F32))
    mid = spread(tables_zero[1].astype(F32))
    end = diagonal(tables_zero[2].astype(F32))
    for g in range(4):
        start[:, g * 256 : g * 256 + 256] = mm(begin, lane_pair(later, g)).astype(start.dtype)
    stored = []
    middle(start, mid, folded, turned, True, 1)
    for g in range(4):
        flat = mm(turned[0:256, g * 256 : g * 256 + 256], end, TN).astype(BF16)
        for index in range(8):
            field[(index % 4) * 8 + 2 * g + index // 4] = flat[index * 32 : index * 32 + 32]
        for qh in range(4):
            at = slice(qh * 8 + 2 * g, qh * 8 + 2 * g + 2)
            stored.append(fetch(field.at[at], adjoint.at[at], quarter_sems.at[g, qh]))
    for copy in stored:
        copy.wait()


def to_native(block, g, field):
    flat = block.T.astype(field.dtype)
    for index in range(8):
        x = (index % 4) * 8 + 2 * g + index // 4
        field[x] = flat[index * 32 : index * 32 + 32]


def x_form_to_native(source, folded, turned, field):
    for b in range(8):
        block = source[b].astype(F32)
        block = jnp.concatenate(
            [
                jnp.concatenate([block[g * 64 : g * 64 + 32], block[g * 64 + 32 : g * 64 + 64]], axis=1)
                for g in range(4)
            ],
            axis=0,
        )
        swap_brick(block, folded, turned, b, 1)
    for g in range(4):
        to_native(turned[0:256, g * 256 : g * 256 + 256], g, field)


def tap(offset):
    value = jnp.zeros(offset.shape, F32)
    for step, weight in TAPS:
        value = jnp.where(offset == step, weight, value)
        value = jnp.where(offset == -step, -weight, value)
    return value


def stencils():
    size = 256
    row, col = iota((size, size), 0), iota((size, size), 1)
    along_y = halves(jnp.where(row // 32 == col // 32, tap(col - row), 0.0))
    along_z = halves(tap(row - col))
    row, col = iota((size, 48), 0), iota((size, 48), 1)
    layer = col // 8
    place = jnp.where(layer < RIM, layer - RIM, layer - RIM + 32)
    rim_y = halves(jnp.where(row // 32 == col % 8, tap(place - row % 32), 0.0))
    return along_y, rim_y, along_z


def rim_picker():
    row, col = iota((48, 256), 0), iota((48, 256), 1)
    layer = row // 8
    place = jnp.where(layer < RIM, layer, layer - RIM + 29)
    return ((row % 8 == col // 32) & (place == col % 32)).astype(F32).astype(BF16)


def difference_x(padded, g):
    total = None
    for step, weight in TAPS:
        ahead = padded[pl.ds(8 * g + RIM + step, 8)]
        behind = padded[pl.ds(8 * g + RIM - step, 8)]
        term = weight * (ahead - behind)
        total = term if total is None else total + term
    return total.reshape(256, 256)


def difference_y(parts, rims, along_y, rim_y):
    total = mm(along_y[0], parts[0]) + mm(along_y[1], parts[0])
    if len(parts) > 1:
        total = total + mm(along_y[0], parts[1])
    return total + mm(rim_y[0], rims) + mm(rim_y[1], rims)


def difference_z(parts, along_z):
    total = mm(parts[0], along_z[0]) + mm(parts[0], along_z[1])
    if len(parts) > 1:
        total = total + mm(parts[1], along_z[0])
    return total


def rim_rows(before, after, base, g):
    rows = [before[base + h, (g // 2) * 16 : (g // 2) * 16 + 16, :].astype(F32) for h in range(RIM)]
    rows += [after[base + h, (g // 2) * 16 : (g // 2) * 16 + 16, :].astype(F32) for h in range(RIM)]
    half = (g % 2) * 8
    return jnp.concatenate([value[half : half + 8] for value in rows], axis=0).astype(BF16)


def put_rims(blocks, base, low_y, high_y):
    picker = rim_picker()
    for pair in range(2):
        left, right = mm(picker, blocks[2 * pair]), mm(picker, blocks[2 * pair + 1])
        for layer in range(2 * RIM):
            value = jnp.concatenate(
                [left[layer * 8 : layer * 8 + 8], right[layer * 8 : layer * 8 + 8]], axis=0
            ).astype(BF16)
            target = low_y if layer < RIM else high_y
            target[base + layer % RIM, pair * 16 : pair * 16 + 16, :] = value


def edge_kernel(template, velocity, sent, low_x, high_x, low_y, high_y, field, first_x, last_x, mid_v, sems):
    loads = [
        fetch(template, field, sems.at[0]),
        fetch(velocity.at[0, 0:RIM], first_x, sems.at[1]),
        fetch(velocity.at[0, 29:32], last_x, sems.at[2]),
        fetch(velocity.at[1], mid_v, sems.at[3]),
    ]
    for load in loads:
        load.wait()
    low_x[0:RIM] = field[0:RIM]
    high_x[0:RIM] = field[29:32]
    low_x[RIM : 2 * RIM] = first_x[...].astype(BF16)
    high_x[RIM : 2 * RIM] = last_x[...].astype(BF16)
    put_rims([field[8 * g : 8 * g + 8].reshape(256, 256) for g in range(4)], 0, low_y, high_y)
    put_rims([mid_v[8 * g : 8 * g + 8].astype(BF16).reshape(256, 256) for g in range(4)], RIM, low_y, high_y)


def prepare_kernel(picks, codes_in, operators, edge, tables, plan_out, codes, plan, sems):
    load = fetch(codes_in, codes, sems.at[0])
    chosen = on_lanes([picks[1, 0, 0, b] for b in range(8)])
    for axis in range(3):
        tables[axis] = table_rows(operators, chosen, axis).astype(BF16)
    load.wait()

    def row(source, carry):
        for b in range(8):
            first = codes[source, 2 * b]
            plan[source, b] = codes[source, 2 * b + 1]
            plan[source, 8 + b] = codes[first >> 3, 2 * (first & 7) + 1]
        return carry

    lax.fori_loop(0, codes.shape[0], row, 0)
    fetch(plan, plan_out, sems.at[0]).wait()


def divergence_kernel(velocity, before_x, after_x, before_y, after_y, sent, divergence, padded):
    along_y, rim_y, along_z = stencils()
    padded[0:RIM] = before_x[RIM : 2 * RIM].astype(F32)
    padded[RIM : RIM + 32] = velocity[0]
    padded[RIM + 32 : 2 * RIM + 32] = after_x[RIM : 2 * RIM].astype(F32)
    for g in range(4):
        along_one = halves(velocity[1, 8 * g : 8 * g + 8].reshape(256, 256))
        along_two = halves(velocity[2, 8 * g : 8 * g + 8].reshape(256, 256))
        total = (
            difference_x(padded, g)
            + difference_y(along_one, rim_rows(before_y, after_y, RIM, g), along_y, rim_y)
            + difference_z(along_two, along_z)
        )
        divergence[8 * g : 8 * g + 8] = total.reshape(8, 32, 256)


def rims_kernel(codes_in, arrived, divergence, sent, native, low_x, high_x, low_y, high_y, codes, slots, total, state, folded, turned, sems):
    loads = [fetch(codes_in, codes, sems.at[0]), fetch(arrived.at[:, 0:512, :], slots, sems.at[1])]
    total[...] = jnp.zeros(total.shape, F32)
    for load in loads:
        load.wait()
    me = lax.axis_index("gx")

    def add(source, carry):
        rank = jnp.int32(0)
        for b in range(8):
            code = codes[source, 2 * b]
            hit = (code >> 3) == me

            @pl.when(hit)
            def _():
                place = pl.ds(pl.multiple_of(rank * 256, 256), 256)
                total[code & 7] += slots[source, place, :].astype(F32)

            rank = rank + hit.astype(jnp.int32)
        return carry

    lax.fori_loop(0, slots.shape[0], add, 0)
    for b in range(8):
        state[b] = total[b].astype(BF16)
    x_form_to_native(state, folded, turned, native)
    low_x[0:RIM] = native[0:RIM]
    high_x[0:RIM] = native[29:32]
    low_x[RIM : 2 * RIM] = divergence[0:RIM].astype(BF16)
    high_x[RIM : 2 * RIM] = divergence[29:32].astype(BF16)
    put_rims([native[8 * g : 8 * g + 8].reshape(256, 256) for g in range(4)], 0, low_y, high_y)
    put_rims(
        [divergence[8 * g : 8 * g + 8].astype(BF16).reshape(256, 256) for g in range(4)], RIM, low_y, high_y
    )


def gradient_kernel(
    template,
    state,
    divergence,
    adjoint_two,
    adjoint_one,
    b0x,
    a0x,
    b0y,
    a0y,
    b1x,
    a1x,
    b1y,
    a1y,
    gradient,
    folded,
    turned,
    weight_two,
    weight_one,
    pad_zero,
    pad_one,
    pad_div,
):
    x_form_to_native(adjoint_one, folded, turned, weight_one)
    for g in range(4):
        to_native(pieces_pair(adjoint_two, 0, g, adjoint_two.shape[1] // 16), g, weight_two)
    along_y, rim_y, along_z = stencils()
    for padded, before, middle, after, base in (
        (pad_zero, b0x, template, a0x, 0),
        (pad_one, b1x, state, a1x, 0),
        (pad_div, b1x, divergence, a1x, RIM),
    ):
        padded[0:RIM] = before[base : base + RIM].astype(F32)
        padded[RIM : RIM + 32] = middle[...].astype(F32)
        padded[RIM + 32 : 2 * RIM + 32] = after[base : base + RIM].astype(F32)
    for g in range(4):
        zero = (template[8 * g : 8 * g + 8].reshape(256, 256),)
        one = (state[8 * g : 8 * g + 8].reshape(256, 256),)
        div = halves(divergence[8 * g : 8 * g + 8].reshape(256, 256))
        weigh_one = 0.5 * weight_one[8 * g : 8 * g + 8].reshape(256, 256)
        weigh_two = 0.5 * weight_two[8 * g : 8 * g + 8].reshape(256, 256)
        for axis in range(3):
            if axis == 0:
                parts = [difference_x(padded, g) for padded in (pad_zero, pad_one, pad_div)]
            elif axis == 1:
                parts = [
                    difference_y(zero, rim_rows(b0y, a0y, 0, g), along_y, rim_y),
                    difference_y(one, rim_rows(b1y, a1y, 0, g), along_y, rim_y),
                    difference_y(div, rim_rows(b1y, a1y, RIM, g), along_y, rim_y),
                ]
            else:
                parts = [difference_z(value, along_z) for value in (zero, one, div)]
            value = weigh_one * parts[0] + weigh_two * parts[1] - 0.25 * parts[2]
            gradient[axis, 8 * g : 8 * g + 8] = value.reshape(8, 32, 256)


SCALAR = pl.BlockSpec(memory_space=pltpu.SMEM)
WHOLE = pl.BlockSpec(memory_space=pltpu.VMEM)
NEAR = pl.BlockSpec(memory_space=pltpu.VMEM)
ANYWHERE = pl.BlockSpec(memory_space=pl.ANY)
FAR = pl.BlockSpec(memory_space=pltpu.HBM)
FOLDED = (32, 64, 128)
FLAT = (256, 1024)
NATIVE = (32, 32, 256)
FORM = (8, 256, 128)
TABLES = (3, 32, 256)


def pinned(value, spec):
    if spec is FAR:
        return pltpu.with_memory_space_constraint(value, pltpu.HBM)
    if spec is NEAR:
        return pltpu.with_memory_space_constraint(value, pltpu.VMEM)
    return value


SHORT, LONG = 1 << 20, 1 << 36


def call(kernel, out, in_specs, out_specs, scratch, work=LONG):
    made = pl.pallas_call(
        kernel,
        out_shape=out,
        in_specs=in_specs,
        out_specs=out_specs,
        scratch_shapes=scratch,
        compiler_params=pltpu.CompilerParams(vmem_limit_bytes=24 * 1024 * 1024),
        cost_estimate=pl.CostEstimate(flops=work, bytes_accessed=1024 * 1024, transcendentals=0),
    )

    def apply(*values):
        return made(*[pinned(value, spec) for value, spec in zip(values, in_specs, strict=True)])

    return apply


def like(shape, dtype):
    return jax.ShapeDtypeStruct(shape, dtype)


def far(shape, dtype):
    return pltpu.HBM(shape, dtype)


def neighbours(low_x, high_x, low_y, high_y):
    moved = []
    for low, high, axis in ((low_x, high_x, "gx"), (low_y, high_y, "gy")):
        size = lax.axis_size(axis)
        up = [(i, i + 1) for i in range(size - 1)]
        down = [(i + 1, i) for i in range(size - 1)]
        moved += [lax.ppermute(high, axis, up), lax.ppermute(low, axis, down)]
    return moved


def swap_slots(send):
    return lax.all_to_all(send, "gx", split_axis=0, concat_axis=0, tiled=True)


def shards(template, target_image, velocity, operators, route, target_brick, operator_index):
    peers = lax.axis_size("gx")
    shared = 8 * (256 // peers)
    sems = pltpu.SemaphoreType.DMA((16,))
    quarter_sems = pltpu.SemaphoreType.DMA((4, 4))
    turning = [pltpu.VMEM(FLAT, F32), pltpu.VMEM(FOLDED, F32), pltpu.VMEM((512, 1024), BF16)]
    form = pltpu.VMEM(FORM, BF16)
    tables = pltpu.VMEM(TABLES, BF16)
    routes_mem = pltpu.SMEM((peers, 128), jnp.int32)
    stage = pltpu.VMEM((peers, shared, 128), BF16)
    meta_half = pltpu.VMEM((peers, 16, 128), BF16)
    table_rows_count = operators.shape[1] * operators.shape[2] * operators.shape[3]
    listed = operators.transpose(1, 2, 3, 0).reshape(table_rows_count, operators.shape[0])
    listed_mem = pltpu.VMEM(listed.shape, BF16)
    route = route.reshape(route.shape[:4])

    send = call(
        target_kernel,
        far((peers, shared + 16, 128), BF16),
        [FAR] * 4,
        FAR,
        [pltpu.SMEM(route.shape, jnp.int32)] * 3
        + [pltpu.VMEM(NATIVE, BF16), stage, pltpu.VMEM((16, 128), F32), meta_half, sems],
        SHORT,
    )(operator_index, route, target_brick, target_image)
    targets = swap_slots(send)

    moved, tables_zero = call(
        first_kernel,
        [like(FORM, BF16), far(TABLES, BF16)],
        [SCALAR, FAR, FAR, FAR],
        [WHOLE, FAR],
        [listed_mem, pltpu.VMEM(NATIVE, BF16)] + turning + [tables, sems],
    )(operator_index, listed, template, send)
    send, tables_far, codes = call(
        second_kernel,
        [far((peers, 512 + shared, 128), BF16), far(TABLES, BF16), far((peers, 128), jnp.int32)],
        [SCALAR, SCALAR, WHOLE, WHOLE, WHOLE],
        [FAR] * 3,
        [pltpu.VMEM((peers, 16, 128), F32), pltpu.VMEM((peers, 128), jnp.int32)]
        + turning
        + [stage, tables, sems, pltpu.SemaphoreType.DMA((8,))],
        SHORT,
    )(route, target_brick, listed, moved, targets)
    arrived = swap_slots(send)

    rim = like((2 * RIM, 32, 256), BF16)
    low_x, high_x, low_y, high_y = call(
        edge_kernel,
        [rim] * 4,
        [FAR] * 3,
        [WHOLE] * 4,
        [pltpu.VMEM(NATIVE, BF16)] + [pltpu.VMEM((RIM, 32, 256), F32)] * 2 + [pltpu.VMEM(NATIVE, F32), sems],
    )(template, velocity, send)
    tables_one, plan = call(
        prepare_kernel,
        [far(TABLES, BF16), far((peers, 128), jnp.int32)],
        [SCALAR, FAR, WHOLE, WHOLE],
        [WHOLE, FAR],
        [routes_mem, routes_mem, sems],
    )(operator_index, codes, listed, low_x)
    b0x, a0x, b0y, a0y = neighbours(low_x, high_x, low_y, high_y)

    send = call(
        share_kernel,
        far((peers, 2 * shared, 128), BF16),
        [SCALAR, WHOLE, WHOLE],
        FAR,
        [pltpu.VMEM((peers, shared, 128), F32), pltpu.VMEM((peers, 2 * shared, 128), BF16)]
        + [pltpu.SemaphoreType.DMA((peers,))],
        SHORT,
    )(plan, arrived, targets)
    pulled = swap_slots(send)

    divergence = call(
        divergence_kernel, like(NATIVE, F32), [WHOLE] * 5 + [FAR], WHOLE, [pltpu.VMEM((38, 32, 256), F32)]
    )(velocity, b0x, a0x, b0y, a0y, send)
    state, low_x, high_x, low_y, high_y = call(
        rims_kernel,
        [like(NATIVE, BF16)] + [rim] * 4,
        [FAR, ANYWHERE, WHOLE, FAR],
        [WHOLE] * 5,
        [routes_mem, pltpu.VMEM((peers, 512, 128), BF16), pltpu.VMEM(FORM, F32), form] + turning[1:] + [sems],
    )(codes, arrived, divergence, send)
    b1x, a1x, b1y, a1y = neighbours(low_x, high_x, low_y, high_y)
    composed = call(
        composed_kernel, far((peers, shared, 128), BF16), [FAR, FAR, WHOLE], FAR, [routes_mem, stage, stage, sems]
    )(plan, send, low_x)

    composed = swap_slots(composed)

    adjoint_one = call(
        adjoint_kernel, like(FORM, BF16), [FAR, NEAR], WHOLE, [tables] + turning + [sems]
    )(tables_one, pulled)
    gradient = call(
        gradient_kernel,
        far((3,) + NATIVE, F32),
        [WHOLE] * 13,
        WHOLE,
        turning[1:] + [pltpu.VMEM(NATIVE, F32)] * 2 + [pltpu.VMEM((38, 32, 256), F32)] * 3,
    )(template, state, divergence, pulled, adjoint_one, b0x, a0x, b0y, a0y, b1x, a1x, b1y, a1y)

    adjoint = call(
        final_kernel,
        far(NATIVE, BF16),
        [WHOLE, WHOLE, FAR, NEAR],
        FAR,
        turning + [form, pltpu.VMEM(NATIVE, BF16), quarter_sems],
        SHORT,
    )(tables_far, tables_zero, gradient, composed)
    return gradient, adjoint


def solution(mesh):
    placed = (
        P("gx", "gy", None),
        P("gx", "gy", None),
        P(None, "gx", "gy", None),
        P(),
        P(None, "gx", "gy", None, None),
        P(None, "gx", "gy", None),
        P(None, "gx", "gy", None),
    )
    return jax.shard_map(
        shards,
        mesh=mesh,
        in_specs=placed,
        out_specs=(P(None, "gx", "gy", None), P("gx", "gy", None)),
        check_vma=False,
    )
```
